32 devices in a mesh: replica: 2 (over y), fsdp: 4 (over x, core), context: 4 (over z).
Axes of the slice: x: 2, y: 2, z: 4, core: 2. Of those that a mesh axis runs over, the one named last changes fastest.
Arguments:
- tokens: bfloat16 [8, 1024, 2048], P(('replica', 'fsdp'), 'context'), may hold values from -6 to 6
- places: int32 [8, 1024], P(('replica', 'fsdp')), may hold values from 0 to 1023, as said below
- cotangent: bfloat16 [8, 1024, 2048], P(('replica', 'fsdp'), 'context'), may hold values from -6 to 6
- gain_attn: bfloat16 [2048], P(('fsdp', 'context')), may hold values from 0.5 to 1.5
- gain_mlp: bfloat16 [2048], P(('fsdp', 'context')), may hold values from 0.5 to 1.5
- w_query: bfloat16 [2048, 2048], P(('fsdp', 'context')), may hold values from -0.125 to 0.125
- key_projection: bfloat16 [2048, 512], P(('fsdp', 'context')), may hold values from -0.125 to 0.125
- value_projection: bfloat16 [2048, 512], P(('fsdp', 'context')), may hold values from -0.125 to 0.125
- w_out: bfloat16 [2048, 2048], P(('fsdp', 'context')), may hold values from -0.5 to 0.5
- w_gate: bfloat16 [2048, 8192], P(None, ('fsdp', 'context')), may hold values from -0.125 to 0.125
- w_up: bfloat16 [2048, 8192], P(None, ('fsdp', 'context')), may hold values from -0.125 to 0.125
- w_down: bfloat16 [8192, 2048], P(('fsdp', 'context')), may hold values from -0.0625 to 0.0625
Outputs:
- out: bfloat16 [8, 1024, 2048], P(('replica', 'fsdp'), 'context')
- grad_tokens: bfloat16 [8, 1024, 2048], P(('replica', 'fsdp'), 'context')
- grad_w_query: float32 [2048, 2048], P(('fsdp', 'context'))
- grad_w_key: float32 [2048, 512], P(('fsdp', 'context'))
- grad_w_value: float32 [2048, 512], P(('fsdp', 'context'))
- grad_w_out: float32 [2048, 2048], P(('fsdp', 'context'))
- grad_w_gate: float32 [2048, 8192], P(None, ('fsdp', 'context'))
- grad_w_up: float32 [2048, 8192], P(None, ('fsdp', 'context'))
- grad_w_down: float32 [8192, 2048], P(('fsdp', 'context'))
- grad_gain_attn: float32 [2048], P(('fsdp', 'context'))
- grad_gain_mlp: float32 [2048], P(('fsdp', 'context'))
The draws below stay inside these ranges and needn't reach their ends.
Inputs may be any that keep to these rules, and one draw needn't show every extreme that they name: `places`: each row lists every position of its sequence once, in 8 runs of 128 consecutive ascending positions; the order of the runs varies from sequence to sequence.
All inputs are finite; a program needn't handle non-finite values.
Results may differ from the reference program's by a relative error of at most 0.018.
Values may be sent and summed in bfloat16 or wider, within the bound.
A program may use at most 512 MiB of HBM per device.

```python
import math
import jax
import jax.numpy as jnp
from jax import lax

MODEL_WIDTH = 2048
QUERY_HEADS = 32
KEY_VALUE_HEADS = 8
HEAD_SIZE = 64
FF = 8192
LEN = 1024
PIECES = 8
SEQS = 8


def draw_places(key, part):
    key = jax.random.fold_in(key, 11)
    run_length = LEN // PIECES
    seq_keys = jax.random.split(key, SEQS)
    orders = jax.vmap(lambda seq_key: jax.random.permutation(seq_key, PIECES))(seq_keys)
    offsets = jnp.arange(run_length, dtype=jnp.int32)
    spots = orders.astype(jnp.int32)[:, :, None] * run_length + offsets[None, None, :]
    return spots.reshape(SEQS, LEN).astype(jnp.int32)


def block_levels(rng, shape, pieces, low, top_value):
    level, own = 1.0, jax.random.fold_in(rng, 6)
    for position, blocks in pieces:
        draws = jnp.exp(jax.random.uniform(jax.random.fold_in(own, position), (blocks,), jnp.float32, low / len(pieces), top_value / len(pieces)))
        level = level * jnp.repeat(draws, shape[position] // blocks).reshape([-1 if axis == position else 1 for axis in range(len(shape))])
    return level


def scatter_about(stream_key, dims, scale, bound, pieces=(), kind=jnp.bfloat16):
    values = scale * jax.random.normal(stream_key, dims, jnp.float32)
    if pieces:
        values = values * block_levels(stream_key, dims, pieces, -0.22, 0.18)
    return jnp.clip(values, -bound, bound).astype(kind)


def setup_inputs(seed: int = 0) -> dict:
    key_of = jax.random.split(jax.random.key(seed), 13)
    tokens = scatter_about(key_of[0], (SEQS, LEN, MODEL_WIDTH), 1.0, 6.0, ((0, 8), (1, 4)))
    places = draw_places(jax.random.fold_in(key_of[12], 71), 0)
    cotangent = scatter_about(key_of[2], (SEQS, LEN, MODEL_WIDTH), 1.0, 6.0, ((0, 8), (1, 4)))
    gain_attn = jnp.clip(1.0 + 0.1 * jax.random.normal(key_of[3], (MODEL_WIDTH,), jnp.float32), 0.5, 1.5).astype(jnp.bfloat16)
    gain_mlp = jnp.clip(1.0 + 0.1 * jax.random.normal(key_of[4], (MODEL_WIDTH,), jnp.float32), 0.5, 1.5).astype(jnp.bfloat16)
    w_query = scatter_about(key_of[5], (MODEL_WIDTH, QUERY_HEADS * HEAD_SIZE), MODEL_WIDTH ** -0.5, 0.125, ((0, 16),))
    key_projection = scatter_about(key_of[6], (MODEL_WIDTH, KEY_VALUE_HEADS * HEAD_SIZE), MODEL_WIDTH ** -0.5, 0.125, ((0, 16),))
    value_projection = scatter_about(key_of[7], (MODEL_WIDTH, KEY_VALUE_HEADS * HEAD_SIZE), MODEL_WIDTH ** -0.5, 0.125, ((0, 16),))
    w_out = scatter_about(key_of[8], (QUERY_HEADS * HEAD_SIZE, MODEL_WIDTH), (QUERY_HEADS * HEAD_SIZE // 16) ** -0.5, 0.5, ((0, 16),))
    w_gate = scatter_about(key_of[9], (MODEL_WIDTH, FF), MODEL_WIDTH ** -0.5, 0.125, ((1, 16),))
    w_up = scatter_about(key_of[10], (MODEL_WIDTH, FF), MODEL_WIDTH ** -0.5, 0.125, ((1, 16),))
    w_down = scatter_about(key_of[11], (FF, MODEL_WIDTH), FF ** -0.5, 0.0625, ((0, 16),))
    return dict(tokens=tokens, places=places, cotangent=cotangent, gain_attn=gain_attn, gain_mlp=gain_mlp, w_query=w_query, key_projection=key_projection, value_projection=value_projection, w_out=w_out, w_gate=w_gate, w_up=w_up, w_down=w_down)


norm_eps = 1e-05
rope_base = 500000.0
exact = lax.Precision.HIGHEST

@jax.custom_vjp
def reduced_precision(v):
    return lax.optimization_barrier(v.astype(jnp.bfloat16)).astype(jnp.float32)

@jax.custom_vjp
def reduced_backward(v):
    return v

def low_keep(v):
    return (reduced_precision(v), None)

def low_pass(kept, grad):
    return (grad,)

def back_keep(v):
    return (v, None)

def back_low(kept, grad):
    return (reduced_precision(grad),)
reduced_precision.defvjp(low_keep, low_pass)
reduced_backward.defvjp(back_keep, back_low)

def frequencies(half):
    return rope_base ** (-2.0 * jnp.arange(half, dtype=jnp.float32) / (2.0 * half))

def apply_rotary(angle_table, rotary_angles):
    half = angle_table.shape[-1] // 2
    first_half = angle_table[..., :half]
    second_half = angle_table[..., half:]
    cosine = jnp.cos(rotary_angles)[..., None, :]
    sine = jnp.sin(rotary_angles)[..., None, :]
    return jnp.concatenate([first_half * cosine - second_half * sine, second_half * cosine + first_half * sine], axis=-1)

def rms_norm(angle_table, gain):
    factor = lax.rsqrt(lax.optimization_barrier(jnp.mean(angle_table * angle_table, axis=-1, keepdims=True)) + norm_eps)
    return angle_table * factor * gain

def apply_projection(angle_table, matrix):
    return jnp.einsum('gtd,de->gte', angle_table, matrix, precision=exact)

def head_group(query_rows, key_matrix_rows, value_matrix_rows, allowed):
    scores = jnp.einsum('gqrd,gkd->grqk', query_rows, key_matrix_rows, precision=exact) * HEAD_SIZE ** (-0.5)
    scores = reduced_backward(scores)
    scores = jnp.where(allowed[:, None], scores, -1e+30)
    weights = reduced_precision(jax.nn.softmax(scores, axis=-1))
    return jnp.einsum('grqk,gkd->gqrd', weights, value_matrix_rows, precision=exact)

def layer(tokens_f, places, gain_attn, gain_mlp, w_query, key_projection, value_projection, w_out, w_gate, w_up, w_down):
    query_groups, sequence_length, width = tokens_f.shape
    expand_heads = QUERY_HEADS // KEY_VALUE_HEADS
    rotary_angles = places.astype(jnp.float32)[..., None] * frequencies(HEAD_SIZE // 2)
    normed_tokens = reduced_precision(rms_norm(tokens_f, gain_attn))
    query_rows = reduced_backward(apply_projection(normed_tokens, w_query)).reshape(query_groups, sequence_length, QUERY_HEADS, HEAD_SIZE)
    key_matrix_rows = reduced_backward(apply_projection(normed_tokens, key_projection)).reshape(query_groups, sequence_length, KEY_VALUE_HEADS, HEAD_SIZE)
    value_matrix_rows = reduced_precision(reduced_backward(apply_projection(normed_tokens, value_projection))).reshape(query_groups, sequence_length, KEY_VALUE_HEADS, HEAD_SIZE)
    query_rows = reduced_precision(apply_rotary(query_rows, rotary_angles))
    key_matrix_rows = reduced_precision(apply_rotary(key_matrix_rows, rotary_angles))
    allowed = places[:, None, :] <= places[:, :, None]
    query_head_rows = jnp.transpose(query_rows.reshape(query_groups, sequence_length, KEY_VALUE_HEADS, expand_heads, HEAD_SIZE), (2, 0, 1, 3, 4))
    key_heads = jnp.transpose(key_matrix_rows, (2, 0, 1, 3))
    value_heads = jnp.transpose(value_matrix_rows, (2, 0, 1, 3))

    def one_head(head_items):
        return head_group(head_items[0], head_items[1], head_items[2], allowed)
    attended = lax.map(jax.checkpoint(one_head), (query_head_rows, key_heads, value_heads))
    attended = jnp.transpose(attended, (1, 2, 0, 3, 4)).reshape(query_groups, sequence_length, QUERY_HEADS * HEAD_SIZE)
    attended = reduced_precision(reduced_backward(attended))
    middle = tokens_f + reduced_backward(apply_projection(attended, w_out))
    normed_mlp = reduced_precision(rms_norm(middle, gain_mlp))
    gate_pre = reduced_backward(apply_projection(normed_mlp, w_gate))
    up_proj = reduced_backward(apply_projection(normed_mlp, w_up))
    hidden = reduced_precision(jax.nn.silu(gate_pre) * up_proj)
    return middle + reduced_backward(apply_projection(hidden, w_down))

def reference(tokens, places, cotangent, gain_attn, gain_mlp, w_query, key_projection, value_projection, w_out, w_gate, w_up, w_down):
    params = tuple((param.astype(jnp.float32) for param in (gain_attn, gain_mlp, w_query, key_projection, value_projection, w_out, w_gate, w_up, w_down)))
    group_size = math.gcd(SEQS, 4)
    block_count = SEQS // group_size
    token_blocks = tokens.astype(jnp.float32).reshape(block_count, group_size, LEN, MODEL_WIDTH)
    place_blocks = places.reshape(block_count, group_size, LEN)
    tangent_blocks = cotangent.astype(jnp.float32).reshape(block_count, group_size, LEN, MODEL_WIDTH)

    def one_block(totals, inputs):
        token_part, place_part, tangent_part = inputs

        def forward(angle_table, *weights):
            return layer(angle_table, place_part, *weights)
        result, pullback = jax.vjp(forward, token_part, *params)
        grads = pullback(tangent_part)
        totals = tuple((running + update for running, update in zip(totals, grads[1:])))
        return (totals, (result.astype(jnp.bfloat16), grads[0].astype(jnp.bfloat16)))
    start = tuple((jnp.zeros(param.shape, jnp.float32) for param in params))
    totals, (results, token_grads) = lax.scan(one_block, start, (token_blocks, place_blocks, tangent_blocks))
    out = results.reshape(SEQS, LEN, MODEL_WIDTH)
    grad_tokens = token_grads.reshape(SEQS, LEN, MODEL_WIDTH)
    return (out, grad_tokens, totals[2], totals[3], totals[4], totals[5], totals[6], totals[7], totals[8], totals[0], totals[1])
```

```python
import jax
import jax.numpy as jnp
from jax import lax
from jax.sharding import PartitionSpec as P

QUERY_HEADS = 32
KEY_VALUE_HEADS = 8
HEAD_SIZE = 64


norm_eps = 1e-05
rope_base = 500000.0


def frequencies(half):
    return rope_base ** (-2.0 * jnp.arange(half, dtype=jnp.float32) / (2.0 * half))


def apply_rotary(angle_table, rotary_angles):
    half = angle_table.shape[-1] // 2
    first_half = angle_table[..., :half]
    second_half = angle_table[..., half:]
    cosine = jnp.cos(rotary_angles)[..., None, :]
    sine = jnp.sin(rotary_angles)[..., None, :]
    return jnp.concatenate(
        [first_half * cosine - second_half * sine, second_half * cosine + first_half * sine],
        axis=-1,
    )


def inverse_rotary(angle_table, rotary_angles):
    half = angle_table.shape[-1] // 2
    first_half = angle_table[..., :half]
    second_half = angle_table[..., half:]
    cosine = jnp.cos(rotary_angles)[..., None, :]
    sine = jnp.sin(rotary_angles)[..., None, :]
    return jnp.concatenate(
        [first_half * cosine + second_half * sine, second_half * cosine - first_half * sine],
        axis=-1,
    )


def times_t(left, right):
    return lax.dot_general(
        left, right, (((0,), (0,)), ((), ())), preferred_element_type=jnp.float32
    )


def times_nt(left, right):
    return lax.dot_general(
        left, right, (((1,), (1,)), ((), ())), preferred_element_type=jnp.float32
    )


def query_head_rows(angle_table, sequence_total, segment_length):
    reshaped_heads = angle_table.reshape(
        sequence_total, segment_length, KEY_VALUE_HEADS, QUERY_HEADS // KEY_VALUE_HEADS, HEAD_SIZE
    )
    return jnp.transpose(reshaped_heads, (0, 2, 1, 3, 4)).reshape(
        sequence_total * KEY_VALUE_HEADS, segment_length, QUERY_HEADS // KEY_VALUE_HEADS, HEAD_SIZE
    )


def key_heads(angle_table, sequence_total, total_length):
    reshaped_heads = angle_table.reshape(sequence_total, total_length, KEY_VALUE_HEADS, HEAD_SIZE)
    return jnp.transpose(reshaped_heads, (0, 2, 1, 3)).reshape(
        sequence_total * KEY_VALUE_HEADS, total_length, HEAD_SIZE
    )


def merge_queries(angle_table, sequence_total, segment_length):
    reshaped_heads = angle_table.reshape(
        sequence_total, KEY_VALUE_HEADS, segment_length, QUERY_HEADS // KEY_VALUE_HEADS, HEAD_SIZE
    )
    return jnp.transpose(reshaped_heads, (0, 2, 1, 3, 4)).reshape(
        sequence_total * segment_length, QUERY_HEADS * HEAD_SIZE
    )


def merge_keys(angle_table, sequence_total, total_length):
    reshaped_heads = angle_table.reshape(sequence_total, KEY_VALUE_HEADS, total_length, HEAD_SIZE)
    return jnp.transpose(reshaped_heads, (0, 2, 1, 3)).reshape(
        sequence_total, total_length, KEY_VALUE_HEADS * HEAD_SIZE
    )


def softmax_weights(part_query, part_key, place_query, place_key):
    allowed = place_key[None, :] <= place_query[:, None]
    scores = jnp.einsum(
        "qrd,kd->rqk", part_query, part_key, preferred_element_type=jnp.float32
    ) * HEAD_SIZE ** (-0.5)
    scores = jnp.where(allowed[None], scores, -1e30)
    return jax.nn.softmax(scores, axis=-1)


def forward_head(packed):
    part_query, part_key, part_value, place_query, place_key = packed
    probs = softmax_weights(part_query, part_key, place_query, place_key)
    return jnp.einsum(
        "rqk,kd->qrd", probs.astype(jnp.bfloat16), part_value, preferred_element_type=jnp.float32
    )


def backward_head(packed):
    part_query, part_key, part_value, part_grad, place_query, place_key = packed
    probs = softmax_weights(part_query, part_key, place_query, place_key)
    grad_probs = jnp.einsum(
        "qrd,kd->rqk", part_grad, part_value, preferred_element_type=jnp.float32
    )
    row_delta = jnp.sum(probs * grad_probs, axis=-1, keepdims=True)
    grad_scores = (probs * (grad_probs - row_delta)).astype(jnp.bfloat16)
    grad_query = jnp.einsum(
        "rqk,kd->qrd", grad_scores, part_key, preferred_element_type=jnp.float32
    ) * HEAD_SIZE ** (-0.5)
    grad_key = jnp.einsum(
        "rqk,qrd->kd", grad_scores, part_query, preferred_element_type=jnp.float32
    ) * HEAD_SIZE ** (-0.5)
    value_gradient = jnp.einsum(
        "rqk,qrd->kd", probs.astype(jnp.bfloat16), part_grad, preferred_element_type=jnp.float32
    )
    return (grad_query, grad_key, value_gradient)


def feed_forward(normed_rows, gate_w, up_w, down_w):
    gate_pre = jnp.dot(normed_rows, gate_w, preferred_element_type=jnp.float32)
    up_proj = jnp.dot(normed_rows, up_w, preferred_element_type=jnp.float32)
    sigmoid_gate = jax.nn.sigmoid(gate_pre)
    hidden = (gate_pre * sigmoid_gate * up_proj).astype(jnp.bfloat16)
    return (
        jnp.dot(hidden, down_w, preferred_element_type=jnp.float32),
        (gate_pre, up_proj, sigmoid_gate, hidden),
    )


def feed_back(normed_rows, grad_rows, gate_w, up_w, down_w, kept_values):
    gate_pre, up_proj, sigmoid_gate, hidden = kept_values
    grad_hidden = times_nt(grad_rows, down_w)
    term_down = times_t(hidden, grad_rows)
    grad_gate = (
        grad_hidden * up_proj * (sigmoid_gate * (1.0 + gate_pre * (1.0 - sigmoid_gate)))
    ).astype(jnp.bfloat16)
    grad_up = (grad_hidden * (gate_pre * sigmoid_gate)).astype(jnp.bfloat16)
    grad_normed = times_nt(grad_gate, gate_w) + times_nt(grad_up, up_w)
    return (grad_normed, times_t(normed_rows, grad_gate), times_t(normed_rows, grad_up), term_down)


def body(
    tokens,
    places,
    cotangent,
    gain_attn,
    gain_mlp,
    w_query,
    key_projection,
    value_projection,
    w_out,
    w_gate,
    w_up,
    w_down,
):
    sequence_total, segment_length, width = tokens.shape
    total_length = places.shape[1]
    total_rows = sequence_total * segment_length
    position = lax.axis_index("context")
    local_positions = lax.dynamic_slice_in_dim(places, position * segment_length, segment_length, 1)
    rotary_angles = local_positions.reshape(total_rows).astype(jnp.float32)[:, None] * frequencies(
        HEAD_SIZE // 2
    )
    gain_one, gain_two, query_w, key_weight_local, value_w, out_w = (
        lax.all_gather(gain_attn, ("fsdp", "context"), axis=0, tiled=True),
        lax.all_gather(gain_mlp, ("fsdp", "context"), axis=0, tiled=True),
        lax.all_gather(w_query, ("fsdp", "context"), axis=0, tiled=True),
        lax.all_gather(key_projection, ("fsdp", "context"), axis=0, tiled=True),
        lax.all_gather(value_projection, ("fsdp", "context"), axis=0, tiled=True),
        lax.all_gather(w_out, ("fsdp", "context"), axis=0, tiled=True),
    )
    gain_first = gain_one.astype(jnp.float32)
    gain_second = gain_two.astype(jnp.float32)
    inputs_f = tokens.astype(jnp.float32).reshape(total_rows, width)
    factor_one = lax.rsqrt(jnp.mean(inputs_f * inputs_f, axis=-1, keepdims=True) + norm_eps)
    unit_one = inputs_f * factor_one
    normed_tokens = (unit_one * gain_first).astype(jnp.bfloat16)
    query_pre = jnp.dot(normed_tokens, query_w, preferred_element_type=jnp.float32).reshape(
        total_rows, QUERY_HEADS, HEAD_SIZE
    )
    key_unrotated = jnp.dot(
        normed_tokens, key_weight_local, preferred_element_type=jnp.float32
    ).reshape(total_rows, KEY_VALUE_HEADS, HEAD_SIZE)
    value_matrix_rows = jnp.dot(normed_tokens, value_w, preferred_element_type=jnp.float32).astype(
        jnp.bfloat16
    )
    query_rows = apply_rotary(query_pre, rotary_angles).astype(jnp.bfloat16)
    key_matrix_rows = (
        apply_rotary(key_unrotated, rotary_angles)
        .astype(jnp.bfloat16)
        .reshape(sequence_total, segment_length, KEY_VALUE_HEADS * HEAD_SIZE)
    )
    key_all, value_all = (
        lax.all_gather(key_matrix_rows, "context", axis=1, tiled=True),
        lax.all_gather(
            value_matrix_rows.reshape(sequence_total, segment_length, KEY_VALUE_HEADS * HEAD_SIZE),
            "context",
            axis=1,
            tiled=True,
        ),
    )
    head_query = query_head_rows(query_rows, sequence_total, segment_length)
    head_key = key_heads(key_all, sequence_total, total_length)
    head_value = key_heads(value_all, sequence_total, total_length)
    query_positions = jnp.repeat(local_positions, KEY_VALUE_HEADS, axis=0)
    key_positions = jnp.repeat(places, KEY_VALUE_HEADS, axis=0)
    attended = lax.map(
        forward_head, (head_query, head_key, head_value, query_positions, key_positions)
    )
    attended = merge_queries(attended, sequence_total, segment_length).astype(jnp.bfloat16)
    middle = inputs_f + jnp.dot(attended, out_w, preferred_element_type=jnp.float32)
    factor_two = lax.rsqrt(jnp.mean(middle * middle, axis=-1, keepdims=True) + norm_eps)
    unit_two = middle * factor_two
    normed_mlp = (unit_two * gain_second).astype(jnp.bfloat16)
    tangent = cotangent.reshape(total_rows, width)
    tangent_f = tangent.astype(jnp.float32)
    group = ("fsdp", "context")
    normed_all = lax.all_gather(normed_mlp, group, axis=0, tiled=True)
    tangent_all = lax.all_gather(tangent, group, axis=0, tiled=True)
    branch_part, kept_values = feed_forward(normed_all, w_gate, w_up, w_down)
    grad_part, grad_w_gate, grad_w_up, grad_w_down = feed_back(
        normed_all, tangent_all, w_gate, w_up, w_down, kept_values
    )
    grad_normed = lax.psum_scatter(
        grad_part.astype(jnp.bfloat16), group, scatter_dimension=0, tiled=True
    ).astype(jnp.float32)
    branch = lax.psum_scatter(
        branch_part.astype(jnp.bfloat16), group, scatter_dimension=0, tiled=True
    ).astype(jnp.float32)
    outcome = middle + branch
    scaled_two = grad_normed * gain_second
    term_gain_two = jnp.sum(grad_normed * unit_two, axis=0)
    grad_middle = tangent_f + factor_two * (
        scaled_two - unit_two * jnp.mean(scaled_two * unit_two, axis=-1, keepdims=True)
    )
    grad_branch = grad_middle.astype(jnp.bfloat16)
    term_out = times_t(attended, grad_branch)
    grad_attended = times_nt(grad_branch, out_w).astype(jnp.bfloat16)
    head_grad = query_head_rows(grad_attended, sequence_total, segment_length)
    grad_q, grad_k, grad_v = lax.map(
        backward_head, (head_query, head_key, head_value, head_grad, query_positions, key_positions)
    )
    local_key_gradient, local_value_gradient = (
        lax.psum_scatter(
            merge_keys(grad_k, sequence_total, total_length).astype(jnp.bfloat16),
            "context",
            scatter_dimension=1,
            tiled=True,
        ).astype(jnp.float32),
        lax.psum_scatter(
            merge_keys(grad_v, sequence_total, total_length).astype(jnp.bfloat16),
            "context",
            scatter_dimension=1,
            tiled=True,
        ).astype(jnp.float32),
    )
    grad_query = (
        inverse_rotary(
            merge_queries(grad_q, sequence_total, segment_length).reshape(
                total_rows, QUERY_HEADS, HEAD_SIZE
            ),
            rotary_angles,
        )
        .reshape(total_rows, QUERY_HEADS * HEAD_SIZE)
        .astype(jnp.bfloat16)
    )
    grad_key = (
        inverse_rotary(
            local_key_gradient.reshape(total_rows, KEY_VALUE_HEADS, HEAD_SIZE), rotary_angles
        )
        .reshape(total_rows, KEY_VALUE_HEADS * HEAD_SIZE)
        .astype(jnp.bfloat16)
    )
    value_gradient = local_value_gradient.reshape(total_rows, KEY_VALUE_HEADS * HEAD_SIZE).astype(
        jnp.bfloat16
    )
    grad_normed_one = (
        times_nt(grad_query, query_w)
        + times_nt(grad_key, key_weight_local)
        + times_nt(value_gradient, value_w)
    )
    term_query = times_t(normed_tokens, grad_query)
    term_key = times_t(normed_tokens, grad_key)
    term_value = times_t(normed_tokens, value_gradient)
    scaled_one = grad_normed_one * gain_first
    term_gain_one = jnp.sum(grad_normed_one * unit_one, axis=0)
    grad_inputs = grad_middle + factor_one * (
        scaled_one - unit_one * jnp.mean(scaled_one * unit_one, axis=-1, keepdims=True)
    )
    share_query, share_key, share_value, share_out, share_gain_one, share_gain_two = (
        lax.psum_scatter(term_query.astype(jnp.bfloat16), ("fsdp", "context"), scatter_dimension=0, tiled=True),
        lax.psum_scatter(term_key.astype(jnp.bfloat16), ("fsdp", "context"), scatter_dimension=0, tiled=True),
        lax.psum_scatter(term_value.astype(jnp.bfloat16), ("fsdp", "context"), scatter_dimension=0, tiled=True),
        lax.psum_scatter(term_out.astype(jnp.bfloat16), ("fsdp", "context"), scatter_dimension=0, tiled=True),
        lax.psum_scatter(term_gain_one, ("fsdp", "context"), scatter_dimension=0, tiled=True),
        lax.psum_scatter(term_gain_two, ("fsdp", "context"), scatter_dimension=0, tiled=True),
    )
    summed = (
        lax.psum(share_query.astype(jnp.bfloat16), "replica").astype(jnp.float32),
        lax.psum(share_key.astype(jnp.bfloat16), "replica").astype(jnp.float32),
        lax.psum(share_value.astype(jnp.bfloat16), "replica").astype(jnp.float32),
        lax.psum(share_out.astype(jnp.bfloat16), "replica").astype(jnp.float32),
        lax.psum(grad_w_gate.astype(jnp.bfloat16), "replica").astype(jnp.float32),
        lax.psum(grad_w_up.astype(jnp.bfloat16), "replica").astype(jnp.float32),
        lax.psum(grad_w_down.astype(jnp.bfloat16), "replica").astype(jnp.float32),
        lax.psum(share_gain_one.astype(jnp.bfloat16), "replica").astype(jnp.float32),
        lax.psum(share_gain_two.astype(jnp.bfloat16), "replica").astype(jnp.float32),
    )
    out = outcome.astype(jnp.bfloat16).reshape(sequence_total, segment_length, width)
    grad_tokens = grad_inputs.astype(jnp.bfloat16).reshape(sequence_total, segment_length, width)
    return (
        out,
        grad_tokens,
        summed[0],
        summed[1],
        summed[2],
        summed[3],
        summed[4],
        summed[5],
        summed[6],
        summed[7],
        summed[8],
    )


def solution(mesh):
    placed = (
        P(("replica", "fsdp"), "context", None),
        P(("replica", "fsdp"), None),
        P(("replica", "fsdp"), "context", None),
        P(("fsdp", "context")),
        P(("fsdp", "context")),
        P(("fsdp", "context"), None),
        P(("fsdp", "context"), None),
        P(("fsdp", "context"), None),
        P(("fsdp", "context"), None),
        P(None, ("fsdp", "context")),
        P(None, ("fsdp", "context")),
        P(("fsdp", "context"), None),
    )
    return jax.shard_map(
        body,
        mesh=mesh,
        in_specs=placed,
        out_specs=(
            P(("replica", "fsdp"), "context", None),
            P(("replica", "fsdp"), "context", None),
            P(("fsdp", "context"), None),
            P(("fsdp", "context"), None),
            P(("fsdp", "context"), None),
            P(("fsdp", "context"), None),
            P(None, ("fsdp", "context")),
            P(None, ("fsdp", "context")),
            P(("fsdp", "context"), None),
            P(("fsdp", "context")),
            P(("fsdp", "context")),
        ),
        check_vma=False,
    )
```

```python
import functools

import jax
import jax.numpy as jnp
from jax import lax
from jax.experimental import pallas as pl
from jax.experimental.pallas import tpu as pltpu
from jax.sharding import PartitionSpec as P

QUERY_HEADS = 32
KEY_VALUE_HEADS = 8
HEAD_SIZE = 64


norm_eps = 1e-05
rope_base = 500000.0


def frequencies(half):
    return rope_base ** (-2.0 * jnp.arange(half, dtype=jnp.float32) / (2.0 * half))


def apply_rotary(angle_table, rotary_angles):
    half = angle_table.shape[-1] // 2
    first_half = angle_table[..., :half]
    second_half = angle_table[..., half:]
    cosine = jnp.cos(rotary_angles)[..., None, :]
    sine = jnp.sin(rotary_angles)[..., None, :]
    return jnp.concatenate(
        [first_half * cosine - second_half * sine, second_half * cosine + first_half * sine],
        axis=-1,
    )


def inverse_rotary(angle_table, rotary_angles):
    half = angle_table.shape[-1] // 2
    first_half = angle_table[..., :half]
    second_half = angle_table[..., half:]
    cosine = jnp.cos(rotary_angles)[..., None, :]
    sine = jnp.sin(rotary_angles)[..., None, :]
    return jnp.concatenate(
        [first_half * cosine + second_half * sine, second_half * cosine - first_half * sine],
        axis=-1,
    )


def times_t(left, right):
    return lax.dot_general(
        left, right, (((0,), (0,)), ((), ())), preferred_element_type=jnp.float32
    )


def times_nt(left, right):
    return lax.dot_general(
        left, right, (((1,), (1,)), ((), ())), preferred_element_type=jnp.float32
    )


def query_head_rows(angle_table, sequence_total, segment_length):
    reshaped_heads = angle_table.reshape(
        sequence_total, segment_length, KEY_VALUE_HEADS, QUERY_HEADS // KEY_VALUE_HEADS, HEAD_SIZE
    )
    return jnp.transpose(reshaped_heads, (0, 2, 1, 3, 4)).reshape(
        sequence_total * KEY_VALUE_HEADS, segment_length, QUERY_HEADS // KEY_VALUE_HEADS, HEAD_SIZE
    )


def key_heads(angle_table, sequence_total, total_length):
    reshaped_heads = angle_table.reshape(sequence_total, total_length, KEY_VALUE_HEADS, HEAD_SIZE)
    return jnp.transpose(reshaped_heads, (0, 2, 1, 3)).reshape(
        sequence_total * KEY_VALUE_HEADS, total_length, HEAD_SIZE
    )


def merge_queries(angle_table, sequence_total, segment_length):
    reshaped_heads = angle_table.reshape(
        sequence_total, KEY_VALUE_HEADS, segment_length, QUERY_HEADS // KEY_VALUE_HEADS, HEAD_SIZE
    )
    return jnp.transpose(reshaped_heads, (0, 2, 1, 3, 4)).reshape(
        sequence_total * segment_length, QUERY_HEADS * HEAD_SIZE
    )


def merge_keys(angle_table, sequence_total, total_length):
    reshaped_heads = angle_table.reshape(sequence_total, KEY_VALUE_HEADS, total_length, HEAD_SIZE)
    return jnp.transpose(reshaped_heads, (0, 2, 1, 3)).reshape(
        sequence_total, total_length, KEY_VALUE_HEADS * HEAD_SIZE
    )


def softmax_weights(part_query, part_key, place_query, place_key):
    allowed = place_key[None, :] <= place_query[:, None]
    scores = jnp.einsum(
        "qrd,kd->rqk", part_query, part_key, preferred_element_type=jnp.float32
    ) * HEAD_SIZE ** (-0.5)
    scores = jnp.where(allowed[None], scores, -1e30)
    return jax.nn.softmax(scores, axis=-1)


def forward_head(packed):
    part_query, part_key, part_value, place_query, place_key = packed
    probs = softmax_weights(part_query, part_key, place_query, place_key)
    return jnp.einsum(
        "rqk,kd->qrd", probs.astype(jnp.bfloat16), part_value, preferred_element_type=jnp.float32
    )


def backward_head(packed):
    part_query, part_key, part_value, part_grad, place_query, place_key = packed
    probs = softmax_weights(part_query, part_key, place_query, place_key)
    grad_probs = jnp.einsum(
        "qrd,kd->rqk", part_grad, part_value, preferred_element_type=jnp.float32
    )
    row_delta = jnp.sum(probs * grad_probs, axis=-1, keepdims=True)
    grad_scores = (probs * (grad_probs - row_delta)).astype(jnp.bfloat16)
    grad_query = jnp.einsum(
        "rqk,kd->qrd", grad_scores, part_key, preferred_element_type=jnp.float32
    ) * HEAD_SIZE ** (-0.5)
    grad_key = jnp.einsum(
        "rqk,qrd->kd", grad_scores, part_query, preferred_element_type=jnp.float32
    ) * HEAD_SIZE ** (-0.5)
    value_gradient = jnp.einsum(
        "rqk,qrd->kd", probs.astype(jnp.bfloat16), part_grad, preferred_element_type=jnp.float32
    )
    return (grad_query, grad_key, value_gradient)


def feed_forward(normed_rows, gate_w, up_w, down_w):
    gate_pre = jnp.dot(normed_rows, gate_w, preferred_element_type=jnp.float32)
    up_proj = jnp.dot(normed_rows, up_w, preferred_element_type=jnp.float32)
    sigmoid_gate = jax.nn.sigmoid(gate_pre)
    hidden = (gate_pre * sigmoid_gate * up_proj).astype(jnp.bfloat16)
    return (
        jnp.dot(hidden, down_w, preferred_element_type=jnp.float32),
        (gate_pre, up_proj, sigmoid_gate, hidden),
    )


def feed_back(normed_rows, grad_rows, gate_w, up_w, down_w, kept_values):
    gate_pre, up_proj, sigmoid_gate, hidden = kept_values
    grad_hidden = times_nt(grad_rows, down_w)
    term_down = times_t(hidden, grad_rows)
    grad_gate = (
        grad_hidden * up_proj * (sigmoid_gate * (1.0 + gate_pre * (1.0 - sigmoid_gate)))
    ).astype(jnp.bfloat16)
    grad_up = (grad_hidden * (gate_pre * sigmoid_gate)).astype(jnp.bfloat16)
    grad_normed = times_nt(grad_gate, gate_w) + times_nt(grad_up, up_w)
    return (grad_normed, times_t(normed_rows, grad_gate), times_t(normed_rows, grad_up), term_down)


MESH = pl.DeviceIdType.MESH
ANY = pl.BlockSpec(memory_space=pl.ANY)
BF = jnp.bfloat16
F32 = jnp.float32
NN = (((1,), (0,)), ((), ()))
NT = (((1,), (1,)), ((), ()))
TN = (((0,), (0,)), ((), ()))


def dot(left, right, dims):
    return lax.dot_general(left, right, dims, preferred_element_type=F32)


class Grid:
    def __init__(self, chips, line):
        self.chips, self.line = chips, line
        self.replica = lax.axis_index("replica")
        flat = lax.axis_index("fsdp")
        self.x, self.core = flat // 2, flat % 2
        self.z = lax.axis_index("context")
        self.has_left, self.has_right = self.z > 0, self.z + 1 < line
        self.left = (self.replica, flat, self.z - 1)
        self.right = (self.replica, flat, self.z + 1)
        self.across = (self.replica, (1 - self.x) * 2 + self.core, self.z)
        self.twin = (self.replica, self.x * 2 + 1 - self.core, self.z)

    def order(self, k):
        z, n = self.z, self.line
        near = 2 * jnp.minimum(z, n - 1 - z)
        alternate = jnp.where(k % 2 == 1, z - (k + 1) // 2, z + k // 2)
        return jnp.where(k <= near, alternate, jnp.where(2 * z < n, k, n - 1 - k))

    def slot(self, x, z):
        return x * self.line + z

    def greet(self, twin):
        barrier = pltpu.get_barrier_semaphore()

        def tell(device):
            pl.semaphore_signal(barrier, inc=1, device_id=device, device_id_type=MESH)

        pl.when(self.has_left)(lambda: tell(self.left))
        pl.when(self.has_right)(lambda: tell(self.right))
        tell(self.across)
        if twin:
            tell(self.twin)
        count = 1 + int(twin) + self.has_left.astype(jnp.int32) + self.has_right.astype(jnp.int32)
        pl.semaphore_wait(barrier, count)


def remote(src, dst, send, recv, device):
    return pltpu.make_async_remote_copy(
        src_ref=src, dst_ref=dst, send_sem=send, recv_sem=recv, device_id=device, device_id_type=MESH
    )


class Gather:
    def __init__(self, grid, everything, send, recv, parts):
        self.grid, self.everything, self.send, self.recv = grid, everything, send, recv
        self.parts = parts
        self.rows = everything.shape[1] // parts

    def piece(self, x, z, part):
        return self.everything.at[self.grid.slot(x, z), pl.ds(part * self.rows, self.rows)]

    def copy(self, z, part, link):
        grid = self.grid
        device = (grid.right, grid.left, grid.across)[link]
        here = self.piece(grid.x, z, part)
        return remote(
            here, here, self.send.at[z, part, link], self.recv.at[grid.slot(grid.x, z), part], device
        )

    def links(self, z, action):
        grid = self.grid
        for part in range(self.parts):
            for link, go in (
                (0, jnp.logical_and(z <= grid.z, grid.has_right)),
                (1, jnp.logical_and(z >= grid.z, grid.has_left)),
            ):
                pl.when(go)(lambda part=part, link=link: action(self.copy(z, part, link)))
            action(self.copy(z, part, 2))

    def send_own(self):
        self.links(self.grid.z, lambda c: c.start())

    def forward(self, z):
        grid = self.grid
        for part in range(self.parts):
            self.copy(z, part, 2).wait_recv()
            for link, go in (
                (0, jnp.logical_and(z < grid.z, grid.has_right)),
                (1, jnp.logical_and(z > grid.z, grid.has_left)),
            ):
                pl.when(go)(lambda part=part, link=link: self.copy(z, part, link).start())
            self.copy(z, part, 2).start()

    def wait_across(self, z):
        grid = self.grid
        for part in range(self.parts):
            here = self.piece(1 - grid.x, z, part)
            sem = self.recv.at[grid.slot(1 - grid.x, z), part]
            remote(here, here, self.send.at[z, part, 2], sem, grid.across).wait_recv()

    def finish(self):
        def step(z, carry):
            self.links(z, lambda c: c.wait_send())
            return carry

        lax.fori_loop(0, self.grid.line, step, 0)


class Scatter:
    def __init__(self, grid, partial, from_across, from_line, total, sems, parts):
        self.grid, self.partial, self.from_across = grid, partial, from_across
        self.from_line, self.total = from_line, total
        self.across_send, self.across_recv, self.line_send, self.line_recv = sems
        self.parts = parts
        self.rows = partial.shape[1] // parts

    def run(self, part):
        return pl.ds(part * self.rows, self.rows)

    def across(self, z, part):
        grid = self.grid
        return remote(
            self.partial.at[grid.slot(1 - grid.x, z), self.run(part)],
            self.from_across.at[z, self.run(part)],
            self.across_send.at[z, part],
            self.across_recv.at[z, part],
            grid.across,
        )

    def along(self, z, part, leftward):
        grid = self.grid
        place = z if leftward else z - 1 + grid.line - 1
        return remote(
            self.partial.at[grid.slot(grid.x, z), self.run(part)],
            self.from_line.at[place, self.run(part)],
            self.line_send.at[z, part],
            self.line_recv.at[place, part],
            grid.left if leftward else grid.right,
        )

    def send_across(self, z):
        for part in range(self.parts):
            self.across(z, part).start()

    def add_line(self, z, part, leftward):
        self.along(z, part, leftward).wait_recv()
        place = z if leftward else z - 1 + self.grid.line - 1
        self.total[...] += self.from_line[place, self.run(part)].astype(F32)

    def gather_sum(self, z, part):
        grid = self.grid
        self.across(z, part).wait_recv()
        self.total[...] = (
            self.partial[grid.slot(grid.x, z), self.run(part)].astype(F32)
            + self.from_across[z, self.run(part)].astype(F32)
        )
        pl.when(jnp.logical_and(z <= grid.z, grid.has_right))(lambda: self.add_line(z, part, True))
        pl.when(jnp.logical_and(z >= grid.z, grid.has_left))(lambda: self.add_line(z, part, False))

    def pass_on(self, z):
        grid = self.grid
        for part in range(self.parts):
            self.gather_sum(z, part)
            self.partial[grid.slot(grid.x, z), self.run(part)] = self.total[...].astype(BF)
            pl.when(z < grid.z)(lambda part=part: self.along(z, part, True).start())
            pl.when(z > grid.z)(lambda part=part: self.along(z, part, False).start())

    def own(self, result):
        for part in range(self.parts):
            self.gather_sum(self.grid.z, part)
            result[self.run(part)] = self.total[...]

    def finish(self):
        grid = self.grid

        def step(z, carry):
            for part in range(self.parts):
                self.across(z, part).wait_send()
                pl.when(z < grid.z)(lambda part=part: self.along(z, part, True).wait_send())
                pl.when(z > grid.z)(lambda part=part: self.along(z, part, False).wait_send())
            return carry

        lax.fori_loop(0, grid.line, step, 0)


def scatter_scratch(line, rows, width, parts):
    return [
        pltpu.VMEM((2 * line, rows, width), BF),
        pltpu.VMEM((line, rows, width), BF),
        pltpu.VMEM((2 * line - 2, rows, width), BF),
        pltpu.VMEM((rows // parts, width), F32),
        pltpu.SemaphoreType.DMA((line, parts)),
        pltpu.SemaphoreType.DMA((line, parts)),
        pltpu.SemaphoreType.DMA((line, parts)),
        pltpu.SemaphoreType.DMA((2 * line - 2, parts)),
    ]


def load_pairs(pairs, sems):
    copies = [pltpu.make_async_copy(src, dst, sems.at[i]) for i, (src, dst) in enumerate(pairs)]
    for copy in copies:
        copy.start()
    for copy in copies:
        copy.wait()


def feed_kernel(
    line, parts, tile,
    normed, tangent, gate_own, gate_twin, up_own, up_twin, down_own, down_twin,
    grad_sum, normed_all, tangent_all, hidden_all, grad_gate, grad_up, grad_down,
    part_gate, part_up, part_down,
    gate_w, up_w, down_w, hidden, dgate, dup, rows_n, rows_t,
    partial, from_across, from_line, total, across_send, across_recv, line_send, line_recv,
    gather_send, gather_recv, load_sem, wide, tile_sem, stage_a, stage_b, stage_sem, stage_recv, piece_a, piece_b, piece_sem, hidden_sem,
):
    grid = Grid(2, line)
    rows, width = normed.shape
    cols = gate_own.shape[1]
    blocks = 2 * line
    me = grid.slot(grid.x, grid.z)
    grid.greet(True)
    load_pairs([(normed, normed_all.at[me]), (tangent, tangent_all.at[me])], load_sem)
    gathers = [
        Gather(grid, normed_all, gather_send.at[0], gather_recv.at[0], parts),
        Gather(grid, tangent_all, gather_send.at[1], gather_recv.at[1], parts),
    ]
    scatter = Scatter(
        grid, partial, from_across, from_line, total,
        (across_send, across_recv, line_send, line_recv), parts,
    )
    for gather in gathers:
        gather.send_own()
    load_pairs(
        [
            (gate_own, gate_w.at[:, pl.ds(0, cols)]),
            (gate_twin, gate_w.at[:, pl.ds(cols, cols)]),
            (up_own, up_w.at[:, pl.ds(0, cols)]),
            (up_twin, up_w.at[:, pl.ds(cols, cols)]),
            (down_own, down_w.at[pl.ds(0, cols)]),
            (down_twin, down_w.at[pl.ds(cols, cols)]),
        ],
        load_sem,
    )

    def work(slot):
        load_pairs([(normed_all.at[slot], rows_n), (tangent_all.at[slot], rows_t)], load_sem)
        spot = pl.ds(pl.multiple_of(slot * rows, rows), rows)

        def hidden_tile(j, carry):
            c = pl.ds(pl.multiple_of(j * cols, cols), cols)
            gate = dot(rows_n[...], gate_w[:, c], NN)
            up = dot(rows_n[...], up_w[:, c], NN)
            grad = dot(rows_t[...], down_w[c, :], NT)
            sig = jax.nn.sigmoid(gate)
            silu = gate * sig
            hidden[spot, c] = (silu * up).astype(BF)
            dgate[spot, c] = (grad * up * (sig * (1.0 + gate * (1.0 - sig)))).astype(BF)
            dup[spot, c] = (grad * silu).astype(BF)
            return carry

        lax.fori_loop(0, 2, hidden_tile, 0)

        def back_tile(j, carry):
            c = pl.ds(pl.multiple_of(j * cols, cols), cols)
            sums = dot(dgate[spot, :], gate_w[c, :], NT) + dot(dup[spot, :], up_w[c, :], NT)
            partial[slot, :, c] = sums.astype(BF)
            return carry

        lax.fori_loop(0, width // cols, back_tile, 0)

    def stage(k, carry):
        @pl.when(k + 1 < line)
        def _():
            for gather in gathers:
                gather.forward(grid.order(k + 1))

        z = grid.order(k)

        def side(j, inner):
            @pl.when(j == 1)
            def _():
                for gather in gathers:
                    gather.wait_across(z)

            work(grid.slot(jnp.where(j == 0, grid.x, 1 - grid.x), z))
            return inner

        lax.fori_loop(0, 2, side, 0)
        return carry

    lax.fori_loop(0, line, stage, 0)
    hidden_copy = pltpu.make_async_copy(hidden, hidden_all, hidden_sem)
    hidden_copy.start()
    for k in range(line - 1, -1, -1):
        scatter.send_across(grid.order(k))

    tiles = width // tile

    def wide_loads(t, start):
        j, buf = t % tiles, t % 2
        c = pl.ds(pl.multiple_of(j * tile, tile), tile)
        for i, source in enumerate((normed_all, tangent_all)):
            copy = pltpu.make_async_copy(source.at[:, :, c], wide.at[buf, i], tile_sem.at[buf, i])
            copy.start() if start else copy.wait()

    def stages(t):
        j, buf = t % tiles, t % 2
        c = pl.ds(pl.multiple_of(j * tile, tile), tile)
        return [
            remote(src, dst, stage_sem.at[buf, i], stage_recv.at[j, i], grid.twin)
            for i, (src, dst) in enumerate(
                (
                    (stage_a.at[buf, 0], part_gate.at[c, :]),
                    (stage_a.at[buf, 1], part_up.at[c, :]),
                    (stage_b.at[buf], part_down.at[:, c]),
                )
            )
        ]

    def results(t):
        j, buf = t % tiles, t % 2
        c = pl.ds(pl.multiple_of(j * tile, tile), tile)
        return [
            pltpu.make_async_copy(src, dst, stage_sem.at[buf, i])
            for i, (src, dst) in enumerate(
                (
                    (stage_a.at[buf, 0], grad_gate.at[c, :]),
                    (stage_a.at[buf, 1], grad_up.at[c, :]),
                    (stage_b.at[buf], grad_down.at[:, c]),
                )
            )
        ]

    def pieces(t):
        c = pl.ds(pl.multiple_of((t % tiles) * tile, tile), tile)
        return [
            (part_gate.at[c, :], piece_a.at[0]),
            (part_up.at[c, :], piece_a.at[1]),
            (part_down.at[:, c], piece_b),
        ]

    wide_loads(0, True)

    def weights(t, carry):
        buf = t % 2
        pl.when(t + 1 < 2 * tiles)(lambda: wide_loads(t + 1, True))
        wide_loads(t, False)
        tall = blocks * rows
        tokens = wide[buf, 0].reshape(tall, tile)
        tangents = wide[buf, 1].reshape(tall, tile)

        @pl.when(t < tiles)
        def _():
            theirs = slice(cols, 2 * cols)

            @pl.when(t >= 2)
            def _():
                for copy in stages(t - 2):
                    copy.wait_send()

            stage_a[buf, 0] = dot(tokens, dgate[:, theirs], TN).astype(BF)
            stage_a[buf, 1] = dot(tokens, dup[:, theirs], TN).astype(BF)
            stage_b[buf] = dot(hidden[:, theirs], tangents, TN).astype(BF)
            for copy in stages(t):
                copy.start()

        @pl.when(t >= tiles)
        def _():
            for copy in stages(t):
                copy.wait_recv()
            loads = [
                pltpu.make_async_copy(src, dst, piece_sem.at[i])
                for i, (src, dst) in enumerate(pieces(t))
            ]
            for copy in loads:
                copy.start()

            @pl.when(t < tiles + 2)
            def _():
                for copy in stages(t - 2):
                    copy.wait_send()

            @pl.when(t >= tiles + 2)
            def _():
                for copy in results(t - 2):
                    copy.wait()

            mine = slice(0, cols)
            own_gate = dot(tokens, dgate[:, mine], TN)
            own_up = dot(tokens, dup[:, mine], TN)
            own_down = dot(hidden[:, mine], tangents, TN)
            for copy in loads:
                copy.wait()
            stage_a[buf, 0] = (own_gate + piece_a[0].astype(F32)).astype(BF)
            stage_a[buf, 1] = (own_up + piece_a[1].astype(F32)).astype(BF)
            stage_b[buf] = (own_down + piece_b[...].astype(F32)).astype(BF)
            for copy in results(t):
                copy.start()

        for k in range(line - 1, 0, -1):
            when = 2 * tiles - 1 - (k - 1) * (tiles // (line - 1))
            pl.when(t == when)(lambda k=k: scatter.pass_on(grid.order(k)))
        return carry

    lax.fori_loop(0, 2 * tiles, weights, 0)
    scatter.own(grad_sum)
    for t in (2 * tiles - 2, 2 * tiles - 1):
        for copy in results(t):
            copy.wait()
    for gather in gathers:
        gather.finish()
    scatter.finish()
    hidden_copy.wait()


def feed_call(normed, tangent, gates, ups, downs, line):
    rows, width = normed.shape
    cols = gates[0].shape[1]
    blocks, parts, tile = 2 * line, 2, 256
    tiles = width // tile
    tall = blocks * rows
    shapes = jax.ShapeDtypeStruct
    hbm = lambda *s: shapes(s, BF)
    return pl.pallas_call(
        functools.partial(feed_kernel, line, parts, tile),
        out_shape=(
            shapes((rows, width), F32),
            hbm(blocks, rows, width), hbm(blocks, rows, width), hbm(tall, 2 * cols),
            hbm(width, cols), hbm(width, cols), hbm(cols, width),
            hbm(width, cols), hbm(width, cols), hbm(cols, width),
        ),
        in_specs=[ANY] * 8,
        out_specs=(pl.BlockSpec(memory_space=pltpu.VMEM),) + (ANY,) * 9,
        scratch_shapes=[
            pltpu.VMEM((width, 2 * cols), BF), pltpu.VMEM((width, 2 * cols), BF), pltpu.VMEM((2 * cols, width), BF),
            pltpu.VMEM((tall, 2 * cols), BF), pltpu.VMEM((tall, 2 * cols), BF), pltpu.VMEM((tall, 2 * cols), BF),
            pltpu.VMEM((rows, width), BF), pltpu.VMEM((rows, width), BF),
            *scatter_scratch(line, rows, width, parts),
            pltpu.SemaphoreType.DMA((2, line, parts, 3)), pltpu.SemaphoreType.DMA((2, blocks, parts)),
            pltpu.SemaphoreType.DMA((6,)),
            pltpu.VMEM((2, 2, blocks, rows, tile), BF), pltpu.SemaphoreType.DMA((2, 2)),
            pltpu.VMEM((2, 2, tile, cols), BF), pltpu.VMEM((2, cols, tile), BF),
            pltpu.SemaphoreType.DMA((2, 3)), pltpu.SemaphoreType.DMA((tiles, 3)),
            pltpu.VMEM((2, tile, cols), BF), pltpu.VMEM((cols, tile), BF), pltpu.SemaphoreType.DMA((3,)),
            pltpu.SemaphoreType.DMA,
        ],
        compiler_params=pltpu.CompilerParams(
            collective_id=1, has_side_effects=True, vmem_limit_bytes=63 * 2**20
        ),
        name="feed",
    )(normed, tangent, gates[0], gates[1], ups[0], ups[1], downs[0], downs[1])


def branch_kernel(
    line, parts,
    hidden_all, down_own, down_twin,
    result,
    down_w, hidden, load_sem,
    partial, from_across, from_line, total, across_send, across_recv, line_send, line_recv,
):
    grid = Grid(2, line)
    cols, width = down_own.shape
    rows = partial.shape[1]
    grid.greet(False)
    load_pairs(
        [
            (down_own, down_w.at[pl.ds(0, cols)]),
            (down_twin, down_w.at[pl.ds(cols, cols)]),
            (hidden_all, hidden),
        ],
        load_sem,
    )
    scatter = Scatter(
        grid, partial, from_across, from_line, total,
        (across_send, across_recv, line_send, line_recv), parts,
    )

    def work(i, carry):
        z = grid.order(line - 1 - i // 2)
        slot = grid.slot(jnp.where(i % 2 == 0, 1 - grid.x, grid.x), z)
        spot = pl.ds(pl.multiple_of(slot * rows, rows), rows)

        def tile(j, inner):
            c = pl.ds(pl.multiple_of(j * cols, cols), cols)
            partial[slot, :, c] = dot(hidden[spot, :], down_w[:, c], NN).astype(BF)
            return inner

        lax.fori_loop(0, width // cols, tile, 0)
        pl.when(i % 2 == 0)(lambda: scatter.send_across(z))
        return carry

    lax.fori_loop(0, 2 * line, work, 0)

    def along(i, carry):
        scatter.pass_on(grid.order(line - 1 - i))
        return carry

    lax.fori_loop(0, line - 1, along, 0)
    scatter.own(result)
    scatter.finish()


def branch_call(hidden_all, downs, line, rows):
    cols, width = downs[0].shape
    parts = 2
    return pl.pallas_call(
        functools.partial(branch_kernel, line, parts),
        out_shape=jax.ShapeDtypeStruct((rows, width), F32),
        in_specs=[ANY] * 3,
        out_specs=pl.BlockSpec(memory_space=pltpu.VMEM),
        scratch_shapes=[
            pltpu.VMEM((2 * cols, width), BF),
            pltpu.VMEM(hidden_all.shape, BF),
            pltpu.SemaphoreType.DMA((3,)),
            *scatter_scratch(line, rows, width, parts),
        ],
        compiler_params=pltpu.CompilerParams(
            collective_id=2, has_side_effects=True, vmem_limit_bytes=60 * 2**20
        ),
        name="branch",
    )(hidden_all, downs[0], downs[1])


def body(
    tokens,
    places,
    cotangent,
    gain_attn,
    gain_mlp,
    w_query,
    key_projection,
    value_projection,
    w_out,
    w_gate,
    w_up,
    w_down,
    kernels,
):
    sequence_total, segment_length, width = tokens.shape
    total_length = places.shape[1]
    total_rows = sequence_total * segment_length
    position = lax.axis_index("context")
    local_positions = lax.dynamic_slice_in_dim(places, position * segment_length, segment_length, 1)
    rotary_angles = local_positions.reshape(total_rows).astype(jnp.float32)[:, None] * frequencies(
        HEAD_SIZE // 2
    )
    gain_one, gain_two, query_w, key_weight_local, value_w, out_w = (
        lax.all_gather(gain_attn, ("fsdp", "context"), axis=0, tiled=True),
        lax.all_gather(gain_mlp, ("fsdp", "context"), axis=0, tiled=True),
        lax.all_gather(w_query, ("fsdp", "context"), axis=0, tiled=True),
        lax.all_gather(key_projection, ("fsdp", "context"), axis=0, tiled=True),
        lax.all_gather(value_projection, ("fsdp", "context"), axis=0, tiled=True),
        lax.all_gather(w_out, ("fsdp", "context"), axis=0, tiled=True),
    )
    gain_first = gain_one.astype(jnp.float32)
    gain_second = gain_two.astype(jnp.float32)
    inputs_f = tokens.astype(jnp.float32).reshape(total_rows, width)
    factor_one = lax.rsqrt(jnp.mean(inputs_f * inputs_f, axis=-1, keepdims=True) + norm_eps)
    unit_one = inputs_f * factor_one
    normed_tokens = (unit_one * gain_first).astype(jnp.bfloat16)
    query_pre = jnp.dot(normed_tokens, query_w, preferred_element_type=jnp.float32).reshape(
        total_rows, QUERY_HEADS, HEAD_SIZE
    )
    key_unrotated = jnp.dot(
        normed_tokens, key_weight_local, preferred_element_type=jnp.float32
    ).reshape(total_rows, KEY_VALUE_HEADS, HEAD_SIZE)
    value_matrix_rows = jnp.dot(normed_tokens, value_w, preferred_element_type=jnp.float32).astype(
        jnp.bfloat16
    )
    query_rows = apply_rotary(query_pre, rotary_angles).astype(jnp.bfloat16)
    key_matrix_rows = (
        apply_rotary(key_unrotated, rotary_angles)
        .astype(jnp.bfloat16)
        .reshape(sequence_total, segment_length, KEY_VALUE_HEADS * HEAD_SIZE)
    )
    key_all, value_all = (
        lax.all_gather(key_matrix_rows, "context", axis=1, tiled=True),
        lax.all_gather(
            value_matrix_rows.reshape(sequence_total, segment_length, KEY_VALUE_HEADS * HEAD_SIZE),
            "context",
            axis=1,
            tiled=True,
        ),
    )
    head_query = query_head_rows(query_rows, sequence_total, segment_length)
    head_key = key_heads(key_all, sequence_total, total_length)
    head_value = key_heads(value_all, sequence_total, total_length)
    query_positions = jnp.repeat(local_positions, KEY_VALUE_HEADS, axis=0)
    key_positions = jnp.repeat(places, KEY_VALUE_HEADS, axis=0)
    attended = lax.map(
        forward_head, (head_query, head_key, head_value, query_positions, key_positions)
    )
    attended = merge_queries(attended, sequence_total, segment_length).astype(jnp.bfloat16)
    middle = inputs_f + jnp.dot(attended, out_w, preferred_element_type=jnp.float32)
    factor_two = lax.rsqrt(jnp.mean(middle * middle, axis=-1, keepdims=True) + norm_eps)
    unit_two = middle * factor_two
    normed_mlp = (unit_two * gain_second).astype(jnp.bfloat16)
    tangent = cotangent.reshape(total_rows, width)
    tangent_f = tangent.astype(jnp.float32)
    if kernels:
        line = lax.axis_size("context")
        swap = [(i, i ^ 1) for i in range(lax.axis_size("fsdp"))]
        gates, ups, downs = (
            (w, lax.ppermute(w, "fsdp", swap)) for w in (w_gate, w_up, w_down)
        )
        grad_normed, _, _, hidden_all, *sums = feed_call(
            normed_mlp, tangent, gates, ups, downs, line
        )[:7]
        branch = branch_call(hidden_all, downs, line, total_rows)
        flip = [(i, 1 - i) for i in range(2)]
        grad_w_gate, grad_w_up, grad_w_down = (
            g.astype(jnp.float32) + lax.ppermute(g, "replica", flip).astype(jnp.float32)
            for g in sums
        )
    else:
        group = ("fsdp", "context")
        normed_all = lax.all_gather(normed_mlp, group, axis=0, tiled=True)
        tangent_all = lax.all_gather(tangent, group, axis=0, tiled=True)
        branch_part, kept_values = feed_forward(normed_all, w_gate, w_up, w_down)
        grad_part, grad_w_gate, grad_w_up, grad_w_down = feed_back(
            normed_all, tangent_all, w_gate, w_up, w_down, kept_values
        )
        grad_normed = lax.psum_scatter(
            grad_part.astype(jnp.bfloat16), group, scatter_dimension=0, tiled=True
        ).astype(jnp.float32)
        branch = lax.psum_scatter(
            branch_part.astype(jnp.bfloat16), group, scatter_dimension=0, tiled=True
        ).astype(jnp.float32)
        grad_w_gate, grad_w_up, grad_w_down = (
            lax.psum(g.astype(jnp.bfloat16), "replica").astype(jnp.float32)
            for g in (grad_w_gate, grad_w_up, grad_w_down)
        )
    outcome = middle + branch
    scaled_two = grad_normed * gain_second
    term_gain_two = jnp.sum(grad_normed * unit_two, axis=0)
    grad_middle = tangent_f + factor_two * (
        scaled_two - unit_two * jnp.mean(scaled_two * unit_two, axis=-1, keepdims=True)
    )
    grad_branch = grad_middle.astype(jnp.bfloat16)
    term_out = times_t(attended, grad_branch)
    grad_attended = times_nt(grad_branch, out_w).astype(jnp.bfloat16)
    head_grad = query_head_rows(grad_attended, sequence_total, segment_length)
    grad_q, grad_k, grad_v = lax.map(
        backward_head, (head_query, head_key, head_value, head_grad, query_positions, key_positions)
    )
    local_key_gradient, local_value_gradient = (
        lax.psum_scatter(
            merge_keys(grad_k, sequence_total, total_length).astype(jnp.bfloat16),
            "context",
            scatter_dimension=1,
            tiled=True,
        ).astype(jnp.float32),
        lax.psum_scatter(
            merge_keys(grad_v, sequence_total, total_length).astype(jnp.bfloat16),
            "context",
            scatter_dimension=1,
            tiled=True,
        ).astype(jnp.float32),
    )
    grad_query = (
        inverse_rotary(
            merge_queries(grad_q, sequence_total, segment_length).reshape(
                total_rows, QUERY_HEADS, HEAD_SIZE
            ),
            rotary_angles,
        )
        .reshape(total_rows, QUERY_HEADS * HEAD_SIZE)
        .astype(jnp.bfloat16)
    )
    grad_key = (
        inverse_rotary(
            local_key_gradient.reshape(total_rows, KEY_VALUE_HEADS, HEAD_SIZE), rotary_angles
        )
        .reshape(total_rows, KEY_VALUE_HEADS * HEAD_SIZE)
        .astype(jnp.bfloat16)
    )
    value_gradient = local_value_gradient.reshape(total_rows, KEY_VALUE_HEADS * HEAD_SIZE).astype(
        jnp.bfloat16
    )
    grad_normed_one = (
        times_nt(grad_query, query_w)
        + times_nt(grad_key, key_weight_local)
        + times_nt(value_gradient, value_w)
    )
    term_query = times_t(normed_tokens, grad_query)
    term_key = times_t(normed_tokens, grad_key)
    term_value = times_t(normed_tokens, value_gradient)
    scaled_one = grad_normed_one * gain_first
    term_gain_one = jnp.sum(grad_normed_one * unit_one, axis=0)
    grad_inputs = grad_middle + factor_one * (
        scaled_one - unit_one * jnp.mean(scaled_one * unit_one, axis=-1, keepdims=True)
    )
    share_query, share_key, share_value, share_out, share_gain_one, share_gain_two = (
        lax.psum_scatter(term_query.astype(jnp.bfloat16), ("fsdp", "context"), scatter_dimension=0, tiled=True),
        lax.psum_scatter(term_key.astype(jnp.bfloat16), ("fsdp", "context"), scatter_dimension=0, tiled=True),
        lax.psum_scatter(term_value.astype(jnp.bfloat16), ("fsdp", "context"), scatter_dimension=0, tiled=True),
        lax.psum_scatter(term_out.astype(jnp.bfloat16), ("fsdp", "context"), scatter_dimension=0, tiled=True),
        lax.psum_scatter(term_gain_one, ("fsdp", "context"), scatter_dimension=0, tiled=True),
        lax.psum_scatter(term_gain_two, ("fsdp", "context"), scatter_dimension=0, tiled=True),
    )
    summed = (
        lax.psum(share_query.astype(jnp.bfloat16), "replica").astype(jnp.float32),
        lax.psum(share_key.astype(jnp.bfloat16), "replica").astype(jnp.float32),
        lax.psum(share_value.astype(jnp.bfloat16), "replica").astype(jnp.float32),
        lax.psum(share_out.astype(jnp.bfloat16), "replica").astype(jnp.float32),
        grad_w_gate,
        grad_w_up,
        grad_w_down,
        lax.psum(share_gain_one.astype(jnp.bfloat16), "replica").astype(jnp.float32),
        lax.psum(share_gain_two.astype(jnp.bfloat16), "replica").astype(jnp.float32),
    )
    out = outcome.astype(jnp.bfloat16).reshape(sequence_total, segment_length, width)
    grad_tokens = grad_inputs.astype(jnp.bfloat16).reshape(sequence_total, segment_length, width)
    return (
        out,
        grad_tokens,
        summed[0],
        summed[1],
        summed[2],
        summed[3],
        summed[4],
        summed[5],
        summed[6],
        summed[7],
        summed[8],
    )


def solution(mesh):
    placed = (
        P(("replica", "fsdp"), "context", None),
        P(("replica", "fsdp"), None),
        P(("replica", "fsdp"), "context", None),
        P(("fsdp", "context")),
        P(("fsdp", "context")),
        P(("fsdp", "context"), None),
        P(("fsdp", "context"), None),
        P(("fsdp", "context"), None),
        P(("fsdp", "context"), None),
        P(None, ("fsdp", "context")),
        P(None, ("fsdp", "context")),
        P(("fsdp", "context"), None),
    )
    kernels = (mesh.shape["replica"], mesh.shape["fsdp"], mesh.shape["context"]) == (2, 4, 4)
    return jax.shard_map(
        functools.partial(body, kernels=kernels),
        mesh=mesh,
        in_specs=placed,
        out_specs=(
            P(("replica", "fsdp"), "context", None),
            P(("replica", "fsdp"), "context", None),
            P(("fsdp", "context"), None),
            P(("fsdp", "context"), None),
            P(("fsdp", "context"), None),
            P(("fsdp", "context"), None),
            P(None, ("fsdp", "context")),
            P(None, ("fsdp", "context")),
            P(("fsdp", "context"), None),
            P(("fsdp", "context")),
            P(("fsdp", "context")),
        ),
        check_vma=False,
    )
```

```python
import functools

import jax
import jax.numpy as jnp
from jax import lax
from jax.experimental import pallas as pl
from jax.experimental.pallas import tpu as pltpu
from jax.sharding import PartitionSpec as P

QUERY_HEADS = 32
KEY_VALUE_HEADS = 8
HEAD_SIZE = 64


norm_eps = 1e-05
rope_base = 500000.0


def frequencies(half):
    return rope_base ** (-2.0 * jnp.arange(half, dtype=jnp.float32) / (2.0 * half))


def apply_rotary(angle_table, rotary_angles):
    half = angle_table.shape[-1] // 2
    first_half = angle_table[..., :half]
    second_half = angle_table[..., half:]
    cosine = jnp.cos(rotary_angles)[..., None, :]
    sine = jnp.sin(rotary_angles)[..., None, :]
    return jnp.concatenate(
        [first_half * cosine - second_half * sine, second_half * cosine + first_half * sine],
        axis=-1,
    )


def inverse_rotary(angle_table, rotary_angles):
    half = angle_table.shape[-1] // 2
    first_half = angle_table[..., :half]
    second_half = angle_table[..., half:]
    cosine = jnp.cos(rotary_angles)[..., None, :]
    sine = jnp.sin(rotary_angles)[..., None, :]
    return jnp.concatenate(
        [first_half * cosine + second_half * sine, second_half * cosine - first_half * sine],
        axis=-1,
    )


def times_t(left, right):
    return lax.dot_general(
        left, right, (((0,), (0,)), ((), ())), preferred_element_type=jnp.float32
    )


def times_nt(left, right):
    return lax.dot_general(
        left, right, (((1,), (1,)), ((), ())), preferred_element_type=jnp.float32
    )


def query_head_rows(angle_table, sequence_total, segment_length):
    reshaped_heads = angle_table.reshape(
        sequence_total, segment_length, KEY_VALUE_HEADS, QUERY_HEADS // KEY_VALUE_HEADS, HEAD_SIZE
    )
    return jnp.transpose(reshaped_heads, (0, 2, 1, 3, 4)).reshape(
        sequence_total * KEY_VALUE_HEADS, segment_length, QUERY_HEADS // KEY_VALUE_HEADS, HEAD_SIZE
    )


def key_heads(angle_table, sequence_total, total_length):
    reshaped_heads = angle_table.reshape(sequence_total, total_length, KEY_VALUE_HEADS, HEAD_SIZE)
    return jnp.transpose(reshaped_heads, (0, 2, 1, 3)).reshape(
        sequence_total * KEY_VALUE_HEADS, total_length, HEAD_SIZE
    )


def merge_queries(angle_table, sequence_total, segment_length):
    reshaped_heads = angle_table.reshape(
        sequence_total, KEY_VALUE_HEADS, segment_length, QUERY_HEADS // KEY_VALUE_HEADS, HEAD_SIZE
    )
    return jnp.transpose(reshaped_heads, (0, 2, 1, 3, 4)).reshape(
        sequence_total * segment_length, QUERY_HEADS * HEAD_SIZE
    )


def merge_keys(angle_table, sequence_total, total_length):
    reshaped_heads = angle_table.reshape(sequence_total, KEY_VALUE_HEADS, total_length, HEAD_SIZE)
    return jnp.transpose(reshaped_heads, (0, 2, 1, 3)).reshape(
        sequence_total, total_length, KEY_VALUE_HEADS * HEAD_SIZE
    )


def softmax_weights(part_query, part_key, place_query, place_key):
    allowed = place_key[None, :] <= place_query[:, None]
    scores = jnp.einsum(
        "qrd,kd->rqk", part_query, part_key, preferred_element_type=jnp.float32
    ) * HEAD_SIZE ** (-0.5)
    scores = jnp.where(allowed[None], scores, -1e30)
    return jax.nn.softmax(scores, axis=-1)


def forward_head(packed):
    part_query, part_key, part_value, place_query, place_key = packed
    probs = softmax_weights(part_query, part_key, place_query, place_key)
    return jnp.einsum(
        "rqk,kd->qrd", probs.astype(jnp.bfloat16), part_value, preferred_element_type=jnp.float32
    )


def backward_head(packed):
    part_query, part_key, part_value, part_grad, place_query, place_key = packed
    probs = softmax_weights(part_query, part_key, place_query, place_key)
    grad_probs = jnp.einsum(
        "qrd,kd->rqk", part_grad, part_value, preferred_element_type=jnp.float32
    )
    row_delta = jnp.sum(probs * grad_probs, axis=-1, keepdims=True)
    grad_scores = (probs * (grad_probs - row_delta)).astype(jnp.bfloat16)
    grad_query = jnp.einsum(
        "rqk,kd->qrd", grad_scores, part_key, preferred_element_type=jnp.float32
    ) * HEAD_SIZE ** (-0.5)
    grad_key = jnp.einsum(
        "rqk,qrd->kd", grad_scores, part_query, preferred_element_type=jnp.float32
    ) * HEAD_SIZE ** (-0.5)
    value_gradient = jnp.einsum(
        "rqk,qrd->kd", probs.astype(jnp.bfloat16), part_grad, preferred_element_type=jnp.float32
    )
    return (grad_query, grad_key, value_gradient)


def feed_forward(normed_rows, gate_w, up_w, down_w):
    gate_pre = jnp.dot(normed_rows, gate_w, preferred_element_type=jnp.float32)
    up_proj = jnp.dot(normed_rows, up_w, preferred_element_type=jnp.float32)
    sigmoid_gate = jax.nn.sigmoid(gate_pre)
    hidden = (gate_pre * sigmoid_gate * up_proj).astype(jnp.bfloat16)
    return (
        jnp.dot(hidden, down_w, preferred_element_type=jnp.float32),
        (gate_pre, up_proj, sigmoid_gate, hidden),
    )


def feed_back(normed_rows, grad_rows, gate_w, up_w, down_w, kept_values):
    gate_pre, up_proj, sigmoid_gate, hidden = kept_values
    grad_hidden = times_nt(grad_rows, down_w)
    term_down = times_t(hidden, grad_rows)
    grad_gate = (
        grad_hidden * up_proj * (sigmoid_gate * (1.0 + gate_pre * (1.0 - sigmoid_gate)))
    ).astype(jnp.bfloat16)
    grad_up = (grad_hidden * (gate_pre * sigmoid_gate)).astype(jnp.bfloat16)
    grad_normed = times_nt(grad_gate, gate_w) + times_nt(grad_up, up_w)
    return (grad_normed, times_t(normed_rows, grad_gate), times_t(normed_rows, grad_up), term_down)


MESH = pl.DeviceIdType.MESH
ANY = pl.BlockSpec(memory_space=pl.ANY)
BF = jnp.bfloat16
F32 = jnp.float32
NN = (((1,), (0,)), ((), ()))
NT = (((1,), (1,)), ((), ()))
TN = (((0,), (0,)), ((), ()))


def dot(left, right, dims):
    return lax.dot_general(left, right, dims, preferred_element_type=F32)


class Grid:
    def __init__(self, chips, line):
        self.chips, self.line = chips, line
        self.replica = lax.axis_index("replica")
        flat = lax.axis_index("fsdp")
        self.x, self.core = flat // 2, flat % 2
        self.z = lax.axis_index("context")
        self.has_left, self.has_right = self.z > 0, self.z + 1 < line
        self.left = (self.replica, flat, self.z - 1)
        self.right = (self.replica, flat, self.z + 1)
        self.across = (self.replica, (1 - self.x) * 2 + self.core, self.z)
        self.twin = (self.replica, self.x * 2 + 1 - self.core, self.z)
        self.mirror = (1 - self.replica, flat, self.z)

    def order(self, k):
        z, n = self.z, self.line
        near = 2 * jnp.minimum(z, n - 1 - z)
        alternate = jnp.where(k % 2 == 1, z - (k + 1) // 2, z + k // 2)
        return jnp.where(k <= near, alternate, jnp.where(2 * z < n, k, n - 1 - k))

    def slot(self, x, z):
        return x * self.line + z

    def greet(self, twin, mirror=False):
        barrier = pltpu.get_barrier_semaphore()

        def tell(device):
            pl.semaphore_signal(barrier, inc=1, device_id=device, device_id_type=MESH)

        pl.when(self.has_left)(lambda: tell(self.left))
        pl.when(self.has_right)(lambda: tell(self.right))
        tell(self.across)
        if twin:
            tell(self.twin)
        if mirror:
            tell(self.mirror)
        count = 1 + int(twin) + int(mirror) + self.has_left.astype(jnp.int32) + self.has_right.astype(jnp.int32)
        pl.semaphore_wait(barrier, count)


def remote(src, dst, send, recv, device):
    return pltpu.make_async_remote_copy(
        src_ref=src, dst_ref=dst, send_sem=send, recv_sem=recv, device_id=device, device_id_type=MESH
    )


class Gather:
    def __init__(self, grid, block, everything, send, recv, parts):
        self.grid, self.everything, self.send, self.recv = grid, everything, send, recv
        self.block = block
        self.parts = parts
        self.rows = everything.shape[1] // parts

    def piece(self, x, z, part):
        return self.everything.at[self.grid.slot(x, z), pl.ds(part * self.rows, self.rows)]

    def copy(self, z, part, link, first=False):
        grid = self.grid
        device = (grid.right, grid.left, grid.across)[link]
        there = self.piece(grid.x, z, part)
        here = self.block.at[pl.ds(part * self.rows, self.rows)] if first else there
        return remote(
            here, there, self.send.at[z, part, link], self.recv.at[grid.slot(grid.x, z), part], device
        )

    def links(self, z, action, first=False):
        grid = self.grid
        for part in range(self.parts):
            for link, go in (
                (0, jnp.logical_and(z <= grid.z, grid.has_right)),
                (1, jnp.logical_and(z >= grid.z, grid.has_left)),
            ):
                pl.when(go)(lambda part=part, link=link: action(self.copy(z, part, link, first)))
            action(self.copy(z, part, 2, first))

    def send_own(self):
        self.links(self.grid.z, lambda c: c.start(), True)

    def forward(self, distance, part):
        grid = self.grid
        for z, there, link, go in (
            (grid.z - distance, grid.z >= distance, 0, grid.has_right),
            (grid.z + distance, grid.z + distance < grid.line, 1, grid.has_left),
        ):

            @pl.when(there)
            def _(z=z, link=link, go=go):
                self.copy(z, part, 2).wait_recv()
                pl.when(go)(lambda: self.copy(z, part, link).start())
                self.copy(z, part, 2).start()

    def wait_across(self, z):
        grid = self.grid
        for part in range(self.parts):
            here = self.piece(1 - grid.x, z, part)
            sem = self.recv.at[grid.slot(1 - grid.x, z), part]
            remote(here, here, self.send.at[z, part, 2], sem, grid.across).wait_recv()

    def finish(self):
        def step(z, carry):
            self.links(z, lambda c: c.wait_send())
            return carry

        lax.fori_loop(0, self.grid.line, step, 0)


class Scatter:
    def __init__(self, grid, partial, from_across, from_line, total, sems, parts):
        self.grid, self.partial, self.from_across = grid, partial, from_across
        self.from_line, self.total = from_line, total
        self.across_send, self.across_recv, self.line_send, self.line_recv = sems
        self.parts = parts
        self.rows = partial.shape[1] // parts

    def run(self, part):
        return pl.ds(part * self.rows, self.rows)

    def across(self, z, part):
        grid = self.grid
        return remote(
            self.partial.at[grid.slot(1 - grid.x, z), self.run(part)],
            self.from_across.at[z, self.run(part)],
            self.across_send.at[z, part],
            self.across_recv.at[z, part],
            grid.across,
        )

    def along(self, z, part, leftward):
        grid = self.grid
        place = z if leftward else z - 1 + grid.line - 1
        return remote(
            self.partial.at[grid.slot(grid.x, z), self.run(part)],
            self.from_line.at[place, self.run(part)],
            self.line_send.at[z, part],
            self.line_recv.at[place, part],
            grid.left if leftward else grid.right,
        )

    def send_across(self, z):
        for part in range(self.parts):
            self.across(z, part).start()

    def add_line(self, z, part, leftward):
        self.along(z, part, leftward).wait_recv()
        place = z if leftward else z - 1 + self.grid.line - 1
        self.total[...] += self.from_line[place, self.run(part)].astype(F32)

    def gather_sum(self, z, part):
        grid = self.grid
        self.across(z, part).wait_recv()
        self.total[...] = (
            self.partial[grid.slot(grid.x, z), self.run(part)].astype(F32)
            + self.from_across[z, self.run(part)].astype(F32)
        )
        pl.when(jnp.logical_and(z <= grid.z, grid.has_right))(lambda: self.add_line(z, part, True))
        pl.when(jnp.logical_and(z >= grid.z, grid.has_left))(lambda: self.add_line(z, part, False))

    def pass_on(self, z):
        grid = self.grid
        for part in range(self.parts):
            self.gather_sum(z, part)
            self.partial[grid.slot(grid.x, z), self.run(part)] = self.total[...].astype(BF)
            pl.when(z < grid.z)(lambda part=part: self.along(z, part, True).start())
            pl.when(z > grid.z)(lambda part=part: self.along(z, part, False).start())

    def own(self, result, after=None):
        for part in range(self.parts):
            self.gather_sum(self.grid.z, part)
            result[self.run(part)] = self.total[...].astype(result.dtype)
            if after is not None:
                after(part)

    def finish(self):
        grid = self.grid

        def step(z, carry):
            for part in range(self.parts):
                self.across(z, part).wait_send()
                pl.when(z < grid.z)(lambda part=part: self.along(z, part, True).wait_send())
                pl.when(z > grid.z)(lambda part=part: self.along(z, part, False).wait_send())
            return carry

        lax.fori_loop(0, grid.line, step, 0)


def scatter_scratch(line, rows, width, parts):
    return [
        pltpu.VMEM((2 * line, rows, width), BF),
        pltpu.VMEM((line, rows, width), BF),
        pltpu.VMEM((2 * line - 2, rows, width), BF),
        pltpu.VMEM((rows // parts, width), F32),
        pltpu.SemaphoreType.DMA((line, parts)),
        pltpu.SemaphoreType.DMA((line, parts)),
        pltpu.SemaphoreType.DMA((line, parts)),
        pltpu.SemaphoreType.DMA((2 * line - 2, parts)),
    ]


def load_pairs(pairs, sems):
    copies = [pltpu.make_async_copy(src, dst, sems.at[i]) for i, (src, dst) in enumerate(pairs)]
    for copy in copies:
        copy.start()
    for copy in copies:
        copy.wait()


def feed_kernel(
    line, parts, tile,
    normed, tangent, gate_own, gate_twin, up_own, up_twin, down_own, down_twin,
    grad_sum, normed_all, tangent_all, hidden_all, grad_gate, grad_up, grad_down,
    part_gate, part_up, part_down,
    gate_w, up_w, down_w, hidden, dgate, dup, rows_n, rows_t,
    partial, from_across, from_line, total, across_send, across_recv, line_send, line_recv,
    gather_send, gather_recv, load_sem, wide, tile_sem, stage_a, stage_b, stage_sem, stage_recv, piece_a, piece_b, piece_sem, hidden_sem,
):
    grid = Grid(2, line)
    rows, width = normed.shape
    cols = gate_own.shape[1]
    blocks = 2 * line
    me = grid.slot(grid.x, grid.z)
    grid.greet(True)
    gathers = [
        Gather(grid, normed, normed_all, gather_send.at[0], gather_recv.at[0], parts),
        Gather(grid, tangent, tangent_all, gather_send.at[1], gather_recv.at[1], parts),
    ]
    scatter = Scatter(
        grid, partial, from_across, from_line, total,
        (across_send, across_recv, line_send, line_recv), parts,
    )
    for gather in gathers:
        gather.send_own()
    load_pairs(
        [
            (gate_own, gate_w.at[:, pl.ds(0, cols)]),
            (gate_twin, gate_w.at[:, pl.ds(cols, cols)]),
            (up_own, up_w.at[:, pl.ds(0, cols)]),
            (up_twin, up_w.at[:, pl.ds(cols, cols)]),
            (down_own, down_w.at[pl.ds(0, cols)]),
            (down_twin, down_w.at[pl.ds(cols, cols)]),
            (normed, rows_n),
            (tangent, rows_t),
        ],
        load_sem,
    )
    load_pairs([(rows_n, normed_all.at[me]), (rows_t, tangent_all.at[me])], load_sem)

    def work(slot):
        load_pairs([(normed_all.at[slot], rows_n), (tangent_all.at[slot], rows_t)], load_sem)
        spot = pl.ds(pl.multiple_of(slot * rows, rows), rows)

        def hidden_tile(j, carry):
            c = pl.ds(pl.multiple_of(j * cols, cols), cols)
            gate = dot(rows_n[...], gate_w[:, c], NN)
            up = dot(rows_n[...], up_w[:, c], NN)
            grad = dot(rows_t[...], down_w[c, :], NT)
            sig = jax.nn.sigmoid(gate)
            silu = gate * sig
            hidden[spot, c] = (silu * up).astype(BF)
            dgate[spot, c] = (grad * up * (sig * (1.0 + gate * (1.0 - sig)))).astype(BF)
            dup[spot, c] = (grad * silu).astype(BF)
            return carry

        lax.fori_loop(0, 2, hidden_tile, 0)

        def back_tile(j, carry):
            c = pl.ds(pl.multiple_of(j * cols, cols), cols)
            sums = dot(dgate[spot, :], gate_w[c, :], NT) + dot(dup[spot, :], up_w[c, :], NT)
            partial[slot, :, c] = sums.astype(BF)
            return carry

        lax.fori_loop(0, width // cols, back_tile, 0)

    def stage(distance, carry):
        @pl.when(distance + 1 < line)
        def _():
            for gather in gathers:
                for part in range(parts):
                    gather.forward(distance + 1, part)

        def visit(i, inner):
            z = grid.z + jnp.where(i % 2 == 0, -distance, distance)
            inside = jnp.logical_and(z >= 0, z < line)

            @pl.when(jnp.logical_and(inside, jnp.logical_or(distance > 0, i % 2 == 0)))
            def _():
                @pl.when(i >= 2)
                def _():
                    for gather in gathers:
                        gather.wait_across(z)

                work(grid.slot(jnp.where(i < 2, grid.x, 1 - grid.x), z))

            return inner

        lax.fori_loop(0, 4, visit, 0)
        return carry

    lax.fori_loop(0, line, stage, 0)
    hidden_copy = pltpu.make_async_copy(hidden, hidden_all, hidden_sem)
    hidden_copy.start()
    for k in range(line - 1, -1, -1):
        scatter.send_across(grid.order(k))

    tiles = width // tile

    def wide_loads(t, start):
        j, buf = t % tiles, t % 2
        c = pl.ds(pl.multiple_of(j * tile, tile), tile)
        for i, source in enumerate((normed_all, tangent_all)):
            copy = pltpu.make_async_copy(source.at[:, :, c], wide.at[buf, i], tile_sem.at[buf, i])
            copy.start() if start else copy.wait()

    def stages(t):
        j, buf = t % tiles, t % 2
        c = pl.ds(pl.multiple_of(j * tile, tile), tile)
        return [
            remote(src, dst, stage_sem.at[buf, i], stage_recv.at[j, i], grid.twin)
            for i, (src, dst) in enumerate(
                (
                    (stage_a.at[buf, 0], part_gate.at[c, :]),
                    (stage_a.at[buf, 1], part_up.at[c, :]),
                    (stage_b.at[buf], part_down.at[:, c]),
                )
            )
        ]

    def results(t):
        j, buf = t % tiles, t % 2
        c = pl.ds(pl.multiple_of(j * tile, tile), tile)
        return [
            pltpu.make_async_copy(src, dst, stage_sem.at[buf, i])
            for i, (src, dst) in enumerate(
                (
                    (stage_a.at[buf, 0], grad_gate.at[c, :]),
                    (stage_a.at[buf, 1], grad_up.at[c, :]),
                    (stage_b.at[buf], grad_down.at[:, c]),
                )
            )
        ]

    def pieces(t):
        c = pl.ds(pl.multiple_of((t % tiles) * tile, tile), tile)
        return [
            (part_gate.at[c, :], piece_a.at[0]),
            (part_up.at[c, :], piece_a.at[1]),
            (part_down.at[:, c], piece_b),
        ]

    wide_loads(0, True)

    def weights(t, carry):
        buf = t % 2
        pl.when(t + 1 < 2 * tiles)(lambda: wide_loads(t + 1, True))
        wide_loads(t, False)
        tall = blocks * rows
        tokens = wide[buf, 0].reshape(tall, tile)
        tangents = wide[buf, 1].reshape(tall, tile)

        @pl.when(t < tiles)
        def _():
            theirs = slice(cols, 2 * cols)

            @pl.when(t >= 2)
            def _():
                for copy in stages(t - 2):
                    copy.wait_send()

            stage_a[buf, 0] = dot(tokens, dgate[:, theirs], TN).astype(BF)
            stage_a[buf, 1] = dot(tokens, dup[:, theirs], TN).astype(BF)
            stage_b[buf] = dot(hidden[:, theirs], tangents, TN).astype(BF)
            for copy in stages(t):
                copy.start()

        @pl.when(t >= tiles)
        def _():
            for copy in stages(t):
                copy.wait_recv()
            loads = [
                pltpu.make_async_copy(src, dst, piece_sem.at[i])
                for i, (src, dst) in enumerate(pieces(t))
            ]
            for copy in loads:
                copy.start()

            @pl.when(t < tiles + 2)
            def _():
                for copy in stages(t - 2):
                    copy.wait_send()

            @pl.when(t >= tiles + 2)
            def _():
                for copy in results(t - 2):
                    copy.wait()

            mine = slice(0, cols)
            own_gate = dot(tokens, dgate[:, mine], TN)
            own_up = dot(tokens, dup[:, mine], TN)
            own_down = dot(hidden[:, mine], tangents, TN)
            for copy in loads:
                copy.wait()
            stage_a[buf, 0] = (own_gate + piece_a[0].astype(F32)).astype(BF)
            stage_a[buf, 1] = (own_up + piece_a[1].astype(F32)).astype(BF)
            stage_b[buf] = (own_down + piece_b[...].astype(F32)).astype(BF)
            for copy in results(t):
                copy.start()

        for k in range(line - 1, 0, -1):
            when = 2 * tiles - 1 - (k - 1) * (tiles // (line - 1))
            pl.when(t == when)(lambda k=k: scatter.pass_on(grid.order(k)))
        return carry

    lax.fori_loop(0, 2 * tiles, weights, 0)
    scatter.own(grad_sum)
    for t in (2 * tiles - 2, 2 * tiles - 1):
        for copy in results(t):
            copy.wait()
    for gather in gathers:
        gather.finish()
    scatter.finish()
    hidden_copy.wait()


def feed_call(normed, tangent, gates, ups, downs, line):
    rows, width = normed.shape
    cols = gates[0].shape[1]
    blocks, parts, tile = 2 * line, 2, 256
    tiles = width // tile
    tall = blocks * rows
    shapes = jax.ShapeDtypeStruct
    hbm = lambda *s: shapes(s, BF)
    return pl.pallas_call(
        functools.partial(feed_kernel, line, parts, tile),
        out_shape=(
            shapes((rows, width), F32),
            hbm(blocks, rows, width), hbm(blocks, rows, width), hbm(tall, 2 * cols),
            hbm(width, cols), hbm(width, cols), hbm(cols, width),
            hbm(width, cols), hbm(width, cols), hbm(cols, width),
        ),
        in_specs=[ANY] * 8,
        out_specs=(pl.BlockSpec(memory_space=pltpu.VMEM),) + (ANY,) * 9,
        scratch_shapes=[
            pltpu.VMEM((width, 2 * cols), BF), pltpu.VMEM((width, 2 * cols), BF), pltpu.VMEM((2 * cols, width), BF),
            pltpu.VMEM((tall, 2 * cols), BF), pltpu.VMEM((tall, 2 * cols), BF), pltpu.VMEM((tall, 2 * cols), BF),
            pltpu.VMEM((rows, width), BF), pltpu.VMEM((rows, width), BF),
            *scatter_scratch(line, rows, width, parts),
            pltpu.SemaphoreType.DMA((2, line, parts, 3)), pltpu.SemaphoreType.DMA((2, blocks, parts)),
            pltpu.SemaphoreType.DMA((8,)),
            pltpu.VMEM((2, 2, blocks, rows, tile), BF), pltpu.SemaphoreType.DMA((2, 2)),
            pltpu.VMEM((2, 2, tile, cols), BF), pltpu.VMEM((2, cols, tile), BF),
            pltpu.SemaphoreType.DMA((2, 3)), pltpu.SemaphoreType.DMA((tiles, 3)),
            pltpu.VMEM((2, tile, cols), BF), pltpu.VMEM((cols, tile), BF), pltpu.SemaphoreType.DMA((3,)),
            pltpu.SemaphoreType.DMA,
        ],
        compiler_params=pltpu.CompilerParams(
            collective_id=1, has_side_effects=True, vmem_limit_bytes=63 * 2**20
        ),
        name="feed",
    )(normed, tangent, gates[0], gates[1], ups[0], ups[1], downs[0], downs[1])


def branch_kernel(
    line, parts,
    hidden_all, down_own, down_twin,
    result,
    down_w, hidden, load_sem,
    partial, from_across, from_line, total, across_send, across_recv, line_send, line_recv,
):
    grid = Grid(2, line)
    cols, width = down_own.shape
    rows = partial.shape[1]
    grid.greet(False)
    load_pairs(
        [
            (down_own, down_w.at[pl.ds(0, cols)]),
            (down_twin, down_w.at[pl.ds(cols, cols)]),
            (hidden_all, hidden),
        ],
        load_sem,
    )
    scatter = Scatter(
        grid, partial, from_across, from_line, total,
        (across_send, across_recv, line_send, line_recv), parts,
    )

    def work(i, carry):
        z = grid.order(line - 1 - i // 2)
        slot = grid.slot(jnp.where(i % 2 == 0, 1 - grid.x, grid.x), z)
        spot = pl.ds(pl.multiple_of(slot * rows, rows), rows)

        def tile(j, inner):
            c = pl.ds(pl.multiple_of(j * cols, cols), cols)
            partial[slot, :, c] = dot(hidden[spot, :], down_w[:, c], NN).astype(BF)
            return inner

        lax.fori_loop(0, width // cols, tile, 0)
        pl.when(i % 2 == 0)(lambda: scatter.send_across(z))
        return carry

    lax.fori_loop(0, 2 * line, work, 0)

    def along(i, carry):
        scatter.pass_on(grid.order(line - 1 - i))
        return carry

    lax.fori_loop(0, line - 1, along, 0)
    scatter.own(result)
    scatter.finish()


def branch_call(hidden_all, downs, line, rows):
    cols, width = downs[0].shape
    parts = 2
    return pl.pallas_call(
        functools.partial(branch_kernel, line, parts),
        out_shape=jax.ShapeDtypeStruct((rows, width), F32),
        in_specs=[ANY] * 3,
        out_specs=pl.BlockSpec(memory_space=pltpu.VMEM),
        scratch_shapes=[
            pltpu.VMEM((2 * cols, width), BF),
            pltpu.VMEM(hidden_all.shape, BF),
            pltpu.SemaphoreType.DMA((3,)),
            *scatter_scratch(line, rows, width, parts),
        ],
        compiler_params=pltpu.CompilerParams(
            collective_id=2, has_side_effects=True, vmem_limit_bytes=60 * 2**20
        ),
        name="branch",
    )(hidden_all, downs[0], downs[1])


def sums_kernel(
    line, parts,
    normed, attended, grad_qkv, grad_out, gains,
    result,
    both_normed, both_attended, both_qkv, both_out, both_gains, load_sem, twin_send, twin_recv,
    partial, from_across, from_line, total, across_send, across_recv, line_send, line_recv,
    mine, theirs, mirror_send, mirror_recv,
):
    grid = Grid(2, line)
    rows, width = normed.shape
    run = partial.shape[1]
    narrow = grad_qkv.shape[1]
    grid.greet(True, True)
    scatter = Scatter(
        grid, partial, from_across, from_line, total,
        (across_send, across_recv, line_send, line_recv), parts,
    )
    own, twin = pl.ds(0, rows), pl.ds(rows, rows)
    pairs = [
        (normed, both_normed.at[own], both_normed.at[twin]),
        (grad_qkv, both_qkv.at[own], both_qkv.at[twin]),
        (attended, both_attended.at[own], both_attended.at[twin]),
        (grad_out, both_out.at[own], both_out.at[twin]),
        (gains, both_gains.at[0], both_gains.at[1]),
    ]
    swaps = [
        remote(src, there, twin_send.at[i], twin_recv.at[i], grid.twin)
        for i, (src, _, there) in enumerate(pairs)
    ]
    for copy in swaps:
        copy.start()
    load_pairs([(src, here) for src, here, _ in pairs], load_sem)
    for copy in swaps:
        copy.wait()
    tall = line * run
    tile = 512

    def column(j, carry):
        x = jnp.where(j == 0, 1 - grid.x, grid.x)
        features = pl.ds(pl.multiple_of((x * 2 + grid.core) * tall, tall), tall)
        blocks = pl.ds(x * line, line)

        def wide(left, right, first):
            def step(i, inner):
                c = pl.ds(pl.multiple_of(i * tile, tile), tile)
                to = pl.ds(pl.multiple_of(first + i * tile, 128), tile)
                value = dot(left[:, features], right[:, c], TN).astype(BF)
                partial[blocks, :, to] = value.reshape(line, run, tile)
                return inner

            lax.fori_loop(0, right.shape[1] // tile, step, 0)

        wide(both_normed, both_qkv, 0)
        wide(both_attended, both_out, narrow)
        pair = both_gains[0, features].astype(F32) + both_gains[1, features].astype(F32)
        partial[blocks, :, narrow + width :] = pair.astype(BF).reshape(line, run, gains.shape[1])

        @pl.when(j == 0)
        def _():
            for k in range(line - 1, -1, -1):
                scatter.send_across(grid.order(k))

        return carry

    lax.fori_loop(0, 2, column, 0)

    def along(i, carry):
        scatter.pass_on(grid.order(line - 1 - i))
        return carry

    lax.fori_loop(0, line - 1, along, 0)

    def swap(part):
        here = scatter.run(part)
        return remote(
            mine.at[here], theirs.at[here], mirror_send.at[part], mirror_recv.at[part], grid.mirror
        )

    scatter.own(mine, lambda part: swap(part).start())
    for part in range(parts):
        swap(part).wait()
        here = scatter.run(part)
        result[here] = mine[here].astype(F32) + theirs[here].astype(F32)
    scatter.finish()


def sums_call(normed, attended, grad_qkv, grad_out, gains, line, run):
    rows, width = normed.shape
    narrow, few = grad_qkv.shape[1], gains.shape[1]
    whole, parts = narrow + width + few, 4
    return pl.pallas_call(
        functools.partial(sums_kernel, line, parts),
        out_shape=jax.ShapeDtypeStruct((run, whole), F32),
        in_specs=[ANY] * 5,
        out_specs=pl.BlockSpec(memory_space=pltpu.VMEM),
        scratch_shapes=[
            pltpu.VMEM((2 * rows, width), BF), pltpu.VMEM((2 * rows, width), BF),
            pltpu.VMEM((2 * rows, narrow), BF), pltpu.VMEM((2 * rows, width), BF),
            pltpu.VMEM((2, width, few), BF),
            pltpu.SemaphoreType.DMA((5,)), pltpu.SemaphoreType.DMA((5,)), pltpu.SemaphoreType.DMA((5,)),
            *scatter_scratch(line, run, whole, parts),
            pltpu.VMEM((run, whole), BF), pltpu.VMEM((run, whole), BF),
            pltpu.SemaphoreType.DMA((parts,)), pltpu.SemaphoreType.DMA((parts,)),
        ],
        compiler_params=pltpu.CompilerParams(
            collective_id=3, has_side_effects=True, vmem_limit_bytes=60 * 2**20
        ),
        name="sums",
    )(normed, attended, grad_qkv, grad_out, gains)


def body(
    tokens,
    places,
    cotangent,
    gain_attn,
    gain_mlp,
    w_query,
    key_projection,
    value_projection,
    w_out,
    w_gate,
    w_up,
    w_down,
    kernels,
):
    sequence_total, segment_length, width = tokens.shape
    total_length = places.shape[1]
    total_rows = sequence_total * segment_length
    position = lax.axis_index("context")
    local_positions = lax.dynamic_slice_in_dim(places, position * segment_length, segment_length, 1)
    rotary_angles = local_positions.reshape(total_rows).astype(jnp.float32)[:, None] * frequencies(
        HEAD_SIZE // 2
    )
    gain_one, gain_two, query_w, key_weight_local, value_w, out_w = (
        lax.all_gather(gain_attn, ("fsdp", "context"), axis=0, tiled=True),
        lax.all_gather(gain_mlp, ("fsdp", "context"), axis=0, tiled=True),
        lax.all_gather(w_query, ("fsdp", "context"), axis=0, tiled=True),
        lax.all_gather(key_projection, ("fsdp", "context"), axis=0, tiled=True),
        lax.all_gather(value_projection, ("fsdp", "context"), axis=0, tiled=True),
        lax.all_gather(w_out, ("fsdp", "context"), axis=0, tiled=True),
    )
    gain_first = gain_one.astype(jnp.float32)
    gain_second = gain_two.astype(jnp.float32)
    inputs_f = tokens.astype(jnp.float32).reshape(total_rows, width)
    factor_one = lax.rsqrt(jnp.mean(inputs_f * inputs_f, axis=-1, keepdims=True) + norm_eps)
    unit_one = inputs_f * factor_one
    normed_tokens = (unit_one * gain_first).astype(jnp.bfloat16)
    query_pre = jnp.dot(normed_tokens, query_w, preferred_element_type=jnp.float32).reshape(
        total_rows, QUERY_HEADS, HEAD_SIZE
    )
    key_unrotated = jnp.dot(
        normed_tokens, key_weight_local, preferred_element_type=jnp.float32
    ).reshape(total_rows, KEY_VALUE_HEADS, HEAD_SIZE)
    value_matrix_rows = jnp.dot(normed_tokens, value_w, preferred_element_type=jnp.float32).astype(
        jnp.bfloat16
    )
    query_rows = apply_rotary(query_pre, rotary_angles).astype(jnp.bfloat16)
    key_matrix_rows = (
        apply_rotary(key_unrotated, rotary_angles)
        .astype(jnp.bfloat16)
        .reshape(sequence_total, segment_length, KEY_VALUE_HEADS * HEAD_SIZE)
    )
    key_all, value_all = (
        lax.all_gather(key_matrix_rows, "context", axis=1, tiled=True),
        lax.all_gather(
            value_matrix_rows.reshape(sequence_total, segment_length, KEY_VALUE_HEADS * HEAD_SIZE),
            "context",
            axis=1,
            tiled=True,
        ),
    )
    head_query = query_head_rows(query_rows, sequence_total, segment_length)
    head_key = key_heads(key_all, sequence_total, total_length)
    head_value = key_heads(value_all, sequence_total, total_length)
    query_positions = jnp.repeat(local_positions, KEY_VALUE_HEADS, axis=0)
    key_positions = jnp.repeat(places, KEY_VALUE_HEADS, axis=0)
    attended = lax.map(
        forward_head, (head_query, head_key, head_value, query_positions, key_positions)
    )
    attended = merge_queries(attended, sequence_total, segment_length).astype(jnp.bfloat16)
    middle = inputs_f + jnp.dot(attended, out_w, preferred_element_type=jnp.float32)
    factor_two = lax.rsqrt(jnp.mean(middle * middle, axis=-1, keepdims=True) + norm_eps)
    unit_two = middle * factor_two
    normed_mlp = (unit_two * gain_second).astype(jnp.bfloat16)
    tangent = cotangent.reshape(total_rows, width)
    tangent_f = tangent.astype(jnp.float32)
    if kernels:
        line = lax.axis_size("context")
        swap = [(i, i ^ 1) for i in range(lax.axis_size("fsdp"))]
        gates, ups, downs = (
            (w, lax.ppermute(w, "fsdp", swap)) for w in (w_gate, w_up, w_down)
        )
        grad_normed, _, _, hidden_all, *sums = feed_call(
            normed_mlp, tangent, gates, ups, downs, line
        )[:7]
        branch = branch_call(hidden_all, downs, line, total_rows)
        flip = [(i, 1 - i) for i in range(2)]
        grad_w_gate, grad_w_up, grad_w_down = (
            g.astype(jnp.float32) + lax.ppermute(g, "replica", flip).astype(jnp.float32)
            for g in sums
        )
    else:
        group = ("fsdp", "context")
        normed_all = lax.all_gather(normed_mlp, group, axis=0, tiled=True)
        tangent_all = lax.all_gather(tangent, group, axis=0, tiled=True)
        branch_part, kept_values = feed_forward(normed_all, w_gate, w_up, w_down)
        grad_part, grad_w_gate, grad_w_up, grad_w_down = feed_back(
            normed_all, tangent_all, w_gate, w_up, w_down, kept_values
        )
        grad_normed = lax.psum_scatter(
            grad_part.astype(jnp.bfloat16), group, scatter_dimension=0, tiled=True
        ).astype(jnp.float32)
        branch = lax.psum_scatter(
            branch_part.astype(jnp.bfloat16), group, scatter_dimension=0, tiled=True
        ).astype(jnp.float32)
        grad_w_gate, grad_w_up, grad_w_down = (
            lax.psum(g.astype(jnp.bfloat16), "replica").astype(jnp.float32)
            for g in (grad_w_gate, grad_w_up, grad_w_down)
        )
    outcome = middle + branch
    scaled_two = grad_normed * gain_second
    term_gain_two = jnp.sum(grad_normed * unit_two, axis=0)
    grad_middle = tangent_f + factor_two * (
        scaled_two - unit_two * jnp.mean(scaled_two * unit_two, axis=-1, keepdims=True)
    )
    grad_branch = grad_middle.astype(jnp.bfloat16)
    grad_attended = times_nt(grad_branch, out_w).astype(jnp.bfloat16)
    head_grad = query_head_rows(grad_attended, sequence_total, segment_length)
    grad_q, grad_k, grad_v = lax.map(
        backward_head, (head_query, head_key, head_value, head_grad, query_positions, key_positions)
    )
    local_key_gradient, local_value_gradient = (
        lax.psum_scatter(
            merge_keys(grad_k, sequence_total, total_length).astype(jnp.bfloat16),
            "context",
            scatter_dimension=1,
            tiled=True,
        ).astype(jnp.float32),
        lax.psum_scatter(
            merge_keys(grad_v, sequence_total, total_length).astype(jnp.bfloat16),
            "context",
            scatter_dimension=1,
            tiled=True,
        ).astype(jnp.float32),
    )
    grad_query = (
        inverse_rotary(
            merge_queries(grad_q, sequence_total, segment_length).reshape(
                total_rows, QUERY_HEADS, HEAD_SIZE
            ),
            rotary_angles,
        )
        .reshape(total_rows, QUERY_HEADS * HEAD_SIZE)
        .astype(jnp.bfloat16)
    )
    grad_key = (
        inverse_rotary(
            local_key_gradient.reshape(total_rows, KEY_VALUE_HEADS, HEAD_SIZE), rotary_angles
        )
        .reshape(total_rows, KEY_VALUE_HEADS * HEAD_SIZE)
        .astype(jnp.bfloat16)
    )
    value_gradient = local_value_gradient.reshape(total_rows, KEY_VALUE_HEADS * HEAD_SIZE).astype(
        jnp.bfloat16
    )
    grad_normed_one = (
        times_nt(grad_query, query_w)
        + times_nt(grad_key, key_weight_local)
        + times_nt(value_gradient, value_w)
    )
    scaled_one = grad_normed_one * gain_first
    term_gain_one = jnp.sum(grad_normed_one * unit_one, axis=0)
    grad_inputs = grad_middle + factor_one * (
        scaled_one - unit_one * jnp.mean(scaled_one * unit_one, axis=-1, keepdims=True)
    )
    if kernels:
        gains = jnp.stack([term_gain_one, term_gain_two], axis=1).astype(jnp.bfloat16)
        gains = jnp.pad(gains, ((0, 0), (0, 126)))
        grad_qkv = jnp.concatenate([grad_query, grad_key, value_gradient], axis=1)
        packed = sums_call(
            normed_tokens, attended, grad_qkv, grad_branch, gains, line, w_query.shape[0]
        )
        ends, start = [], 0
        for size in (width, grad_key.shape[1], grad_key.shape[1], width, 1, 1):
            ends.append(packed[:, start : start + size])
            start += size
        summed = (*ends[:4], grad_w_gate, grad_w_up, grad_w_down, ends[4][:, 0], ends[5][:, 0])
    else:
        term_out = times_t(attended, grad_branch)
        term_query = times_t(normed_tokens, grad_query)
        term_key = times_t(normed_tokens, grad_key)
        term_value = times_t(normed_tokens, value_gradient)
        share_query, share_key, share_value, share_out, share_gain_one, share_gain_two = (
            lax.psum_scatter(term_query.astype(jnp.bfloat16), ("fsdp", "context"), scatter_dimension=0, tiled=True),
            lax.psum_scatter(term_key.astype(jnp.bfloat16), ("fsdp", "context"), scatter_dimension=0, tiled=True),
            lax.psum_scatter(term_value.astype(jnp.bfloat16), ("fsdp", "context"), scatter_dimension=0, tiled=True),
            lax.psum_scatter(term_out.astype(jnp.bfloat16), ("fsdp", "context"), scatter_dimension=0, tiled=True),
            lax.psum_scatter(term_gain_one, ("fsdp", "context"), scatter_dimension=0, tiled=True),
            lax.psum_scatter(term_gain_two, ("fsdp", "context"), scatter_dimension=0, tiled=True),
        )
        summed = (
            lax.psum(share_query.astype(jnp.bfloat16), "replica").astype(jnp.float32),
            lax.psum(share_key.astype(jnp.bfloat16), "replica").astype(jnp.float32),
            lax.psum(share_value.astype(jnp.bfloat16), "replica").astype(jnp.float32),
            lax.psum(share_out.astype(jnp.bfloat16), "replica").astype(jnp.float32),
            grad_w_gate,
            grad_w_up,
            grad_w_down,
            lax.psum(share_gain_one.astype(jnp.bfloat16), "replica").astype(jnp.float32),
            lax.psum(share_gain_two.astype(jnp.bfloat16), "replica").astype(jnp.float32),
        )
    out = outcome.astype(jnp.bfloat16).reshape(sequence_total, segment_length, width)
    grad_tokens = grad_inputs.astype(jnp.bfloat16).reshape(sequence_total, segment_length, width)
    return (
        out,
        grad_tokens,
        summed[0],
        summed[1],
        summed[2],
        summed[3],
        summed[4],
        summed[5],
        summed[6],
        summed[7],
        summed[8],
    )


def solution(mesh):
    placed = (
        P(("replica", "fsdp"), "context", None),
        P(("replica", "fsdp"), None),
        P(("replica", "fsdp"), "context", None),
        P(("fsdp", "context")),
        P(("fsdp", "context")),
        P(("fsdp", "context"), None),
        P(("fsdp", "context"), None),
        P(("fsdp", "context"), None),
        P(("fsdp", "context"), None),
        P(None, ("fsdp", "context")),
        P(None, ("fsdp", "context")),
        P(("fsdp", "context"), None),
    )
    kernels = (mesh.shape["replica"], mesh.shape["fsdp"], mesh.shape["context"]) == (2, 4, 4)
    return jax.shard_map(
        functools.partial(body, kernels=kernels),
        mesh=mesh,
        in_specs=placed,
        out_specs=(
            P(("replica", "fsdp"), "context", None),
            P(("replica", "fsdp"), "context", None),
            P(("fsdp", "context"), None),
            P(("fsdp", "context"), None),
            P(("fsdp", "context"), None),
            P(("fsdp", "context"), None),
            P(None, ("fsdp", "context")),
            P(None, ("fsdp", "context")),
            P(("fsdp", "context"), None),
            P(("fsdp", "context")),
            P(("fsdp", "context")),
        ),
        check_vma=False,
    )
```

```python
import functools

import jax
import jax.numpy as jnp
from jax import lax
from jax.experimental import pallas as pl
from jax.experimental.pallas import tpu as pltpu
from jax.sharding import PartitionSpec as P

QUERY_HEADS = 32
KEY_VALUE_HEADS = 8
HEAD_SIZE = 64


norm_eps = 1e-05
rope_base = 500000.0


def frequencies(half):
    return rope_base ** (-2.0 * jnp.arange(half, dtype=jnp.float32) / (2.0 * half))


def apply_rotary(angle_table, rotary_angles):
    half = angle_table.shape[-1] // 2
    first_half = angle_table[..., :half]
    second_half = angle_table[..., half:]
    cosine = jnp.cos(rotary_angles)[..., None, :]
    sine = jnp.sin(rotary_angles)[..., None, :]
    return jnp.concatenate(
        [first_half * cosine - second_half * sine, second_half * cosine + first_half * sine],
        axis=-1,
    )


def inverse_rotary(angle_table, rotary_angles):
    half = angle_table.shape[-1] // 2
    first_half = angle_table[..., :half]
    second_half = angle_table[..., half:]
    cosine = jnp.cos(rotary_angles)[..., None, :]
    sine = jnp.sin(rotary_angles)[..., None, :]
    return jnp.concatenate(
        [first_half * cosine + second_half * sine, second_half * cosine - first_half * sine],
        axis=-1,
    )


def times_t(left, right):
    return lax.dot_general(
        left, right, (((0,), (0,)), ((), ())), preferred_element_type=jnp.float32
    )


def times_nt(left, right):
    return lax.dot_general(
        left, right, (((1,), (1,)), ((), ())), preferred_element_type=jnp.float32
    )


def query_head_rows(angle_table, sequence_total, segment_length):
    reshaped_heads = angle_table.reshape(
        sequence_total, segment_length, KEY_VALUE_HEADS, QUERY_HEADS // KEY_VALUE_HEADS, HEAD_SIZE
    )
    return jnp.transpose(reshaped_heads, (0, 2, 1, 3, 4)).reshape(
        sequence_total * KEY_VALUE_HEADS, segment_length, QUERY_HEADS // KEY_VALUE_HEADS, HEAD_SIZE
    )


def key_heads(angle_table, sequence_total, total_length):
    reshaped_heads = angle_table.reshape(sequence_total, total_length, KEY_VALUE_HEADS, HEAD_SIZE)
    return jnp.transpose(reshaped_heads, (0, 2, 1, 3)).reshape(
        sequence_total * KEY_VALUE_HEADS, total_length, HEAD_SIZE
    )


def merge_queries(angle_table, sequence_total, segment_length):
    reshaped_heads = angle_table.reshape(
        sequence_total, KEY_VALUE_HEADS, segment_length, QUERY_HEADS // KEY_VALUE_HEADS, HEAD_SIZE
    )
    return jnp.transpose(reshaped_heads, (0, 2, 1, 3, 4)).reshape(
        sequence_total * segment_length, QUERY_HEADS * HEAD_SIZE
    )


def merge_keys(angle_table, sequence_total, total_length):
    reshaped_heads = angle_table.reshape(sequence_total, KEY_VALUE_HEADS, total_length, HEAD_SIZE)
    return jnp.transpose(reshaped_heads, (0, 2, 1, 3)).reshape(
        sequence_total, total_length, KEY_VALUE_HEADS * HEAD_SIZE
    )


def softmax_weights(part_query, part_key, place_query, place_key):
    allowed = place_key[None, :] <= place_query[:, None]
    scores = jnp.einsum(
        "qrd,kd->rqk", part_query, part_key, preferred_element_type=jnp.float32
    ) * HEAD_SIZE ** (-0.5)
    scores = jnp.where(allowed[None], scores, -1e30)
    return jax.nn.softmax(scores, axis=-1)


def forward_head(packed):
    part_query, part_key, part_value, place_query, place_key = packed
    probs = softmax_weights(part_query, part_key, place_query, place_key)
    return jnp.einsum(
        "rqk,kd->qrd", probs.astype(jnp.bfloat16), part_value, preferred_element_type=jnp.float32
    )


def backward_head(packed):
    part_query, part_key, part_value, part_grad, place_query, place_key = packed
    probs = softmax_weights(part_query, part_key, place_query, place_key)
    grad_probs = jnp.einsum(
        "qrd,kd->rqk", part_grad, part_value, preferred_element_type=jnp.float32
    )
    row_delta = jnp.sum(probs * grad_probs, axis=-1, keepdims=True)
    grad_scores = (probs * (grad_probs - row_delta)).astype(jnp.bfloat16)
    grad_query = jnp.einsum(
        "rqk,kd->qrd", grad_scores, part_key, preferred_element_type=jnp.float32
    ) * HEAD_SIZE ** (-0.5)
    grad_key = jnp.einsum(
        "rqk,qrd->kd", grad_scores, part_query, preferred_element_type=jnp.float32
    ) * HEAD_SIZE ** (-0.5)
    value_gradient = jnp.einsum(
        "rqk,qrd->kd", probs.astype(jnp.bfloat16), part_grad, preferred_element_type=jnp.float32
    )
    return (grad_query, grad_key, value_gradient)


def feed_forward(normed_rows, gate_w, up_w, down_w):
    gate_pre = jnp.dot(normed_rows, gate_w, preferred_element_type=jnp.float32)
    up_proj = jnp.dot(normed_rows, up_w, preferred_element_type=jnp.float32)
    sigmoid_gate = jax.nn.sigmoid(gate_pre)
    hidden = (gate_pre * sigmoid_gate * up_proj).astype(jnp.bfloat16)
    return (
        jnp.dot(hidden, down_w, preferred_element_type=jnp.float32),
        (gate_pre, up_proj, sigmoid_gate, hidden),
    )


def feed_back(normed_rows, grad_rows, gate_w, up_w, down_w, kept_values):
    gate_pre, up_proj, sigmoid_gate, hidden = kept_values
    grad_hidden = times_nt(grad_rows, down_w)
    term_down = times_t(hidden, grad_rows)
    grad_gate = (
        grad_hidden * up_proj * (sigmoid_gate * (1.0 + gate_pre * (1.0 - sigmoid_gate)))
    ).astype(jnp.bfloat16)
    grad_up = (grad_hidden * (gate_pre * sigmoid_gate)).astype(jnp.bfloat16)
    grad_normed = times_nt(grad_gate, gate_w) + times_nt(grad_up, up_w)
    return (grad_normed, times_t(normed_rows, grad_gate), times_t(normed_rows, grad_up), term_down)


MESH = pl.DeviceIdType.MESH
ANY = pl.BlockSpec(memory_space=pl.ANY)
BF = jnp.bfloat16
F32 = jnp.float32
NN = (((1,), (0,)), ((), ()))
NT = (((1,), (1,)), ((), ()))
TN = (((0,), (0,)), ((), ()))


def dot(left, right, dims):
    return lax.dot_general(left, right, dims, preferred_element_type=F32)


class Grid:
    def __init__(self, chips, line):
        self.chips, self.line = chips, line
        self.replica = lax.axis_index("replica")
        flat = lax.axis_index("fsdp")
        self.x, self.core = flat // 2, flat % 2
        self.z = lax.axis_index("context")
        self.has_left, self.has_right = self.z > 0, self.z + 1 < line
        self.left = (self.replica, flat, self.z - 1)
        self.right = (self.replica, flat, self.z + 1)
        self.across = (self.replica, (1 - self.x) * 2 + self.core, self.z)
        self.twin = (self.replica, self.x * 2 + 1 - self.core, self.z)
        self.mirror = (1 - self.replica, flat, self.z)

    def order(self, k):
        z, n = self.z, self.line
        near = 2 * jnp.minimum(z, n - 1 - z)
        alternate = jnp.where(k % 2 == 1, z - (k + 1) // 2, z + k // 2)
        return jnp.where(k <= near, alternate, jnp.where(2 * z < n, k, n - 1 - k))

    def slot(self, x, z):
        return x * self.line + z

    def greet(self, twin, mirror=False):
        barrier = pltpu.get_barrier_semaphore()

        def tell(device):
            pl.semaphore_signal(barrier, inc=1, device_id=device, device_id_type=MESH)

        pl.when(self.has_left)(lambda: tell(self.left))
        pl.when(self.has_right)(lambda: tell(self.right))
        tell(self.across)
        if twin:
            tell(self.twin)
        if mirror:
            tell(self.mirror)
        count = 1 + int(twin) + int(mirror) + self.has_left.astype(jnp.int32) + self.has_right.astype(jnp.int32)
        pl.semaphore_wait(barrier, count)


def remote(src, dst, send, recv, device):
    return pltpu.make_async_remote_copy(
        src_ref=src, dst_ref=dst, send_sem=send, recv_sem=recv, device_id=device, device_id_type=MESH
    )


class Gather:
    def __init__(self, grid, block, everything, send, recv, parts):
        self.grid, self.everything, self.send, self.recv = grid, everything, send, recv
        self.block = block
        self.parts = parts
        self.rows = everything.shape[1] // parts

    def piece(self, x, z, part):
        start = pl.multiple_of(part * self.rows, self.rows)
        return self.everything.at[self.grid.slot(x, z), pl.ds(start, self.rows)]

    def copy(self, z, part, link, first=False):
        grid = self.grid
        device = (grid.right, grid.left, grid.across)[link]
        there = self.piece(grid.x, z, part)
        here = self.block.at[pl.ds(part * self.rows, self.rows)] if first else there
        return remote(
            here, there, self.send.at[z, part, link], self.recv.at[grid.slot(grid.x, z), part], device
        )

    def links(self, z, action, first=False):
        grid = self.grid
        for part in range(self.parts):
            for link, go in (
                (0, jnp.logical_and(z <= grid.z, grid.has_right)),
                (1, jnp.logical_and(z >= grid.z, grid.has_left)),
            ):
                pl.when(go)(lambda part=part, link=link: action(self.copy(z, part, link, first)))
            action(self.copy(z, part, 2, first))

    def send_own(self):
        self.links(self.grid.z, lambda c: c.start(), True)

    def forward(self, distance, part):
        grid = self.grid
        for z, there, link, go in (
            (grid.z - distance, grid.z >= distance, 0, grid.has_right),
            (grid.z + distance, grid.z + distance < grid.line, 1, grid.has_left),
        ):

            @pl.when(there)
            def _(z=z, link=link, go=go):
                self.copy(z, part, 2).wait_recv()
                pl.when(go)(lambda: self.copy(z, part, link).start())
                self.copy(z, part, 2).start()

    def wait_across(self, z):
        grid = self.grid
        for part in range(self.parts):
            here = self.piece(1 - grid.x, z, part)
            sem = self.recv.at[grid.slot(1 - grid.x, z), part]
            remote(here, here, self.send.at[z, part, 2], sem, grid.across).wait_recv()

    def finish(self):
        def step(z, carry):
            self.links(z, lambda c: c.wait_send())
            return carry

        lax.fori_loop(0, self.grid.line, step, 0)


class Scatter:
    def __init__(self, grid, partial, from_across, from_line, total, sems, parts):
        self.grid, self.partial, self.from_across = grid, partial, from_across
        self.from_line, self.total = from_line, total
        self.across_send, self.across_recv, self.line_send, self.line_recv = sems
        self.parts = parts
        self.rows = partial.shape[1] // parts

    def run(self, part):
        return pl.ds(part * self.rows, self.rows)

    def place(self, z):
        return z if self.from_across is None else self.grid.slot(self.grid.x, z)

    def across(self, z, part):
        grid = self.grid
        return remote(
            self.partial.at[grid.slot(1 - grid.x, z), self.run(part)],
            self.from_across.at[z, self.run(part)],
            self.across_send.at[z, part],
            self.across_recv.at[z, part],
            grid.across,
        )

    def along(self, z, part, leftward):
        grid = self.grid
        place = z if leftward else z - 1 + grid.line - 1
        return remote(
            self.partial.at[self.place(z), self.run(part)],
            self.from_line.at[place, self.run(part)],
            self.line_send.at[z, part],
            self.line_recv.at[place, part],
            grid.left if leftward else grid.right,
        )

    def send_across(self, z):
        for part in range(self.parts):
            self.across(z, part).start()

    def add_line(self, z, part, leftward):
        self.along(z, part, leftward).wait_recv()
        place = z if leftward else z - 1 + self.grid.line - 1
        self.total[...] += self.from_line[place, self.run(part)].astype(F32)

    def gather_sum(self, z, part):
        grid = self.grid
        value = self.partial[self.place(z), self.run(part)].astype(F32)
        if self.from_across is not None:
            self.across(z, part).wait_recv()
            value = value + self.from_across[z, self.run(part)].astype(F32)
        self.total[...] = value
        pl.when(jnp.logical_and(z <= grid.z, grid.has_right))(lambda: self.add_line(z, part, True))
        pl.when(jnp.logical_and(z >= grid.z, grid.has_left))(lambda: self.add_line(z, part, False))

    def pass_on(self, z):
        grid = self.grid
        for part in range(self.parts):
            self.gather_sum(z, part)
            self.partial[self.place(z), self.run(part)] = self.total[...].astype(BF)
            pl.when(z < grid.z)(lambda part=part: self.along(z, part, True).start())
            pl.when(z > grid.z)(lambda part=part: self.along(z, part, False).start())

    def own(self, result, after=None):
        for part in range(self.parts):
            self.gather_sum(self.grid.z, part)
            result[self.run(part)] = self.total[...].astype(result.dtype)
            if after is not None:
                after(part)

    def finish(self):
        grid = self.grid

        def step(z, carry):
            for part in range(self.parts):
                if self.from_across is not None:
                    self.across(z, part).wait_send()
                pl.when(z < grid.z)(lambda part=part: self.along(z, part, True).wait_send())
                pl.when(z > grid.z)(lambda part=part: self.along(z, part, False).wait_send())
            return carry

        lax.fori_loop(0, grid.line, step, 0)


def scatter_scratch(line, rows, width, parts):
    return [
        pltpu.VMEM((2 * line, rows, width), BF),
        pltpu.VMEM((line, rows, width), BF),
        pltpu.VMEM((2 * line - 2, rows, width), BF),
        pltpu.VMEM((rows // parts, width), F32),
        pltpu.SemaphoreType.DMA((line, parts)),
        pltpu.SemaphoreType.DMA((line, parts)),
        pltpu.SemaphoreType.DMA((line, parts)),
        pltpu.SemaphoreType.DMA((2 * line - 2, parts)),
    ]


def load_pairs(pairs, sems):
    copies = [pltpu.make_async_copy(src, dst, sems.at[i]) for i, (src, dst) in enumerate(pairs)]
    for copy in copies:
        copy.start()
    for copy in copies:
        copy.wait()


def feed_kernel(
    line, parts, tile,
    normed, tangent_all, gate_own, gate_twin, up_own, up_twin, down_own, down_twin,
    grad_sum, normed_all, hidden_all, grad_gate, grad_up, grad_down,
    part_gate, part_up, part_down,
    gate_w, up_w, down_w, hidden, dgate, dup, rows_n, rows_t,
    partial, from_across, from_line, total, across_send, across_recv, line_send, line_recv,
    gather_send, gather_recv, load_sem, wide, tile_sem, stage_a, stage_b, stage_sem, stage_recv, piece_a, piece_b, piece_sem, hidden_sem,
):
    grid = Grid(2, line)
    rows, width = normed.shape
    cols = gate_own.shape[1]
    blocks = 2 * line
    me = grid.slot(grid.x, grid.z)
    grid.greet(True)
    gathers = [
        Gather(grid, normed, normed_all, gather_send.at[0], gather_recv.at[0], parts),
    ]
    scatter = Scatter(
        grid, partial, from_across, from_line, total,
        (across_send, across_recv, line_send, line_recv), parts,
    )
    for gather in gathers:
        gather.send_own()
    load_pairs(
        [
            (gate_own, gate_w.at[:, pl.ds(0, cols)]),
            (gate_twin, gate_w.at[:, pl.ds(cols, cols)]),
            (up_own, up_w.at[:, pl.ds(0, cols)]),
            (up_twin, up_w.at[:, pl.ds(cols, cols)]),
            (down_own, down_w.at[pl.ds(0, cols)]),
            (down_twin, down_w.at[pl.ds(cols, cols)]),
            (normed, rows_n),
        ],
        load_sem,
    )
    load_pairs([(rows_n, normed_all.at[me])], load_sem)

    def work(slot):
        load_pairs([(normed_all.at[slot], rows_n), (tangent_all.at[slot], rows_t)], load_sem)
        spot = pl.ds(pl.multiple_of(slot * rows, rows), rows)

        def hidden_tile(j, carry):
            c = pl.ds(pl.multiple_of(j * cols, cols), cols)
            gate = dot(rows_n[...], gate_w[:, c], NN)
            up = dot(rows_n[...], up_w[:, c], NN)
            grad = dot(rows_t[...], down_w[c, :], NT)
            sig = jax.nn.sigmoid(gate)
            silu = gate * sig
            hidden[spot, c] = (silu * up).astype(BF)
            dgate[spot, c] = (grad * up * (sig * (1.0 + gate * (1.0 - sig)))).astype(BF)
            dup[spot, c] = (grad * silu).astype(BF)
            return carry

        lax.fori_loop(0, 2, hidden_tile, 0)

        def back_tile(j, carry):
            c = pl.ds(pl.multiple_of(j * cols, cols), cols)
            sums = dot(dgate[spot, :], gate_w[c, :], NT) + dot(dup[spot, :], up_w[c, :], NT)
            partial[slot, :, c] = sums.astype(BF)
            return carry

        lax.fori_loop(0, width // cols, back_tile, 0)

    def stage(distance, carry):
        @pl.when(distance + 1 < line)
        def _():
            for gather in gathers:
                for part in range(parts):
                    gather.forward(distance + 1, part)

        def visit(i, inner):
            z = grid.z + jnp.where(i % 2 == 0, -distance, distance)
            inside = jnp.logical_and(z >= 0, z < line)

            @pl.when(jnp.logical_and(inside, jnp.logical_or(distance > 0, i % 2 == 0)))
            def _():
                @pl.when(i >= 2)
                def _():
                    for gather in gathers:
                        gather.wait_across(z)

                work(grid.slot(jnp.where(i < 2, grid.x, 1 - grid.x), z))

            return inner

        lax.fori_loop(0, 4, visit, 0)
        return carry

    lax.fori_loop(0, line, stage, 0)
    hidden_copy = pltpu.make_async_copy(hidden, hidden_all, hidden_sem)
    hidden_copy.start()
    for k in range(line - 1, -1, -1):
        scatter.send_across(grid.order(k))

    tiles = width // tile

    def wide_loads(t, start):
        j, buf = t % tiles, t % 2
        c = pl.ds(pl.multiple_of(j * tile, tile), tile)
        for i, source in enumerate((normed_all, tangent_all)):
            copy = pltpu.make_async_copy(source.at[:, :, c], wide.at[buf, i], tile_sem.at[buf, i])
            copy.start() if start else copy.wait()

    def stages(t):
        j, buf = t % tiles, t % 2
        c = pl.ds(pl.multiple_of(j * tile, tile), tile)
        return [
            remote(src, dst, stage_sem.at[buf, i], stage_recv.at[j, i], grid.twin)
            for i, (src, dst) in enumerate(
                (
                    (stage_a.at[buf, 0], part_gate.at[c, :]),
                    (stage_a.at[buf, 1], part_up.at[c, :]),
                    (stage_b.at[buf], part_down.at[:, c]),
                )
            )
        ]

    def results(t):
        j, buf = t % tiles, t % 2
        c = pl.ds(pl.multiple_of(j * tile, tile), tile)
        return [
            pltpu.make_async_copy(src, dst, stage_sem.at[buf, i])
            for i, (src, dst) in enumerate(
                (
                    (stage_a.at[buf, 0], grad_gate.at[c, :]),
                    (stage_a.at[buf, 1], grad_up.at[c, :]),
                    (stage_b.at[buf], grad_down.at[:, c]),
                )
            )
        ]

    def pieces(t):
        c = pl.ds(pl.multiple_of((t % tiles) * tile, tile), tile)
        return [
            (part_gate.at[c, :], piece_a.at[0]),
            (part_up.at[c, :], piece_a.at[1]),
            (part_down.at[:, c], piece_b),
        ]

    wide_loads(0, True)

    def weights(t, carry):
        buf = t % 2
        pl.when(t + 1 < 2 * tiles)(lambda: wide_loads(t + 1, True))
        wide_loads(t, False)
        tall = blocks * rows
        tokens = wide[buf, 0].reshape(tall, tile)
        tangents = wide[buf, 1].reshape(tall, tile)

        @pl.when(t < tiles)
        def _():
            theirs = slice(cols, 2 * cols)

            @pl.when(t >= 2)
            def _():
                for copy in stages(t - 2):
                    copy.wait_send()

            stage_a[buf, 0] = dot(tokens, dgate[:, theirs], TN).astype(BF)
            stage_a[buf, 1] = dot(tokens, dup[:, theirs], TN).astype(BF)
            stage_b[buf] = dot(hidden[:, theirs], tangents, TN).astype(BF)
            for copy in stages(t):
                copy.start()

        @pl.when(t >= tiles)
        def _():
            for copy in stages(t):
                copy.wait_recv()
            loads = [
                pltpu.make_async_copy(src, dst, piece_sem.at[i])
                for i, (src, dst) in enumerate(pieces(t))
            ]
            for copy in loads:
                copy.start()

            @pl.when(t < tiles + 2)
            def _():
                for copy in stages(t - 2):
                    copy.wait_send()

            @pl.when(t >= tiles + 2)
            def _():
                for copy in results(t - 2):
                    copy.wait()

            mine = slice(0, cols)
            own_gate = dot(tokens, dgate[:, mine], TN)
            own_up = dot(tokens, dup[:, mine], TN)
            own_down = dot(hidden[:, mine], tangents, TN)
            for copy in loads:
                copy.wait()
            stage_a[buf, 0] = (own_gate + piece_a[0].astype(F32)).astype(BF)
            stage_a[buf, 1] = (own_up + piece_a[1].astype(F32)).astype(BF)
            stage_b[buf] = (own_down + piece_b[...].astype(F32)).astype(BF)
            for copy in results(t):
                copy.start()

        for k in range(line - 1, 0, -1):
            when = 2 * tiles - 1 - (k - 1) * (tiles // (line - 1))
            pl.when(t == when)(lambda k=k: scatter.pass_on(grid.order(k)))
        return carry

    lax.fori_loop(0, 2 * tiles, weights, 0)
    scatter.own(grad_sum)
    for t in (2 * tiles - 2, 2 * tiles - 1):
        for copy in results(t):
            copy.wait()
    for gather in gathers:
        gather.finish()
    scatter.finish()
    hidden_copy.wait()


def feed_call(normed, tangent_all, gates, ups, downs, line):
    rows, width = normed.shape
    cols = gates[0].shape[1]
    blocks, parts, tile = 2 * line, 2, 256
    tiles = width // tile
    tall = blocks * rows
    shapes = jax.ShapeDtypeStruct
    hbm = lambda *s: shapes(s, BF)
    return pl.pallas_call(
        functools.partial(feed_kernel, line, parts, tile),
        out_shape=(
            shapes((rows, width), F32),
            hbm(blocks, rows, width), hbm(tall, 2 * cols),
            hbm(width, cols), hbm(width, cols), hbm(cols, width),
            hbm(width, cols), hbm(width, cols), hbm(cols, width),
        ),
        in_specs=[ANY] * 8,
        out_specs=(pl.BlockSpec(memory_space=pltpu.VMEM),) + (ANY,) * 8,
        scratch_shapes=[
            pltpu.VMEM((width, 2 * cols), BF), pltpu.VMEM((width, 2 * cols), BF), pltpu.VMEM((2 * cols, width), BF),
            pltpu.VMEM((tall, 2 * cols), BF), pltpu.VMEM((tall, 2 * cols), BF), pltpu.VMEM((tall, 2 * cols), BF),
            pltpu.VMEM((rows, width), BF), pltpu.VMEM((rows, width), BF),
            *scatter_scratch(line, rows, width, parts),
            pltpu.SemaphoreType.DMA((1, line, parts, 3)), pltpu.SemaphoreType.DMA((1, blocks, parts)),
            pltpu.SemaphoreType.DMA((8,)),
            pltpu.VMEM((2, 2, blocks, rows, tile), BF), pltpu.SemaphoreType.DMA((2, 2)),
            pltpu.VMEM((2, 2, tile, cols), BF), pltpu.VMEM((2, cols, tile), BF),
            pltpu.SemaphoreType.DMA((2, 3)), pltpu.SemaphoreType.DMA((tiles, 3)),
            pltpu.VMEM((2, tile, cols), BF), pltpu.VMEM((cols, tile), BF), pltpu.SemaphoreType.DMA((3,)),
            pltpu.SemaphoreType.DMA,
        ],
        compiler_params=pltpu.CompilerParams(
            collective_id=1, has_side_effects=True, vmem_limit_bytes=63 * 2**20
        ),
        name="feed",
    )(normed, tangent_all, gates[0], gates[1], ups[0], ups[1], downs[0], downs[1])


def sums_kernel(
    line, parts,
    normed, attended, grad_qkv, grad_out, gains,
    result,
    both_normed, both_attended, both_qkv, both_out, both_gains, load_sem, twin_send, twin_recv,
    partial, from_across, from_line, total, across_send, across_recv, line_send, line_recv,
    mine, theirs, mirror_send, mirror_recv,
):
    grid = Grid(2, line)
    rows, width = normed.shape
    run = partial.shape[1]
    narrow = grad_qkv.shape[1]
    grid.greet(True, True)
    scatter = Scatter(
        grid, partial, from_across, from_line, total,
        (across_send, across_recv, line_send, line_recv), parts,
    )
    own, twin = pl.ds(0, rows), pl.ds(rows, rows)
    pairs = [
        (normed, both_normed.at[own], both_normed.at[twin]),
        (grad_qkv, both_qkv.at[own], both_qkv.at[twin]),
        (attended, both_attended.at[own], both_attended.at[twin]),
        (grad_out, both_out.at[own], both_out.at[twin]),
        (gains, both_gains.at[0], both_gains.at[1]),
    ]
    swaps = [
        remote(src, there, twin_send.at[i], twin_recv.at[i], grid.twin)
        for i, (src, _, there) in enumerate(pairs)
    ]
    for copy in swaps:
        copy.start()
    load_pairs([(src, here) for src, here, _ in pairs], load_sem)
    for copy in swaps:
        copy.wait()
    tall = line * run
    tile = 512

    def column(j, carry):
        x = jnp.where(j == 0, 1 - grid.x, grid.x)
        features = pl.ds(pl.multiple_of((x * 2 + grid.core) * tall, tall), tall)
        blocks = pl.ds(x * line, line)

        def wide(left, right, first):
            def step(i, inner):
                c = pl.ds(pl.multiple_of(i * tile, tile), tile)
                to = pl.ds(pl.multiple_of(first + i * tile, 128), tile)
                value = dot(left[:, features], right[:, c], TN).astype(BF)
                partial[blocks, :, to] = value.reshape(line, run, tile)
                return inner

            lax.fori_loop(0, right.shape[1] // tile, step, 0)

        wide(both_normed, both_qkv, 0)
        wide(both_attended, both_out, narrow)
        pair = both_gains[0, features].astype(F32) + both_gains[1, features].astype(F32)
        partial[blocks, :, narrow + width :] = pair.astype(BF).reshape(line, run, gains.shape[1])

        @pl.when(j == 0)
        def _():
            for k in range(line - 1, -1, -1):
                scatter.send_across(grid.order(k))

        return carry

    lax.fori_loop(0, 2, column, 0)

    def along(i, carry):
        scatter.pass_on(grid.order(line - 1 - i))
        return carry

    lax.fori_loop(0, line - 1, along, 0)

    def swap(part):
        here = scatter.run(part)
        return remote(
            mine.at[here], theirs.at[here], mirror_send.at[part], mirror_recv.at[part], grid.mirror
        )

    scatter.own(mine, lambda part: swap(part).start())
    for part in range(parts):
        swap(part).wait()
        here = scatter.run(part)
        result[here] = mine[here].astype(F32) + theirs[here].astype(F32)
    scatter.finish()


def sums_call(normed, attended, grad_qkv, grad_out, gains, line, run):
    rows, width = normed.shape
    narrow, few = grad_qkv.shape[1], gains.shape[1]
    whole, parts = narrow + width + few, 4
    return pl.pallas_call(
        functools.partial(sums_kernel, line, parts),
        out_shape=jax.ShapeDtypeStruct((run, whole), F32),
        in_specs=[ANY] * 5,
        out_specs=pl.BlockSpec(memory_space=pltpu.VMEM),
        scratch_shapes=[
            pltpu.VMEM((2 * rows, width), BF), pltpu.VMEM((2 * rows, width), BF),
            pltpu.VMEM((2 * rows, narrow), BF), pltpu.VMEM((2 * rows, width), BF),
            pltpu.VMEM((2, width, few), BF),
            pltpu.SemaphoreType.DMA((5,)), pltpu.SemaphoreType.DMA((5,)), pltpu.SemaphoreType.DMA((5,)),
            *scatter_scratch(line, run, whole, parts),
            pltpu.VMEM((run, whole), BF), pltpu.VMEM((run, whole), BF),
            pltpu.SemaphoreType.DMA((parts,)), pltpu.SemaphoreType.DMA((parts,)),
        ],
        compiler_params=pltpu.CompilerParams(
            collective_id=3, has_side_effects=True, vmem_limit_bytes=60 * 2**20
        ),
        name="sums",
    )(normed, attended, grad_qkv, grad_out, gains)


def weights_kernel(line, block, everything, send, recv, twin_send, twin_recv, staged, load_sem):
    grid = Grid(2, line)
    rows = block.shape[0] // 4
    grid.greet(True, True)
    near = grid.x * line + grid.z
    carry_a, carry_b = grid.replica * 2, grid.replica * 2 + 1
    other_a, other_b = (1 - grid.replica) * 2, (1 - grid.replica) * 2 + 1
    right, left, across, mirror = range(4)
    devices = (grid.right, grid.left, grid.across, grid.mirror)

    def run(quarter):
        return pl.ds(pl.multiple_of(quarter * rows, rows), rows)

    def place(x, core, z, quarter):
        return everything.at[(x * 2 + core) * line + z, run(quarter)]

    def copy(x, z, quarter, link, first=False):
        there = place(x, grid.core, z, quarter)
        here = block.at[run(quarter)] if first else there
        unit = x * line + z
        return remote(
            here, there, send.at[quarter, unit, link], recv.at[quarter, unit], devices[link]
        )

    def share(x, z, quarter, first=False):
        there = place(x, grid.core, z, quarter)
        here = block.at[run(quarter)] if first else there
        unit = x * line + z
        return remote(
            here, there, twin_send.at[quarter, unit], twin_recv.at[quarter, unit], grid.twin
        )

    def arrived(x, z, quarter):
        copy(x, z, quarter, across).wait_recv()
        share(x, z, quarter).start()

    copy(grid.x, grid.z, carry_b, across, True).start()
    copy(grid.x, grid.z, carry_a, across, True).start()
    copy(grid.x, grid.z, other_a, across, True).start()
    for link, go in ((right, grid.has_right), (left, grid.has_left)):

        @pl.when(go)
        def _(link=link):
            copy(grid.x, grid.z, carry_a, link, True).start()
            copy(grid.x, grid.z, carry_b, link, True).start()

    for quarter in range(4):
        share(grid.x, grid.z, quarter, True).start()
    load_pairs([(block, staged)], load_sem)
    load_pairs([(staged, everything.at[(grid.x * 2 + grid.core) * line + grid.z])], load_sem)

    arrived(1 - grid.x, grid.z, carry_b)
    copy(1 - grid.x, grid.z, carry_b, mirror).start()
    for link, go in ((right, grid.has_right), (left, grid.has_left)):
        pl.when(go)(lambda link=link: copy(1 - grid.x, grid.z, carry_b, link).start())

    def sides(distance):
        return (
            (grid.z - distance, grid.z >= distance, right, grid.has_right),
            (grid.z + distance, grid.z + distance < line, left, grid.has_left),
        )

    def step(distance, carry):
        for z, there, link, go in sides(distance):

            @pl.when(there)
            def _(z=z, link=link, go=go):
                for x, quarter in (
                    (grid.x, carry_a),
                    (grid.x, carry_b),
                    (1 - grid.x, carry_b),
                ):
                    arrived(x, z, quarter)
                    copy(x, z, quarter, mirror).start()
                    pl.when(go)(lambda x=x, quarter=quarter: copy(x, z, quarter, link).start())
                copy(grid.x, z, carry_a, across).start()

        for z, there, _, _ in sides(distance - 1):

            @pl.when(jnp.logical_and(there, distance > 1))
            def _(z=z):
                arrived(grid.x, z, other_a)
                copy(grid.x, z, other_a, across).start()

        return carry

    lax.fori_loop(1, line + 1, step, 0)

    def last(z, carry):
        arrived(1 - grid.x, z, carry_a)
        arrived(1 - grid.x, z, other_a)
        arrived(1 - grid.x, z, other_b)
        pl.when(z != grid.z)(lambda: arrived(grid.x, z, other_b))
        return carry

    lax.fori_loop(0, line, last, 0)

    def finish(z, carry):
        away = z != grid.z
        for x in (grid.x, 1 - grid.x):
            for quarter in range(4):
                share(x, z, quarter).wait()
        for x, quarter in ((grid.x, carry_a), (grid.x, carry_b), (1 - grid.x, carry_b)):
            to_mirror = jnp.logical_or(away, jnp.bool_(x is not grid.x))
            pl.when(to_mirror)(
                lambda x=x, quarter=quarter: copy(x, z, quarter, mirror).wait_send()
            )
            for link, go in (
                (right, jnp.logical_and(z <= grid.z, grid.has_right)),
                (left, jnp.logical_and(z >= grid.z, grid.has_left)),
            ):
                pl.when(go)(
                    lambda x=x, quarter=quarter, link=link: copy(x, z, quarter, link).wait_send()
                )
        copy(grid.x, z, carry_a, across).wait_send()
        copy(grid.x, z, other_a, across).wait_send()
        return carry

    lax.fori_loop(0, line, finish, 0)
    copy(grid.x, grid.z, carry_b, across, True).wait_send()


def weights_call(block, line):
    rows, width = block.shape
    units = 2 * line
    return pl.pallas_call(
        functools.partial(weights_kernel, line),
        out_shape=jax.ShapeDtypeStruct((2 * units, rows, width), BF),
        in_specs=[ANY],
        out_specs=ANY,
        scratch_shapes=[
            pltpu.SemaphoreType.DMA((4, units, 4)), pltpu.SemaphoreType.DMA((4, units)),
            pltpu.SemaphoreType.DMA((4, units)), pltpu.SemaphoreType.DMA((4, units)),
            pltpu.VMEM((rows, width), BF), pltpu.SemaphoreType.DMA((1,)),
        ],
        compiler_params=pltpu.CompilerParams(
            collective_id=4, has_side_effects=True, vmem_limit_bytes=32 * 2**20
        ),
        name="weights",
    )(block)


class Line:
    def __init__(self, grid, block, everything, send, recv):
        self.grid, self.block, self.everything = grid, block, everything
        self.send, self.recv = send, recv

    def copy(self, z, link, first=False):
        grid = self.grid
        there = self.everything.at[z]
        here = self.block if first else there
        device = (grid.right, grid.left)[link]
        return remote(here, there, self.send.at[z, link], self.recv.at[z], device)

    def send_own(self):
        grid = self.grid
        for link, go in ((0, grid.has_right), (1, grid.has_left)):
            pl.when(go)(lambda link=link: self.copy(grid.z, link, True).start())

    def forward(self, distance):
        grid = self.grid
        for z, there, link, go in (
            (grid.z - distance, grid.z >= distance, 0, grid.has_right),
            (grid.z + distance, grid.z + distance < grid.line, 1, grid.has_left),
        ):

            @pl.when(there)
            def _(z=z, link=link, go=go):
                self.copy(z, link).wait_recv()
                pl.when(go)(lambda: self.copy(z, link).start())

    def finish(self):
        grid = self.grid

        def step(z, carry):
            for link, go in (
                (0, jnp.logical_and(z <= grid.z, grid.has_right)),
                (1, jnp.logical_and(z >= grid.z, grid.has_left)),
            ):
                pl.when(go)(lambda link=link: self.copy(z, link).wait_send())
            return carry

        lax.fori_loop(0, grid.line, step, 0)


def halves(pair, half):
    pair = pair.astype(F32)
    turned = pltpu.roll(pair, HEAD_SIZE, 1)
    lane = lax.broadcasted_iota(jnp.int32, pair.shape, 1) // HEAD_SIZE
    first = jnp.where(half == 0, pair, turned)
    second = jnp.where(half == 0, turned, pair)
    both = jnp.concatenate([first, second], axis=0)
    return jnp.where(jnp.concatenate([lane, lane], axis=0) == half, both, 0.0).astype(BF)


def unhalves(both, half):
    rows = both.shape[0] // 2
    first, second = both[:rows], both[rows:]
    lane = lax.broadcasted_iota(jnp.int32, first.shape, 1) // HEAD_SIZE
    first = jnp.where(half == 0, first, pltpu.roll(first, HEAD_SIZE, 1))
    second = jnp.where(half == 0, pltpu.roll(second, HEAD_SIZE, 1), second)
    return jnp.where(lane == 0, first, second)


def attend_kernel(
    line, parts,
    queries, keyed, tangent, bias, tokens, weights, gain,
    attended, middle, normed, logs, keyed_out, tangent_all,
    keyed_all, query_v, bias_v, token_v, weight_v, scores, probs, sums, stage, load_sem,
    key_send, key_recv, send, recv, own_sem,
):
    grid = Grid(2, line)
    rows, width = queries.shape
    narrow = keyed.shape[1] // 2
    total = bias.shape[1]
    me = grid.slot(grid.x, grid.z)
    grid.greet(False)
    line_keys = Line(grid, keyed, keyed_all, key_send, key_recv)
    gather = Gather(grid, tangent, tangent_all, send, recv, parts)
    line_keys.send_own()
    for part in range(parts):
        gather.copy(grid.z, part, 2, True).start()
    load_pairs(
        [
            (keyed, keyed_all.at[grid.z]),
            (tangent, stage),
            (queries, query_v),
            (bias, bias_v),
            (tokens, token_v),
            (weights, weight_v),
        ],
        load_sem,
    )
    load_pairs([(stage, tangent_all.at[me])], own_sem)
    for distance in range(line):
        if distance:
            line_keys.forward(distance)
        for link, go in (
            (0, jnp.logical_and(grid.z == distance, grid.has_right)),
            (1, jnp.logical_and(line - 1 - grid.z == distance, grid.has_left)),
        ):

            @pl.when(go)
            def _(link=link):
                for part in range(parts):
                    gather.copy(grid.z, part, link, True).start()


    logs[...] = jnp.zeros_like(logs)
    deep = 2 * rows
    chunk = rows
    pairs = width // (2 * HEAD_SIZE)
    group = pairs // (narrow // (2 * HEAD_SIZE))

    def advance(n):
        gather.forward(n // parts + 1, n % parts)

    def pair_step(i, carry):
        c = pl.ds(pl.multiple_of(i * 128, 128), 128)
        half = (i // (group // 2)) % 2
        first_key = pl.multiple_of((i // group) * 128, 128)
        keys = keyed_all[:, :, pl.ds(first_key, 128)].reshape(total, 128)
        values = keyed_all[:, :, pl.ds(first_key + narrow, 128)].reshape(total, 128)
        scores[...] = dot(halves(query_v[:, c], half), keys, NT)

        def soft(j, inner):
            here = pl.ds(pl.multiple_of(j * chunk, chunk), chunk)
            there = pl.ds(pl.multiple_of((j * chunk) % rows, chunk), chunk)
            value = scores[here, :] + bias_v[there, :]
            top = jnp.max(value, axis=1, keepdims=True)
            power = jnp.exp(value - top)
            size = jnp.sum(power, axis=1, keepdims=True)
            probs[here, :] = power.astype(BF)
            sums[here, :] = jnp.broadcast_to(1.0 / size, (chunk, 128))
            lane = lax.broadcasted_iota(jnp.int32, (chunk, 128), 1)
            logs[here, :] = jnp.where(lane == i, top + jnp.log(size), logs[here, :])
            return inner

        lax.fori_loop(0, deep // chunk, soft, 0)
        out = dot(probs[...], values, NN) * sums[...]
        attended[:, c] = unhalves(out, half).astype(BF)

        pl.when(i % 3 == 2)(lambda: advance(i // 3))
        return carry

    lax.fori_loop(0, pairs, pair_step, 0)
    keyed_copy = pltpu.make_async_copy(keyed_all, keyed_out, load_sem.at[0])
    keyed_copy.start()
    advance(pairs // 3)
    tile = 512

    def out_step(j, carry):
        c = pl.ds(pl.multiple_of(j * tile, tile), tile)
        middle[:, c] = token_v[:, c].astype(F32) + dot(attended[...], weight_v[:, c], NN)
        return carry

    lax.fori_loop(0, width // tile, out_step, 0)

    def norm_step(j, carry):
        here = pl.ds(pl.multiple_of(j * chunk, chunk), chunk)
        value = middle[here, :]
        factor = lax.rsqrt(jnp.mean(value * value, axis=1, keepdims=True) + norm_eps)
        normed[here, :] = (value * factor * gain[...]).astype(BF)
        return carry

    lax.fori_loop(0, rows // chunk, norm_step, 0)

    def rest(n, carry):
        advance(n)
        return carry

    lax.fori_loop(pairs // 3 + 1, (line - 1) * parts, rest, 0)
    for z in range(line):
        gather.wait_across(z)
    keyed_copy.wait()
    line_keys.finish()
    gather.finish()


def attend_call(queries, keyed, tangent, bias, tokens, weights, gain, line):
    rows, width = queries.shape
    both = keyed.shape[1]
    total = bias.shape[1]
    blocks, parts = 2 * line, 4
    shapes = jax.ShapeDtypeStruct
    vmem = pl.BlockSpec(memory_space=pltpu.VMEM)
    return pl.pallas_call(
        functools.partial(attend_kernel, line, parts),
        out_shape=(
            shapes((rows, width), BF), shapes((rows, width), F32), shapes((rows, width), BF),
            shapes((2 * rows, 128), F32), shapes((line, rows, both), BF),
            shapes((blocks, rows, width), BF),
        ),
        in_specs=[ANY] * 6 + [vmem],
        out_specs=(vmem, vmem, vmem, vmem, ANY, ANY),
        scratch_shapes=[
            pltpu.VMEM((line, rows, both), BF),
            pltpu.VMEM((rows, width), BF), pltpu.VMEM((rows, total), F32), pltpu.VMEM((rows, width), BF),
            pltpu.VMEM(weights.shape, BF), pltpu.VMEM((2 * rows, total), F32), pltpu.VMEM((2 * rows, total), BF),
            pltpu.VMEM((2 * rows, 128), F32), pltpu.VMEM((rows, width), BF), pltpu.SemaphoreType.DMA((6,)),
            pltpu.SemaphoreType.DMA((line, 2)), pltpu.SemaphoreType.DMA((line,)),
            pltpu.SemaphoreType.DMA((line, parts, 3)), pltpu.SemaphoreType.DMA((blocks, parts)),
            pltpu.SemaphoreType.DMA((1,)),
        ],
        compiler_params=pltpu.CompilerParams(
            collective_id=5, has_side_effects=True, vmem_limit_bytes=60 * 2**20
        ),
        name="attend",
    )(queries, keyed, tangent, bias, tokens, weights, gain)


def back_kernel(
    line, parts, pass_at,
    queries, keyed_all, grads, bias, logs, hidden_all, down_own, down_twin,
    branch, grad_query, grad_keyed,
    query_v, keyed_v, grad_v, bias_v, log_v, scores, gradients, probs, slopes, key_sum, value_sum,
    down_w, hidden, load_sem,
    partial, from_across, from_line, total, across_send, across_recv, line_send, line_recv,
    key_partial, key_line, key_total, key_send, key_recv,
):
    grid = Grid(2, line)
    cols, width = down_own.shape
    rows = partial.shape[1]
    narrow = keyed_all.shape[2] // 2
    length = bias.shape[1]
    grid.greet(False)
    load_pairs(
        [
            (down_own, down_w.at[pl.ds(0, cols)]),
            (down_twin, down_w.at[pl.ds(cols, cols)]),
            (hidden_all, hidden),
            (queries, query_v),
            (keyed_all, keyed_v),
            (grads, grad_v),
            (bias, bias_v),
            (logs, log_v),
        ],
        load_sem,
    )
    scatter = Scatter(
        grid, partial, from_across, from_line, total,
        (across_send, across_recv, line_send, line_recv), parts,
    )
    keyed_scatter = Scatter(
        grid, key_partial, None, key_line, key_total, (None, None, key_send, key_recv), parts
    )

    def work(i, carry):
        z = grid.order(line - 1 - i % line)
        slot = grid.slot(jnp.where(i < line, 1 - grid.x, grid.x), z)
        spot = pl.ds(pl.multiple_of(slot * rows, rows), rows)

        def tile(j, inner):
            c = pl.ds(pl.multiple_of(j * cols, cols), cols)
            partial[slot, :, c] = dot(hidden[spot, :], down_w[:, c], NN).astype(BF)
            return inner

        lax.fori_loop(0, width // cols, tile, 0)
        pl.when(i < line)(lambda: scatter.send_across(z))
        return carry

    lax.fori_loop(0, 2 * line, work, 0)
    deep = 2 * rows
    chunk = rows // 2
    pairs = width // (2 * HEAD_SIZE)
    group = pairs // (narrow // (2 * HEAD_SIZE))

    def pair_step(i, carry):
        c = pl.ds(pl.multiple_of(i * 128, 128), 128)
        half = (i // (group // 2)) % 2
        key_cols = pl.ds(pl.multiple_of((i // group) * 128, 128), 128)
        value_cols = pl.ds(pl.multiple_of((i // group) * 128 + narrow, 128), 128)
        keys = keyed_v[:, :, key_cols].reshape(length, 128)
        values = keyed_v[:, :, value_cols].reshape(length, 128)
        query = halves(query_v[:, c], half)
        grad = halves(grad_v[:, c], half)
        scores[...] = dot(query, keys, NT)
        gradients[...] = dot(grad, values, NT)

        def soft(j, inner):
            here = pl.ds(pl.multiple_of(j * chunk, chunk), chunk)
            there = pl.ds(pl.multiple_of((j * chunk) % rows, chunk), chunk)
            lane = lax.broadcasted_iota(jnp.int32, (chunk, 128), 1)
            log = jnp.sum(jnp.where(lane == i, log_v[here, :], 0.0), axis=1, keepdims=True)
            prob = jnp.exp(scores[here, :] + bias_v[there, :] - log)
            slope = gradients[here, :]
            delta = jnp.sum(prob * slope, axis=1, keepdims=True)
            probs[here, :] = prob.astype(BF)
            slopes[here, :] = (prob * (slope - delta)).astype(BF)
            return inner

        lax.fori_loop(0, deep // chunk, soft, 0)
        back = dot(slopes[...], keys, NN) * HEAD_SIZE ** (-0.5)
        grad_query[:, c] = unhalves(back, half)
        key_part = dot(slopes[...], query, TN)
        value_part = dot(probs[...], grad, TN)

        @pl.when(i % group == 0)
        def _():
            key_sum[...] = key_part
            value_sum[...] = value_part

        @pl.when(i % group != 0)
        def _():
            key_sum[...] += key_part
            value_sum[...] += value_part

        @pl.when(i % group == group - 1)
        def _():
            key_partial[:, :, key_cols] = key_sum[...].astype(BF).reshape(line, rows, 128)
            key_partial[:, :, value_cols] = value_sum[...].astype(BF).reshape(line, rows, 128)

        for k, when in zip(range(line - 1, 0, -1), pass_at):
            pl.when(i == when)(lambda k=k: scatter.pass_on(grid.order(k)))
        return carry

    lax.fori_loop(0, pairs, pair_step, 0)

    def along(i, carry):
        keyed_scatter.pass_on(grid.order(line - 1 - i))
        return carry

    lax.fori_loop(0, line - 1, along, 0)
    for k in range(line - 1 - len(pass_at), 0, -1):
        scatter.pass_on(grid.order(k))
    scatter.own(branch)
    keyed_scatter.own(grad_keyed)
    scatter.finish()
    keyed_scatter.finish()


def back_call(queries, keyed_all, grads, bias, logs, hidden_all, downs, line):
    rows, width = queries.shape
    both = keyed_all.shape[2]
    cols, length = downs[0].shape[0], bias.shape[1]
    parts = 2
    shapes = jax.ShapeDtypeStruct
    vmem = pl.BlockSpec(memory_space=pltpu.VMEM)
    return pl.pallas_call(
        functools.partial(back_kernel, line, parts, (4, 9, 15)),
        out_shape=(
            shapes((rows, width), F32), shapes((rows, width), F32), shapes((rows, both), F32),
        ),
        in_specs=[ANY] * 8,
        out_specs=(vmem,) * 3,
        scratch_shapes=[
            pltpu.VMEM((rows, width), BF), pltpu.VMEM(keyed_all.shape, BF), pltpu.VMEM((rows, width), BF),
            pltpu.VMEM((rows, length), F32), pltpu.VMEM(logs.shape, F32),
            pltpu.VMEM((2 * rows, length), F32), pltpu.VMEM((2 * rows, length), F32),
            pltpu.VMEM((2 * rows, length), BF), pltpu.VMEM((2 * rows, length), BF),
            pltpu.VMEM((length, 128), F32), pltpu.VMEM((length, 128), F32),
            pltpu.VMEM((2 * cols, width), BF), pltpu.VMEM(hidden_all.shape, BF),
            pltpu.SemaphoreType.DMA((8,)),
            *scatter_scratch(line, rows, width, parts),
            pltpu.VMEM((line, rows, both), BF), pltpu.VMEM((2 * line - 2, rows, both), BF),
            pltpu.VMEM((rows // parts, both), F32),
            pltpu.SemaphoreType.DMA((line, parts)), pltpu.SemaphoreType.DMA((2 * line - 2, parts)),
        ],
        compiler_params=pltpu.CompilerParams(
            collective_id=6, has_side_effects=True, vmem_limit_bytes=62 * 2**20
        ),
        name="back",
    )(queries, keyed_all, grads, bias, logs, hidden_all, downs[0], downs[1])


def body(
    tokens,
    places,
    cotangent,
    gain_attn,
    gain_mlp,
    w_query,
    key_projection,
    value_projection,
    w_out,
    w_gate,
    w_up,
    w_down,
):
    sequence_total, segment_length, width = tokens.shape
    total_length = places.shape[1]
    total_rows = sequence_total * segment_length
    position = lax.axis_index("context")
    local_positions = lax.dynamic_slice_in_dim(places, position * segment_length, segment_length, 1)
    rotary_angles = local_positions.reshape(total_rows).astype(jnp.float32)[:, None] * frequencies(
        HEAD_SIZE // 2
    )
    gain_one, gain_two, query_w, key_weight_local, value_w, out_w = (
        lax.all_gather(gain_attn, ("fsdp", "context"), axis=0, tiled=True),
        lax.all_gather(gain_mlp, ("fsdp", "context"), axis=0, tiled=True),
        lax.all_gather(w_query, ("fsdp", "context"), axis=0, tiled=True),
        lax.all_gather(key_projection, ("fsdp", "context"), axis=0, tiled=True),
        lax.all_gather(value_projection, ("fsdp", "context"), axis=0, tiled=True),
        lax.all_gather(w_out, ("fsdp", "context"), axis=0, tiled=True),
    )
    gain_first = gain_one.astype(jnp.float32)
    gain_second = gain_two.astype(jnp.float32)
    inputs_f = tokens.astype(jnp.float32).reshape(total_rows, width)
    factor_one = lax.rsqrt(jnp.mean(inputs_f * inputs_f, axis=-1, keepdims=True) + norm_eps)
    unit_one = inputs_f * factor_one
    normed_tokens = (unit_one * gain_first).astype(jnp.bfloat16)
    query_pre = jnp.dot(normed_tokens, query_w, preferred_element_type=jnp.float32).reshape(
        total_rows, QUERY_HEADS, HEAD_SIZE
    )
    key_unrotated = jnp.dot(
        normed_tokens, key_weight_local, preferred_element_type=jnp.float32
    ).reshape(total_rows, KEY_VALUE_HEADS, HEAD_SIZE)
    value_matrix_rows = jnp.dot(normed_tokens, value_w, preferred_element_type=jnp.float32).astype(
        jnp.bfloat16
    )
    query_rows = apply_rotary(query_pre, rotary_angles).astype(jnp.bfloat16)
    key_matrix_rows = (
        apply_rotary(key_unrotated, rotary_angles)
        .astype(jnp.bfloat16)
        .reshape(sequence_total, segment_length, KEY_VALUE_HEADS * HEAD_SIZE)
    )
    key_all, value_all = (
        lax.all_gather(key_matrix_rows, "context", axis=1, tiled=True),
        lax.all_gather(
            value_matrix_rows.reshape(sequence_total, segment_length, KEY_VALUE_HEADS * HEAD_SIZE),
            "context",
            axis=1,
            tiled=True,
        ),
    )
    head_query = query_head_rows(query_rows, sequence_total, segment_length)
    head_key = key_heads(key_all, sequence_total, total_length)
    head_value = key_heads(value_all, sequence_total, total_length)
    query_positions = jnp.repeat(local_positions, KEY_VALUE_HEADS, axis=0)
    key_positions = jnp.repeat(places, KEY_VALUE_HEADS, axis=0)
    attended = lax.map(
        forward_head, (head_query, head_key, head_value, query_positions, key_positions)
    )
    attended = merge_queries(attended, sequence_total, segment_length).astype(jnp.bfloat16)
    middle = inputs_f + jnp.dot(attended, out_w, preferred_element_type=jnp.float32)
    factor_two = lax.rsqrt(jnp.mean(middle * middle, axis=-1, keepdims=True) + norm_eps)
    unit_two = middle * factor_two
    normed_mlp = (unit_two * gain_second).astype(jnp.bfloat16)
    tangent = cotangent.reshape(total_rows, width)
    tangent_f = tangent.astype(jnp.float32)
    group = ("fsdp", "context")
    normed_all = lax.all_gather(normed_mlp, group, axis=0, tiled=True)
    tangent_all = lax.all_gather(tangent, group, axis=0, tiled=True)
    branch_part, kept_values = feed_forward(normed_all, w_gate, w_up, w_down)
    grad_part, grad_w_gate, grad_w_up, grad_w_down = feed_back(
        normed_all, tangent_all, w_gate, w_up, w_down, kept_values
    )
    grad_normed = lax.psum_scatter(
        grad_part.astype(jnp.bfloat16), group, scatter_dimension=0, tiled=True
    ).astype(jnp.float32)
    branch = lax.psum_scatter(
        branch_part.astype(jnp.bfloat16), group, scatter_dimension=0, tiled=True
    ).astype(jnp.float32)
    outcome = middle + branch
    scaled_two = grad_normed * gain_second
    term_gain_two = jnp.sum(grad_normed * unit_two, axis=0)
    grad_middle = tangent_f + factor_two * (
        scaled_two - unit_two * jnp.mean(scaled_two * unit_two, axis=-1, keepdims=True)
    )
    grad_branch = grad_middle.astype(jnp.bfloat16)
    term_out = times_t(attended, grad_branch)
    grad_attended = times_nt(grad_branch, out_w).astype(jnp.bfloat16)
    head_grad = query_head_rows(grad_attended, sequence_total, segment_length)
    grad_q, grad_k, grad_v = lax.map(
        backward_head, (head_query, head_key, head_value, head_grad, query_positions, key_positions)
    )
    local_key_gradient, local_value_gradient = (
        lax.psum_scatter(
            merge_keys(grad_k, sequence_total, total_length).astype(jnp.bfloat16),
            "context",
            scatter_dimension=1,
            tiled=True,
        ).astype(jnp.float32),
        lax.psum_scatter(
            merge_keys(grad_v, sequence_total, total_length).astype(jnp.bfloat16),
            "context",
            scatter_dimension=1,
            tiled=True,
        ).astype(jnp.float32),
    )
    grad_query = (
        inverse_rotary(
            merge_queries(grad_q, sequence_total, segment_length).reshape(
                total_rows, QUERY_HEADS, HEAD_SIZE
            ),
            rotary_angles,
        )
        .reshape(total_rows, QUERY_HEADS * HEAD_SIZE)
        .astype(jnp.bfloat16)
    )
    grad_key = (
        inverse_rotary(
            local_key_gradient.reshape(total_rows, KEY_VALUE_HEADS, HEAD_SIZE), rotary_angles
        )
        .reshape(total_rows, KEY_VALUE_HEADS * HEAD_SIZE)
        .astype(jnp.bfloat16)
    )
    value_gradient = local_value_gradient.reshape(total_rows, KEY_VALUE_HEADS * HEAD_SIZE).astype(
        jnp.bfloat16
    )
    grad_normed_one = (
        times_nt(grad_query, query_w)
        + times_nt(grad_key, key_weight_local)
        + times_nt(value_gradient, value_w)
    )
    term_query = times_t(normed_tokens, grad_query)
    term_key = times_t(normed_tokens, grad_key)
    term_value = times_t(normed_tokens, value_gradient)
    scaled_one = grad_normed_one * gain_first
    term_gain_one = jnp.sum(grad_normed_one * unit_one, axis=0)
    grad_inputs = grad_middle + factor_one * (
        scaled_one - unit_one * jnp.mean(scaled_one * unit_one, axis=-1, keepdims=True)
    )
    share_query, share_key, share_value, share_out, share_gain_one, share_gain_two = (
        lax.psum_scatter(term_query.astype(jnp.bfloat16), ("fsdp", "context"), scatter_dimension=0, tiled=True),
        lax.psum_scatter(term_key.astype(jnp.bfloat16), ("fsdp", "context"), scatter_dimension=0, tiled=True),
        lax.psum_scatter(term_value.astype(jnp.bfloat16), ("fsdp", "context"), scatter_dimension=0, tiled=True),
        lax.psum_scatter(term_out.astype(jnp.bfloat16), ("fsdp", "context"), scatter_dimension=0, tiled=True),
        lax.psum_scatter(term_gain_one, ("fsdp", "context"), scatter_dimension=0, tiled=True),
        lax.psum_scatter(term_gain_two, ("fsdp", "context"), scatter_dimension=0, tiled=True),
    )
    summed = (
        lax.psum(share_query.astype(jnp.bfloat16), "replica").astype(jnp.float32),
        lax.psum(share_key.astype(jnp.bfloat16), "replica").astype(jnp.float32),
        lax.psum(share_value.astype(jnp.bfloat16), "replica").astype(jnp.float32),
        lax.psum(share_out.astype(jnp.bfloat16), "replica").astype(jnp.float32),
        lax.psum(grad_w_gate.astype(jnp.bfloat16), "replica").astype(jnp.float32),
        lax.psum(grad_w_up.astype(jnp.bfloat16), "replica").astype(jnp.float32),
        lax.psum(grad_w_down.astype(jnp.bfloat16), "replica").astype(jnp.float32),
        lax.psum(share_gain_one.astype(jnp.bfloat16), "replica").astype(jnp.float32),
        lax.psum(share_gain_two.astype(jnp.bfloat16), "replica").astype(jnp.float32),
    )
    out = outcome.astype(jnp.bfloat16).reshape(sequence_total, segment_length, width)
    grad_tokens = grad_inputs.astype(jnp.bfloat16).reshape(sequence_total, segment_length, width)
    return (
        out,
        grad_tokens,
        summed[0],
        summed[1],
        summed[2],
        summed[3],
        summed[4],
        summed[5],
        summed[6],
        summed[7],
        summed[8],
    )


def kernel_body(
    tokens,
    places,
    cotangent,
    gain_attn,
    gain_mlp,
    w_query,
    key_projection,
    value_projection,
    w_out,
    w_gate,
    w_up,
    w_down,
):
    bf16, f32 = jnp.bfloat16, jnp.float32
    sequence_total, segment_length, width = tokens.shape
    total_length = places.shape[1]
    line = lax.axis_size("context")
    narrow = key_projection.shape[1]
    run = w_query.shape[0]
    flip = [(0, 1), (1, 0)]
    swap = [(i, i ^ 1) for i in range(lax.axis_size("fsdp"))]
    gates, ups, downs = ((w, lax.ppermute(w, "fsdp", swap)) for w in (w_gate, w_up, w_down))
    position = lax.axis_index("context")
    local_positions = lax.dynamic_slice_in_dim(places, position * segment_length, segment_length, 1)
    rotary_angles = local_positions.reshape(segment_length).astype(f32)[:, None] * frequencies(
        HEAD_SIZE // 2
    )
    gain_columns = jnp.pad(jnp.stack([gain_attn, gain_mlp], axis=1), ((0, 0), (0, 126)))
    block = jnp.concatenate([w_query, key_projection, value_projection, gain_columns, w_out], axis=1)
    weights = weights_call(block, line).reshape(width, block.shape[1])
    mid = width + 2 * narrow
    in_w, out_w = weights[:, : mid + 128], weights[:, mid + 128 :]
    gain_first = weights[:, mid].astype(f32)
    gain_second = weights[:, mid + 1].astype(f32)
    inputs_f = tokens.astype(f32).reshape(segment_length, width)
    factor_one = lax.rsqrt(jnp.mean(inputs_f * inputs_f, axis=-1, keepdims=True) + norm_eps)
    unit_one = inputs_f * factor_one
    normed_tokens = (unit_one * gain_first).astype(bf16)
    projected = jnp.dot(normed_tokens, in_w, preferred_element_type=f32)

    def heads(first, size):
        return projected[:, first : first + size].reshape(segment_length, size // HEAD_SIZE, HEAD_SIZE)

    query_rows = apply_rotary(heads(0, width), rotary_angles).astype(bf16)
    scaled_query = (query_rows * HEAD_SIZE ** (-0.5)).astype(bf16).reshape(segment_length, width)
    key_rows = apply_rotary(heads(width, narrow), rotary_angles).astype(bf16)
    value_rows = projected[:, width + narrow : mid].astype(bf16)
    keyed = jnp.concatenate([key_rows.reshape(segment_length, narrow), value_rows], axis=1)
    allowed = places.reshape(1, total_length) <= local_positions.reshape(segment_length, 1)
    bias = jnp.where(allowed, 0.0, -1e30).astype(f32)
    tangent = cotangent.reshape(segment_length, width)
    tangent_f = tangent.astype(f32)
    attended, middle, normed_mlp, logs, keyed_all, tangent_all = attend_call(
        scaled_query, keyed, tangent, bias, tokens.reshape(segment_length, width), out_w,
        gain_second.reshape(1, width), line,
    )
    grad_normed, _, hidden_all, *sums = feed_call(normed_mlp, tangent_all, gates, ups, downs, line)[:6]
    grad_w_gate, grad_w_up, grad_w_down = (
        g.astype(f32) + lax.ppermute(g, "replica", flip).astype(f32) for g in sums
    )
    factor_two = lax.rsqrt(jnp.mean(middle * middle, axis=-1, keepdims=True) + norm_eps)
    unit_two = middle * factor_two
    scaled_two = grad_normed * gain_second
    term_gain_two = jnp.sum(grad_normed * unit_two, axis=0)
    grad_middle = tangent_f + factor_two * (
        scaled_two - unit_two * jnp.mean(scaled_two * unit_two, axis=-1, keepdims=True)
    )
    grad_branch = grad_middle.astype(bf16)
    grad_attended = times_nt(grad_branch, out_w).astype(bf16)
    branch, grad_q, grad_keyed = back_call(
        scaled_query, keyed_all, grad_attended, bias, logs, hidden_all, downs, line
    )
    outcome = middle + branch
    grad_query = inverse_rotary(
        grad_q.reshape(segment_length, QUERY_HEADS, HEAD_SIZE), rotary_angles
    ).reshape(segment_length, width)
    grad_key = inverse_rotary(
        grad_keyed[:, :narrow].reshape(segment_length, KEY_VALUE_HEADS, HEAD_SIZE), rotary_angles
    ).reshape(segment_length, narrow)
    value_gradient = grad_keyed[:, narrow:]
    grad_qkv = jnp.concatenate([grad_query, grad_key, value_gradient], axis=1).astype(bf16)
    grad_normed_one = times_nt(grad_qkv, weights[:, :mid])
    scaled_one = grad_normed_one * gain_first
    term_gain_one = jnp.sum(grad_normed_one * unit_one, axis=0)
    grad_inputs = grad_middle + factor_one * (
        scaled_one - unit_one * jnp.mean(scaled_one * unit_one, axis=-1, keepdims=True)
    )
    gains = jnp.stack([term_gain_one, term_gain_two], axis=1).astype(bf16)
    gains = jnp.pad(gains, ((0, 0), (0, 126)))
    packed = sums_call(normed_tokens, attended, grad_qkv, grad_branch, gains, line, run)
    ends, start = [], 0
    for size in (width, narrow, narrow, width, 1, 1):
        ends.append(packed[:, start : start + size])
        start += size
    return (
        outcome.astype(bf16).reshape(tokens.shape),
        grad_inputs.astype(bf16).reshape(tokens.shape),
        *ends[:4],
        grad_w_gate,
        grad_w_up,
        grad_w_down,
        ends[4][:, 0],
        ends[5][:, 0],
    )


def solution(mesh):
    placed = (
        P(("replica", "fsdp"), "context", None),
        P(("replica", "fsdp"), None),
        P(("replica", "fsdp"), "context", None),
        P(("fsdp", "context")),
        P(("fsdp", "context")),
        P(("fsdp", "context"), None),
        P(("fsdp", "context"), None),
        P(("fsdp", "context"), None),
        P(("fsdp", "context"), None),
        P(None, ("fsdp", "context")),
        P(None, ("fsdp", "context")),
        P(("fsdp", "context"), None),
    )
    kernels = (mesh.shape["replica"], mesh.shape["fsdp"], mesh.shape["context"]) == (2, 4, 4)
    return jax.shard_map(
        kernel_body if kernels else body,
        mesh=mesh,
        in_specs=placed,
        out_specs=(
            P(("replica", "fsdp"), "context", None),
            P(("replica", "fsdp"), "context", None),
            P(("fsdp", "context"), None),
            P(("fsdp", "context"), None),
            P(("fsdp", "context"), None),
            P(("fsdp", "context"), None),
            P(None, ("fsdp", "context")),
            P(None, ("fsdp", "context")),
            P(("fsdp", "context"), None),
            P(("fsdp", "context")),
            P(("fsdp", "context")),
        ),
        check_vma=False,
    )
```

```python
import functools

import jax
import jax.numpy as jnp
from jax import lax
from jax.experimental import pallas as pl
from jax.experimental.pallas import tpu as pltpu
from jax.sharding import PartitionSpec as P

QUERY_HEADS = 32
KEY_VALUE_HEADS = 8
HEAD_SIZE = 64


norm_eps = 1e-05
rope_base = 500000.0


def frequencies(half):
    return rope_base ** (-2.0 * jnp.arange(half, dtype=jnp.float32) / (2.0 * half))


def apply_rotary(angle_table, rotary_angles):
    half = angle_table.shape[-1] // 2
    first_half = angle_table[..., :half]
    second_half = angle_table[..., half:]
    cosine = jnp.cos(rotary_angles)[..., None, :]
    sine = jnp.sin(rotary_angles)[..., None, :]
    return jnp.concatenate(
        [first_half * cosine - second_half * sine, second_half * cosine + first_half * sine],
        axis=-1,
    )


def inverse_rotary(angle_table, rotary_angles):
    half = angle_table.shape[-1] // 2
    first_half = angle_table[..., :half]
    second_half = angle_table[..., half:]
    cosine = jnp.cos(rotary_angles)[..., None, :]
    sine = jnp.sin(rotary_angles)[..., None, :]
    return jnp.concatenate(
        [first_half * cosine + second_half * sine, second_half * cosine - first_half * sine],
        axis=-1,
    )


def times_t(left, right):
    return lax.dot_general(
        left, right, (((0,), (0,)), ((), ())), preferred_element_type=jnp.float32
    )


def times_nt(left, right):
    return lax.dot_general(
        left, right, (((1,), (1,)), ((), ())), preferred_element_type=jnp.float32
    )


def query_head_rows(angle_table, sequence_total, segment_length):
    reshaped_heads = angle_table.reshape(
        sequence_total, segment_length, KEY_VALUE_HEADS, QUERY_HEADS // KEY_VALUE_HEADS, HEAD_SIZE
    )
    return jnp.transpose(reshaped_heads, (0, 2, 1, 3, 4)).reshape(
        sequence_total * KEY_VALUE_HEADS, segment_length, QUERY_HEADS // KEY_VALUE_HEADS, HEAD_SIZE
    )


def key_heads(angle_table, sequence_total, total_length):
    reshaped_heads = angle_table.reshape(sequence_total, total_length, KEY_VALUE_HEADS, HEAD_SIZE)
    return jnp.transpose(reshaped_heads, (0, 2, 1, 3)).reshape(
        sequence_total * KEY_VALUE_HEADS, total_length, HEAD_SIZE
    )


def merge_queries(angle_table, sequence_total, segment_length):
    reshaped_heads = angle_table.reshape(
        sequence_total, KEY_VALUE_HEADS, segment_length, QUERY_HEADS // KEY_VALUE_HEADS, HEAD_SIZE
    )
    return jnp.transpose(reshaped_heads, (0, 2, 1, 3, 4)).reshape(
        sequence_total * segment_length, QUERY_HEADS * HEAD_SIZE
    )


def merge_keys(angle_table, sequence_total, total_length):
    reshaped_heads = angle_table.reshape(sequence_total, KEY_VALUE_HEADS, total_length, HEAD_SIZE)
    return jnp.transpose(reshaped_heads, (0, 2, 1, 3)).reshape(
        sequence_total, total_length, KEY_VALUE_HEADS * HEAD_SIZE
    )


def softmax_weights(part_query, part_key, place_query, place_key):
    allowed = place_key[None, :] <= place_query[:, None]
    scores = jnp.einsum(
        "qrd,kd->rqk", part_query, part_key, preferred_element_type=jnp.float32
    ) * HEAD_SIZE ** (-0.5)
    scores = jnp.where(allowed[None], scores, -1e30)
    return jax.nn.softmax(scores, axis=-1)


def forward_head(packed):
    part_query, part_key, part_value, place_query, place_key = packed
    probs = softmax_weights(part_query, part_key, place_query, place_key)
    return jnp.einsum(
        "rqk,kd->qrd", probs.astype(jnp.bfloat16), part_value, preferred_element_type=jnp.float32
    )


def backward_head(packed):
    part_query, part_key, part_value, part_grad, place_query, place_key = packed
    probs = softmax_weights(part_query, part_key, place_query, place_key)
    grad_probs = jnp.einsum(
        "qrd,kd->rqk", part_grad, part_value, preferred_element_type=jnp.float32
    )
    row_delta = jnp.sum(probs * grad_probs, axis=-1, keepdims=True)
    grad_scores = (probs * (grad_probs - row_delta)).astype(jnp.bfloat16)
    grad_query = jnp.einsum(
        "rqk,kd->qrd", grad_scores, part_key, preferred_element_type=jnp.float32
    ) * HEAD_SIZE ** (-0.5)
    grad_key = jnp.einsum(
        "rqk,qrd->kd", grad_scores, part_query, preferred_element_type=jnp.float32
    ) * HEAD_SIZE ** (-0.5)
    value_gradient = jnp.einsum(
        "rqk,qrd->kd", probs.astype(jnp.bfloat16), part_grad, preferred_element_type=jnp.float32
    )
    return (grad_query, grad_key, value_gradient)


def feed_forward(normed_rows, gate_w, up_w, down_w):
    gate_pre = jnp.dot(normed_rows, gate_w, preferred_element_type=jnp.float32)
    up_proj = jnp.dot(normed_rows, up_w, preferred_element_type=jnp.float32)
    sigmoid_gate = jax.nn.sigmoid(gate_pre)
    hidden = (gate_pre * sigmoid_gate * up_proj).astype(jnp.bfloat16)
    return (
        jnp.dot(hidden, down_w, preferred_element_type=jnp.float32),
        (gate_pre, up_proj, sigmoid_gate, hidden),
    )


def feed_back(normed_rows, grad_rows, gate_w, up_w, down_w, kept_values):
    gate_pre, up_proj, sigmoid_gate, hidden = kept_values
    grad_hidden = times_nt(grad_rows, down_w)
    term_down = times_t(hidden, grad_rows)
    grad_gate = (
        grad_hidden * up_proj * (sigmoid_gate * (1.0 + gate_pre * (1.0 - sigmoid_gate)))
    ).astype(jnp.bfloat16)
    grad_up = (grad_hidden * (gate_pre * sigmoid_gate)).astype(jnp.bfloat16)
    grad_normed = times_nt(grad_gate, gate_w) + times_nt(grad_up, up_w)
    return (grad_normed, times_t(normed_rows, grad_gate), times_t(normed_rows, grad_up), term_down)


MESH = pl.DeviceIdType.MESH
ANY = pl.BlockSpec(memory_space=pl.ANY)
BF = jnp.bfloat16
F32 = jnp.float32
NN = (((1,), (0,)), ((), ()))
NT = (((1,), (1,)), ((), ()))
TN = (((0,), (0,)), ((), ()))


def dot(left, right, dims):
    return lax.dot_general(left, right, dims, preferred_element_type=F32)


class Grid:
    def __init__(self, chips, line):
        self.chips, self.line = chips, line
        self.replica = lax.axis_index("replica")
        flat = lax.axis_index("fsdp")
        self.x, self.core = flat // 2, flat % 2
        self.z = lax.axis_index("context")
        self.has_left, self.has_right = self.z > 0, self.z + 1 < line
        self.left = (self.replica, flat, self.z - 1)
        self.right = (self.replica, flat, self.z + 1)
        self.across = (self.replica, (1 - self.x) * 2 + self.core, self.z)
        self.twin = (self.replica, self.x * 2 + 1 - self.core, self.z)
        self.mirror = (1 - self.replica, flat, self.z)

    def order(self, k):
        z, n = self.z, self.line
        near = 2 * jnp.minimum(z, n - 1 - z)
        alternate = jnp.where(k % 2 == 1, z - (k + 1) // 2, z + k // 2)
        return jnp.where(k <= near, alternate, jnp.where(2 * z < n, k, n - 1 - k))

    def slot(self, x, z):
        return x * self.line + z

    def greet(self, twin, mirror=False):
        barrier = pltpu.get_barrier_semaphore()

        def tell(device):
            pl.semaphore_signal(barrier, inc=1, device_id=device, device_id_type=MESH)

        pl.when(self.has_left)(lambda: tell(self.left))
        pl.when(self.has_right)(lambda: tell(self.right))
        tell(self.across)
        if twin:
            tell(self.twin)
        if mirror:
            tell(self.mirror)
        count = 1 + int(twin) + int(mirror) + self.has_left.astype(jnp.int32) + self.has_right.astype(jnp.int32)
        pl.semaphore_wait(barrier, count)


def remote(src, dst, send, recv, device):
    return pltpu.make_async_remote_copy(
        src_ref=src, dst_ref=dst, send_sem=send, recv_sem=recv, device_id=device, device_id_type=MESH
    )


class Gather:
    def __init__(self, grid, block, everything, send, recv, parts):
        self.grid, self.everything, self.send, self.recv = grid, everything, send, recv
        self.block = block
        self.parts = parts
        self.rows = everything.shape[1] // parts

    def piece(self, x, z, part):
        start = pl.multiple_of(part * self.rows, self.rows)
        return self.everything.at[self.grid.slot(x, z), pl.ds(start, self.rows)]

    def copy(self, z, part, link, first=False):
        grid = self.grid
        device = (grid.right, grid.left, grid.across)[link]
        there = self.piece(grid.x, z, part)
        here = self.block.at[pl.ds(part * self.rows, self.rows)] if first else there
        return remote(
            here, there, self.send.at[z, part, link], self.recv.at[grid.slot(grid.x, z), part], device
        )

    def links(self, z, action, first=False):
        grid = self.grid
        for part in range(self.parts):
            for link, go in (
                (0, jnp.logical_and(z <= grid.z, grid.has_right)),
                (1, jnp.logical_and(z >= grid.z, grid.has_left)),
            ):
                pl.when(go)(lambda part=part, link=link: action(self.copy(z, part, link, first)))
            action(self.copy(z, part, 2, first))

    def send_own(self):
        self.links(self.grid.z, lambda c: c.start(), True)

    def forward(self, distance, part):
        grid = self.grid
        for z, there, link, go in (
            (grid.z - distance, grid.z >= distance, 0, grid.has_right),
            (grid.z + distance, grid.z + distance < grid.line, 1, grid.has_left),
        ):

            @pl.when(there)
            def _(z=z, link=link, go=go):
                self.copy(z, part, 2).wait_recv()
                pl.when(go)(lambda: self.copy(z, part, link).start())
                self.copy(z, part, 2).start()

    def wait_across(self, z):
        grid = self.grid
        for part in range(self.parts):
            here = self.piece(1 - grid.x, z, part)
            sem = self.recv.at[grid.slot(1 - grid.x, z), part]
            remote(here, here, self.send.at[z, part, 2], sem, grid.across).wait_recv()

    def finish(self):
        def step(z, carry):
            self.links(z, lambda c: c.wait_send())
            return carry

        lax.fori_loop(0, self.grid.line, step, 0)


class Scatter:
    def __init__(self, grid, partial, from_across, from_line, total, sems, parts):
        self.grid, self.partial, self.from_across = grid, partial, from_across
        self.from_line, self.total = from_line, total
        self.across_send, self.across_recv, self.line_send, self.line_recv = sems
        self.parts = parts
        self.rows = partial.shape[1] // parts

    def run(self, part):
        return pl.ds(part * self.rows, self.rows)

    def place(self, z):
        return z if self.from_across is None else self.grid.slot(self.grid.x, z)

    def across(self, z, part):
        grid = self.grid
        return remote(
            self.partial.at[grid.slot(1 - grid.x, z), self.run(part)],
            self.from_across.at[z, self.run(part)],
            self.across_send.at[z, part],
            self.across_recv.at[z, part],
            grid.across,
        )

    def along(self, z, part, leftward):
        grid = self.grid
        place = z if leftward else z - 1 + grid.line - 1
        return remote(
            self.partial.at[self.place(z), self.run(part)],
            self.from_line.at[place, self.run(part)],
            self.line_send.at[z, part],
            self.line_recv.at[place, part],
            grid.left if leftward else grid.right,
        )

    def send_across(self, z):
        for part in range(self.parts):
            self.across(z, part).start()

    def add_line(self, z, part, leftward):
        self.along(z, part, leftward).wait_recv()
        place = z if leftward else z - 1 + self.grid.line - 1
        self.total[...] += self.from_line[place, self.run(part)].astype(F32)

    def gather_sum(self, z, part):
        grid = self.grid
        value = self.partial[self.place(z), self.run(part)].astype(F32)
        if self.from_across is not None:
            self.across(z, part).wait_recv()
            value = value + self.from_across[z, self.run(part)].astype(F32)
        self.total[...] = value
        pl.when(jnp.logical_and(z <= grid.z, grid.has_right))(lambda: self.add_line(z, part, True))
        pl.when(jnp.logical_and(z >= grid.z, grid.has_left))(lambda: self.add_line(z, part, False))

    def pass_on(self, z, parts=None):
        grid = self.grid
        for part in parts or range(self.parts):
            self.gather_sum(z, part)
            self.partial[self.place(z), self.run(part)] = self.total[...].astype(BF)
            pl.when(z < grid.z)(lambda part=part: self.along(z, part, True).start())
            pl.when(z > grid.z)(lambda part=part: self.along(z, part, False).start())

    def own(self, result):
        for part in range(self.parts):
            self.gather_sum(self.grid.z, part)
            result[self.run(part)] = self.total[...]

    def finish(self):
        grid = self.grid

        def step(z, carry):
            for part in range(self.parts):
                if self.from_across is not None:
                    self.across(z, part).wait_send()
                pl.when(z < grid.z)(lambda part=part: self.along(z, part, True).wait_send())
                pl.when(z > grid.z)(lambda part=part: self.along(z, part, False).wait_send())
            return carry

        lax.fori_loop(0, grid.line, step, 0)


def scatter_scratch(line, rows, width, parts):
    return [
        pltpu.VMEM((2 * line, rows, width), BF),
        pltpu.VMEM((line, rows, width), BF),
        pltpu.VMEM((2 * line - 2, rows, width), BF),
        pltpu.VMEM((rows // parts, width), F32),
        pltpu.SemaphoreType.DMA((line, parts)),
        pltpu.SemaphoreType.DMA((line, parts)),
        pltpu.SemaphoreType.DMA((line, parts)),
        pltpu.SemaphoreType.DMA((2 * line - 2, parts)),
    ]


def load_pairs(pairs, sems):
    copies = [pltpu.make_async_copy(src, dst, sems.at[i]) for i, (src, dst) in enumerate(pairs)]
    for copy in copies:
        copy.start()
    for copy in copies:
        copy.wait()


def feed_kernel(
    line, parts, tile,
    normed, tangent_all, gate_own, gate_twin, up_own, up_twin, down_own, down_twin,
    grad_sum, normed_all, hidden_all, grad_gate, grad_up, grad_down,
    part_gate, part_up, part_down,
    gate_w, up_w, down_w, hidden, dgate, dup, rows_n, rows_t,
    partial, from_across, from_line, total, across_send, across_recv, line_send, line_recv,
    gather_send, gather_recv, load_sem, wide, tile_sem, stage_a, stage_b, stage_sem, stage_recv, piece_a, piece_b, piece_sem, hidden_sem,
):
    grid = Grid(2, line)
    rows, width = normed.shape
    cols = gate_own.shape[1]
    blocks = 2 * line
    me = grid.slot(grid.x, grid.z)
    grid.greet(True)
    gathers = [
        Gather(grid, normed, normed_all, gather_send.at[0], gather_recv.at[0], parts),
    ]
    scatter = Scatter(
        grid, partial, from_across, from_line, total,
        (across_send, across_recv, line_send, line_recv), parts,
    )
    for gather in gathers:
        gather.send_own()
    load_pairs(
        [
            (gate_own, gate_w.at[:, pl.ds(0, cols)]),
            (gate_twin, gate_w.at[:, pl.ds(cols, cols)]),
            (up_own, up_w.at[:, pl.ds(0, cols)]),
            (up_twin, up_w.at[:, pl.ds(cols, cols)]),
            (down_own, down_w.at[pl.ds(0, cols)]),
            (down_twin, down_w.at[pl.ds(cols, cols)]),
            (normed, rows_n),
        ],
        load_sem,
    )
    load_pairs([(rows_n, normed_all.at[me])], load_sem)

    def work(slot):
        load_pairs([(normed_all.at[slot], rows_n), (tangent_all.at[slot], rows_t)], load_sem)
        spot = pl.ds(pl.multiple_of(slot * rows, rows), rows)

        def hidden_tile(j, carry):
            c = pl.ds(pl.multiple_of(j * cols, cols), cols)
            gate = dot(rows_n[...], gate_w[:, c], NN)
            up = dot(rows_n[...], up_w[:, c], NN)
            grad = dot(rows_t[...], down_w[c, :], NT)
            sig = jax.nn.sigmoid(gate)
            silu = gate * sig
            hidden[spot, c] = (silu * up).astype(BF)
            dgate[spot, c] = (grad * up * (sig * (1.0 + gate * (1.0 - sig)))).astype(BF)
            dup[spot, c] = (grad * silu).astype(BF)
            return carry

        lax.fori_loop(0, 2, hidden_tile, 0)

        def back_tile(j, carry):
            c = pl.ds(pl.multiple_of(j * cols, cols), cols)
            sums = dot(dgate[spot, :], gate_w[c, :], NT) + dot(dup[spot, :], up_w[c, :], NT)
            partial[slot, :, c] = sums.astype(BF)
            return carry

        lax.fori_loop(0, width // cols, back_tile, 0)

    def stage(distance, carry):
        @pl.when(distance + 1 < line)
        def _():
            for gather in gathers:
                for part in range(parts):
                    gather.forward(distance + 1, part)

        def visit(i, inner):
            z = grid.z + jnp.where(i % 2 == 0, -distance, distance)
            inside = jnp.logical_and(z >= 0, z < line)

            @pl.when(jnp.logical_and(inside, jnp.logical_or(distance > 0, i % 2 == 0)))
            def _():
                @pl.when(i >= 2)
                def _():
                    for gather in gathers:
                        gather.wait_across(z)

                work(grid.slot(jnp.where(i < 2, grid.x, 1 - grid.x), z))

            return inner

        lax.fori_loop(0, 4, visit, 0)
        return carry

    lax.fori_loop(0, line, stage, 0)
    hidden_copy = pltpu.make_async_copy(hidden, hidden_all, hidden_sem)
    hidden_copy.start()
    for k in range(line - 1, -1, -1):
        scatter.send_across(grid.order(k))

    tiles = width // tile

    def wide_loads(t, start):
        j, buf = t % tiles, t % 2
        c = pl.ds(pl.multiple_of(j * tile, tile), tile)
        for i, source in enumerate((normed_all, tangent_all)):
            copy = pltpu.make_async_copy(source.at[:, :, c], wide.at[buf, i], tile_sem.at[buf, i])
            copy.start() if start else copy.wait()

    def stages(t):
        j, buf = t % tiles, t % 2
        c = pl.ds(pl.multiple_of(j * tile, tile), tile)
        return [
            remote(src, dst, stage_sem.at[buf, i], stage_recv.at[j, i], grid.twin)
            for i, (src, dst) in enumerate(
                (
                    (stage_a.at[buf, 0], part_gate.at[c, :]),
                    (stage_a.at[buf, 1], part_up.at[c, :]),
                    (stage_b.at[buf], part_down.at[:, c]),
                )
            )
        ]

    def results(t):
        j, buf = t % tiles, t % 2
        c = pl.ds(pl.multiple_of(j * tile, tile), tile)
        return [
            pltpu.make_async_copy(src, dst, stage_sem.at[buf, i])
            for i, (src, dst) in enumerate(
                (
                    (stage_a.at[buf, 0], grad_gate.at[c, :]),
                    (stage_a.at[buf, 1], grad_up.at[c, :]),
                    (stage_b.at[buf], grad_down.at[:, c]),
                )
            )
        ]

    def pieces(t):
        c = pl.ds(pl.multiple_of((t % tiles) * tile, tile), tile)
        return [
            (part_gate.at[c, :], piece_a.at[0]),
            (part_up.at[c, :], piece_a.at[1]),
            (part_down.at[:, c], piece_b),
        ]

    wide_loads(0, True)

    def weights(t, carry):
        buf = t % 2
        pl.when(t + 1 < 2 * tiles)(lambda: wide_loads(t + 1, True))
        wide_loads(t, False)
        tall = blocks * rows
        tokens = wide[buf, 0].reshape(tall, tile)
        tangents = wide[buf, 1].reshape(tall, tile)

        @pl.when(t < tiles)
        def _():
            theirs = slice(cols, 2 * cols)

            @pl.when(t >= 2)
            def _():
                for copy in stages(t - 2):
                    copy.wait_send()

            stage_a[buf, 0] = dot(tokens, dgate[:, theirs], TN).astype(BF)
            stage_a[buf, 1] = dot(tokens, dup[:, theirs], TN).astype(BF)
            stage_b[buf] = dot(hidden[:, theirs], tangents, TN).astype(BF)
            for copy in stages(t):
                copy.start()

        @pl.when(t >= tiles)
        def _():
            for copy in stages(t):
                copy.wait_recv()
            loads = [
                pltpu.make_async_copy(src, dst, piece_sem.at[i])
                for i, (src, dst) in enumerate(pieces(t))
            ]
            for copy in loads:
                copy.start()

            @pl.when(t < tiles + 2)
            def _():
                for copy in stages(t - 2):
                    copy.wait_send()

            @pl.when(t >= tiles + 2)
            def _():
                for copy in results(t - 2):
                    copy.wait()

            mine = slice(0, cols)
            own_gate = dot(tokens, dgate[:, mine], TN)
            own_up = dot(tokens, dup[:, mine], TN)
            own_down = dot(hidden[:, mine], tangents, TN)
            for copy in loads:
                copy.wait()
            stage_a[buf, 0] = (own_gate + piece_a[0].astype(F32)).astype(BF)
            stage_a[buf, 1] = (own_up + piece_a[1].astype(F32)).astype(BF)
            stage_b[buf] = (own_down + piece_b[...].astype(F32)).astype(BF)
            for copy in results(t):
                copy.start()

        for k in range(line - 1, 0, -1):
            when = 2 * tiles - 1 - (k - 1) * (tiles // (line - 1))
            pl.when(t == when)(lambda k=k: scatter.pass_on(grid.order(k)))
        return carry

    lax.fori_loop(0, 2 * tiles, weights, 0)
    scatter.own(grad_sum)
    for t in (2 * tiles - 2, 2 * tiles - 1):
        for copy in results(t):
            copy.wait()
    for gather in gathers:
        gather.finish()
    scatter.finish()
    hidden_copy.wait()


def feed_call(normed, tangent_all, gates, ups, downs, line):
    rows, width = normed.shape
    cols = gates[0].shape[1]
    blocks, parts, tile = 2 * line, 2, 256
    tiles = width // tile
    tall = blocks * rows
    shapes = jax.ShapeDtypeStruct
    hbm = lambda *s: shapes(s, BF)
    return pl.pallas_call(
        functools.partial(feed_kernel, line, parts, tile),
        out_shape=(
            shapes((rows, width), F32),
            hbm(blocks, rows, width), hbm(tall, 2 * cols),
            hbm(width, cols), hbm(width, cols), hbm(cols, width),
            hbm(width, cols), hbm(width, cols), hbm(cols, width),
        ),
        in_specs=[ANY] * 8,
        out_specs=(pl.BlockSpec(memory_space=pltpu.VMEM),) + (ANY,) * 8,
        scratch_shapes=[
            pltpu.VMEM((width, 2 * cols), BF), pltpu.VMEM((width, 2 * cols), BF), pltpu.VMEM((2 * cols, width), BF),
            pltpu.VMEM((tall, 2 * cols), BF), pltpu.VMEM((tall, 2 * cols), BF), pltpu.VMEM((tall, 2 * cols), BF),
            pltpu.VMEM((rows, width), BF), pltpu.VMEM((rows, width), BF),
            *scatter_scratch(line, rows, width, parts),
            pltpu.SemaphoreType.DMA((1, line, parts, 3)), pltpu.SemaphoreType.DMA((1, blocks, parts)),
            pltpu.SemaphoreType.DMA((8,)),
            pltpu.VMEM((2, 2, blocks, rows, tile), BF), pltpu.SemaphoreType.DMA((2, 2)),
            pltpu.VMEM((2, 2, tile, cols), BF), pltpu.VMEM((2, cols, tile), BF),
            pltpu.SemaphoreType.DMA((2, 3)), pltpu.SemaphoreType.DMA((tiles, 3)),
            pltpu.VMEM((2, tile, cols), BF), pltpu.VMEM((cols, tile), BF), pltpu.SemaphoreType.DMA((3,)),
            pltpu.SemaphoreType.DMA,
        ],
        compiler_params=pltpu.CompilerParams(
            collective_id=1, has_side_effects=True, vmem_limit_bytes=63 * 2**20
        ),
        name="feed",
    )(normed, tangent_all, gates[0], gates[1], ups[0], ups[1], downs[0], downs[1])


class Thirds(Scatter):
    def run(self, part):
        quarter = self.rows
        if part == 2:
            return pl.ds(pl.multiple_of(self.grid.replica * quarter, quarter), quarter)
        return pl.ds((2 + part) * quarter, quarter)


def sums_kernel(
    line,
    normed, attended, grad_qkv, grad_out, tokens, grad_middle, weights, gain, term_two,
    result, grad_tokens,
    both_normed, both_attended, both_qkv, both_out, load_sem, twin_send, twin_recv,
    partial, from_across, from_line, total, across_send, across_recv, line_send, line_recv,
    mine, theirs, mirror_send, mirror_recv, from_mirror, quarter_send, quarter_recv,
    in_weights, weight_sem, token_v, middle_v, grad_normed, terms, own_terms, twin_terms,
):
    grid = Grid(2, line)
    rows, width = normed.shape
    run = partial.shape[1]
    quarter = run // 4
    narrow = grad_qkv.shape[1]
    grid.greet(True, True)
    scatter = Thirds(
        grid, partial, from_across, from_line, total,
        (across_send, across_recv, line_send, line_recv), 3,
    )
    scatter.rows = quarter
    own, twin = pl.ds(0, rows), pl.ds(rows, rows)
    pairs = [
        (grad_qkv, both_qkv.at[own], both_qkv.at[twin]),
        (normed, both_normed.at[own], both_normed.at[twin]),
        (grad_out, both_out.at[own], both_out.at[twin]),
        (attended, both_attended.at[own], both_attended.at[twin]),
    ]
    swaps = [
        remote(src, there, twin_send.at[i], twin_recv.at[i], grid.twin)
        for i, (src, _, there) in enumerate(pairs)
    ]
    for copy in swaps:
        copy.start()
    load_pairs([(src, here) for src, here, _ in pairs], load_sem)
    later = [
        pltpu.make_async_copy(src, dst, weight_sem.at[i])
        for i, (src, dst) in enumerate(
            (
                (weights.at[:, :, pl.ds(0, narrow)], in_weights),
                (tokens, token_v),
                (grad_middle, middle_v),
            )
        )
    ]
    for copy in later:
        copy.start()
    for copy in swaps:
        copy.wait()
    tall = line * run
    tile = 512
    away = pl.ds(pl.multiple_of((1 - grid.replica) * quarter, quarter), quarter)
    here = pl.ds(pl.multiple_of(grid.replica * quarter, quarter), quarter)

    def to_mirror(slot):
        return remote(
            partial.at[slot, away], from_mirror.at[slot],
            quarter_send.at[slot], quarter_recv.at[slot], grid.mirror,
        )

    def features(x):
        return pl.ds(pl.multiple_of((x * 2 + grid.core) * tall, tall), tall)

    def column(j, carry):
        x = jnp.where(j == 0, 1 - grid.x, grid.x)
        blocks = pl.ds(x * line, line)

        def wide(left, right, first):
            def step(i, inner):
                c = pl.ds(pl.multiple_of(i * tile, tile), tile)
                to = pl.ds(pl.multiple_of(first + i * tile, 128), tile)
                value = dot(left[:, features(x)], right[:, c], TN).astype(BF)
                partial[blocks, :, to] = value.reshape(line, run, tile)
                return inner

            lax.fori_loop(0, right.shape[1] // tile, step, 0)

        wide(both_normed, both_qkv, 0)
        wide(both_attended, both_out, narrow)
        partial[blocks, :, narrow + width :] = jnp.zeros((line, run, 128), BF)
        for k in range(line - 1, -1, -1):
            z = grid.order(k)
            to_mirror(grid.slot(x, z)).start()
            pl.when(j == 0)(lambda z=z: scatter.across(z, 0).start())
        return carry

    lax.fori_loop(0, 2, column, 0)
    for copy in later:
        copy.wait()

    def back_step(j, carry):
        units = pl.ds(j * (tile // run), tile // run)
        c = pl.ds(pl.multiple_of(j * tile, tile), tile)
        right = in_weights[units].reshape(tile, narrow)
        grad_normed[:, c] = dot(both_qkv[own, :], right, NT)
        return carry

    lax.fori_loop(0, width // tile, back_step, 0)
    terms[...] = jnp.zeros_like(terms)
    chunk = 64

    def norm_step(j, carry):
        r = pl.ds(pl.multiple_of(j * chunk, chunk), chunk)
        value = token_v[r, :].astype(F32)
        factor = lax.rsqrt(jnp.mean(value * value, axis=1, keepdims=True) + norm_eps)
        unit = value * factor
        grad = grad_normed[r, :]
        terms[0:1, :] += jnp.sum(grad * unit, axis=0, keepdims=True)
        scaled = grad * gain[...]
        mean = jnp.mean(scaled * unit, axis=1, keepdims=True)
        grad_tokens[r, :] = (middle_v[r, :] + factor * (scaled - unit * mean)).astype(BF)
        return carry

    lax.fori_loop(0, rows // chunk, norm_step, 0)
    terms[1:2, :] = term_two[...]
    own_terms[...] = terms[...].astype(BF)
    swap_terms = remote(own_terms, twin_terms, twin_send.at[4], twin_recv.at[4], grid.twin)
    swap_terms.start()
    swap_terms.wait()
    for x in range(2):
        for z in range(line):
            first = pl.multiple_of((x * 2 + grid.core) * tall + z * run, run)
            c = pl.ds(first, run)
            value = own_terms[:, c].astype(F32) + twin_terms[:, c].astype(F32)
            partial[x * line + z, 3 * quarter : 3 * quarter + 16, narrow + width :] = value.astype(BF)
    for k in range(line - 1, -1, -1):
        scatter.across(grid.order(k), 1).start()

    def add_mirror(x):
        def step(i, carry):
            slot = grid.slot(x, grid.order(line - 1 - i))
            to_mirror(slot).wait_recv()
            value = partial[slot, here].astype(F32) + from_mirror[slot].astype(F32)
            partial[slot, here] = value.astype(BF)
            return carry

        lax.fori_loop(0, line, step, 0)

    add_mirror(1 - grid.x)
    for k in range(line - 1, -1, -1):
        scatter.across(grid.order(k), 2).start()

    def swap(part, whole=True):
        at = scatter.run(part)
        return remote(
            mine.at[at], theirs.at[at], mirror_send.at[part], mirror_recv.at[part], grid.mirror
        )

    def sweep(part):
        def step(i, carry):
            scatter.pass_on(grid.order(line - 1 - i), (part,))
            return carry

        lax.fori_loop(0, line - 1, step, 0)

    def settle(part):
        scatter.gather_sum(grid.z, part)
        mine[scatter.run(part)] = total[...].astype(BF)
        swap(part).start()

    sweep(0)
    sweep(1)
    add_mirror(grid.x)
    settle(0)
    sweep(2)
    settle(1)
    settle(2)
    result[here] = mine[here].astype(F32)
    for part in range(2):
        swap(part).wait()
        at = scatter.run(part)
        result[at] = mine[at].astype(F32) + theirs[at].astype(F32)
    swap(2).wait_send()
    remote(mine.at[away], theirs.at[away], mirror_send.at[2], mirror_recv.at[2], grid.mirror).wait_recv()
    result[away] = theirs[away].astype(F32)
    scatter.finish()

    def sent(slot, carry):
        to_mirror(slot).wait_send()
        return carry

    lax.fori_loop(0, 2 * line, sent, 0)


def sums_call(normed, attended, grad_qkv, grad_out, tokens, grad_middle, weights, gain, term_two, line):
    rows, width = normed.shape
    narrow = grad_qkv.shape[1]
    run, whole = weights.shape[1:]
    quarter = run // 4
    vmem = pl.BlockSpec(memory_space=pltpu.VMEM)
    dma = pltpu.SemaphoreType.DMA
    like = lambda a: pltpu.VMEM(a.shape, a.dtype)
    return pl.pallas_call(
        functools.partial(sums_kernel, line),
        out_shape=(
            jax.ShapeDtypeStruct((run, whole), F32), jax.ShapeDtypeStruct((rows, width), BF),
        ),
        in_specs=[ANY] * 7 + [vmem] * 2,
        out_specs=(vmem, vmem),
        scratch_shapes=[
            pltpu.VMEM((2 * rows, width), BF), pltpu.VMEM((2 * rows, width), BF),
            pltpu.VMEM((2 * rows, narrow), BF), pltpu.VMEM((2 * rows, width), BF),
            dma((4,)), dma((5,)), dma((5,)),
            pltpu.VMEM((2 * line, run, whole), BF), pltpu.VMEM((line, run, whole), BF),
            pltpu.VMEM((2 * line - 2, run, whole), BF), pltpu.VMEM((quarter, whole), F32),
            dma((line, 3)), dma((line, 3)), dma((line, 3)), dma((2 * line - 2, 3)),
            pltpu.VMEM((run, whole), BF), pltpu.VMEM((run, whole), BF), dma((3,)), dma((3,)),
            pltpu.VMEM((2 * line, quarter, whole), BF), dma((2 * line,)), dma((2 * line,)),
            pltpu.VMEM((weights.shape[0], run, narrow), BF), dma((3,)),
            like(tokens), like(grad_middle), pltpu.VMEM((rows, width), F32),
            pltpu.VMEM((16, width), F32), pltpu.VMEM((16, width), BF), pltpu.VMEM((16, width), BF),
        ],
        compiler_params=pltpu.CompilerParams(
            collective_id=3, has_side_effects=True, vmem_limit_bytes=63 * 2**20
        ),
        name="sums",
    )(normed, attended, grad_qkv, grad_out, tokens, grad_middle, weights, gain, term_two)


def gather_weights(grid, block, everything, send, recv, twin_send, twin_recv, meanwhile):
    line = grid.line
    rows = block.shape[0] // 4
    carry_a, carry_b = grid.replica * 2, grid.replica * 2 + 1
    other_a, other_b = (1 - grid.replica) * 2, (1 - grid.replica) * 2 + 1
    right, left, across, mirror = range(4)
    devices = (grid.right, grid.left, grid.across, grid.mirror)

    def run(quarter):
        return pl.ds(pl.multiple_of(quarter * rows, rows), rows)

    def place(x, core, z, quarter):
        return everything.at[(x * 2 + core) * line + z, run(quarter)]

    def copy(x, z, quarter, link, first=False):
        there = place(x, grid.core, z, quarter)
        here = block.at[run(quarter)] if first else there
        unit = x * line + z
        return remote(
            here, there, send.at[quarter, unit, link], recv.at[quarter, unit], devices[link]
        )

    def share(x, z, quarter, first=False):
        there = place(x, grid.core, z, quarter)
        here = block.at[run(quarter)] if first else there
        unit = x * line + z
        return remote(
            here, there, twin_send.at[quarter, unit], twin_recv.at[quarter, unit], grid.twin
        )

    def arrived(x, z, quarter):
        copy(x, z, quarter, across).wait_recv()
        share(x, z, quarter).start()

    copy(grid.x, grid.z, carry_b, across, True).start()
    copy(grid.x, grid.z, carry_a, across, True).start()
    copy(grid.x, grid.z, other_a, across, True).start()
    for link, go in ((right, grid.has_right), (left, grid.has_left)):

        @pl.when(go)
        def _(link=link):
            copy(grid.x, grid.z, carry_a, link, True).start()
            copy(grid.x, grid.z, carry_b, link, True).start()

    for quarter in range(4):
        share(grid.x, grid.z, quarter, True).start()
    meanwhile()

    arrived(1 - grid.x, grid.z, carry_b)
    copy(1 - grid.x, grid.z, carry_b, mirror).start()
    for link, go in ((right, grid.has_right), (left, grid.has_left)):
        pl.when(go)(lambda link=link: copy(1 - grid.x, grid.z, carry_b, link).start())

    def sides(distance):
        return (
            (grid.z - distance, grid.z >= distance, right, grid.has_right),
            (grid.z + distance, grid.z + distance < line, left, grid.has_left),
        )

    def step(distance, carry):
        for z, there, link, go in sides(distance):

            @pl.when(there)
            def _(z=z, link=link, go=go):
                for x, quarter in (
                    (grid.x, carry_a),
                    (grid.x, carry_b),
                    (1 - grid.x, carry_b),
                ):
                    arrived(x, z, quarter)
                    copy(x, z, quarter, mirror).start()
                    pl.when(go)(lambda x=x, quarter=quarter: copy(x, z, quarter, link).start())
                copy(grid.x, z, carry_a, across).start()

        for z, there, _, _ in sides(distance - 1):

            @pl.when(jnp.logical_and(there, distance > 1))
            def _(z=z):
                arrived(grid.x, z, other_a)
                copy(grid.x, z, other_a, across).start()

        return carry

    lax.fori_loop(1, line + 1, step, 0)

    def last(z, carry):
        arrived(1 - grid.x, z, carry_a)
        arrived(1 - grid.x, z, other_a)
        arrived(1 - grid.x, z, other_b)
        pl.when(z != grid.z)(lambda: arrived(grid.x, z, other_b))
        return carry

    lax.fori_loop(0, line, last, 0)

    def finish(z, carry):
        away = z != grid.z
        for x in (grid.x, 1 - grid.x):
            for quarter in range(4):
                share(x, z, quarter).wait()
        for x, quarter in ((grid.x, carry_a), (grid.x, carry_b), (1 - grid.x, carry_b)):
            to_mirror = jnp.logical_or(away, jnp.bool_(x is not grid.x))
            pl.when(to_mirror)(
                lambda x=x, quarter=quarter: copy(x, z, quarter, mirror).wait_send()
            )
            for link, go in (
                (right, jnp.logical_and(z <= grid.z, grid.has_right)),
                (left, jnp.logical_and(z >= grid.z, grid.has_left)),
            ):
                pl.when(go)(
                    lambda x=x, quarter=quarter, link=link: copy(x, z, quarter, link).wait_send()
                )
        copy(grid.x, z, carry_a, across).wait_send()
        copy(grid.x, z, other_a, across).wait_send()
        return carry

    lax.fori_loop(0, line, finish, 0)
    copy(grid.x, grid.z, carry_b, across, True).wait_send()


class Line:
    def __init__(self, grid, block, everything, send, recv):
        self.grid, self.block, self.everything = grid, block, everything
        self.send, self.recv = send, recv

    def copy(self, z, link, first=False):
        grid = self.grid
        there = self.everything.at[z]
        here = self.block if first else there
        device = (grid.right, grid.left)[link]
        return remote(here, there, self.send.at[z, link], self.recv.at[z], device)

    def send_own(self):
        grid = self.grid
        for link, go in ((0, grid.has_right), (1, grid.has_left)):
            pl.when(go)(lambda link=link: self.copy(grid.z, link, True).start())

    def forward(self, distance):
        grid = self.grid
        for z, there, link, go in (
            (grid.z - distance, grid.z >= distance, 0, grid.has_right),
            (grid.z + distance, grid.z + distance < grid.line, 1, grid.has_left),
        ):

            @pl.when(there)
            def _(z=z, link=link, go=go):
                self.copy(z, link).wait_recv()
                pl.when(go)(lambda: self.copy(z, link).start())

    def finish(self):
        grid = self.grid

        def step(z, carry):
            for link, go in (
                (0, jnp.logical_and(z <= grid.z, grid.has_right)),
                (1, jnp.logical_and(z >= grid.z, grid.has_left)),
            ):
                pl.when(go)(lambda link=link: self.copy(z, link).wait_send())
            return carry

        lax.fori_loop(0, grid.line, step, 0)


def turn(value, cosine, sine, scale):
    parts = []
    lane = lax.broadcasted_iota(jnp.int32, (value.shape[0], 128), 1) % HEAD_SIZE
    for first in range(0, value.shape[1], 128):
        pair = value[:, first : first + 128]
        swapped = jnp.where(
            lane < HEAD_SIZE // 2,
            pltpu.roll(pair, 128 - HEAD_SIZE // 2, 1),
            pltpu.roll(pair, HEAD_SIZE // 2, 1),
        )
        parts.append(((pair * cosine[...] + swapped * sine[...]) * scale).astype(BF))
    return parts[0] if len(parts) == 1 else jnp.concatenate(parts, axis=1)


def halves(pair, half):
    pair = pair.astype(F32)
    turned = pltpu.roll(pair, HEAD_SIZE, 1)
    lane = lax.broadcasted_iota(jnp.int32, pair.shape, 1) // HEAD_SIZE
    first = jnp.where(half == 0, pair, turned)
    second = jnp.where(half == 0, turned, pair)
    both = jnp.concatenate([first, second], axis=0)
    return jnp.where(jnp.concatenate([lane, lane], axis=0) == half, both, 0.0).astype(BF)


def unhalves(both, half):
    rows = both.shape[0] // 2
    first, second = both[:rows], both[rows:]
    lane = lax.broadcasted_iota(jnp.int32, first.shape, 1) // HEAD_SIZE
    first = jnp.where(half == 0, first, pltpu.roll(first, HEAD_SIZE, 1))
    second = jnp.where(half == 0, pltpu.roll(second, HEAD_SIZE, 1), second)
    return jnp.where(lane == 0, first, second)


def front_kernel(
    line, parts,
    block, tokens, tangent, bias, cosine, sine,
    attended, middle, normed, first_normed, queries, logs, keyed_out, tangent_all, weights_out,
    everything, keyed, keyed_all, bias_v, token_v, cosine_v, sine_v, gain, scores, probs, sums, stage, load_sem,
    key_send, key_recv, send, recv, own_sem, weight_send, weight_recv, twin_send, twin_recv,
):
    grid = Grid(2, line)
    rows, width = tokens.shape
    narrow = keyed.shape[1] // 2
    total = bias.shape[1]
    extra = width + 2 * narrow
    after = extra + 128
    me = grid.slot(grid.x, grid.z)
    chunk = rows // 2
    tile = 512
    grid.greet(True, True)

    def meanwhile():
        load_pairs(
            [
                (block, everything.at[(grid.x * 2 + grid.core) * line + grid.z]),
                (tangent, stage),
                (bias, bias_v),
                (tokens, token_v),
                (cosine, cosine_v),
                (sine, sine_v),
            ],
            load_sem,
        )
        load_pairs([(stage, tangent_all.at[me])], own_sem)

    gather_weights(
        grid, block, everything, weight_send, weight_recv, twin_send, twin_recv, meanwhile
    )
    weights_copy = pltpu.make_async_copy(everything, weights_out, own_sem.at[1])
    weights_copy.start()
    units, run = everything.shape[0], everything.shape[1]
    for unit in range(units):
        for which in range(2):
            gain[which : which + 1, unit * run : (unit + 1) * run] = everything[
                unit, which : which + 1, extra:after
            ].astype(F32)

    def norm(source, target, which):
        def step(j, carry):
            here = pl.ds(pl.multiple_of(j * chunk, chunk), chunk)
            value = source[here, :].astype(F32)
            factor = lax.rsqrt(jnp.mean(value * value, axis=1, keepdims=True) + norm_eps)
            target[here, :] = (value * factor * gain[which : which + 1, :]).astype(BF)
            return carry

        lax.fori_loop(0, rows // chunk, step, 0)

    norm(token_v, first_normed, 0)

    def project(c):
        return dot(first_normed[...], everything[:, :, c].reshape(width, tile), NN)

    for first in range(0, narrow, tile):
        keyed[:, first : first + tile] = turn(project(slice(width + first, width + first + tile)), cosine_v, sine_v, 1.0)
        keyed[:, narrow + first : narrow + first + tile] = project(
            slice(width + narrow + first, width + narrow + first + tile)
        ).astype(BF)
    line_keys = Line(grid, keyed, keyed_all, key_send, key_recv)
    gather = Gather(grid, tangent, tangent_all, send, recv, parts)
    line_keys.send_own()
    for part in range(parts):
        gather.copy(grid.z, part, 2, True).start()
    keyed_all[grid.z] = keyed[...]

    def query_step(j, carry):
        c = pl.ds(pl.multiple_of(j * tile, tile), tile)
        queries[:, c] = turn(project(c), cosine_v, sine_v, HEAD_SIZE ** (-0.5))
        return carry

    lax.fori_loop(0, width // tile, query_step, 0)
    for distance in range(line):
        if distance:
            line_keys.forward(distance)
        for link, go in (
            (0, jnp.logical_and(grid.z == distance, grid.has_right)),
            (1, jnp.logical_and(line - 1 - grid.z == distance, grid.has_left)),
        ):

            @pl.when(go)
            def _(link=link):
                for part in range(parts):
                    gather.copy(grid.z, part, link, True).start()


    logs[...] = jnp.zeros_like(logs)
    pairs = width // (2 * HEAD_SIZE)
    group = pairs // (narrow // (2 * HEAD_SIZE))

    def advance(n):
        gather.forward(n // parts + 1, n % parts)

    def pair_step(i, carry):
        c = pl.ds(pl.multiple_of(i * 128, 128), 128)
        half = (i // (group // 2)) % 2
        first_key = pl.multiple_of((i // group) * 128, 128)
        keys = keyed_all[:, :, pl.ds(first_key, 128)].reshape(total, 128)
        values = keyed_all[:, :, pl.ds(first_key + narrow, 128)].reshape(total, 128)
        scores[...] = dot(halves(queries[:, c], half), keys, NT)

        def soft(j, inner):
            here = pl.ds(pl.multiple_of(j * rows, rows), rows)
            value = scores[here, :] + bias_v[...]
            top = jnp.max(value, axis=1, keepdims=True)
            power = jnp.exp(value - top)
            size = jnp.sum(power, axis=1, keepdims=True)
            probs[here, :] = power.astype(BF)
            sums[here, :] = jnp.broadcast_to(1.0 / size, (rows, 128))
            lane = lax.broadcasted_iota(jnp.int32, (rows, 128), 1)
            logs[here, :] = jnp.where(lane == i, top + jnp.log(size), logs[here, :])
            return inner

        lax.fori_loop(0, 2, soft, 0)
        out = dot(probs[...], values, NN) * sums[...]
        attended[:, c] = unhalves(out, half).astype(BF)

        pl.when(i % 3 == 2)(lambda: advance(i // 3))
        return carry

    lax.fori_loop(0, pairs, pair_step, 0)
    keyed_copy = pltpu.make_async_copy(keyed_all, keyed_out, load_sem.at[0])
    keyed_copy.start()
    advance(pairs // 3)

    def out_step(j, carry):
        c = pl.ds(pl.multiple_of(j * tile, tile), tile)
        w = pl.ds(pl.multiple_of(after + j * tile, 128), tile)
        out = dot(attended[...], everything[:, :, w].reshape(width, tile), NN)
        middle[:, c] = token_v[:, c].astype(F32) + out
        return carry

    lax.fori_loop(0, width // tile, out_step, 0)
    norm(middle, normed, 1)

    def rest(n, carry):
        advance(n)
        return carry

    lax.fori_loop(pairs // 3 + 1, (line - 1) * parts, rest, 0)
    for z in range(line):
        gather.wait_across(z)
    keyed_copy.wait()
    weights_copy.wait()
    line_keys.finish()
    gather.finish()


def front_call(block, tokens, tangent, bias, cosine, sine, line, narrow):
    rows, width = tokens.shape
    total = bias.shape[1]
    blocks, parts = 2 * line, 4
    shapes = jax.ShapeDtypeStruct
    vmem = pl.BlockSpec(memory_space=pltpu.VMEM)
    like = lambda a: pltpu.VMEM(a.shape, a.dtype)
    return pl.pallas_call(
        functools.partial(front_kernel, line, parts),
        out_shape=(
            shapes((rows, width), BF), shapes((rows, width), F32), shapes((rows, width), BF),
            shapes((rows, width), BF), shapes((rows, width), BF),
            shapes((2 * rows, 128), F32), shapes((line, rows, 2 * narrow), BF),
            shapes((blocks, rows, width), BF), shapes((2 * blocks,) + block.shape, BF),
        ),
        in_specs=[ANY] * 6,
        out_specs=(vmem,) * 6 + (ANY,) * 3,
        scratch_shapes=[
            pltpu.VMEM((2 * blocks,) + block.shape, BF),
            pltpu.VMEM((rows, 2 * narrow), BF), pltpu.VMEM((line, rows, 2 * narrow), BF),
            like(bias), like(tokens), like(cosine), like(sine), pltpu.VMEM((2, width), F32),
            pltpu.VMEM((2 * rows, total), F32), pltpu.VMEM((2 * rows, total), BF),
            pltpu.VMEM((2 * rows, 128), F32), pltpu.VMEM((rows, width), BF), pltpu.SemaphoreType.DMA((6,)),
            pltpu.SemaphoreType.DMA((line, 2)), pltpu.SemaphoreType.DMA((line,)),
            pltpu.SemaphoreType.DMA((line, parts, 3)), pltpu.SemaphoreType.DMA((blocks, parts)),
            pltpu.SemaphoreType.DMA((2,)),
            pltpu.SemaphoreType.DMA((4, blocks, 4)), pltpu.SemaphoreType.DMA((4, blocks)),
            pltpu.SemaphoreType.DMA((4, blocks)), pltpu.SemaphoreType.DMA((4, blocks)),
        ],
        compiler_params=pltpu.CompilerParams(
            collective_id=5, has_side_effects=True, vmem_limit_bytes=62 * 2**20
        ),
        name="front",
    )(block, tokens, tangent, bias, cosine, sine)


def back_kernel(
    line, parts, pass_at,
    queries, keyed_all, grad_out, bias, logs, hidden_all, down_own, down_twin, weights, cosine, sine,
    gate_sum, up_sum, down_sum,
    branch, grad_qkv, gate_mirror, up_mirror, down_mirror,
    out_v, out_w, cosine_v, sine_v, grad_keyed, mirror_send, mirror_recv,
    query_v, keyed_v, grad_v, bias_v, log_v, scores, gradients, probs, slopes, key_sum, value_sum,
    down_w, hidden, load_sem,
    partial, from_across, from_line, total, across_send, across_recv, line_send, line_recv,
    key_partial, key_line, key_total, key_send, key_recv,
):
    grid = Grid(2, line)
    cols, width = down_own.shape
    rows = partial.shape[1]
    narrow = keyed_all.shape[2] // 2
    length = bias.shape[1]
    grid.greet(False, True)
    mirrored = [
        remote(src, dst, mirror_send.at[i], mirror_recv.at[i], grid.mirror)
        for i, (src, dst) in enumerate(
            ((gate_sum, gate_mirror), (up_sum, up_mirror), (down_sum, down_mirror))
        )
    ]
    for copy in mirrored:
        copy.start()
    load_pairs(
        [
            (down_own, down_w.at[pl.ds(0, cols)]),
            (down_twin, down_w.at[pl.ds(cols, cols)]),
            (hidden_all, hidden),
            (queries, query_v),
            (keyed_all, keyed_v),
            (grad_out, out_v),
            (bias, bias_v),
            (logs, log_v),
            (cosine, cosine_v),
            (sine, sine_v),
        ],
        load_sem,
    )
    scatter = Scatter(
        grid, partial, from_across, from_line, total,
        (across_send, across_recv, line_send, line_recv), parts,
    )
    keyed_scatter = Scatter(
        grid, key_partial, None, key_line, key_total, (None, None, key_send, key_recv), parts
    )

    def work(i, carry):
        z = grid.order(line - 1 - i % line)
        slot = grid.slot(jnp.where(i < line, 1 - grid.x, grid.x), z)
        spot = pl.ds(pl.multiple_of(slot * rows, rows), rows)

        def tile(j, inner):
            c = pl.ds(pl.multiple_of(j * cols, cols), cols)
            partial[slot, :, c] = dot(hidden[spot, :], down_w[:, c], NN).astype(BF)
            return inner

        lax.fori_loop(0, width // cols, tile, 0)
        pl.when(i < line)(lambda: scatter.send_across(z))
        return carry

    lax.fori_loop(0, line, work, 0)
    tile = out_w.shape[0] * out_w.shape[1]
    after = weights.shape[2] - width

    def out_step(j, carry):
        units = pl.ds(j * out_w.shape[0], out_w.shape[0])
        load_pairs([(weights.at[units, :, pl.ds(after, width)], out_w)], load_sem)
        c = pl.ds(pl.multiple_of(j * tile, tile), tile)
        grad_v[:, c] = dot(out_v[...], out_w[...].reshape(tile, width), NT).astype(BF)
        return carry

    lax.fori_loop(0, width // tile, out_step, 0)
    lax.fori_loop(line, 2 * line, work, 0)
    deep = 2 * rows
    chunk = rows // 2
    pairs = width // (2 * HEAD_SIZE)
    group = pairs // (narrow // (2 * HEAD_SIZE))

    def pair_step(i, carry):
        c = pl.ds(pl.multiple_of(i * 128, 128), 128)
        half = (i // (group // 2)) % 2
        key_cols = pl.ds(pl.multiple_of((i // group) * 128, 128), 128)
        value_cols = pl.ds(pl.multiple_of((i // group) * 128 + narrow, 128), 128)
        keys = keyed_v[:, :, key_cols].reshape(length, 128)
        values = keyed_v[:, :, value_cols].reshape(length, 128)
        query = halves(query_v[:, c], half)
        grad = halves(grad_v[:, c], half)
        scores[...] = dot(query, keys, NT)
        gradients[...] = dot(grad, values, NT)

        def soft(j, inner):
            here = pl.ds(pl.multiple_of(j * chunk, chunk), chunk)
            there = pl.ds(pl.multiple_of((j * chunk) % rows, chunk), chunk)
            lane = lax.broadcasted_iota(jnp.int32, (chunk, 128), 1)
            log = jnp.sum(jnp.where(lane == i, log_v[here, :], 0.0), axis=1, keepdims=True)
            prob = jnp.exp(scores[here, :] + bias_v[there, :] - log)
            slope = gradients[here, :]
            delta = jnp.sum(prob * slope, axis=1, keepdims=True)
            probs[here, :] = prob.astype(BF)
            slopes[here, :] = (prob * (slope - delta)).astype(BF)
            return inner

        lax.fori_loop(0, deep // chunk, soft, 0)
        back = dot(slopes[...], keys, NN) * HEAD_SIZE ** (-0.5)
        grad_qkv[:, c] = turn(unhalves(back, half), cosine_v, sine_v, 1.0)
        key_part = dot(slopes[...], query, TN)
        value_part = dot(probs[...], grad, TN)

        @pl.when(i % group == 0)
        def _():
            key_sum[...] = key_part
            value_sum[...] = value_part

        @pl.when(i % group != 0)
        def _():
            key_sum[...] += key_part
            value_sum[...] += value_part

        @pl.when(i % group == group - 1)
        def _():
            key_partial[:, :, key_cols] = key_sum[...].astype(BF).reshape(line, rows, 128)
            key_partial[:, :, value_cols] = value_sum[...].astype(BF).reshape(line, rows, 128)

        for k, when in zip(range(line - 1, 0, -1), pass_at):
            pl.when(i == when)(lambda k=k: scatter.pass_on(grid.order(k)))
        return carry

    lax.fori_loop(0, pairs, pair_step, 0)

    def along(i, carry):
        keyed_scatter.pass_on(grid.order(line - 1 - i))
        return carry

    lax.fori_loop(0, line - 1, along, 0)
    for k in range(line - 1 - len(pass_at), 0, -1):
        scatter.pass_on(grid.order(k))
    scatter.own(branch)
    keyed_scatter.own(grad_keyed)
    grad_qkv[:, width : width + narrow] = turn(grad_keyed[:, :narrow], cosine_v, sine_v, 1.0)
    grad_qkv[:, width + narrow :] = grad_keyed[:, narrow:].astype(BF)
    for copy in mirrored:
        copy.wait()
    scatter.finish()
    keyed_scatter.finish()


def back_call(
    queries, keyed_all, grad_out, bias, logs, hidden_all, downs, weights, cosine, sine, sums, line
):
    rows, width = queries.shape
    both = keyed_all.shape[2]
    cols, length = downs[0].shape[0], bias.shape[1]
    parts = 2
    shapes = jax.ShapeDtypeStruct
    vmem = pl.BlockSpec(memory_space=pltpu.VMEM)
    return pl.pallas_call(
        functools.partial(back_kernel, line, parts, (4, 9, 15)),
        out_shape=(
            shapes((rows, width), F32), shapes((rows, width + both), BF),
            *(shapes(s.shape, BF) for s in sums),
        ),
        in_specs=[ANY] * 14,
        out_specs=(vmem,) * 2 + (ANY,) * 3,
        scratch_shapes=[
            pltpu.VMEM((rows, width), BF), pltpu.VMEM((4, weights.shape[1], width), BF),
            pltpu.VMEM(cosine.shape, F32), pltpu.VMEM(sine.shape, F32), pltpu.VMEM((rows, both), F32),
            pltpu.SemaphoreType.DMA((3,)), pltpu.SemaphoreType.DMA((3,)),
            pltpu.VMEM((rows, width), BF), pltpu.VMEM(keyed_all.shape, BF), pltpu.VMEM((rows, width), BF),
            pltpu.VMEM((rows, length), F32), pltpu.VMEM(logs.shape, F32),
            pltpu.VMEM((2 * rows, length), F32), pltpu.VMEM((2 * rows, length), F32),
            pltpu.VMEM((2 * rows, length), BF), pltpu.VMEM((2 * rows, length), BF),
            pltpu.VMEM((length, 128), F32), pltpu.VMEM((length, 128), F32),
            pltpu.VMEM((2 * cols, width), BF), pltpu.VMEM(hidden_all.shape, BF),
            pltpu.SemaphoreType.DMA((10,)),
            *scatter_scratch(line, rows, width, parts),
            pltpu.VMEM((line, rows, both), BF), pltpu.VMEM((2 * line - 2, rows, both), BF),
            pltpu.VMEM((rows // parts, both), F32),
            pltpu.SemaphoreType.DMA((line, parts)), pltpu.SemaphoreType.DMA((2 * line - 2, parts)),
        ],
        compiler_params=pltpu.CompilerParams(
            collective_id=6, has_side_effects=True, vmem_limit_bytes=62 * 2**20
        ),
        name="back",
    )(
        queries, keyed_all, grad_out, bias, logs, hidden_all, *downs, weights, cosine, sine, *sums
    )


def body(
    tokens,
    places,
    cotangent,
    gain_attn,
    gain_mlp,
    w_query,
    key_projection,
    value_projection,
    w_out,
    w_gate,
    w_up,
    w_down,
):
    sequence_total, segment_length, width = tokens.shape
    total_length = places.shape[1]
    total_rows = sequence_total * segment_length
    position = lax.axis_index("context")
    local_positions = lax.dynamic_slice_in_dim(places, position * segment_length, segment_length, 1)
    rotary_angles = local_positions.reshape(total_rows).astype(jnp.float32)[:, None] * frequencies(
        HEAD_SIZE // 2
    )
    gain_one, gain_two, query_w, key_weight_local, value_w, out_w = (
        lax.all_gather(gain_attn, ("fsdp", "context"), axis=0, tiled=True),
        lax.all_gather(gain_mlp, ("fsdp", "context"), axis=0, tiled=True),
        lax.all_gather(w_query, ("fsdp", "context"), axis=0, tiled=True),
        lax.all_gather(key_projection, ("fsdp", "context"), axis=0, tiled=True),
        lax.all_gather(value_projection, ("fsdp", "context"), axis=0, tiled=True),
        lax.all_gather(w_out, ("fsdp", "context"), axis=0, tiled=True),
    )
    gain_first = gain_one.astype(jnp.float32)
    gain_second = gain_two.astype(jnp.float32)
    inputs_f = tokens.astype(jnp.float32).reshape(total_rows, width)
    factor_one = lax.rsqrt(jnp.mean(inputs_f * inputs_f, axis=-1, keepdims=True) + norm_eps)
    unit_one = inputs_f * factor_one
    normed_tokens = (unit_one * gain_first).astype(jnp.bfloat16)
    query_pre = jnp.dot(normed_tokens, query_w, preferred_element_type=jnp.float32).reshape(
        total_rows, QUERY_HEADS, HEAD_SIZE
    )
    key_unrotated = jnp.dot(
        normed_tokens, key_weight_local, preferred_element_type=jnp.float32
    ).reshape(total_rows, KEY_VALUE_HEADS, HEAD_SIZE)
    value_matrix_rows = jnp.dot(normed_tokens, value_w, preferred_element_type=jnp.float32).astype(
        jnp.bfloat16
    )
    query_rows = apply_rotary(query_pre, rotary_angles).astype(jnp.bfloat16)
    key_matrix_rows = (
        apply_rotary(key_unrotated, rotary_angles)
        .astype(jnp.bfloat16)
        .reshape(sequence_total, segment_length, KEY_VALUE_HEADS * HEAD_SIZE)
    )
    key_all, value_all = (
        lax.all_gather(key_matrix_rows, "context", axis=1, tiled=True),
        lax.all_gather(
            value_matrix_rows.reshape(sequence_total, segment_length, KEY_VALUE_HEADS * HEAD_SIZE),
            "context",
            axis=1,
            tiled=True,
        ),
    )
    head_query = query_head_rows(query_rows, sequence_total, segment_length)
    head_key = key_heads(key_all, sequence_total, total_length)
    head_value = key_heads(value_all, sequence_total, total_length)
    query_positions = jnp.repeat(local_positions, KEY_VALUE_HEADS, axis=0)
    key_positions = jnp.repeat(places, KEY_VALUE_HEADS, axis=0)
    attended = lax.map(
        forward_head, (head_query, head_key, head_value, query_positions, key_positions)
    )
    attended = merge_queries(attended, sequence_total, segment_length).astype(jnp.bfloat16)
    middle = inputs_f + jnp.dot(attended, out_w, preferred_element_type=jnp.float32)
    factor_two = lax.rsqrt(jnp.mean(middle * middle, axis=-1, keepdims=True) + norm_eps)
    unit_two = middle * factor_two
    normed_mlp = (unit_two * gain_second).astype(jnp.bfloat16)
    tangent = cotangent.reshape(total_rows, width)
    tangent_f = tangent.astype(jnp.float32)
    group = ("fsdp", "context")
    normed_all = lax.all_gather(normed_mlp, group, axis=0, tiled=True)
    tangent_all = lax.all_gather(tangent, group, axis=0, tiled=True)
    branch_part, kept_values = feed_forward(normed_all, w_gate, w_up, w_down)
    grad_part, grad_w_gate, grad_w_up, grad_w_down = feed_back(
        normed_all, tangent_all, w_gate, w_up, w_down, kept_values
    )
    grad_normed = lax.psum_scatter(
        grad_part.astype(jnp.bfloat16), group, scatter_dimension=0, tiled=True
    ).astype(jnp.float32)
    branch = lax.psum_scatter(
        branch_part.astype(jnp.bfloat16), group, scatter_dimension=0, tiled=True
    ).astype(jnp.float32)
    outcome = middle + branch
    scaled_two = grad_normed * gain_second
    term_gain_two = jnp.sum(grad_normed * unit_two, axis=0)
    grad_middle = tangent_f + factor_two * (
        scaled_two - unit_two * jnp.mean(scaled_two * unit_two, axis=-1, keepdims=True)
    )
    grad_branch = grad_middle.astype(jnp.bfloat16)
    term_out = times_t(attended, grad_branch)
    grad_attended = times_nt(grad_branch, out_w).astype(jnp.bfloat16)
    head_grad = query_head_rows(grad_attended, sequence_total, segment_length)
    grad_q, grad_k, grad_v = lax.map(
        backward_head, (head_query, head_key, head_value, head_grad, query_positions, key_positions)
    )
    local_key_gradient, local_value_gradient = (
        lax.psum_scatter(
            merge_keys(grad_k, sequence_total, total_length).astype(jnp.bfloat16),
            "context",
            scatter_dimension=1,
            tiled=True,
        ).astype(jnp.float32),
        lax.psum_scatter(
            merge_keys(grad_v, sequence_total, total_length).astype(jnp.bfloat16),
            "context",
            scatter_dimension=1,
            tiled=True,
        ).astype(jnp.float32),
    )
    grad_query = (
        inverse_rotary(
            merge_queries(grad_q, sequence_total, segment_length).reshape(
                total_rows, QUERY_HEADS, HEAD_SIZE
            ),
            rotary_angles,
        )
        .reshape(total_rows, QUERY_HEADS * HEAD_SIZE)
        .astype(jnp.bfloat16)
    )
    grad_key = (
        inverse_rotary(
            local_key_gradient.reshape(total_rows, KEY_VALUE_HEADS, HEAD_SIZE), rotary_angles
        )
        .reshape(total_rows, KEY_VALUE_HEADS * HEAD_SIZE)
        .astype(jnp.bfloat16)
    )
    value_gradient = local_value_gradient.reshape(total_rows, KEY_VALUE_HEADS * HEAD_SIZE).astype(
        jnp.bfloat16
    )
    grad_normed_one = (
        times_nt(grad_query, query_w)
        + times_nt(grad_key, key_weight_local)
        + times_nt(value_gradient, value_w)
    )
    term_query = times_t(normed_tokens, grad_query)
    term_key = times_t(normed_tokens, grad_key)
    term_value = times_t(normed_tokens, value_gradient)
    scaled_one = grad_normed_one * gain_first
    term_gain_one = jnp.sum(grad_normed_one * unit_one, axis=0)
    grad_inputs = grad_middle + factor_one * (
        scaled_one - unit_one * jnp.mean(scaled_one * unit_one, axis=-1, keepdims=True)
    )
    share_query, share_key, share_value, share_out, share_gain_one, share_gain_two = (
        lax.psum_scatter(term_query.astype(jnp.bfloat16), ("fsdp", "context"), scatter_dimension=0, tiled=True),
        lax.psum_scatter(term_key.astype(jnp.bfloat16), ("fsdp", "context"), scatter_dimension=0, tiled=True),
        lax.psum_scatter(term_value.astype(jnp.bfloat16), ("fsdp", "context"), scatter_dimension=0, tiled=True),
        lax.psum_scatter(term_out.astype(jnp.bfloat16), ("fsdp", "context"), scatter_dimension=0, tiled=True),
        lax.psum_scatter(term_gain_one, ("fsdp", "context"), scatter_dimension=0, tiled=True),
        lax.psum_scatter(term_gain_two, ("fsdp", "context"), scatter_dimension=0, tiled=True),
    )
    summed = (
        lax.psum(share_query.astype(jnp.bfloat16), "replica").astype(jnp.float32),
        lax.psum(share_key.astype(jnp.bfloat16), "replica").astype(jnp.float32),
        lax.psum(share_value.astype(jnp.bfloat16), "replica").astype(jnp.float32),
        lax.psum(share_out.astype(jnp.bfloat16), "replica").astype(jnp.float32),
        lax.psum(grad_w_gate.astype(jnp.bfloat16), "replica").astype(jnp.float32),
        lax.psum(grad_w_up.astype(jnp.bfloat16), "replica").astype(jnp.float32),
        lax.psum(grad_w_down.astype(jnp.bfloat16), "replica").astype(jnp.float32),
        lax.psum(share_gain_one.astype(jnp.bfloat16), "replica").astype(jnp.float32),
        lax.psum(share_gain_two.astype(jnp.bfloat16), "replica").astype(jnp.float32),
    )
    out = outcome.astype(jnp.bfloat16).reshape(sequence_total, segment_length, width)
    grad_tokens = grad_inputs.astype(jnp.bfloat16).reshape(sequence_total, segment_length, width)
    return (
        out,
        grad_tokens,
        summed[0],
        summed[1],
        summed[2],
        summed[3],
        summed[4],
        summed[5],
        summed[6],
        summed[7],
        summed[8],
    )


def kernel_body(
    tokens,
    places,
    cotangent,
    gain_attn,
    gain_mlp,
    w_query,
    key_projection,
    value_projection,
    w_out,
    w_gate,
    w_up,
    w_down,
):
    bf16, f32 = jnp.bfloat16, jnp.float32
    sequence_total, segment_length, width = tokens.shape
    total_length = places.shape[1]
    line = lax.axis_size("context")
    narrow = key_projection.shape[1]
    run = w_query.shape[0]
    swap = [(i, i ^ 1) for i in range(lax.axis_size("fsdp"))]
    gates, ups, downs = ((w, lax.ppermute(w, "fsdp", swap)) for w in (w_gate, w_up, w_down))
    position = lax.axis_index("context")
    local_positions = lax.dynamic_slice_in_dim(places, position * segment_length, segment_length, 1)
    rotary_angles = local_positions.reshape(segment_length).astype(f32)[:, None] * frequencies(
        HEAD_SIZE // 2
    )
    extra = jnp.pad(jnp.stack([gain_attn, gain_mlp]), ((0, run - 2), (0, 0)))
    block = jnp.concatenate([w_query, key_projection, value_projection, extra, w_out], axis=1)
    cosine, sine = jnp.cos(rotary_angles), jnp.sin(rotary_angles)
    cosine = jnp.concatenate([cosine] * 4, axis=1)
    sine = jnp.concatenate([-sine, sine] * 2, axis=1)
    allowed = places.reshape(1, total_length) <= local_positions.reshape(segment_length, 1)
    bias = jnp.where(allowed, 0.0, -1e30).astype(f32)
    tangent = cotangent.reshape(segment_length, width)
    tangent_f = tangent.astype(f32)
    rows = tokens.reshape(segment_length, width)
    (
        attended, middle, normed_mlp, normed_tokens, scaled_query, logs, keyed_all, tangent_all, weights,
    ) = front_call(block, rows, tangent, bias, cosine, sine, line, narrow)
    mid = width + 2 * narrow
    gain_first = weights[:, 0, mid : mid + run].reshape(width).astype(f32)
    gain_second = weights[:, 1, mid : mid + run].reshape(width).astype(f32)
    grad_normed, _, hidden_all, *sums = feed_call(normed_mlp, tangent_all, gates, ups, downs, line)[:6]
    factor_two = lax.rsqrt(jnp.mean(middle * middle, axis=-1, keepdims=True) + norm_eps)
    unit_two = middle * factor_two
    scaled_two = grad_normed * gain_second
    term_gain_two = jnp.sum(grad_normed * unit_two, axis=0)
    grad_middle = tangent_f + factor_two * (
        scaled_two - unit_two * jnp.mean(scaled_two * unit_two, axis=-1, keepdims=True)
    )
    grad_branch = grad_middle.astype(bf16)
    branch, grad_qkv, *mirrored = back_call(
        scaled_query, keyed_all, grad_branch, bias, logs, hidden_all, downs, weights, cosine, -sine,
        sums, line,
    )
    outcome = middle + branch
    grad_w_gate, grad_w_up, grad_w_down = (
        a.astype(f32) + b.astype(f32) for a, b in zip(sums, mirrored)
    )
    packed, grad_tokens = sums_call(
        normed_tokens, attended, grad_qkv, grad_branch, rows, grad_middle, weights,
        gain_first.reshape(1, width), term_gain_two.reshape(1, width), line,
    )
    gains = packed[run * 3 // 4 : run * 3 // 4 + 2, mid + width :]
    ends, start = [], 0
    for size in (width, narrow, narrow, width):
        ends.append(packed[:, start : start + size])
        start += size
    return (
        outcome.astype(bf16).reshape(tokens.shape),
        grad_tokens.reshape(tokens.shape),
        *ends,
        grad_w_gate,
        grad_w_up,
        grad_w_down,
        gains[0],
        gains[1],
    )


def solution(mesh):
    placed = (
        P(("replica", "fsdp"), "context", None),
        P(("replica", "fsdp"), None),
        P(("replica", "fsdp"), "context", None),
        P(("fsdp", "context")),
        P(("fsdp", "context")),
        P(("fsdp", "context"), None),
        P(("fsdp", "context"), None),
        P(("fsdp", "context"), None),
        P(("fsdp", "context"), None),
        P(None, ("fsdp", "context")),
        P(None, ("fsdp", "context")),
        P(("fsdp", "context"), None),
    )
    kernels = (mesh.shape["replica"], mesh.shape["fsdp"], mesh.shape["context"]) == (2, 4, 4)
    return jax.shard_map(
        kernel_body if kernels else body,
        mesh=mesh,
        in_specs=placed,
        out_specs=(
            P(("replica", "fsdp"), "context", None),
            P(("replica", "fsdp"), "context", None),
            P(("fsdp", "context"), None),
            P(("fsdp", "context"), None),
            P(("fsdp", "context"), None),
            P(("fsdp", "context"), None),
            P(None, ("fsdp", "context")),
            P(None, ("fsdp", "context")),
            P(("fsdp", "context"), None),
            P(("fsdp", "context")),
            P(("fsdp", "context")),
        ),
        check_vma=False,
    )
```

```python
import functools

import jax
import jax.numpy as jnp
from jax import lax
from jax.experimental import pallas as pl
from jax.experimental.pallas import tpu as pltpu
from jax.sharding import PartitionSpec as P

QUERY_HEADS = 32
KEY_VALUE_HEADS = 8
HEAD_SIZE = 64


norm_eps = 1e-05
rope_base = 500000.0


def frequencies(half):
    return rope_base ** (-2.0 * jnp.arange(half, dtype=jnp.float32) / (2.0 * half))


def apply_rotary(angle_table, rotary_angles):
    half = angle_table.shape[-1] // 2
    first_half = angle_table[..., :half]
    second_half = angle_table[..., half:]
    cosine = jnp.cos(rotary_angles)[..., None, :]
    sine = jnp.sin(rotary_angles)[..., None, :]
    return jnp.concatenate(
        [first_half * cosine - second_half * sine, second_half * cosine + first_half * sine],
        axis=-1,
    )


def inverse_rotary(angle_table, rotary_angles):
    half = angle_table.shape[-1] // 2
    first_half = angle_table[..., :half]
    second_half = angle_table[..., half:]
    cosine = jnp.cos(rotary_angles)[..., None, :]
    sine = jnp.sin(rotary_angles)[..., None, :]
    return jnp.concatenate(
        [first_half * cosine + second_half * sine, second_half * cosine - first_half * sine],
        axis=-1,
    )


def times_t(left, right):
    return lax.dot_general(
        left, right, (((0,), (0,)), ((), ())), preferred_element_type=jnp.float32
    )


def times_nt(left, right):
    return lax.dot_general(
        left, right, (((1,), (1,)), ((), ())), preferred_element_type=jnp.float32
    )


def query_head_rows(angle_table, sequence_total, segment_length):
    reshaped_heads = angle_table.reshape(
        sequence_total, segment_length, KEY_VALUE_HEADS, QUERY_HEADS // KEY_VALUE_HEADS, HEAD_SIZE
    )
    return jnp.transpose(reshaped_heads, (0, 2, 1, 3, 4)).reshape(
        sequence_total * KEY_VALUE_HEADS, segment_length, QUERY_HEADS // KEY_VALUE_HEADS, HEAD_SIZE
    )


def key_heads(angle_table, sequence_total, total_length):
    reshaped_heads = angle_table.reshape(sequence_total, total_length, KEY_VALUE_HEADS, HEAD_SIZE)
    return jnp.transpose(reshaped_heads, (0, 2, 1, 3)).reshape(
        sequence_total * KEY_VALUE_HEADS, total_length, HEAD_SIZE
    )


def merge_queries(angle_table, sequence_total, segment_length):
    reshaped_heads = angle_table.reshape(
        sequence_total, KEY_VALUE_HEADS, segment_length, QUERY_HEADS // KEY_VALUE_HEADS, HEAD_SIZE
    )
    return jnp.transpose(reshaped_heads, (0, 2, 1, 3, 4)).reshape(
        sequence_total * segment_length, QUERY_HEADS * HEAD_SIZE
    )


def merge_keys(angle_table, sequence_total, total_length):
    reshaped_heads = angle_table.reshape(sequence_total, KEY_VALUE_HEADS, total_length, HEAD_SIZE)
    return jnp.transpose(reshaped_heads, (0, 2, 1, 3)).reshape(
        sequence_total, total_length, KEY_VALUE_HEADS * HEAD_SIZE
    )


def softmax_weights(part_query, part_key, place_query, place_key):
    allowed = place_key[None, :] <= place_query[:, None]
    scores = jnp.einsum(
        "qrd,kd->rqk", part_query, part_key, preferred_element_type=jnp.float32
    ) * HEAD_SIZE ** (-0.5)
    scores = jnp.where(allowed[None], scores, -1e30)
    return jax.nn.softmax(scores, axis=-1)


def forward_head(packed):
    part_query, part_key, part_value, place_query, place_key = packed
    probs = softmax_weights(part_query, part_key, place_query, place_key)
    return jnp.einsum(
        "rqk,kd->qrd", probs.astype(jnp.bfloat16), part_value, preferred_element_type=jnp.float32
    )


def backward_head(packed):
    part_query, part_key, part_value, part_grad, place_query, place_key = packed
    probs = softmax_weights(part_query, part_key, place_query, place_key)
    grad_probs = jnp.einsum(
        "qrd,kd->rqk", part_grad, part_value, preferred_element_type=jnp.float32
    )
    row_delta = jnp.sum(probs * grad_probs, axis=-1, keepdims=True)
    grad_scores = (probs * (grad_probs - row_delta)).astype(jnp.bfloat16)
    grad_query = jnp.einsum(
        "rqk,kd->qrd", grad_scores, part_key, preferred_element_type=jnp.float32
    ) * HEAD_SIZE ** (-0.5)
    grad_key = jnp.einsum(
        "rqk,qrd->kd", grad_scores, part_query, preferred_element_type=jnp.float32
    ) * HEAD_SIZE ** (-0.5)
    value_gradient = jnp.einsum(
        "rqk,qrd->kd", probs.astype(jnp.bfloat16), part_grad, preferred_element_type=jnp.float32
    )
    return (grad_query, grad_key, value_gradient)


def feed_forward(normed_rows, gate_w, up_w, down_w):
    gate_pre = jnp.dot(normed_rows, gate_w, preferred_element_type=jnp.float32)
    up_proj = jnp.dot(normed_rows, up_w, preferred_element_type=jnp.float32)
    sigmoid_gate = jax.nn.sigmoid(gate_pre)
    hidden = (gate_pre * sigmoid_gate * up_proj).astype(jnp.bfloat16)
    return (
        jnp.dot(hidden, down_w, preferred_element_type=jnp.float32),
        (gate_pre, up_proj, sigmoid_gate, hidden),
    )


def feed_back(normed_rows, grad_rows, gate_w, up_w, down_w, kept_values):
    gate_pre, up_proj, sigmoid_gate, hidden = kept_values
    grad_hidden = times_nt(grad_rows, down_w)
    term_down = times_t(hidden, grad_rows)
    grad_gate = (
        grad_hidden * up_proj * (sigmoid_gate * (1.0 + gate_pre * (1.0 - sigmoid_gate)))
    ).astype(jnp.bfloat16)
    grad_up = (grad_hidden * (gate_pre * sigmoid_gate)).astype(jnp.bfloat16)
    grad_normed = times_nt(grad_gate, gate_w) + times_nt(grad_up, up_w)
    return (grad_normed, times_t(normed_rows, grad_gate), times_t(normed_rows, grad_up), term_down)


MESH = pl.DeviceIdType.MESH
ANY = pl.BlockSpec(memory_space=pl.ANY)
BF = jnp.bfloat16
F32 = jnp.float32
NN = (((1,), (0,)), ((), ()))
NT = (((1,), (1,)), ((), ()))
TN = (((0,), (0,)), ((), ()))


def dot(left, right, dims):
    return lax.dot_general(left, right, dims, preferred_element_type=F32)


class Grid:
    def __init__(self, chips, line):
        self.chips, self.line = chips, line
        self.replica = lax.axis_index("replica")
        flat = lax.axis_index("fsdp")
        self.x, self.core = flat // 2, flat % 2
        self.z = lax.axis_index("context")
        self.has_left, self.has_right = self.z > 0, self.z + 1 < line
        self.left = (self.replica, flat, self.z - 1)
        self.right = (self.replica, flat, self.z + 1)
        self.across = (self.replica, (1 - self.x) * 2 + self.core, self.z)
        self.twin = (self.replica, self.x * 2 + 1 - self.core, self.z)
        self.mirror = (1 - self.replica, flat, self.z)

    def order(self, k):
        z, n = self.z, self.line
        low = 2 * z < n
        near = 2 * jnp.minimum(z, n - 1 - z)
        away = jnp.where(k % 2 == 1, -((k + 1) // 2), k // 2)
        return jnp.where(
            k <= near, z + jnp.where(low, away, -away), jnp.where(low, k, n - 1 - k)
        )

    def slot(self, x, z):
        return x * self.line + z

    def greet(self, twin, mirror=False):
        barrier = pltpu.get_barrier_semaphore()

        def tell(device):
            pl.semaphore_signal(barrier, inc=1, device_id=device, device_id_type=MESH)

        pl.when(self.has_left)(lambda: tell(self.left))
        pl.when(self.has_right)(lambda: tell(self.right))
        tell(self.across)
        if twin:
            tell(self.twin)
        if mirror:
            tell(self.mirror)
        count = 1 + int(twin) + int(mirror) + self.has_left.astype(jnp.int32) + self.has_right.astype(jnp.int32)
        pl.semaphore_wait(barrier, count)


def remote(src, dst, send, recv, device):
    return pltpu.make_async_remote_copy(
        src_ref=src, dst_ref=dst, send_sem=send, recv_sem=recv, device_id=device, device_id_type=MESH
    )


def each(count, action):
    def step(i, carry):
        action(i)
        return carry

    lax.fori_loop(0, count, step, 0)


class Gather:
    def __init__(self, grid, block, everything, send, recv, parts, cross=None):
        self.grid, self.everything, self.send, self.recv = grid, everything, send, recv
        self.block, self.cross = block, cross
        self.rows = everything.shape[1] // parts
        self.last = parts - 1
        self.early = parts if cross is None else parts - 1

    def piece(self, x, z, part):
        start = pl.multiple_of(part * self.rows, self.rows)
        return self.everything.at[self.grid.slot(x, z), pl.ds(start, self.rows)]

    def copy(self, z, part, link, first=False):
        grid = self.grid
        device = (grid.right, grid.left, grid.across)[link]
        there = self.piece(grid.x, z, part)
        start = pl.multiple_of(part * self.rows, self.rows)
        here = self.block.at[pl.ds(start, self.rows)] if first else there
        return remote(
            here, there, self.send.at[z, part, link], self.recv.at[grid.slot(grid.x, z), part], device
        )

    def other(self, z, link):
        grid = self.grid
        here = self.piece(1 - grid.x, z, self.last)
        sem = self.recv.at[grid.slot(1 - grid.x, z), self.last]
        return remote(here, here, self.cross.at[z, link], sem, (grid.right, grid.left)[link])

    def ways(self, z):
        grid = self.grid
        return (
            (0, jnp.logical_and(z <= grid.z, grid.has_right)),
            (1, jnp.logical_and(z >= grid.z, grid.has_left)),
        )

    def sides(self, distance):
        grid = self.grid
        return (
            (grid.z - distance, grid.z >= distance, 0, grid.has_right),
            (grid.z + distance, grid.z + distance < grid.line, 1, grid.has_left),
        )

    def links(self, z, part, action, first=False, across=True):
        for link, go in self.ways(z):
            pl.when(go)(lambda link=link: action(self.copy(z, part, link, first)))
        if across:
            action(self.copy(z, part, 2, first))

    def send_own(self):
        grid = self.grid
        start = lambda c: c.start()
        if self.cross is not None:
            self.copy(grid.z, self.last, 2, True).start()
        each(self.early, lambda part: self.links(grid.z, part, start, True))
        if self.cross is not None:
            self.links(grid.z, self.last, start, True, False)

    def turn_in(self):
        grid = self.grid
        self.other(grid.z, 0).wait_recv()
        for link, go in self.ways(grid.z):
            pl.when(go)(lambda link=link: self.other(grid.z, link).start())

    def forward(self, distance, part, wait=True, along=True, across=True):
        for z, there, link, go in self.sides(distance):

            @pl.when(there)
            def _(z=z, link=link, go=go):
                if wait:
                    self.copy(z, part, 2).wait_recv()
                if along:
                    pl.when(go)(lambda: self.copy(z, part, link).start())
                if across:
                    self.copy(z, part, 2).start()

    def forward_last(self, distance):
        for z, there, link, go in self.sides(distance):

            @pl.when(there)
            def _(z=z, link=link, go=go):
                self.copy(z, self.last, 2).wait_recv()
                pl.when(go)(lambda: self.copy(z, self.last, link).start())
                self.other(z, link).wait_recv()
                pl.when(go)(lambda: self.other(z, link).start())

    def wait_across(self, z):
        grid = self.grid

        def wait(part):
            here = self.piece(1 - grid.x, z, part)
            sem = self.recv.at[grid.slot(1 - grid.x, z), part]
            remote(here, here, self.send.at[z, part, 2], sem, grid.across).wait_recv()

        each(self.early, wait)

    def finish(self):
        done = lambda c: c.wait_send()

        def place(z):
            each(self.early, lambda part: self.links(z, part, done))
            if self.cross is not None:
                self.links(z, self.last, done, across=False)
                for link, go in self.ways(z):
                    pl.when(go)(lambda link=link: self.other(z, link).wait_send())

        each(self.grid.line, place)
        if self.cross is not None:
            self.copy(self.grid.z, self.last, 2).wait_send()


class Scatter:
    def __init__(self, grid, partial, from_across, from_line, total, sems, parts, cross=None):
        self.grid, self.partial, self.from_across = grid, partial, from_across
        self.from_line, self.total = from_line, total
        self.across_send, self.across_recv, self.line_send, self.line_recv = sems
        self.parts, self.cross = parts, cross
        self.rows = partial.shape[1] // parts
        self.early = parts if cross is None else parts - 1
        self.last = parts - 1

    def run(self, part):
        return pl.ds(pl.multiple_of(part * self.rows, self.rows), self.rows)

    def steps(self):
        return (self.grid.line - 1) * self.early

    def rank(self, j):
        return self.grid.order(self.grid.line - 1 - j)

    def step(self, n):
        self.pass_on(self.rank(n // self.early), n % self.early)

    def place(self, z):
        return z if self.from_across is None else self.grid.slot(self.grid.x, z)

    def across(self, z, part):
        grid = self.grid
        return remote(
            self.partial.at[grid.slot(1 - grid.x, z), self.run(part)],
            self.from_across.at[z, self.run(part)],
            self.across_send.at[z, part],
            self.across_recv.at[z, part],
            grid.across,
        )

    def arrival(self, z, leftward):
        return z if leftward else z - 1 + self.grid.line - 1

    def along(self, z, part, leftward):
        grid = self.grid
        arrival = self.arrival(z, leftward)
        return remote(
            self.partial.at[self.place(z), self.run(part)],
            self.from_line.at[arrival, self.run(part)],
            self.line_send.at[z, part],
            self.line_recv.at[arrival, part],
            grid.left if leftward else grid.right,
        )

    def other(self, z, leftward):
        grid = self.grid
        buffer, send, recv = self.cross
        arrival = self.arrival(z, leftward)
        return remote(
            self.partial.at[grid.slot(1 - grid.x, z), self.run(self.last)],
            buffer.at[arrival],
            send.at[z],
            recv.at[arrival],
            grid.left if leftward else grid.right,
        )

    def send_across(self, z):
        each(self.early, lambda part: self.across(z, part).start())

    def both_ways(self, z, action):
        grid = self.grid
        pl.when(jnp.logical_and(z <= grid.z, grid.has_right))(lambda: action(True))
        pl.when(jnp.logical_and(z >= grid.z, grid.has_left))(lambda: action(False))

    def add_line(self, z, part):
        def add(leftward):
            self.along(z, part, leftward).wait_recv()
            arrival = self.arrival(z, leftward)
            self.total[...] += self.from_line[arrival, self.run(part)].astype(F32)

        self.both_ways(z, add)

    def gather_sum(self, z, part):
        value = self.partial[self.place(z), self.run(part)].astype(F32)
        if self.from_across is not None:
            self.across(z, part).wait_recv()
            value = value + self.from_across[z, self.run(part)].astype(F32)
        self.total[...] = value
        self.add_line(z, part)

    def send_along(self, z, part):
        grid = self.grid
        self.partial[self.place(z), self.run(part)] = self.total[...].astype(BF)
        pl.when(z < grid.z)(lambda: self.along(z, part, True).start())
        pl.when(z > grid.z)(lambda: self.along(z, part, False).start())

    def pass_on(self, z, part):
        self.gather_sum(z, part)
        self.send_along(z, part)

    def add_other(self, z):
        grid, run = self.grid, self.run(self.last)
        slot = grid.slot(1 - grid.x, z)
        self.total[...] = self.partial[slot, run].astype(F32)

        def add(leftward):
            self.other(z, leftward).wait_recv()
            self.total[...] += self.cross[0][self.arrival(z, leftward)].astype(F32)

        self.both_ways(z, add)
        self.partial[slot, run] = self.total[...].astype(BF)

    def last_step(self, m):
        grid = self.grid
        z = grid.order(grid.line - 1 - m)
        self.add_other(z)

        @pl.when(z == grid.z)
        def _():
            self.across(z, self.last).start()

        @pl.when(z != grid.z)
        def _():
            pl.when(z < grid.z)(lambda: self.other(z, True).start())
            pl.when(z > grid.z)(lambda: self.other(z, False).start())
            self.total[...] = self.partial[self.place(z), self.run(self.last)].astype(F32)
            self.add_line(z, self.last)
            self.send_along(z, self.last)

    def own(self, result):
        def part_sum(part):
            self.gather_sum(self.grid.z, part)
            result[self.run(part)] = self.total[...]

        each(self.parts, part_sum)

    def finish(self):
        grid = self.grid

        def place(z):
            def part_done(part):
                pl.when(z < grid.z)(lambda: self.along(z, part, True).wait_send())
                pl.when(z > grid.z)(lambda: self.along(z, part, False).wait_send())

            each(self.parts, part_done)
            if self.from_across is not None:
                each(self.early, lambda part: self.across(z, part).wait_send())
            if self.cross is not None:
                pl.when(z < grid.z)(lambda: self.other(z, True).wait_send())
                pl.when(z > grid.z)(lambda: self.other(z, False).wait_send())

        each(grid.line, place)
        if self.cross is not None:
            self.across(grid.z, self.last).wait_send()


def scatter_scratch(line, rows, width, parts):
    return [
        pltpu.VMEM((2 * line, rows, width), BF),
        pltpu.VMEM((line, rows, width), BF),
        pltpu.VMEM((2 * line - 2, rows, width), BF),
        pltpu.VMEM((rows // parts, width), F32),
        pltpu.SemaphoreType.DMA((line, parts)),
        pltpu.SemaphoreType.DMA((line, parts)),
        pltpu.SemaphoreType.DMA((line, parts)),
        pltpu.SemaphoreType.DMA((2 * line - 2, parts)),
    ]


def load_pairs(pairs, sems):
    copies = [pltpu.make_async_copy(src, dst, sems.at[i]) for i, (src, dst) in enumerate(pairs)]
    for copy in copies:
        copy.start()
    for copy in copies:
        copy.wait()


def feed_kernel(
    line, parts, tile,
    normed, tangent_all, gate_own, gate_twin, up_own, up_twin, down_own, down_twin,
    grad_sum, normed_all, hidden_all, grad_gate, grad_up, grad_down,
    part_gate, part_up, part_down,
    gate_w, up_w, down_w, hidden, dgate, dup, rows_n, rows_t,
    partial, from_across, from_line, total, across_send, across_recv, line_send, line_recv,
    other_line, other_send, other_recv, gather_cross,
    gather_send, gather_recv, load_sem, wide, tile_sem, stage_a, stage_b, stage_sem, stage_recv, piece_a, piece_b, piece_sem, hidden_sem,
):
    grid = Grid(2, line)
    rows, width = normed.shape
    cols = gate_own.shape[1]
    blocks = 2 * line
    me = grid.slot(grid.x, grid.z)
    grid.greet(True)
    gather = Gather(grid, normed, normed_all, gather_send, gather_recv, parts, gather_cross)
    scatter = Scatter(
        grid, partial, from_across, from_line, total,
        (across_send, across_recv, line_send, line_recv), parts,
        (other_line, other_send, other_recv),
    )
    gather.send_own()
    load_pairs(
        [
            (gate_own, gate_w.at[:, pl.ds(0, cols)]),
            (gate_twin, gate_w.at[:, pl.ds(cols, cols)]),
            (up_own, up_w.at[:, pl.ds(0, cols)]),
            (up_twin, up_w.at[:, pl.ds(cols, cols)]),
            (down_own, down_w.at[pl.ds(0, cols)]),
            (down_twin, down_w.at[pl.ds(cols, cols)]),
            (normed, rows_n),
        ],
        load_sem,
    )
    load_pairs([(rows_n, normed_all.at[me])], load_sem)
    gather.turn_in()

    forwards = (line - 1) * parts

    def advance(n):
        distance, part = n // parts + 1, n % parts

        @pl.when(n < forwards)
        def _():
            pl.when(part < gather.early)(lambda: gather.forward(distance, part))
            pl.when(part == gather.last)(lambda: gather.forward_last(distance))

        return n + 1

    def work(slot, n):
        tangent_load = pltpu.make_async_copy(tangent_all.at[slot], rows_t, load_sem.at[1])
        tangent_load.start()
        load_pairs([(normed_all.at[slot], rows_n)], load_sem)
        spot = pl.ds(pl.multiple_of(slot * rows, rows), rows)

        def hidden_tile(j, n):
            c = pl.ds(pl.multiple_of(j * cols, cols), cols)
            gate = dot(rows_n[...], gate_w[:, c], NN)
            up = dot(rows_n[...], up_w[:, c], NN)
            pl.when(j == 0)(tangent_load.wait)
            grad = dot(rows_t[...], down_w[c, :], NT)
            sig = jax.nn.sigmoid(gate)
            silu = gate * sig
            hidden[spot, c] = (silu * up).astype(BF)
            dgate[spot, c] = (grad * up * (sig * (1.0 + gate * (1.0 - sig)))).astype(BF)
            dup[spot, c] = (grad * silu).astype(BF)
            return advance(n)

        n = lax.fori_loop(0, 2, hidden_tile, n)

        def back_tile(j, carry):
            c = pl.ds(pl.multiple_of(j * cols, cols), cols)
            sums = dot(dgate[spot, :], gate_w[c, :], NT) + dot(dup[spot, :], up_w[c, :], NT)
            partial[slot, :, c] = sums.astype(BF)
            return carry

        lax.fori_loop(0, width // cols, back_tile, 0)
        return advance(n)

    def stage(distance, n):
        def visit(i, n):
            z = grid.z + jnp.where(i % 2 == 0, -distance, distance)
            inside = jnp.logical_and(z >= 0, z < line)

            def block(n):
                n = lax.fori_loop(n, jnp.maximum(n, distance * parts), lambda m, c: advance(m), n)
                pl.when(i >= 2)(lambda: gather.wait_across(z))
                return work(grid.slot(jnp.where(i < 2, grid.x, 1 - grid.x), z), n)

            go = jnp.logical_and(inside, jnp.logical_or(distance > 0, i % 2 == 0))
            return lax.cond(go, block, lambda n: n, n)

        return lax.fori_loop(0, 4, visit, n)

    count = lax.fori_loop(0, line, stage, 0)
    lax.fori_loop(count, jnp.maximum(count, forwards), lambda m, c: advance(m), 0)
    hidden_copy = pltpu.make_async_copy(hidden, hidden_all, hidden_sem)
    hidden_copy.start()
    for j in range(line):
        scatter.send_across(scatter.rank(j))

    tiles = width // tile

    def wide_loads(t, start):
        j, buf = t % tiles, t % 2
        c = pl.ds(pl.multiple_of(j * tile, tile), tile)
        for i, source in enumerate((normed_all, tangent_all)):
            copy = pltpu.make_async_copy(source.at[:, :, c], wide.at[buf, i], tile_sem.at[buf, i])
            copy.start() if start else copy.wait()

    def stages(t):
        j, buf = t % tiles, t % 2
        c = pl.ds(pl.multiple_of(j * tile, tile), tile)
        return [
            remote(src, dst, stage_sem.at[buf, i], stage_recv.at[j, i], grid.twin)
            for i, (src, dst) in enumerate(
                (
                    (stage_a.at[buf, 0], part_gate.at[c, :]),
                    (stage_a.at[buf, 1], part_up.at[c, :]),
                    (stage_b.at[buf], part_down.at[:, c]),
                )
            )
        ]

    def results(t):
        j, buf = t % tiles, t % 2
        c = pl.ds(pl.multiple_of(j * tile, tile), tile)
        return [
            pltpu.make_async_copy(src, dst, stage_sem.at[buf, i])
            for i, (src, dst) in enumerate(
                (
                    (stage_a.at[buf, 0], grad_gate.at[c, :]),
                    (stage_a.at[buf, 1], grad_up.at[c, :]),
                    (stage_b.at[buf], grad_down.at[:, c]),
                )
            )
        ]

    def pieces(t):
        c = pl.ds(pl.multiple_of((t % tiles) * tile, tile), tile)
        return [
            (part_gate.at[c, :], piece_a.at[0]),
            (part_up.at[c, :], piece_a.at[1]),
            (part_down.at[:, c], piece_b),
        ]

    wide_loads(0, True)

    def weights(t, carry):
        buf = t % 2
        pl.when(t + 1 < 2 * tiles)(lambda: wide_loads(t + 1, True))
        wide_loads(t, False)
        tall = blocks * rows
        tokens = wide[buf, 0].reshape(tall, tile)
        tangents = wide[buf, 1].reshape(tall, tile)

        @pl.when(t < tiles)
        def _():
            theirs = slice(cols, 2 * cols)

            @pl.when(t >= 2)
            def _():
                for copy in stages(t - 2):
                    copy.wait_send()

            stage_a[buf, 0] = dot(tokens, dgate[:, theirs], TN).astype(BF)
            stage_a[buf, 1] = dot(tokens, dup[:, theirs], TN).astype(BF)
            stage_b[buf] = dot(hidden[:, theirs], tangents, TN).astype(BF)
            for copy in stages(t):
                copy.start()

        @pl.when(t >= tiles)
        def _():
            for copy in stages(t):
                copy.wait_recv()
            loads = [
                pltpu.make_async_copy(src, dst, piece_sem.at[i])
                for i, (src, dst) in enumerate(pieces(t))
            ]
            for copy in loads:
                copy.start()

            @pl.when(t < tiles + 2)
            def _():
                for copy in stages(t - 2):
                    copy.wait_send()

            @pl.when(t >= tiles + 2)
            def _():
                for copy in results(t - 2):
                    copy.wait()

            mine = slice(0, cols)
            own_gate = dot(tokens, dgate[:, mine], TN)
            own_up = dot(tokens, dup[:, mine], TN)
            own_down = dot(hidden[:, mine], tangents, TN)
            for copy in loads:
                copy.wait()
            stage_a[buf, 0] = (own_gate + piece_a[0].astype(F32)).astype(BF)
            stage_a[buf, 1] = (own_up + piece_a[1].astype(F32)).astype(BF)
            stage_b[buf] = (own_down + piece_b[...].astype(F32)).astype(BF)
            for copy in results(t):
                copy.start()

        n = t - 2 * lag
        pl.when(n >= 0)(lambda: scatter.step(n))
        m = t // 3 - lag
        ready = jnp.logical_and(t % 3 == 2, jnp.logical_and(m >= 0, m < line))
        pl.when(ready)(lambda: scatter.last_step(m))
        return carry

    lag = jnp.where(jnp.logical_and(grid.has_left, grid.has_right), 1, 0)
    lax.fori_loop(0, 2 * tiles, weights, 0)

    def rest(n, carry):
        scatter.step(n)
        return carry

    lax.fori_loop(2 * tiles - 2 * lag, scatter.steps(), rest, 0)
    scatter.own(grad_sum)
    for t in (2 * tiles - 2, 2 * tiles - 1):
        for copy in results(t):
            copy.wait()
    gather.finish()
    scatter.finish()
    hidden_copy.wait()


def feed_call(normed, tangent_all, gates, ups, downs, line):
    rows, width = normed.shape
    cols = gates[0].shape[1]
    blocks, parts, tile = 2 * line, 8, 256
    tiles = width // tile
    tall = blocks * rows
    shapes = jax.ShapeDtypeStruct
    hbm = lambda *s: shapes(s, BF)
    return pl.pallas_call(
        functools.partial(feed_kernel, line, parts, tile),
        out_shape=(
            shapes((rows, width), F32),
            hbm(blocks, rows, width), hbm(tall, 2 * cols),
            hbm(width, cols), hbm(width, cols), hbm(cols, width),
            hbm(width, cols), hbm(width, cols), hbm(cols, width),
        ),
        in_specs=[ANY] * 8,
        out_specs=(pl.BlockSpec(memory_space=pltpu.VMEM),) + (ANY,) * 8,
        scratch_shapes=[
            pltpu.VMEM((width, 2 * cols), BF), pltpu.VMEM((width, 2 * cols), BF), pltpu.VMEM((2 * cols, width), BF),
            pltpu.VMEM((tall, 2 * cols), BF), pltpu.VMEM((tall, 2 * cols), BF), pltpu.VMEM((tall, 2 * cols), BF),
            pltpu.VMEM((rows, width), BF), pltpu.VMEM((rows, width), BF),
            *scatter_scratch(line, rows, width, parts),
            pltpu.VMEM((2 * line - 2, rows // parts, width), BF),
            pltpu.SemaphoreType.DMA((line,)), pltpu.SemaphoreType.DMA((2 * line - 2,)),
            pltpu.SemaphoreType.DMA((line, 2)),
            pltpu.SemaphoreType.DMA((line, parts, 3)), pltpu.SemaphoreType.DMA((blocks, parts)),
            pltpu.SemaphoreType.DMA((8,)),
            pltpu.VMEM((2, 2, blocks, rows, tile), BF), pltpu.SemaphoreType.DMA((2, 2)),
            pltpu.VMEM((2, 2, tile, cols), BF), pltpu.VMEM((2, cols, tile), BF),
            pltpu.SemaphoreType.DMA((2, 3)), pltpu.SemaphoreType.DMA((tiles, 3)),
            pltpu.VMEM((2, tile, cols), BF), pltpu.VMEM((cols, tile), BF), pltpu.SemaphoreType.DMA((3,)),
            pltpu.SemaphoreType.DMA,
        ],
        compiler_params=pltpu.CompilerParams(
            collective_id=1, has_side_effects=True, vmem_limit_bytes=63 * 2**20
        ),
        name="feed",
    )(normed, tangent_all, gates[0], gates[1], ups[0], ups[1], downs[0], downs[1])


class Thirds(Scatter):
    def run(self, part):
        quarter = self.rows
        start = jnp.where(part == 2, self.grid.replica, 2 + part) * quarter
        return pl.ds(pl.multiple_of(start, quarter), quarter)


def sums_kernel(
    line,
    normed, attended, grad_qkv, grad_out, twin_normed, twin_attended, twin_out,
    tokens, grad_middle, weights, gain, term_two,
    result, grad_tokens,
    both_normed, both_attended, both_qkv, both_out, load_sem, twin_send, twin_recv,
    partial, from_across, from_line, total, across_send, across_recv, line_send, line_recv,
    mine, theirs, mirror_send, mirror_recv, from_mirror, quarter_send, quarter_recv,
    in_weights, weight_sem, token_v, middle_v, grad_normed, terms, own_terms, twin_terms,
):
    grid = Grid(2, line)
    rows, width = normed.shape
    run = partial.shape[1]
    quarter = run // 4
    narrow = grad_qkv.shape[1]
    grid.greet(True, True)
    scatter = Thirds(
        grid, partial, from_across, from_line, total,
        (across_send, across_recv, line_send, line_recv), 3,
    )
    scatter.rows = quarter
    own, twin = pl.ds(0, rows), pl.ds(rows, rows)
    swap_qkv = remote(grad_qkv, both_qkv.at[twin], twin_send.at[0], twin_recv.at[0], grid.twin)
    swap_qkv.start()
    load_pairs(
        [
            (attended, both_attended.at[own]),
            (twin_attended, both_attended.at[twin]),
            (grad_out, both_out.at[own]),
            (twin_out, both_out.at[twin]),
            (normed, both_normed.at[own]),
            (twin_normed, both_normed.at[twin]),
            (grad_qkv, both_qkv.at[own]),
        ],
        load_sem,
    )
    later = [
        pltpu.make_async_copy(src, dst, weight_sem.at[i])
        for i, (src, dst) in enumerate(
            (
                (weights.at[:, :, pl.ds(0, narrow)], in_weights),
                (tokens, token_v),
                (grad_middle, middle_v),
            )
        )
    ]
    for copy in later:
        copy.start()
    tall = line * run
    tile = 512
    away = pl.ds(pl.multiple_of((1 - grid.replica) * quarter, quarter), quarter)
    here = pl.ds(pl.multiple_of(grid.replica * quarter, quarter), quarter)

    def to_mirror(slot):
        return remote(
            partial.at[slot, away], from_mirror.at[slot],
            quarter_send.at[slot], quarter_recv.at[slot], grid.mirror,
        )

    def features(x):
        return pl.ds(pl.multiple_of((x * 2 + grid.core) * tall, tall), tall)

    def column(j, carry):
        x = jnp.where(j == 0, 1 - grid.x, grid.x)
        blocks = pl.ds(x * line, line)

        def wide(left, right, first):
            def step(i, inner):
                c = pl.ds(pl.multiple_of(i * tile, tile), tile)
                to = pl.ds(pl.multiple_of(first + i * tile, 128), tile)
                value = dot(left[:, features(x)], right[:, c], TN).astype(BF)
                partial[blocks, :, to] = value.reshape(line, run, tile)
                return inner

            lax.fori_loop(0, right.shape[1] // tile, step, 0)

        wide(both_attended, both_out, narrow)
        pl.when(j == 0)(swap_qkv.wait)
        wide(both_normed, both_qkv, 0)
        partial[blocks, :, narrow + width :] = jnp.zeros((line, run, 128), BF)
        for k in range(line - 1, -1, -1):
            z = grid.order(k)
            to_mirror(grid.slot(x, z)).start()
            pl.when(j == 0)(lambda z=z: scatter.across(z, 0).start())
        return carry

    lax.fori_loop(0, 2, column, 0)
    for copy in later:
        copy.wait()

    def back_step(j, carry):
        units = pl.ds(j * (tile // run), tile // run)
        c = pl.ds(pl.multiple_of(j * tile, tile), tile)
        right = in_weights[units].reshape(tile, narrow)
        grad_normed[:, c] = dot(both_qkv[own, :], right, NT)
        return carry

    lax.fori_loop(0, width // tile, back_step, 0)
    terms[...] = jnp.zeros_like(terms)
    chunk = 64

    def norm_step(j, carry):
        r = pl.ds(pl.multiple_of(j * chunk, chunk), chunk)
        value = token_v[r, :].astype(F32)
        factor = lax.rsqrt(jnp.mean(value * value, axis=1, keepdims=True) + norm_eps)
        unit = value * factor
        grad = grad_normed[r, :]
        terms[0:1, :] += jnp.sum(grad * unit, axis=0, keepdims=True)
        scaled = grad * gain[...]
        mean = jnp.mean(scaled * unit, axis=1, keepdims=True)
        grad_tokens[r, :] = (middle_v[r, :] + factor * (scaled - unit * mean)).astype(BF)
        return carry

    lax.fori_loop(0, rows // chunk, norm_step, 0)
    terms[1:2, :] = term_two[...]
    own_terms[...] = terms[...].astype(BF)
    swap_terms = remote(own_terms, twin_terms, twin_send.at[1], twin_recv.at[1], grid.twin)
    swap_terms.start()
    swap_terms.wait()
    for x in range(2):
        for z in range(line):
            first = pl.multiple_of((x * 2 + grid.core) * tall + z * run, run)
            c = pl.ds(first, run)
            value = own_terms[:, c].astype(F32) + twin_terms[:, c].astype(F32)
            partial[x * line + z, 3 * quarter : 3 * quarter + 16, narrow + width :] = value.astype(BF)
    for k in range(line - 1, -1, -1):
        scatter.across(grid.order(k), 1).start()

    def add_mirror(x):
        def step(i, carry):
            slot = grid.slot(x, grid.order(line - 1 - i))
            to_mirror(slot).wait_recv()
            value = partial[slot, here].astype(F32) + from_mirror[slot].astype(F32)
            partial[slot, here] = value.astype(BF)
            return carry

        lax.fori_loop(0, line, step, 0)

    add_mirror(1 - grid.x)
    for k in range(line - 1, -1, -1):
        scatter.across(grid.order(k), 2).start()

    def swap(part, whole=True):
        at = scatter.run(part)
        return remote(
            mine.at[at], theirs.at[at], mirror_send.at[part], mirror_recv.at[part], grid.mirror
        )

    def sweep(part):
        def step(i, carry):
            scatter.pass_on(grid.order(line - 1 - i), part)
            return carry

        lax.fori_loop(0, line - 1, step, 0)

    def settle(part):
        scatter.gather_sum(grid.z, part)
        mine[scatter.run(part)] = total[...].astype(BF)
        swap(part).start()

    sweep(0)
    sweep(1)
    add_mirror(grid.x)
    settle(0)
    sweep(2)
    settle(1)
    settle(2)
    result[here] = mine[here].astype(F32)
    for part in range(2):
        swap(part).wait()
        at = scatter.run(part)
        result[at] = mine[at].astype(F32) + theirs[at].astype(F32)
    swap(2).wait_send()
    remote(mine.at[away], theirs.at[away], mirror_send.at[2], mirror_recv.at[2], grid.mirror).wait_recv()
    result[away] = theirs[away].astype(F32)
    scatter.finish()

    def sent(slot, carry):
        to_mirror(slot).wait_send()
        return carry

    lax.fori_loop(0, 2 * line, sent, 0)


def sums_call(
    normed, attended, grad_qkv, grad_out, twins, tokens, grad_middle, weights, gain, term_two, line
):
    rows, width = normed.shape
    narrow = grad_qkv.shape[1]
    run, whole = weights.shape[1:]
    quarter = run // 4
    vmem = pl.BlockSpec(memory_space=pltpu.VMEM)
    dma = pltpu.SemaphoreType.DMA
    like = lambda a: pltpu.VMEM(a.shape, a.dtype)
    return pl.pallas_call(
        functools.partial(sums_kernel, line),
        out_shape=(
            jax.ShapeDtypeStruct((run, whole), F32), jax.ShapeDtypeStruct((rows, width), BF),
        ),
        in_specs=[ANY] * 10 + [vmem] * 2,
        out_specs=(vmem, vmem),
        scratch_shapes=[
            pltpu.VMEM((2 * rows, width), BF), pltpu.VMEM((2 * rows, width), BF),
            pltpu.VMEM((2 * rows, narrow), BF), pltpu.VMEM((2 * rows, width), BF),
            dma((7,)), dma((2,)), dma((2,)),
            pltpu.VMEM((2 * line, run, whole), BF), pltpu.VMEM((line, run, whole), BF),
            pltpu.VMEM((2 * line - 2, run, whole), BF), pltpu.VMEM((quarter, whole), F32),
            dma((line, 3)), dma((line, 3)), dma((line, 3)), dma((2 * line - 2, 3)),
            pltpu.VMEM((run, whole), BF), pltpu.VMEM((run, whole), BF), dma((3,)), dma((3,)),
            pltpu.VMEM((2 * line, quarter, whole), BF), dma((2 * line,)), dma((2 * line,)),
            pltpu.VMEM((weights.shape[0], run, narrow), BF), dma((3,)),
            like(tokens), like(grad_middle), pltpu.VMEM((rows, width), F32),
            pltpu.VMEM((16, width), F32), pltpu.VMEM((16, width), BF), pltpu.VMEM((16, width), BF),
        ],
        compiler_params=pltpu.CompilerParams(
            collective_id=3, has_side_effects=True, vmem_limit_bytes=63 * 2**20
        ),
        name="sums",
    )(
        normed, attended, grad_qkv, grad_out, *twins, tokens, grad_middle, weights, gain, term_two
    )


def gather_weights(
    grid, block, everything, send, recv, twin_send, twin_recv, meanwhile, afterwards
):
    line = grid.line
    rows = block.shape[0] // 4
    carry_a, carry_b = grid.replica * 2, grid.replica * 2 + 1
    other_a, other_b = (1 - grid.replica) * 2, (1 - grid.replica) * 2 + 1
    right, left, across, mirror = range(4)
    devices = (grid.right, grid.left, grid.across, grid.mirror)

    def run(quarter):
        return pl.ds(pl.multiple_of(quarter * rows, rows), rows)

    def place(x, core, z, quarter):
        return everything.at[(x * 2 + core) * line + z, run(quarter)]

    def copy(x, z, quarter, link, first=False):
        there = place(x, grid.core, z, quarter)
        here = block.at[run(quarter)] if first else there
        unit = x * line + z
        return remote(
            here, there, send.at[quarter, unit, link], recv.at[quarter, unit], devices[link]
        )

    def share(x, z, quarter, first=False):
        there = place(x, grid.core, z, quarter)
        here = block.at[run(quarter)] if first else there
        unit = x * line + z
        return remote(
            here, there, twin_send.at[quarter, unit], twin_recv.at[quarter, unit], grid.twin
        )

    def arrived(x, z, quarter):
        copy(x, z, quarter, across).wait_recv()
        share(x, z, quarter).start()

    copy(grid.x, grid.z, carry_b, across, True).start()
    copy(grid.x, grid.z, carry_a, across, True).start()
    copy(grid.x, grid.z, other_a, across, True).start()
    for link, go in ((right, grid.has_right), (left, grid.has_left)):

        @pl.when(go)
        def _(link=link):
            copy(grid.x, grid.z, carry_a, link, True).start()
            copy(grid.x, grid.z, carry_b, link, True).start()

    for quarter in range(4):
        share(grid.x, grid.z, quarter, True).start()
    meanwhile()

    arrived(1 - grid.x, grid.z, carry_b)
    copy(1 - grid.x, grid.z, carry_b, mirror).start()
    for link, go in ((right, grid.has_right), (left, grid.has_left)):
        pl.when(go)(lambda link=link: copy(1 - grid.x, grid.z, carry_b, link).start())

    def sides(distance):
        return (
            (grid.z - distance, grid.z >= distance, right, grid.has_right),
            (grid.z + distance, grid.z + distance < line, left, grid.has_left),
        )

    def step(distance, carry):
        for x, quarter in (
            (grid.x, carry_a),
            (grid.x, carry_b),
            (1 - grid.x, carry_b),
        ):
            for z, there, link, go in sides(distance):

                @pl.when(there)
                def _(x=x, quarter=quarter, z=z, link=link, go=go):
                    copy(x, z, quarter, across).wait_recv()
                    pl.when(go)(lambda: copy(x, z, quarter, link).start())
                    copy(x, z, quarter, mirror).start()
                    if quarter is carry_a:
                        copy(x, z, quarter, across).start()
                    share(x, z, quarter).start()

        for z, there, _, _ in sides(distance - 1):

            @pl.when(jnp.logical_and(there, distance > 1))
            def _(z=z):
                arrived(grid.x, z, other_a)
                copy(grid.x, z, other_a, across).start()

        return carry

    lax.fori_loop(1, line + 1, step, 0)
    afterwards()

    def last(z, carry):
        arrived(1 - grid.x, z, carry_a)
        arrived(1 - grid.x, z, other_a)
        arrived(1 - grid.x, z, other_b)
        pl.when(z != grid.z)(lambda: arrived(grid.x, z, other_b))
        return carry

    lax.fori_loop(0, line, last, 0)

    def finish(z, carry):
        away = z != grid.z
        for x in (grid.x, 1 - grid.x):
            for quarter in range(4):
                share(x, z, quarter).wait()
        for x, quarter in ((grid.x, carry_a), (grid.x, carry_b), (1 - grid.x, carry_b)):
            to_mirror = jnp.logical_or(away, jnp.bool_(x is not grid.x))
            pl.when(to_mirror)(
                lambda x=x, quarter=quarter: copy(x, z, quarter, mirror).wait_send()
            )
            for link, go in (
                (right, jnp.logical_and(z <= grid.z, grid.has_right)),
                (left, jnp.logical_and(z >= grid.z, grid.has_left)),
            ):
                pl.when(go)(
                    lambda x=x, quarter=quarter, link=link: copy(x, z, quarter, link).wait_send()
                )
        copy(grid.x, z, carry_a, across).wait_send()
        copy(grid.x, z, other_a, across).wait_send()
        return carry

    lax.fori_loop(0, line, finish, 0)
    copy(grid.x, grid.z, carry_b, across, True).wait_send()


class Line:
    def __init__(self, grid, block, everything, send, recv):
        self.grid, self.block, self.everything = grid, block, everything
        self.send, self.recv = send, recv

    def copy(self, z, link, first=False):
        grid = self.grid
        there = self.everything.at[z]
        here = self.block if first else there
        device = (grid.right, grid.left)[link]
        return remote(here, there, self.send.at[z, link], self.recv.at[z], device)

    def send_own(self):
        grid = self.grid
        for link, go in ((0, grid.has_right), (1, grid.has_left)):
            pl.when(go)(lambda link=link: self.copy(grid.z, link, True).start())

    def forward(self, distance):
        grid = self.grid
        for z, there, link, go in (
            (grid.z - distance, grid.z >= distance, 0, grid.has_right),
            (grid.z + distance, grid.z + distance < grid.line, 1, grid.has_left),
        ):

            @pl.when(there)
            def _(z=z, link=link, go=go):
                self.copy(z, link).wait_recv()
                pl.when(go)(lambda: self.copy(z, link).start())

    def finish(self):
        grid = self.grid

        def step(z, carry):
            for link, go in (
                (0, jnp.logical_and(z <= grid.z, grid.has_right)),
                (1, jnp.logical_and(z >= grid.z, grid.has_left)),
            ):
                pl.when(go)(lambda link=link: self.copy(z, link).wait_send())
            return carry

        lax.fori_loop(0, grid.line, step, 0)


def turn(value, cosine, sine, scale):
    parts = []
    lane = lax.broadcasted_iota(jnp.int32, (value.shape[0], 128), 1) % HEAD_SIZE
    for first in range(0, value.shape[1], 128):
        pair = value[:, first : first + 128]
        swapped = jnp.where(
            lane < HEAD_SIZE // 2,
            pltpu.roll(pair, 128 - HEAD_SIZE // 2, 1),
            pltpu.roll(pair, HEAD_SIZE // 2, 1),
        )
        parts.append(((pair * cosine[...] + swapped * sine[...]) * scale).astype(BF))
    return parts[0] if len(parts) == 1 else jnp.concatenate(parts, axis=1)


def halves(pair, half):
    pair = pair.astype(F32)
    turned = pltpu.roll(pair, HEAD_SIZE, 1)
    lane = lax.broadcasted_iota(jnp.int32, pair.shape, 1) // HEAD_SIZE
    first = jnp.where(half == 0, pair, turned)
    second = jnp.where(half == 0, turned, pair)
    both = jnp.concatenate([first, second], axis=0)
    return jnp.where(jnp.concatenate([lane, lane], axis=0) == half, both, 0.0).astype(BF)


def unhalves(both, half):
    rows = both.shape[0] // 2
    first, second = both[:rows], both[rows:]
    lane = lax.broadcasted_iota(jnp.int32, first.shape, 1) // HEAD_SIZE
    first = jnp.where(half == 0, first, pltpu.roll(first, HEAD_SIZE, 1))
    second = jnp.where(half == 0, pltpu.roll(second, HEAD_SIZE, 1), second)
    return jnp.where(lane == 0, first, second)


def front_kernel(
    line, parts,
    query_w, key_w, value_w, extra_w, out_w, tokens, tangent, bias, cosine, sine,
    attended, middle, normed, first_normed, queries, logs, keyed_out, tangent_all, weights_out,
    everything, keyed, keyed_all, bias_v, token_v, cosine_v, sine_v, gain, scores, probs, sums, stage, load_sem,
    key_send, key_recv, send, recv, own_sem, weight_send, weight_recv, twin_send, twin_recv,
):
    grid = Grid(2, line)
    rows, width = tokens.shape
    narrow = keyed.shape[1] // 2
    total = bias.shape[1]
    extra = width + 2 * narrow
    after = extra + 128
    me = grid.slot(grid.x, grid.z)
    chunk = rows // 2
    tile = 512
    block = everything.at[(grid.x * 2 + grid.core) * line + grid.z]
    first, packs = 0, []
    for part in (query_w, key_w, value_w, extra_w, out_w):
        packs.append((part, block.at[:, pl.ds(first, part.shape[1])]))
        first += part.shape[1]
    load_pairs(packs, load_sem)
    grid.greet(True, True)

    def meanwhile():
        load_pairs(
            [
                (tangent, stage),
                (bias, bias_v),
                (tokens, token_v),
                (cosine, cosine_v),
                (sine, sine_v),
            ],
            load_sem,
        )
        load_pairs([(stage, tangent_all.at[me])], own_sem)

    gather = Gather(grid, tangent, tangent_all, send, recv, parts)
    gather_weights(
        grid, block, everything, weight_send, weight_recv, twin_send, twin_recv, meanwhile,
        gather.send_own,
    )
    weights_copy = pltpu.make_async_copy(everything, weights_out, own_sem.at[1])
    weights_copy.start()
    units, run = everything.shape[0], everything.shape[1]
    for unit in range(units):
        for which in range(2):
            gain[which : which + 1, unit * run : (unit + 1) * run] = everything[
                unit, which : which + 1, extra:after
            ].astype(F32)

    def norm(source, target, which):
        def step(j, carry):
            here = pl.ds(pl.multiple_of(j * chunk, chunk), chunk)
            value = source[here, :].astype(F32)
            factor = lax.rsqrt(jnp.mean(value * value, axis=1, keepdims=True) + norm_eps)
            target[here, :] = (value * factor * gain[which : which + 1, :]).astype(BF)
            return carry

        lax.fori_loop(0, rows // chunk, step, 0)

    norm(token_v, first_normed, 0)

    def project(c):
        return dot(first_normed[...], everything[:, :, c].reshape(width, tile), NN)

    for first in range(0, narrow, tile):
        keyed[:, first : first + tile] = turn(project(slice(width + first, width + first + tile)), cosine_v, sine_v, 1.0)
        keyed[:, narrow + first : narrow + first + tile] = project(
            slice(width + narrow + first, width + narrow + first + tile)
        ).astype(BF)
    line_keys = Line(grid, keyed, keyed_all, key_send, key_recv)
    line_keys.send_own()
    for part in range(parts):
        gather.forward(1, part, along=False)
    keyed_all[grid.z] = keyed[...]

    def query_step(j, carry):
        c = pl.ds(pl.multiple_of(j * tile, tile), tile)
        queries[:, c] = turn(project(c), cosine_v, sine_v, HEAD_SIZE ** (-0.5))
        return carry

    lax.fori_loop(0, width // tile, query_step, 0)
    for distance in range(1, line):
        line_keys.forward(distance)
    for part in range(parts):
        gather.forward(1, part, wait=False, across=False)

    logs[...] = jnp.zeros_like(logs)
    pairs = width // (2 * HEAD_SIZE)
    group = pairs // (narrow // (2 * HEAD_SIZE))

    def advance(n):
        gather.forward(n // parts + 2, n % parts)

    def pair_step(i, carry):
        c = pl.ds(pl.multiple_of(i * 128, 128), 128)
        half = (i // (group // 2)) % 2
        first_key = pl.multiple_of((i // group) * 128, 128)
        keys = keyed_all[:, :, pl.ds(first_key, 128)].reshape(total, 128)
        values = keyed_all[:, :, pl.ds(first_key + narrow, 128)].reshape(total, 128)
        scores[...] = dot(halves(queries[:, c], half), keys, NT)

        def soft(j, inner):
            here = pl.ds(pl.multiple_of(j * rows, rows), rows)
            value = scores[here, :] + bias_v[...]
            top = jnp.max(value, axis=1, keepdims=True)
            power = jnp.exp(value - top)
            size = jnp.sum(power, axis=1, keepdims=True)
            probs[here, :] = power.astype(BF)
            sums[here, :] = jnp.broadcast_to(1.0 / size, (rows, 128))
            lane = lax.broadcasted_iota(jnp.int32, (rows, 128), 1)
            logs[here, :] = jnp.where(lane == i, top + jnp.log(size), logs[here, :])
            return inner

        lax.fori_loop(0, 2, soft, 0)
        out = dot(probs[...], values, NN) * sums[...]
        attended[:, c] = unhalves(out, half).astype(BF)

        pl.when(i % 2 == 1)(lambda: advance(i // 2))
        return carry

    lax.fori_loop(0, pairs, pair_step, 0)
    keyed_copy = pltpu.make_async_copy(keyed_all, keyed_out, load_sem.at[0])
    keyed_copy.start()

    def out_step(j, carry):
        c = pl.ds(pl.multiple_of(j * tile, tile), tile)
        w = pl.ds(pl.multiple_of(after + j * tile, 128), tile)
        out = dot(attended[...], everything[:, :, w].reshape(width, tile), NN)
        middle[:, c] = token_v[:, c].astype(F32) + out
        return carry

    lax.fori_loop(0, width // tile, out_step, 0)
    norm(middle, normed, 1)

    def rest(n, carry):
        advance(n)
        return carry

    lax.fori_loop(pairs // 2, (line - 2) * parts, rest, 0)
    for z in range(line):
        gather.wait_across(z)
    keyed_copy.wait()
    weights_copy.wait()
    line_keys.finish()
    gather.finish()


def front_call(pieces, tokens, tangent, bias, cosine, sine, line):
    rows, width = tokens.shape
    narrow = pieces[1].shape[1]
    unit = (pieces[0].shape[0], sum(p.shape[1] for p in pieces))
    total = bias.shape[1]
    blocks, parts = 2 * line, 4
    shapes = jax.ShapeDtypeStruct
    vmem = pl.BlockSpec(memory_space=pltpu.VMEM)
    like = lambda a: pltpu.VMEM(a.shape, a.dtype)
    return pl.pallas_call(
        functools.partial(front_kernel, line, parts),
        out_shape=(
            shapes((rows, width), BF), shapes((rows, width), F32), shapes((rows, width), BF),
            shapes((rows, width), BF), shapes((rows, width), BF),
            shapes((2 * rows, 128), F32), shapes((line, rows, 2 * narrow), BF),
            shapes((blocks, rows, width), BF), shapes((2 * blocks,) + unit, BF),
        ),
        in_specs=[ANY] * 10,
        out_specs=(vmem,) * 6 + (ANY,) * 3,
        scratch_shapes=[
            pltpu.VMEM((2 * blocks,) + unit, BF),
            pltpu.VMEM((rows, 2 * narrow), BF), pltpu.VMEM((line, rows, 2 * narrow), BF),
            like(bias), like(tokens), like(cosine), like(sine), pltpu.VMEM((2, width), F32),
            pltpu.VMEM((2 * rows, total), F32), pltpu.VMEM((2 * rows, total), BF),
            pltpu.VMEM((2 * rows, 128), F32), pltpu.VMEM((rows, width), BF), pltpu.SemaphoreType.DMA((6,)),
            pltpu.SemaphoreType.DMA((line, 2)), pltpu.SemaphoreType.DMA((line,)),
            pltpu.SemaphoreType.DMA((line, parts, 3)), pltpu.SemaphoreType.DMA((blocks, parts)),
            pltpu.SemaphoreType.DMA((2,)),
            pltpu.SemaphoreType.DMA((4, blocks, 4)), pltpu.SemaphoreType.DMA((4, blocks)),
            pltpu.SemaphoreType.DMA((4, blocks)), pltpu.SemaphoreType.DMA((4, blocks)),
        ],
        compiler_params=pltpu.CompilerParams(
            collective_id=5, has_side_effects=True, vmem_limit_bytes=62 * 2**20
        ),
        name="front",
    )(*pieces, tokens, tangent, bias, cosine, sine)


def back_kernel(
    line, parts,
    queries, keyed_all, grad_out, bias, logs, hidden_all, down_own, down_twin, weights, cosine, sine,
    gate_sum, up_sum, down_sum, normed, attended,
    branch, grad_qkv, gate_mirror, up_mirror, down_mirror, twin_normed, twin_attended, twin_out,
    out_v, out_w, cosine_v, sine_v, grad_keyed, mirror_send, mirror_recv,
    query_v, keyed_v, grad_v, bias_v, log_v, scores, gradients, probs, slopes, key_sum, value_sum,
    down_w, hidden, load_sem,
    partial, from_across, from_line, total, across_send, across_recv, line_send, line_recv,
    key_partial, key_line, key_total, key_send, key_recv,
):
    grid = Grid(2, line)
    cols, width = down_own.shape
    rows = partial.shape[1]
    narrow = keyed_all.shape[2] // 2
    length = bias.shape[1]
    grid.greet(True, True)
    swapped = [
        remote(src, dst, mirror_send.at[3 + i], mirror_recv.at[3 + i], grid.twin)
        for i, (src, dst) in enumerate(
            ((normed, twin_normed), (attended, twin_attended), (grad_out, twin_out))
        )
    ]
    for copy in swapped:
        copy.start()
    mirrored = [
        remote(src, dst, mirror_send.at[i], mirror_recv.at[i], grid.mirror)
        for i, (src, dst) in enumerate(
            ((gate_sum, gate_mirror), (up_sum, up_mirror), (down_sum, down_mirror))
        )
    ]
    for copy in mirrored:
        copy.start()
    load_pairs(
        [
            (down_own, down_w.at[pl.ds(0, cols)]),
            (down_twin, down_w.at[pl.ds(cols, cols)]),
            (hidden_all, hidden),
            (queries, query_v),
            (keyed_all, keyed_v),
            (grad_out, out_v),
            (bias, bias_v),
            (logs, log_v),
            (cosine, cosine_v),
            (sine, sine_v),
        ],
        load_sem,
    )
    scatter = Scatter(
        grid, partial, from_across, from_line, total,
        (across_send, across_recv, line_send, line_recv), parts,
    )
    keyed_scatter = Scatter(
        grid, key_partial, None, key_line, key_total, (None, None, key_send, key_recv), parts
    )

    def work(i, carry):
        z = grid.order(line - 1 - i % line)
        slot = grid.slot(jnp.where(i < line, 1 - grid.x, grid.x), z)
        spot = pl.ds(pl.multiple_of(slot * rows, rows), rows)

        def tile(j, inner):
            c = pl.ds(pl.multiple_of(j * cols, cols), cols)
            partial[slot, :, c] = dot(hidden[spot, :], down_w[:, c], NN).astype(BF)
            return inner

        lax.fori_loop(0, width // cols, tile, 0)
        pl.when(i < line)(lambda: scatter.send_across(z))
        return carry

    lax.fori_loop(0, line, work, 0)
    tile = out_w.shape[0] * out_w.shape[1]
    after = weights.shape[2] - width

    def out_step(j, carry):
        units = pl.ds(j * out_w.shape[0], out_w.shape[0])
        load_pairs([(weights.at[units, :, pl.ds(after, width)], out_w)], load_sem)
        c = pl.ds(pl.multiple_of(j * tile, tile), tile)
        grad_v[:, c] = dot(out_v[...], out_w[...].reshape(tile, width), NT).astype(BF)
        return carry

    lax.fori_loop(0, width // tile, out_step, 0)
    lax.fori_loop(line, 2 * line, work, 0)
    deep = 2 * rows
    chunk = rows // 2
    pairs = width // (2 * HEAD_SIZE)
    group = pairs // (narrow // (2 * HEAD_SIZE))

    def pair_step(i, carry):
        c = pl.ds(pl.multiple_of(i * 128, 128), 128)
        half = (i // (group // 2)) % 2
        key_cols = pl.ds(pl.multiple_of((i // group) * 128, 128), 128)
        value_cols = pl.ds(pl.multiple_of((i // group) * 128 + narrow, 128), 128)
        keys = keyed_v[:, :, key_cols].reshape(length, 128)
        values = keyed_v[:, :, value_cols].reshape(length, 128)
        query = halves(query_v[:, c], half)
        grad = halves(grad_v[:, c], half)
        scores[...] = dot(query, keys, NT)
        gradients[...] = dot(grad, values, NT)

        def soft(j, inner):
            here = pl.ds(pl.multiple_of(j * chunk, chunk), chunk)
            there = pl.ds(pl.multiple_of((j * chunk) % rows, chunk), chunk)
            lane = lax.broadcasted_iota(jnp.int32, (chunk, 128), 1)
            log = jnp.sum(jnp.where(lane == i, log_v[here, :], 0.0), axis=1, keepdims=True)
            prob = jnp.exp(scores[here, :] + bias_v[there, :] - log)
            slope = gradients[here, :]
            delta = jnp.sum(prob * slope, axis=1, keepdims=True)
            probs[here, :] = prob.astype(BF)
            slopes[here, :] = (prob * (slope - delta)).astype(BF)
            return inner

        lax.fori_loop(0, deep // chunk, soft, 0)
        back = dot(slopes[...], keys, NN) * HEAD_SIZE ** (-0.5)
        grad_qkv[:, c] = turn(unhalves(back, half), cosine_v, sine_v, 1.0)
        key_part = dot(slopes[...], query, TN)
        value_part = dot(probs[...], grad, TN)

        @pl.when(i % group == 0)
        def _():
            key_sum[...] = key_part
            value_sum[...] = value_part

        @pl.when(i % group != 0)
        def _():
            key_sum[...] += key_part
            value_sum[...] += value_part

        @pl.when(i % group == group - 1)
        def _():
            key_partial[:, :, key_cols] = key_sum[...].astype(BF).reshape(line, rows, 128)
            key_partial[:, :, value_cols] = value_sum[...].astype(BF).reshape(line, rows, 128)

        pl.when(i % pace == 0)(lambda: scatter.step(i // pace + early))
        return carry

    pace = 4
    early = jnp.where(jnp.logical_and(grid.has_left, grid.has_right), 0, 1)
    pl.when(early == 1)(lambda: scatter.step(0))
    lax.fori_loop(0, pairs, pair_step, 0)

    def rest(n, carry):
        scatter.step(n)
        return carry

    lax.fori_loop(pairs // pace + early, scatter.steps(), rest, 0)

    def along(i, carry):
        keyed_scatter.step(i)
        return carry

    lax.fori_loop(0, keyed_scatter.steps(), along, 0)
    scatter.own(branch)
    keyed_scatter.own(grad_keyed)
    grad_qkv[:, width : width + narrow] = turn(grad_keyed[:, :narrow], cosine_v, sine_v, 1.0)
    grad_qkv[:, width + narrow :] = grad_keyed[:, narrow:].astype(BF)
    for copy in mirrored + swapped:
        copy.wait()
    scatter.finish()
    keyed_scatter.finish()


def back_call(
    queries, keyed_all, grad_out, bias, logs, hidden_all, downs, weights, cosine, sine, sums,
    normed, attended, line,
):
    rows, width = queries.shape
    both = keyed_all.shape[2]
    cols, length = downs[0].shape[0], bias.shape[1]
    parts = 2
    shapes = jax.ShapeDtypeStruct
    vmem = pl.BlockSpec(memory_space=pltpu.VMEM)
    return pl.pallas_call(
        functools.partial(back_kernel, line, parts),
        out_shape=(
            shapes((rows, width), F32), shapes((rows, width + both), BF),
            *(shapes(s.shape, BF) for s in sums), *(shapes((rows, width), BF),) * 3,
        ),
        in_specs=[ANY] * 16,
        out_specs=(vmem,) * 2 + (ANY,) * 6,
        scratch_shapes=[
            pltpu.VMEM((rows, width), BF), pltpu.VMEM((4, weights.shape[1], width), BF),
            pltpu.VMEM(cosine.shape, F32), pltpu.VMEM(sine.shape, F32), pltpu.VMEM((rows, both), F32),
            pltpu.SemaphoreType.DMA((6,)), pltpu.SemaphoreType.DMA((6,)),
            pltpu.VMEM((rows, width), BF), pltpu.VMEM(keyed_all.shape, BF), pltpu.VMEM((rows, width), BF),
            pltpu.VMEM((rows, length), F32), pltpu.VMEM(logs.shape, F32),
            pltpu.VMEM((2 * rows, length), F32), pltpu.VMEM((2 * rows, length), F32),
            pltpu.VMEM((2 * rows, length), BF), pltpu.VMEM((2 * rows, length), BF),
            pltpu.VMEM((length, 128), F32), pltpu.VMEM((length, 128), F32),
            pltpu.VMEM((2 * cols, width), BF), pltpu.VMEM(hidden_all.shape, BF),
            pltpu.SemaphoreType.DMA((10,)),
            *scatter_scratch(line, rows, width, parts),
            pltpu.VMEM((line, rows, both), BF), pltpu.VMEM((2 * line - 2, rows, both), BF),
            pltpu.VMEM((rows // parts, both), F32),
            pltpu.SemaphoreType.DMA((line, parts)), pltpu.SemaphoreType.DMA((2 * line - 2, parts)),
        ],
        compiler_params=pltpu.CompilerParams(
            collective_id=6, has_side_effects=True, vmem_limit_bytes=62 * 2**20
        ),
        name="back",
    )(
        queries, keyed_all, grad_out, bias, logs, hidden_all, *downs, weights, cosine, sine, *sums,
        normed, attended,
    )


def body(
    tokens,
    places,
    cotangent,
    gain_attn,
    gain_mlp,
    w_query,
    key_projection,
    value_projection,
    w_out,
    w_gate,
    w_up,
    w_down,
):
    sequence_total, segment_length, width = tokens.shape
    total_length = places.shape[1]
    total_rows = sequence_total * segment_length
    position = lax.axis_index("context")
    local_positions = lax.dynamic_slice_in_dim(places, position * segment_length, segment_length, 1)
    rotary_angles = local_positions.reshape(total_rows).astype(jnp.float32)[:, None] * frequencies(
        HEAD_SIZE // 2
    )
    gain_one, gain_two, query_w, key_weight_local, value_w, out_w = (
        lax.all_gather(gain_attn, ("fsdp", "context"), axis=0, tiled=True),
        lax.all_gather(gain_mlp, ("fsdp", "context"), axis=0, tiled=True),
        lax.all_gather(w_query, ("fsdp", "context"), axis=0, tiled=True),
        lax.all_gather(key_projection, ("fsdp", "context"), axis=0, tiled=True),
        lax.all_gather(value_projection, ("fsdp", "context"), axis=0, tiled=True),
        lax.all_gather(w_out, ("fsdp", "context"), axis=0, tiled=True),
    )
    gain_first = gain_one.astype(jnp.float32)
    gain_second = gain_two.astype(jnp.float32)
    inputs_f = tokens.astype(jnp.float32).reshape(total_rows, width)
    factor_one = lax.rsqrt(jnp.mean(inputs_f * inputs_f, axis=-1, keepdims=True) + norm_eps)
    unit_one = inputs_f * factor_one
    normed_tokens = (unit_one * gain_first).astype(jnp.bfloat16)
    query_pre = jnp.dot(normed_tokens, query_w, preferred_element_type=jnp.float32).reshape(
        total_rows, QUERY_HEADS, HEAD_SIZE
    )
    key_unrotated = jnp.dot(
        normed_tokens, key_weight_local, preferred_element_type=jnp.float32
    ).reshape(total_rows, KEY_VALUE_HEADS, HEAD_SIZE)
    value_matrix_rows = jnp.dot(normed_tokens, value_w, preferred_element_type=jnp.float32).astype(
        jnp.bfloat16
    )
    query_rows = apply_rotary(query_pre, rotary_angles).astype(jnp.bfloat16)
    key_matrix_rows = (
        apply_rotary(key_unrotated, rotary_angles)
        .astype(jnp.bfloat16)
        .reshape(sequence_total, segment_length, KEY_VALUE_HEADS * HEAD_SIZE)
    )
    key_all, value_all = (
        lax.all_gather(key_matrix_rows, "context", axis=1, tiled=True),
        lax.all_gather(
            value_matrix_rows.reshape(sequence_total, segment_length, KEY_VALUE_HEADS * HEAD_SIZE),
            "context",
            axis=1,
            tiled=True,
        ),
    )
    head_query = query_head_rows(query_rows, sequence_total, segment_length)
    head_key = key_heads(key_all, sequence_total, total_length)
    head_value = key_heads(value_all, sequence_total, total_length)
    query_positions = jnp.repeat(local_positions, KEY_VALUE_HEADS, axis=0)
    key_positions = jnp.repeat(places, KEY_VALUE_HEADS, axis=0)
    attended = lax.map(
        forward_head, (head_query, head_key, head_value, query_positions, key_positions)
    )
    attended = merge_queries(attended, sequence_total, segment_length).astype(jnp.bfloat16)
    middle = inputs_f + jnp.dot(attended, out_w, preferred_element_type=jnp.float32)
    factor_two = lax.rsqrt(jnp.mean(middle * middle, axis=-1, keepdims=True) + norm_eps)
    unit_two = middle * factor_two
    normed_mlp = (unit_two * gain_second).astype(jnp.bfloat16)
    tangent = cotangent.reshape(total_rows, width)
    tangent_f = tangent.astype(jnp.float32)
    group = ("fsdp", "context")
    normed_all = lax.all_gather(normed_mlp, group, axis=0, tiled=True)
    tangent_all = lax.all_gather(tangent, group, axis=0, tiled=True)
    branch_part, kept_values = feed_forward(normed_all, w_gate, w_up, w_down)
    grad_part, grad_w_gate, grad_w_up, grad_w_down = feed_back(
        normed_all, tangent_all, w_gate, w_up, w_down, kept_values
    )
    grad_normed = lax.psum_scatter(
        grad_part.astype(jnp.bfloat16), group, scatter_dimension=0, tiled=True
    ).astype(jnp.float32)
    branch = lax.psum_scatter(
        branch_part.astype(jnp.bfloat16), group, scatter_dimension=0, tiled=True
    ).astype(jnp.float32)
    outcome = middle + branch
    scaled_two = grad_normed * gain_second
    term_gain_two = jnp.sum(grad_normed * unit_two, axis=0)
    grad_middle = tangent_f + factor_two * (
        scaled_two - unit_two * jnp.mean(scaled_two * unit_two, axis=-1, keepdims=True)
    )
    grad_branch = grad_middle.astype(jnp.bfloat16)
    term_out = times_t(attended, grad_branch)
    grad_attended = times_nt(grad_branch, out_w).astype(jnp.bfloat16)
    head_grad = query_head_rows(grad_attended, sequence_total, segment_length)
    grad_q, grad_k, grad_v = lax.map(
        backward_head, (head_query, head_key, head_value, head_grad, query_positions, key_positions)
    )
    local_key_gradient, local_value_gradient = (
        lax.psum_scatter(
            merge_keys(grad_k, sequence_total, total_length).astype(jnp.bfloat16),
            "context",
            scatter_dimension=1,
            tiled=True,
        ).astype(jnp.float32),
        lax.psum_scatter(
            merge_keys(grad_v, sequence_total, total_length).astype(jnp.bfloat16),
            "context",
            scatter_dimension=1,
            tiled=True,
        ).astype(jnp.float32),
    )
    grad_query = (
        inverse_rotary(
            merge_queries(grad_q, sequence_total, segment_length).reshape(
                total_rows, QUERY_HEADS, HEAD_SIZE
            ),
            rotary_angles,
        )
        .reshape(total_rows, QUERY_HEADS * HEAD_SIZE)
        .astype(jnp.bfloat16)
    )
    grad_key = (
        inverse_rotary(
            local_key_gradient.reshape(total_rows, KEY_VALUE_HEADS, HEAD_SIZE), rotary_angles
        )
        .reshape(total_rows, KEY_VALUE_HEADS * HEAD_SIZE)
        .astype(jnp.bfloat16)
    )
    value_gradient = local_value_gradient.reshape(total_rows, KEY_VALUE_HEADS * HEAD_SIZE).astype(
        jnp.bfloat16
    )
    grad_normed_one = (
        times_nt(grad_query, query_w)
        + times_nt(grad_key, key_weight_local)
        + times_nt(value_gradient, value_w)
    )
    term_query = times_t(normed_tokens, grad_query)
    term_key = times_t(normed_tokens, grad_key)
    term_value = times_t(normed_tokens, value_gradient)
    scaled_one = grad_normed_one * gain_first
    term_gain_one = jnp.sum(grad_normed_one * unit_one, axis=0)
    grad_inputs = grad_middle + factor_one * (
        scaled_one - unit_one * jnp.mean(scaled_one * unit_one, axis=-1, keepdims=True)
    )
    share_query, share_key, share_value, share_out, share_gain_one, share_gain_two = (
        lax.psum_scatter(term_query.astype(jnp.bfloat16), ("fsdp", "context"), scatter_dimension=0, tiled=True),
        lax.psum_scatter(term_key.astype(jnp.bfloat16), ("fsdp", "context"), scatter_dimension=0, tiled=True),
        lax.psum_scatter(term_value.astype(jnp.bfloat16), ("fsdp", "context"), scatter_dimension=0, tiled=True),
        lax.psum_scatter(term_out.astype(jnp.bfloat16), ("fsdp", "context"), scatter_dimension=0, tiled=True),
        lax.psum_scatter(term_gain_one, ("fsdp", "context"), scatter_dimension=0, tiled=True),
        lax.psum_scatter(term_gain_two, ("fsdp", "context"), scatter_dimension=0, tiled=True),
    )
    summed = (
        lax.psum(share_query.astype(jnp.bfloat16), "replica").astype(jnp.float32),
        lax.psum(share_key.astype(jnp.bfloat16), "replica").astype(jnp.float32),
        lax.psum(share_value.astype(jnp.bfloat16), "replica").astype(jnp.float32),
        lax.psum(share_out.astype(jnp.bfloat16), "replica").astype(jnp.float32),
        lax.psum(grad_w_gate.astype(jnp.bfloat16), "replica").astype(jnp.float32),
        lax.psum(grad_w_up.astype(jnp.bfloat16), "replica").astype(jnp.float32),
        lax.psum(grad_w_down.astype(jnp.bfloat16), "replica").astype(jnp.float32),
        lax.psum(share_gain_one.astype(jnp.bfloat16), "replica").astype(jnp.float32),
        lax.psum(share_gain_two.astype(jnp.bfloat16), "replica").astype(jnp.float32),
    )
    out = outcome.astype(jnp.bfloat16).reshape(sequence_total, segment_length, width)
    grad_tokens = grad_inputs.astype(jnp.bfloat16).reshape(sequence_total, segment_length, width)
    return (
        out,
        grad_tokens,
        summed[0],
        summed[1],
        summed[2],
        summed[3],
        summed[4],
        summed[5],
        summed[6],
        summed[7],
        summed[8],
    )


def kernel_body(
    tokens,
    places,
    cotangent,
    gain_attn,
    gain_mlp,
    w_query,
    key_projection,
    value_projection,
    w_out,
    w_gate,
    w_up,
    w_down,
):
    bf16, f32 = jnp.bfloat16, jnp.float32
    sequence_total, segment_length, width = tokens.shape
    total_length = places.shape[1]
    line = lax.axis_size("context")
    narrow = key_projection.shape[1]
    run = w_query.shape[0]
    swap = [(i, i ^ 1) for i in range(lax.axis_size("fsdp"))]
    gates, ups, downs = ((w, lax.ppermute(w, "fsdp", swap)) for w in (w_gate, w_up, w_down))
    position = lax.axis_index("context")
    local_positions = lax.dynamic_slice_in_dim(places, position * segment_length, segment_length, 1)
    rotary_angles = local_positions.reshape(segment_length).astype(f32)[:, None] * frequencies(
        HEAD_SIZE // 2
    )
    extra = jnp.pad(jnp.stack([gain_attn, gain_mlp]), ((0, run - 2), (0, 0)))
    pieces = (w_query, key_projection, value_projection, extra, w_out)
    cosine, sine = jnp.cos(rotary_angles), jnp.sin(rotary_angles)
    cosine = jnp.concatenate([cosine] * 4, axis=1)
    sine = jnp.concatenate([-sine, sine] * 2, axis=1)
    allowed = places.reshape(1, total_length) <= local_positions.reshape(segment_length, 1)
    bias = jnp.where(allowed, 0.0, -1e30).astype(f32)
    tangent = cotangent.reshape(segment_length, width)
    tangent_f = tangent.astype(f32)
    rows = tokens.reshape(segment_length, width)
    (
        attended, middle, normed_mlp, normed_tokens, scaled_query, logs, keyed_all, tangent_all, weights,
    ) = front_call(pieces, rows, tangent, bias, cosine, sine, line)
    mid = width + 2 * narrow
    gain_first = weights[:, 0, mid : mid + run].reshape(width).astype(f32)
    gain_second = weights[:, 1, mid : mid + run].reshape(width).astype(f32)
    grad_normed, _, hidden_all, *sums = feed_call(normed_mlp, tangent_all, gates, ups, downs, line)[:6]
    factor_two = lax.rsqrt(jnp.mean(middle * middle, axis=-1, keepdims=True) + norm_eps)
    unit_two = middle * factor_two
    scaled_two = grad_normed * gain_second
    term_gain_two = jnp.sum(grad_normed * unit_two, axis=0)
    grad_middle = tangent_f + factor_two * (
        scaled_two - unit_two * jnp.mean(scaled_two * unit_two, axis=-1, keepdims=True)
    )
    grad_branch = grad_middle.astype(bf16)
    branch, grad_qkv, *others = back_call(
        scaled_query, keyed_all, grad_branch, bias, logs, hidden_all, downs, weights, cosine, -sine,
        sums, normed_tokens, attended, line,
    )
    outcome = middle + branch
    grad_w_gate, grad_w_up, grad_w_down = (
        a.astype(f32) + b.astype(f32) for a, b in zip(sums, others[:3])
    )
    packed, grad_tokens = sums_call(
        normed_tokens, attended, grad_qkv, grad_branch, others[3:], rows, grad_middle, weights,
        gain_first.reshape(1, width), term_gain_two.reshape(1, width), line,
    )
    gains = packed[run * 3 // 4 : run * 3 // 4 + 2, mid + width :]
    ends, start = [], 0
    for size in (width, narrow, narrow, width):
        ends.append(packed[:, start : start + size])
        start += size
    return (
        outcome.astype(bf16).reshape(tokens.shape),
        grad_tokens.reshape(tokens.shape),
        *ends,
        grad_w_gate,
        grad_w_up,
        grad_w_down,
        gains[0],
        gains[1],
    )


def solution(mesh):
    placed = (
        P(("replica", "fsdp"), "context", None),
        P(("replica", "fsdp"), None),
        P(("replica", "fsdp"), "context", None),
        P(("fsdp", "context")),
        P(("fsdp", "context")),
        P(("fsdp", "context"), None),
        P(("fsdp", "context"), None),
        P(("fsdp", "context"), None),
        P(("fsdp", "context"), None),
        P(None, ("fsdp", "context")),
        P(None, ("fsdp", "context")),
        P(("fsdp", "context"), None),
    )
    kernels = (mesh.shape["replica"], mesh.shape["fsdp"], mesh.shape["context"]) == (2, 4, 4)
    return jax.shard_map(
        kernel_body if kernels else body,
        mesh=mesh,
        in_specs=placed,
        out_specs=(
            P(("replica", "fsdp"), "context", None),
            P(("replica", "fsdp"), "context", None),
            P(("fsdp", "context"), None),
            P(("fsdp", "context"), None),
            P(("fsdp", "context"), None),
            P(("fsdp", "context"), None),
            P(None, ("fsdp", "context")),
            P(None, ("fsdp", "context")),
            P(("fsdp", "context"), None),
            P(("fsdp", "context")),
            P(("fsdp", "context")),
        ),
        check_vma=False,
    )
```

```python
import functools

import jax
import jax.numpy as jnp
from jax import lax
from jax.experimental import pallas as pl
from jax.experimental.pallas import tpu as pltpu
from jax.sharding import PartitionSpec as P

QUERY_HEADS = 32
KEY_VALUE_HEADS = 8
HEAD_SIZE = 64


norm_eps = 1e-05
rope_base = 500000.0


def frequencies(half):
    return rope_base ** (-2.0 * jnp.arange(half, dtype=jnp.float32) / (2.0 * half))


def apply_rotary(angle_table, rotary_angles):
    half = angle_table.shape[-1] // 2
    first_half = angle_table[..., :half]
    second_half = angle_table[..., half:]
    cosine = jnp.cos(rotary_angles)[..., None, :]
    sine = jnp.sin(rotary_angles)[..., None, :]
    return jnp.concatenate(
        [first_half * cosine - second_half * sine, second_half * cosine + first_half * sine],
        axis=-1,
    )


def inverse_rotary(angle_table, rotary_angles):
    half = angle_table.shape[-1] // 2
    first_half = angle_table[..., :half]
    second_half = angle_table[..., half:]
    cosine = jnp.cos(rotary_angles)[..., None, :]
    sine = jnp.sin(rotary_angles)[..., None, :]
    return jnp.concatenate(
        [first_half * cosine + second_half * sine, second_half * cosine - first_half * sine],
        axis=-1,
    )


def times_t(left, right):
    return lax.dot_general(
        left, right, (((0,), (0,)), ((), ())), preferred_element_type=jnp.float32
    )


def times_nt(left, right):
    return lax.dot_general(
        left, right, (((1,), (1,)), ((), ())), preferred_element_type=jnp.float32
    )


def query_head_rows(angle_table, sequence_total, segment_length):
    reshaped_heads = angle_table.reshape(
        sequence_total, segment_length, KEY_VALUE_HEADS, QUERY_HEADS // KEY_VALUE_HEADS, HEAD_SIZE
    )
    return jnp.transpose(reshaped_heads, (0, 2, 1, 3, 4)).reshape(
        sequence_total * KEY_VALUE_HEADS, segment_length, QUERY_HEADS // KEY_VALUE_HEADS, HEAD_SIZE
    )


def key_heads(angle_table, sequence_total, total_length):
    reshaped_heads = angle_table.reshape(sequence_total, total_length, KEY_VALUE_HEADS, HEAD_SIZE)
    return jnp.transpose(reshaped_heads, (0, 2, 1, 3)).reshape(
        sequence_total * KEY_VALUE_HEADS, total_length, HEAD_SIZE
    )


def merge_queries(angle_table, sequence_total, segment_length):
    reshaped_heads = angle_table.reshape(
        sequence_total, KEY_VALUE_HEADS, segment_length, QUERY_HEADS // KEY_VALUE_HEADS, HEAD_SIZE
    )
    return jnp.transpose(reshaped_heads, (0, 2, 1, 3, 4)).reshape(
        sequence_total * segment_length, QUERY_HEADS * HEAD_SIZE
    )


def merge_keys(angle_table, sequence_total, total_length):
    reshaped_heads = angle_table.reshape(sequence_total, KEY_VALUE_HEADS, total_length, HEAD_SIZE)
    return jnp.transpose(reshaped_heads, (0, 2, 1, 3)).reshape(
        sequence_total, total_length, KEY_VALUE_HEADS * HEAD_SIZE
    )


def softmax_weights(part_query, part_key, place_query, place_key):
    allowed = place_key[None, :] <= place_query[:, None]
    scores = jnp.einsum(
        "qrd,kd->rqk", part_query, part_key, preferred_element_type=jnp.float32
    ) * HEAD_SIZE ** (-0.5)
    scores = jnp.where(allowed[None], scores, -1e30)
    return jax.nn.softmax(scores, axis=-1)


def forward_head(packed):
    part_query, part_key, part_value, place_query, place_key = packed
    probs = softmax_weights(part_query, part_key, place_query, place_key)
    return jnp.einsum(
        "rqk,kd->qrd", probs.astype(jnp.bfloat16), part_value, preferred_element_type=jnp.float32
    )


def backward_head(packed):
    part_query, part_key, part_value, part_grad, place_query, place_key = packed
    probs = softmax_weights(part_query, part_key, place_query, place_key)
    grad_probs = jnp.einsum(
        "qrd,kd->rqk", part_grad, part_value, preferred_element_type=jnp.float32
    )
    row_delta = jnp.sum(probs * grad_probs, axis=-1, keepdims=True)
    grad_scores = (probs * (grad_probs - row_delta)).astype(jnp.bfloat16)
    grad_query = jnp.einsum(
        "rqk,kd->qrd", grad_scores, part_key, preferred_element_type=jnp.float32
    ) * HEAD_SIZE ** (-0.5)
    grad_key = jnp.einsum(
        "rqk,qrd->kd", grad_scores, part_query, preferred_element_type=jnp.float32
    ) * HEAD_SIZE ** (-0.5)
    value_gradient = jnp.einsum(
        "rqk,qrd->kd", probs.astype(jnp.bfloat16), part_grad, preferred_element_type=jnp.float32
    )
    return (grad_query, grad_key, value_gradient)


def feed_forward(normed_rows, gate_w, up_w, down_w):
    gate_pre = jnp.dot(normed_rows, gate_w, preferred_element_type=jnp.float32)
    up_proj = jnp.dot(normed_rows, up_w, preferred_element_type=jnp.float32)
    sigmoid_gate = jax.nn.sigmoid(gate_pre)
    hidden = (gate_pre * sigmoid_gate * up_proj).astype(jnp.bfloat16)
    return (
        jnp.dot(hidden, down_w, preferred_element_type=jnp.float32),
        (gate_pre, up_proj, sigmoid_gate, hidden),
    )


def feed_back(normed_rows, grad_rows, gate_w, up_w, down_w, kept_values):
    gate_pre, up_proj, sigmoid_gate, hidden = kept_values
    grad_hidden = times_nt(grad_rows, down_w)
    term_down = times_t(hidden, grad_rows)
    grad_gate = (
        grad_hidden * up_proj * (sigmoid_gate * (1.0 + gate_pre * (1.0 - sigmoid_gate)))
    ).astype(jnp.bfloat16)
    grad_up = (grad_hidden * (gate_pre * sigmoid_gate)).astype(jnp.bfloat16)
    grad_normed = times_nt(grad_gate, gate_w) + times_nt(grad_up, up_w)
    return (grad_normed, times_t(normed_rows, grad_gate), times_t(normed_rows, grad_up), term_down)


MESH = pl.DeviceIdType.MESH
ANY = pl.BlockSpec(memory_space=pl.ANY)
BF = jnp.bfloat16
F32 = jnp.float32
NN = (((1,), (0,)), ((), ()))
NT = (((1,), (1,)), ((), ()))
TN = (((0,), (0,)), ((), ()))


EARLY = 3


def dot(left, right, dims):
    return lax.dot_general(left, right, dims, preferred_element_type=F32)


class Grid:
    def __init__(self, chips, line):
        self.chips, self.line = chips, line
        self.replica = lax.axis_index("replica")
        flat = lax.axis_index("fsdp")
        self.x, self.core = flat // 2, flat % 2
        self.z = lax.axis_index("context")
        self.has_left, self.has_right = self.z > 0, self.z + 1 < line
        self.left = (self.replica, flat, self.z - 1)
        self.right = (self.replica, flat, self.z + 1)
        self.across = (self.replica, (1 - self.x) * 2 + self.core, self.z)
        self.twin = (self.replica, self.x * 2 + 1 - self.core, self.z)
        self.mirror = (1 - self.replica, flat, self.z)

    def order(self, k):
        z, n = self.z, self.line
        low = 2 * z < n
        near = 2 * jnp.minimum(z, n - 1 - z)
        away = jnp.where(k % 2 == 1, -((k + 1) // 2), k // 2)
        return jnp.where(
            k <= near, z + jnp.where(low, away, -away), jnp.where(low, k, n - 1 - k)
        )

    def slot(self, x, z):
        return x * self.line + z

    def greet(self, twin, mirror=False):
        barrier = pltpu.get_barrier_semaphore()

        def tell(device):
            pl.semaphore_signal(barrier, inc=1, device_id=device, device_id_type=MESH)

        pl.when(self.has_left)(lambda: tell(self.left))
        pl.when(self.has_right)(lambda: tell(self.right))
        tell(self.across)
        if twin:
            tell(self.twin)
        if mirror:
            tell(self.mirror)
        count = 1 + int(twin) + int(mirror) + self.has_left.astype(jnp.int32) + self.has_right.astype(jnp.int32)
        pl.semaphore_wait(barrier, count)


def remote(src, dst, send, recv, device):
    return pltpu.make_async_remote_copy(
        src_ref=src, dst_ref=dst, send_sem=send, recv_sem=recv, device_id=device, device_id_type=MESH
    )


def each(count, action):
    def step(i, carry):
        action(i)
        return carry

    lax.fori_loop(0, count, step, 0)


class Gather:
    def __init__(self, grid, block, everything, send, recv, parts, cross=None):
        self.grid, self.everything, self.send, self.recv = grid, everything, send, recv
        self.block, self.cross = block, cross
        self.rows = everything.shape[1] // parts
        self.last = parts - 1
        self.early = parts if cross is None else parts - 1

    def piece(self, x, z, part):
        start = pl.multiple_of(part * self.rows, self.rows)
        return self.everything.at[self.grid.slot(x, z), pl.ds(start, self.rows)]

    def copy(self, z, part, link, first=False):
        grid = self.grid
        device = (grid.right, grid.left, grid.across)[link]
        there = self.piece(grid.x, z, part)
        start = pl.multiple_of(part * self.rows, self.rows)
        here = self.block.at[pl.ds(start, self.rows)] if first else there
        return remote(
            here, there, self.send.at[z, part, link], self.recv.at[grid.slot(grid.x, z), part], device
        )

    def other(self, z, link):
        grid = self.grid
        here = self.piece(1 - grid.x, z, self.last)
        sem = self.recv.at[grid.slot(1 - grid.x, z), self.last]
        return remote(here, here, self.cross.at[z, link], sem, (grid.right, grid.left)[link])

    def ways(self, z):
        grid = self.grid
        return (
            (0, jnp.logical_and(z <= grid.z, grid.has_right)),
            (1, jnp.logical_and(z >= grid.z, grid.has_left)),
        )

    def sides(self, distance):
        grid = self.grid
        return (
            (grid.z - distance, grid.z >= distance, 0, grid.has_right),
            (grid.z + distance, grid.z + distance < grid.line, 1, grid.has_left),
        )

    def links(self, z, part, action, first=False, across=True):
        for link, go in self.ways(z):
            pl.when(go)(lambda link=link: action(self.copy(z, part, link, first)))
        if across:
            action(self.copy(z, part, 2, first))

    def send_own(self):
        grid = self.grid
        start = lambda c: c.start()
        if self.cross is not None:
            self.copy(grid.z, self.last, 2, True).start()
        each(self.early, lambda part: self.links(grid.z, part, start, True))
        if self.cross is not None:
            self.links(grid.z, self.last, start, True, False)

    def turn_in(self):
        grid = self.grid
        self.other(grid.z, 0).wait_recv()
        for link, go in self.ways(grid.z):
            pl.when(go)(lambda link=link: self.other(grid.z, link).start())

    def forward(self, distance, part, wait=True, along=True, across=True):
        for z, there, link, go in self.sides(distance):

            @pl.when(there)
            def _(z=z, link=link, go=go):
                if wait:
                    self.copy(z, part, 2).wait_recv()
                if along:
                    pl.when(go)(lambda: self.copy(z, part, link).start())
                if across:
                    self.copy(z, part, 2).start()

    def forward_last(self, distance):
        for z, there, link, go in self.sides(distance):

            @pl.when(there)
            def _(z=z, link=link, go=go):
                self.copy(z, self.last, 2).wait_recv()
                pl.when(go)(lambda: self.copy(z, self.last, link).start())
                self.other(z, link).wait_recv()
                pl.when(go)(lambda: self.other(z, link).start())

    def wait_across(self, z):
        grid = self.grid

        def wait(part):
            here = self.piece(1 - grid.x, z, part)
            sem = self.recv.at[grid.slot(1 - grid.x, z), part]
            remote(here, here, self.send.at[z, part, 2], sem, grid.across).wait_recv()

        each(self.early, wait)

    def finish(self):
        done = lambda c: c.wait_send()

        def place(z):
            each(self.early, lambda part: self.links(z, part, done))
            if self.cross is not None:
                self.links(z, self.last, done, across=False)
                for link, go in self.ways(z):
                    pl.when(go)(lambda link=link: self.other(z, link).wait_send())

        each(self.grid.line, place)
        if self.cross is not None:
            self.copy(self.grid.z, self.last, 2).wait_send()


class Scatter:
    def __init__(self, grid, partial, from_across, from_line, total, sems, parts, cross=None):
        self.grid, self.partial, self.from_across = grid, partial, from_across
        self.from_line, self.total = from_line, total
        self.across_send, self.across_recv, self.line_send, self.line_recv = sems
        self.parts, self.cross = parts, cross
        self.rows = partial.shape[1] // parts
        self.early = parts if cross is None else parts - 1
        self.last = parts - 1

    def run(self, part):
        return pl.ds(pl.multiple_of(part * self.rows, self.rows), self.rows)

    def steps(self):
        return (self.grid.line - 1) * self.early

    def rank(self, j):
        return self.grid.order(self.grid.line - 1 - j)

    def step(self, n):
        self.pass_on(self.rank(n // self.early), n % self.early)

    def place(self, z):
        return z if self.from_across is None else self.grid.slot(self.grid.x, z)

    def across(self, z, part):
        grid = self.grid
        return remote(
            self.partial.at[grid.slot(1 - grid.x, z), self.run(part)],
            self.from_across.at[z, self.run(part)],
            self.across_send.at[z, part],
            self.across_recv.at[z, part],
            grid.across,
        )

    def arrival(self, z, leftward):
        return z if leftward else z - 1 + self.grid.line - 1

    def along(self, z, part, leftward):
        grid = self.grid
        arrival = self.arrival(z, leftward)
        return remote(
            self.partial.at[self.place(z), self.run(part)],
            self.from_line.at[arrival, self.run(part)],
            self.line_send.at[z, part],
            self.line_recv.at[arrival, part],
            grid.left if leftward else grid.right,
        )

    def other(self, z, leftward):
        grid = self.grid
        buffer, send, recv = self.cross
        arrival = self.arrival(z, leftward)
        return remote(
            self.partial.at[grid.slot(1 - grid.x, z), self.run(self.last)],
            buffer.at[arrival],
            send.at[z],
            recv.at[arrival],
            grid.left if leftward else grid.right,
        )

    def send_across(self, z):
        each(self.early, lambda part: self.across(z, part).start())

    def both_ways(self, z, action):
        grid = self.grid
        pl.when(jnp.logical_and(z <= grid.z, grid.has_right))(lambda: action(True))
        pl.when(jnp.logical_and(z >= grid.z, grid.has_left))(lambda: action(False))

    def add_line(self, z, part):
        def add(leftward):
            self.along(z, part, leftward).wait_recv()
            arrival = self.arrival(z, leftward)
            self.total[...] += self.from_line[arrival, self.run(part)].astype(F32)

        self.both_ways(z, add)

    def gather_sum(self, z, part):
        value = self.partial[self.place(z), self.run(part)].astype(F32)
        if self.from_across is not None:
            self.across(z, part).wait_recv()
            value = value + self.from_across[z, self.run(part)].astype(F32)
        self.total[...] = value
        self.add_line(z, part)

    def send_along(self, z, part):
        grid = self.grid
        self.partial[self.place(z), self.run(part)] = self.total[...].astype(BF)
        pl.when(z < grid.z)(lambda: self.along(z, part, True).start())
        pl.when(z > grid.z)(lambda: self.along(z, part, False).start())

    def pass_on(self, z, part):
        self.gather_sum(z, part)
        self.send_along(z, part)

    def add_other(self, z):
        grid, run = self.grid, self.run(self.last)
        slot = grid.slot(1 - grid.x, z)
        self.total[...] = self.partial[slot, run].astype(F32)

        def add(leftward):
            self.other(z, leftward).wait_recv()
            self.total[...] += self.cross[0][self.arrival(z, leftward)].astype(F32)

        self.both_ways(z, add)
        self.partial[slot, run] = self.total[...].astype(BF)

    def last_step(self, m):
        grid = self.grid
        z = grid.order(grid.line - 1 - m)
        self.add_other(z)

        @pl.when(z == grid.z)
        def _():
            self.across(z, self.last).start()

        @pl.when(z != grid.z)
        def _():
            pl.when(z < grid.z)(lambda: self.other(z, True).start())
            pl.when(z > grid.z)(lambda: self.other(z, False).start())
            self.total[...] = self.partial[self.place(z), self.run(self.last)].astype(F32)
            self.add_line(z, self.last)
            self.send_along(z, self.last)

    def own(self, result):
        def part_sum(part):
            self.gather_sum(self.grid.z, part)
            result[self.run(part)] = self.total[...]

        each(self.parts, part_sum)

    def finish(self):
        grid = self.grid

        def place(z):
            def part_done(part):
                pl.when(z < grid.z)(lambda: self.along(z, part, True).wait_send())
                pl.when(z > grid.z)(lambda: self.along(z, part, False).wait_send())

            each(self.parts, part_done)
            if self.from_across is not None:
                each(self.early, lambda part: self.across(z, part).wait_send())
            if self.cross is not None:
                pl.when(z < grid.z)(lambda: self.other(z, True).wait_send())
                pl.when(z > grid.z)(lambda: self.other(z, False).wait_send())

        each(grid.line, place)
        if self.cross is not None:
            self.across(grid.z, self.last).wait_send()


def scatter_scratch(line, rows, width, parts):
    return [
        pltpu.VMEM((2 * line, rows, width), BF),
        pltpu.VMEM((line, rows, width), BF),
        pltpu.VMEM((2 * line - 2, rows, width), BF),
        pltpu.VMEM((rows // parts, width), F32),
        pltpu.SemaphoreType.DMA((line, parts)),
        pltpu.SemaphoreType.DMA((line, parts)),
        pltpu.SemaphoreType.DMA((line, parts)),
        pltpu.SemaphoreType.DMA((2 * line - 2, parts)),
    ]


def load_pairs(pairs, sems):
    copies = [pltpu.make_async_copy(src, dst, sems.at[i]) for i, (src, dst) in enumerate(pairs)]
    for copy in copies:
        copy.start()
    for copy in copies:
        copy.wait()


def feed_kernel(
    line, parts, tile,
    normed, tangent_all, gate_own, gate_twin, up_own, up_twin, down_own, down_twin,
    grad_sum, normed_all, hidden_all, grad_gate, grad_up, grad_down,
    mirror_gate, mirror_up, mirror_down, part_gate, part_up, part_down,
    mirror_send, mirror_recv,
    gate_w, up_w, down_w, hidden, dgate, dup, rows_n, rows_t,
    partial, from_across, from_line, total, across_send, across_recv, line_send, line_recv,
    other_line, other_send, other_recv, gather_cross,
    gather_send, gather_recv, load_sem, wide, tile_sem, stage_a, stage_b, stage_sem, stage_recv, piece_a, piece_b, piece_sem, hidden_sem,
):
    grid = Grid(2, line)
    rows, width = normed.shape
    cols = gate_own.shape[1]
    blocks = 2 * line
    me = grid.slot(grid.x, grid.z)
    grid.greet(True, True)
    gather = Gather(grid, normed, normed_all, gather_send, gather_recv, parts, gather_cross)
    scatter = Scatter(
        grid, partial, from_across, from_line, total,
        (across_send, across_recv, line_send, line_recv), parts,
        (other_line, other_send, other_recv),
    )
    gather.send_own()
    load_pairs(
        [
            (gate_own, gate_w.at[:, pl.ds(0, cols)]),
            (gate_twin, gate_w.at[:, pl.ds(cols, cols)]),
            (up_own, up_w.at[:, pl.ds(0, cols)]),
            (up_twin, up_w.at[:, pl.ds(cols, cols)]),
            (down_own, down_w.at[pl.ds(0, cols)]),
            (down_twin, down_w.at[pl.ds(cols, cols)]),
            (normed, rows_n),
        ],
        load_sem,
    )
    load_pairs([(rows_n, normed_all.at[me])], load_sem)
    gather.turn_in()

    forwards = (line - 1) * parts

    def advance(n):
        distance, part = n // parts + 1, n % parts

        @pl.when(n < forwards)
        def _():
            pl.when(part < gather.early)(lambda: gather.forward(distance, part))
            pl.when(part == gather.last)(lambda: gather.forward_last(distance))

        return n + 1

    def work(slot, n):
        tangent_load = pltpu.make_async_copy(tangent_all.at[slot], rows_t, load_sem.at[1])
        tangent_load.start()
        load_pairs([(normed_all.at[slot], rows_n)], load_sem)
        spot = pl.ds(pl.multiple_of(slot * rows, rows), rows)

        def hidden_tile(j, n):
            c = pl.ds(pl.multiple_of(j * cols, cols), cols)
            gate = dot(rows_n[...], gate_w[:, c], NN)
            up = dot(rows_n[...], up_w[:, c], NN)
            pl.when(j == 0)(tangent_load.wait)
            grad = dot(rows_t[...], down_w[c, :], NT)
            sig = jax.nn.sigmoid(gate)
            silu = gate * sig
            hidden[spot, c] = (silu * up).astype(BF)
            dgate[spot, c] = (grad * up * (sig * (1.0 + gate * (1.0 - sig)))).astype(BF)
            dup[spot, c] = (grad * silu).astype(BF)
            return advance(n)

        n = lax.fori_loop(0, 2, hidden_tile, n)

        def back_tile(j, carry):
            c = pl.ds(pl.multiple_of(j * cols, cols), cols)
            sums = dot(dgate[spot, :], gate_w[c, :], NT) + dot(dup[spot, :], up_w[c, :], NT)
            partial[slot, :, c] = sums.astype(BF)
            return carry

        lax.fori_loop(0, width // cols, back_tile, 0)
        return advance(n)

    def stage(distance, n):
        def visit(i, n):
            z = grid.z + jnp.where(i % 2 == 0, -distance, distance)
            inside = jnp.logical_and(z >= 0, z < line)

            def block(n):
                n = lax.fori_loop(n, jnp.maximum(n, distance * parts), lambda m, c: advance(m), n)
                pl.when(i >= 2)(lambda: gather.wait_across(z))
                return work(grid.slot(jnp.where(i < 2, grid.x, 1 - grid.x), z), n)

            go = jnp.logical_and(inside, jnp.logical_or(distance > 0, i % 2 == 0))
            return lax.cond(go, block, lambda n: n, n)

        return lax.fori_loop(0, 4, visit, n)

    count = lax.fori_loop(0, line, stage, 0)
    lax.fori_loop(count, jnp.maximum(count, forwards), lambda m, c: advance(m), 0)
    hidden_copy = pltpu.make_async_copy(hidden, hidden_all, hidden_sem)
    hidden_copy.start()
    for j in range(line):
        scatter.send_across(scatter.rank(j))

    tiles = width // tile

    early_tiles = mirror_send.shape[0]

    def wide_loads(t, start):
        j, buf = t % tiles, t % 2
        c = pl.ds(pl.multiple_of(j * tile, tile), tile)
        for i, source in enumerate((normed_all, tangent_all)):
            copy = pltpu.make_async_copy(source.at[:, :, c], wide.at[buf, i], tile_sem.at[buf, i])
            copy.start() if start else copy.wait()

    def stages(t):
        j, buf = t % tiles, t % 2
        c = pl.ds(pl.multiple_of(j * tile, tile), tile)
        return [
            remote(src, dst, stage_sem.at[buf, i], stage_recv.at[j, i], grid.twin)
            for i, (src, dst) in enumerate(
                (
                    (stage_a.at[buf, 0], part_gate.at[c, :]),
                    (stage_a.at[buf, 1], part_up.at[c, :]),
                    (stage_b.at[buf], part_down.at[:, c]),
                )
            )
        ]

    def results(t):
        j, buf = t % tiles, t % 2
        c = pl.ds(pl.multiple_of(j * tile, tile), tile)
        return [
            pltpu.make_async_copy(src, dst, stage_sem.at[buf, i])
            for i, (src, dst) in enumerate(
                (
                    (stage_a.at[buf, 0], grad_gate.at[c, :]),
                    (stage_a.at[buf, 1], grad_up.at[c, :]),
                    (stage_b.at[buf], grad_down.at[:, c]),
                )
            )
        ]

    def mirrored(t):
        j = t % tiles
        c = pl.ds(pl.multiple_of(j * tile, tile), tile)
        return [
            remote(src, dst, mirror_send.at[j, i], mirror_recv.at[j, i], grid.mirror)
            for i, (src, dst) in enumerate(
                (
                    (grad_gate.at[c, :], mirror_gate.at[c, :]),
                    (grad_up.at[c, :], mirror_up.at[c, :]),
                    (grad_down.at[:, c], mirror_down.at[:, c]),
                )
            )
        ]

    def pieces(t):
        c = pl.ds(pl.multiple_of((t % tiles) * tile, tile), tile)
        return [
            (part_gate.at[c, :], piece_a.at[0]),
            (part_up.at[c, :], piece_a.at[1]),
            (part_down.at[:, c], piece_b),
        ]

    wide_loads(0, True)

    def weights(t, carry):
        buf = t % 2
        pl.when(t + 1 < 2 * tiles)(lambda: wide_loads(t + 1, True))
        wide_loads(t, False)
        tall = blocks * rows
        tokens = wide[buf, 0].reshape(tall, tile)
        tangents = wide[buf, 1].reshape(tall, tile)

        @pl.when(t < tiles)
        def _():
            theirs = slice(cols, 2 * cols)

            @pl.when(t >= 2)
            def _():
                for copy in stages(t - 2):
                    copy.wait_send()

            stage_a[buf, 0] = dot(tokens, dgate[:, theirs], TN).astype(BF)
            stage_a[buf, 1] = dot(tokens, dup[:, theirs], TN).astype(BF)
            stage_b[buf] = dot(hidden[:, theirs], tangents, TN).astype(BF)
            for copy in stages(t):
                copy.start()

        @pl.when(t >= tiles)
        def _():
            for copy in stages(t):
                copy.wait_recv()
            loads = [
                pltpu.make_async_copy(src, dst, piece_sem.at[i])
                for i, (src, dst) in enumerate(pieces(t))
            ]
            for copy in loads:
                copy.start()

            @pl.when(t < tiles + 2)
            def _():
                for copy in stages(t - 2):
                    copy.wait_send()

            @pl.when(t >= tiles + 2)
            def _():
                for copy in results(t - 2):
                    copy.wait()

                @pl.when(t < tiles + 2 + early_tiles)
                def _():
                    for copy in mirrored(t - 2):
                        copy.start()

            mine = slice(0, cols)
            own_gate = dot(tokens, dgate[:, mine], TN)
            own_up = dot(tokens, dup[:, mine], TN)
            own_down = dot(hidden[:, mine], tangents, TN)
            for copy in loads:
                copy.wait()
            stage_a[buf, 0] = (own_gate + piece_a[0].astype(F32)).astype(BF)
            stage_a[buf, 1] = (own_up + piece_a[1].astype(F32)).astype(BF)
            stage_b[buf] = (own_down + piece_b[...].astype(F32)).astype(BF)
            for copy in results(t):
                copy.start()

        n = t - 2 * lag
        pl.when(n >= 0)(lambda: scatter.step(n))
        m = t // 3 - lag
        ready = jnp.logical_and(t % 3 == 2, jnp.logical_and(m >= 0, m < line))
        pl.when(ready)(lambda: scatter.last_step(m))
        return carry

    lag = jnp.where(jnp.logical_and(grid.has_left, grid.has_right), 1, 0)
    lax.fori_loop(0, 2 * tiles, weights, 0)

    def rest(n, carry):
        scatter.step(n)
        return carry

    lax.fori_loop(2 * tiles - 2 * lag, scatter.steps(), rest, 0)
    scatter.own(grad_sum)
    for t in (2 * tiles - 2, 2 * tiles - 1):
        for copy in results(t):
            copy.wait()
    gather.finish()
    scatter.finish()
    hidden_copy.wait()
    for t in range(early_tiles):
        for copy in mirrored(t):
            copy.wait()


def feed_call(normed, tangent_all, gates, ups, downs, line):
    rows, width = normed.shape
    cols = gates[0].shape[1]
    blocks, parts, tile = 2 * line, 8, 256
    tiles = width // tile
    tall = blocks * rows
    shapes = jax.ShapeDtypeStruct
    hbm = lambda *s: shapes(s, BF)
    return pl.pallas_call(
        functools.partial(feed_kernel, line, parts, tile),
        out_shape=(
            shapes((rows, width), F32),
            hbm(blocks, rows, width), hbm(tall, 2 * cols),
            hbm(width, cols), hbm(width, cols), hbm(cols, width),
            hbm(width, cols), hbm(width, cols), hbm(cols, width),
            hbm(width, cols), hbm(width, cols), hbm(cols, width),
        ),
        in_specs=[ANY] * 8,
        out_specs=(pl.BlockSpec(memory_space=pltpu.VMEM),) + (ANY,) * 11,
        scratch_shapes=[
            pltpu.SemaphoreType.DMA((EARLY, 3)), pltpu.SemaphoreType.DMA((EARLY, 3)),
            pltpu.VMEM((width, 2 * cols), BF), pltpu.VMEM((width, 2 * cols), BF), pltpu.VMEM((2 * cols, width), BF),
            pltpu.VMEM((tall, 2 * cols), BF), pltpu.VMEM((tall, 2 * cols), BF), pltpu.VMEM((tall, 2 * cols), BF),
            pltpu.VMEM((rows, width), BF), pltpu.VMEM((rows, width), BF),
            *scatter_scratch(line, rows, width, parts),
            pltpu.VMEM((2 * line - 2, rows // parts, width), BF),
            pltpu.SemaphoreType.DMA((line,)), pltpu.SemaphoreType.DMA((2 * line - 2,)),
            pltpu.SemaphoreType.DMA((line, 2)),
            pltpu.SemaphoreType.DMA((line, parts, 3)), pltpu.SemaphoreType.DMA((blocks, parts)),
            pltpu.SemaphoreType.DMA((8,)),
            pltpu.VMEM((2, 2, blocks, rows, tile), BF), pltpu.SemaphoreType.DMA((2, 2)),
            pltpu.VMEM((2, 2, tile, cols), BF), pltpu.VMEM((2, cols, tile), BF),
            pltpu.SemaphoreType.DMA((2, 3)), pltpu.SemaphoreType.DMA((tiles, 3)),
            pltpu.VMEM((2, tile, cols), BF), pltpu.VMEM((cols, tile), BF), pltpu.SemaphoreType.DMA((3,)),
            pltpu.SemaphoreType.DMA,
        ],
        compiler_params=pltpu.CompilerParams(
            collective_id=1, has_side_effects=True, vmem_limit_bytes=63 * 2**20
        ),
        name="feed",
    )(normed, tangent_all, gates[0], gates[1], ups[0], ups[1], downs[0], downs[1])


class Thirds(Scatter):
    def run(self, part):
        quarter = self.rows
        start = jnp.where(part == 2, self.grid.replica, 2 + part) * quarter
        return pl.ds(pl.multiple_of(start, quarter), quarter)


def sums_kernel(
    line,
    normed, attended, grad_qkv, grad_out, twin_normed, twin_attended, twin_out, out_across,
    tokens, grad_middle, weights, gain, term_two,
    result, result_out, grad_tokens,
    across_v, out_partial, out_line, out_total, out_send, out_recv, out_mine, out_theirs, out_sem,
    near_send, near_recv,
    both_normed, both_attended, both_qkv, both_out, load_sem, twin_send, twin_recv,
    partial, from_across, from_line, total, across_send, across_recv, line_send, line_recv,
    mine, theirs, mirror_send, mirror_recv, from_mirror, quarter_send, quarter_recv,
    in_weights, weight_sem, token_v, middle_v, grad_normed, terms, own_terms, twin_terms,
):
    grid = Grid(2, line)
    rows, width = normed.shape
    run = partial.shape[1]
    quarter = run // 4
    narrow = grad_qkv.shape[1]
    grid.greet(True, True)
    scatter = Thirds(
        grid, partial, from_across, from_line, total,
        (across_send, across_recv, line_send, line_recv), 3,
    )
    scatter.rows = quarter
    own, twin = pl.ds(0, rows), pl.ds(rows, rows)
    swap_qkv = remote(grad_qkv, both_qkv.at[twin], twin_send.at[0], twin_recv.at[0], grid.twin)
    swap_qkv.start()
    load_pairs(
        [
            (attended, both_attended.at[own]),
            (twin_attended, both_attended.at[twin]),
            (grad_out, both_out.at[own]),
            (twin_out, both_out.at[twin]),
            (out_across, across_v),
            (normed, both_normed.at[own]),
            (twin_normed, both_normed.at[twin]),
            (grad_qkv, both_qkv.at[own]),
        ],
        load_sem,
    )
    later = [
        pltpu.make_async_copy(src, dst, weight_sem.at[i])
        for i, (src, dst) in enumerate(
            (
                (weights.at[:, :, pl.ds(0, narrow)], in_weights),
                (tokens, token_v),
                (grad_middle, middle_v),
            )
        )
    ]
    for copy in later:
        copy.start()
    tall = line * run
    tile = 512
    away = pl.ds(pl.multiple_of((1 - grid.replica) * quarter, quarter), quarter)
    here = pl.ds(pl.multiple_of(grid.replica * quarter, quarter), quarter)

    outs = Scatter(
        grid, out_partial, None, out_line, out_total, (None, None, out_send, out_recv), 4
    )

    near = remote(near_send, near_recv, out_sem.at[2], out_sem.at[3], grid.across)

    def near_step(i):
        c = pl.ds(pl.multiple_of(i * tile, tile), tile)
        first = ((1 - grid.x) * 2 + grid.core) * tall + grid.z * run
        mine = pl.ds(pl.multiple_of(first, run), run)
        near_send[:, c] = dot(both_attended[:, mine], both_out[:, c], TN).astype(BF)

    def out_step(i):
        c = pl.ds(pl.multiple_of(i * tile, tile), tile)
        value = dot(both_attended[:, features(grid.x)], both_out[:, c], TN)
        value = value.reshape(line, run, tile) + across_v[:, :, c].astype(F32)
        out_partial[:, :, c] = value.astype(BF)

    def to_mirror(slot):
        return remote(
            partial.at[slot, away], from_mirror.at[slot],
            quarter_send.at[slot], quarter_recv.at[slot], grid.mirror,
        )

    def features(x):
        return pl.ds(pl.multiple_of((x * 2 + grid.core) * tall, tall), tall)

    def column(j, carry):
        x = jnp.where(j == 0, 1 - grid.x, grid.x)
        blocks = pl.ds(x * line, line)

        def wide(left, right, first):
            def step(i, inner):
                c = pl.ds(pl.multiple_of(i * tile, tile), tile)
                to = pl.ds(pl.multiple_of(first + i * tile, 128), tile)
                value = dot(left[:, features(x)], right[:, c], TN).astype(BF)
                partial[blocks, :, to] = value.reshape(line, run, tile)
                return inner

            lax.fori_loop(0, right.shape[1] // tile, step, 0)

        wide(both_normed, both_qkv, 0)
        partial[blocks, :, narrow:] = jnp.zeros((line, run, 128), BF)
        for k in range(line - 1, -1, -1):
            z = grid.order(k)
            to_mirror(grid.slot(x, z)).start()
            pl.when(j == 0)(lambda z=z: scatter.across(z, 0).start())
        return carry

    across_v[grid.z] = jnp.zeros((run, width), BF)
    each(width // tile, out_step)
    each(width // tile, near_step)
    swap_qkv.wait()
    lax.fori_loop(0, 2, column, 0)
    near.start()
    each(outs.steps(), outs.step)
    for copy in later:
        copy.wait()

    def back_step(j, carry):
        units = pl.ds(j * (tile // run), tile // run)
        c = pl.ds(pl.multiple_of(j * tile, tile), tile)
        right = in_weights[units].reshape(tile, narrow)
        grad_normed[:, c] = dot(both_qkv[own, :], right, NT)
        return carry

    lax.fori_loop(0, width // tile, back_step, 0)
    terms[...] = jnp.zeros_like(terms)
    chunk = 64

    def norm_step(j, carry):
        r = pl.ds(pl.multiple_of(j * chunk, chunk), chunk)
        value = token_v[r, :].astype(F32)
        factor = lax.rsqrt(jnp.mean(value * value, axis=1, keepdims=True) + norm_eps)
        unit = value * factor
        grad = grad_normed[r, :]
        terms[0:1, :] += jnp.sum(grad * unit, axis=0, keepdims=True)
        scaled = grad * gain[...]
        mean = jnp.mean(scaled * unit, axis=1, keepdims=True)
        grad_tokens[r, :] = (middle_v[r, :] + factor * (scaled - unit * mean)).astype(BF)
        return carry

    lax.fori_loop(0, rows // chunk, norm_step, 0)
    terms[1:2, :] = term_two[...]
    own_terms[...] = terms[...].astype(BF)
    swap_terms = remote(own_terms, twin_terms, twin_send.at[1], twin_recv.at[1], grid.twin)
    swap_terms.start()
    swap_terms.wait()
    for x in range(2):
        for z in range(line):
            first = pl.multiple_of((x * 2 + grid.core) * tall + z * run, run)
            c = pl.ds(first, run)
            value = own_terms[:, c].astype(F32) + twin_terms[:, c].astype(F32)
            partial[x * line + z, 3 * quarter : 3 * quarter + 16, narrow:] = value.astype(BF)
    for k in range(line - 1, -1, -1):
        scatter.across(grid.order(k), 1).start()

    def add_mirror(x):
        def step(i, carry):
            slot = grid.slot(x, grid.order(line - 1 - i))
            to_mirror(slot).wait_recv()
            value = partial[slot, here].astype(F32) + from_mirror[slot].astype(F32)
            partial[slot, here] = value.astype(BF)
            return carry

        lax.fori_loop(0, line, step, 0)

    add_mirror(1 - grid.x)
    for k in range(line - 1, -1, -1):
        scatter.across(grid.order(k), 2).start()

    def swap(part, whole=True):
        at = scatter.run(part)
        return remote(
            mine.at[at], theirs.at[at], mirror_send.at[part], mirror_recv.at[part], grid.mirror
        )

    def sweep(part):
        def step(i, carry):
            scatter.pass_on(grid.order(line - 1 - i), part)
            return carry

        lax.fori_loop(0, line - 1, step, 0)

    def settle(part):
        scatter.gather_sum(grid.z, part)
        mine[scatter.run(part)] = total[...].astype(BF)
        swap(part).start()

    outs.own(result_out)
    near.wait()
    result_out[...] += near_recv[...].astype(F32)
    out_mine[...] = result_out[...].astype(BF)
    out_swap = remote(out_mine, out_theirs, out_sem.at[0], out_sem.at[1], grid.mirror)
    out_swap.start()
    sweep(0)
    sweep(1)
    add_mirror(grid.x)
    settle(0)
    sweep(2)
    settle(1)
    settle(2)
    result[here] = mine[here].astype(F32)
    for part in range(2):
        swap(part).wait()
        at = scatter.run(part)
        result[at] = mine[at].astype(F32) + theirs[at].astype(F32)
    swap(2).wait_send()
    remote(mine.at[away], theirs.at[away], mirror_send.at[2], mirror_recv.at[2], grid.mirror).wait_recv()
    result[away] = theirs[away].astype(F32)
    out_swap.wait()
    result_out[...] = out_mine[...].astype(F32) + out_theirs[...].astype(F32)
    outs.finish()
    scatter.finish()

    def sent(slot, carry):
        to_mirror(slot).wait_send()
        return carry

    lax.fori_loop(0, 2 * line, sent, 0)


def sums_call(
    normed, attended, grad_qkv, grad_out, others, tokens, grad_middle, weights, gain, term_two, line
):
    rows, width = normed.shape
    narrow = grad_qkv.shape[1]
    run, whole = weights.shape[1], narrow + 128
    quarter = run // 4
    vmem = pl.BlockSpec(memory_space=pltpu.VMEM)
    dma = pltpu.SemaphoreType.DMA
    like = lambda a: pltpu.VMEM(a.shape, a.dtype)
    return pl.pallas_call(
        functools.partial(sums_kernel, line),
        out_shape=(
            jax.ShapeDtypeStruct((run, whole), F32), jax.ShapeDtypeStruct((run, width), F32),
            jax.ShapeDtypeStruct((rows, width), BF),
        ),
        in_specs=[ANY] * 11 + [vmem] * 2,
        out_specs=(vmem,) * 3,
        scratch_shapes=[
            pltpu.VMEM((line, run, width), BF), pltpu.VMEM((line, run, width), BF),
            pltpu.VMEM((2 * line - 2, run, width), BF), pltpu.VMEM((quarter, width), F32),
            dma((line, 4)), dma((2 * line - 2, 4)),
            pltpu.VMEM((run, width), BF), pltpu.VMEM((run, width), BF), dma((4,)),
            pltpu.VMEM((run, width), BF), pltpu.VMEM((run, width), BF),
            pltpu.VMEM((2 * rows, width), BF), pltpu.VMEM((2 * rows, width), BF),
            pltpu.VMEM((2 * rows, narrow), BF), pltpu.VMEM((2 * rows, width), BF),
            dma((8,)), dma((2,)), dma((2,)),
            pltpu.VMEM((2 * line, run, whole), BF), pltpu.VMEM((line, run, whole), BF),
            pltpu.VMEM((2 * line - 2, run, whole), BF), pltpu.VMEM((quarter, whole), F32),
            dma((line, 3)), dma((line, 3)), dma((line, 3)), dma((2 * line - 2, 3)),
            pltpu.VMEM((run, whole), BF), pltpu.VMEM((run, whole), BF), dma((3,)), dma((3,)),
            pltpu.VMEM((2 * line, quarter, whole), BF), dma((2 * line,)), dma((2 * line,)),
            pltpu.VMEM((weights.shape[0], run, narrow), BF), dma((3,)),
            like(tokens), like(grad_middle), pltpu.VMEM((rows, width), F32),
            pltpu.VMEM((16, width), F32), pltpu.VMEM((16, width), BF), pltpu.VMEM((16, width), BF),
        ],
        compiler_params=pltpu.CompilerParams(
            collective_id=3, has_side_effects=True, vmem_limit_bytes=63 * 2**20
        ),
        name="sums",
    )(
        normed, attended, grad_qkv, grad_out, *others, tokens, grad_middle, weights, gain, term_two
    )


def gather_weights(
    grid, block, everything, send, recv, twin_send, twin_recv, meanwhile, afterwards
):
    line = grid.line
    rows = block.shape[0] // 4
    carry_a, carry_b = grid.replica * 2, grid.replica * 2 + 1
    other_a, other_b = (1 - grid.replica) * 2, (1 - grid.replica) * 2 + 1
    right, left, across, mirror = range(4)
    devices = (grid.right, grid.left, grid.across, grid.mirror)

    def run(quarter):
        return pl.ds(pl.multiple_of(quarter * rows, rows), rows)

    def place(x, core, z, quarter):
        return everything.at[(x * 2 + core) * line + z, run(quarter)]

    def copy(x, z, quarter, link, first=False):
        there = place(x, grid.core, z, quarter)
        here = block.at[run(quarter)] if first else there
        unit = x * line + z
        return remote(
            here, there, send.at[quarter, unit, link], recv.at[quarter, unit], devices[link]
        )

    def share(x, z, quarter, first=False):
        there = place(x, grid.core, z, quarter)
        here = block.at[run(quarter)] if first else there
        unit = x * line + z
        return remote(
            here, there, twin_send.at[quarter, unit], twin_recv.at[quarter, unit], grid.twin
        )

    def arrived(x, z, quarter):
        copy(x, z, quarter, across).wait_recv()
        share(x, z, quarter).start()

    copy(grid.x, grid.z, carry_b, across, True).start()
    copy(grid.x, grid.z, carry_a, across, True).start()
    copy(grid.x, grid.z, other_a, across, True).start()
    for link, go in ((right, grid.has_right), (left, grid.has_left)):

        @pl.when(go)
        def _(link=link):
            copy(grid.x, grid.z, carry_a, link, True).start()
            copy(grid.x, grid.z, carry_b, link, True).start()

    for quarter in range(4):
        share(grid.x, grid.z, quarter, True).start()
    meanwhile()

    arrived(1 - grid.x, grid.z, carry_b)
    copy(1 - grid.x, grid.z, carry_b, mirror).start()
    for link, go in ((right, grid.has_right), (left, grid.has_left)):
        pl.when(go)(lambda link=link: copy(1 - grid.x, grid.z, carry_b, link).start())

    def sides(distance):
        return (
            (grid.z - distance, grid.z >= distance, right, grid.has_right),
            (grid.z + distance, grid.z + distance < line, left, grid.has_left),
        )

    def step(distance, carry):
        for x, quarter in (
            (grid.x, carry_a),
            (grid.x, carry_b),
            (1 - grid.x, carry_b),
        ):
            for z, there, link, go in sides(distance):

                @pl.when(there)
                def _(x=x, quarter=quarter, z=z, link=link, go=go):
                    copy(x, z, quarter, across).wait_recv()
                    pl.when(go)(lambda: copy(x, z, quarter, link).start())
                    copy(x, z, quarter, mirror).start()
                    if quarter is carry_a:
                        copy(x, z, quarter, across).start()
                    share(x, z, quarter).start()

        for z, there, _, _ in sides(distance - 1):

            @pl.when(jnp.logical_and(there, distance > 1))
            def _(z=z):
                arrived(grid.x, z, other_a)
                copy(grid.x, z, other_a, across).start()

        return carry

    lax.fori_loop(1, line + 1, step, 0)
    afterwards()

    def last(z, carry):
        arrived(1 - grid.x, z, carry_a)
        arrived(1 - grid.x, z, other_a)
        arrived(1 - grid.x, z, other_b)
        pl.when(z != grid.z)(lambda: arrived(grid.x, z, other_b))
        return carry

    lax.fori_loop(0, line, last, 0)

    def finish(z, carry):
        away = z != grid.z
        for x in (grid.x, 1 - grid.x):
            for quarter in range(4):
                share(x, z, quarter).wait()
        for x, quarter in ((grid.x, carry_a), (grid.x, carry_b), (1 - grid.x, carry_b)):
            to_mirror = jnp.logical_or(away, jnp.bool_(x is not grid.x))
            pl.when(to_mirror)(
                lambda x=x, quarter=quarter: copy(x, z, quarter, mirror).wait_send()
            )
            for link, go in (
                (right, jnp.logical_and(z <= grid.z, grid.has_right)),
                (left, jnp.logical_and(z >= grid.z, grid.has_left)),
            ):
                pl.when(go)(
                    lambda x=x, quarter=quarter, link=link: copy(x, z, quarter, link).wait_send()
                )
        copy(grid.x, z, carry_a, across).wait_send()
        copy(grid.x, z, other_a, across).wait_send()
        return carry

    lax.fori_loop(0, line, finish, 0)
    copy(grid.x, grid.z, carry_b, across, True).wait_send()


class Line:
    def __init__(self, grid, block, everything, send, recv):
        self.grid, self.block, self.everything = grid, block, everything
        self.send, self.recv = send, recv

    def copy(self, z, link, first=False):
        grid = self.grid
        there = self.everything.at[z]
        here = self.block if first else there
        device = (grid.right, grid.left)[link]
        return remote(here, there, self.send.at[z, link], self.recv.at[z], device)

    def send_own(self):
        grid = self.grid
        for link, go in ((0, grid.has_right), (1, grid.has_left)):
            pl.when(go)(lambda link=link: self.copy(grid.z, link, True).start())

    def forward(self, distance):
        grid = self.grid
        for z, there, link, go in (
            (grid.z - distance, grid.z >= distance, 0, grid.has_right),
            (grid.z + distance, grid.z + distance < grid.line, 1, grid.has_left),
        ):

            @pl.when(there)
            def _(z=z, link=link, go=go):
                self.copy(z, link).wait_recv()
                pl.when(go)(lambda: self.copy(z, link).start())

    def finish(self):
        grid = self.grid

        def step(z, carry):
            for link, go in (
                (0, jnp.logical_and(z <= grid.z, grid.has_right)),
                (1, jnp.logical_and(z >= grid.z, grid.has_left)),
            ):
                pl.when(go)(lambda link=link: self.copy(z, link).wait_send())
            return carry

        lax.fori_loop(0, grid.line, step, 0)


def turn(value, cosine, sine, scale):
    parts = []
    lane = lax.broadcasted_iota(jnp.int32, (value.shape[0], 128), 1) % HEAD_SIZE
    for first in range(0, value.shape[1], 128):
        pair = value[:, first : first + 128]
        swapped = jnp.where(
            lane < HEAD_SIZE // 2,
            pltpu.roll(pair, 128 - HEAD_SIZE // 2, 1),
            pltpu.roll(pair, HEAD_SIZE // 2, 1),
        )
        parts.append(((pair * cosine[...] + swapped * sine[...]) * scale).astype(BF))
    return parts[0] if len(parts) == 1 else jnp.concatenate(parts, axis=1)


def halves(pair, half):
    pair = pair.astype(F32)
    turned = pltpu.roll(pair, HEAD_SIZE, 1)
    lane = lax.broadcasted_iota(jnp.int32, pair.shape, 1) // HEAD_SIZE
    first = jnp.where(half == 0, pair, turned)
    second = jnp.where(half == 0, turned, pair)
    both = jnp.concatenate([first, second], axis=0)
    return jnp.where(jnp.concatenate([lane, lane], axis=0) == half, both, 0.0).astype(BF)


def unhalves(both, half):
    rows = both.shape[0] // 2
    first, second = both[:rows], both[rows:]
    lane = lax.broadcasted_iota(jnp.int32, first.shape, 1) // HEAD_SIZE
    first = jnp.where(half == 0, first, pltpu.roll(first, HEAD_SIZE, 1))
    second = jnp.where(half == 0, pltpu.roll(second, HEAD_SIZE, 1), second)
    return jnp.where(lane == 0, first, second)


def front_kernel(
    line, parts,
    query_w, key_w, value_w, extra_w, out_w, tokens, tangent, bias, cosine, sine,
    attended, middle, normed, first_normed, queries, logs, keyed_out, tangent_all, weights_out,
    everything, keyed, keyed_all, bias_v, token_v, cosine_v, sine_v, gain, scores, probs, sums, stage, load_sem,
    key_send, key_recv, send, recv, own_sem, weight_send, weight_recv, twin_send, twin_recv,
):
    grid = Grid(2, line)
    rows, width = tokens.shape
    narrow = keyed.shape[1] // 2
    total = bias.shape[1]
    extra = width + 2 * narrow
    after = extra + 128
    me = grid.slot(grid.x, grid.z)
    chunk = rows // 2
    tile = 512
    block = everything.at[(grid.x * 2 + grid.core) * line + grid.z]
    first, packs = 0, []
    for part in (query_w, key_w, value_w, extra_w, out_w):
        packs.append((part, block.at[:, pl.ds(first, part.shape[1])]))
        first += part.shape[1]
    load_pairs(packs, load_sem)
    grid.greet(True, True)

    def meanwhile():
        load_pairs(
            [
                (tangent, stage),
                (bias, bias_v),
                (tokens, token_v),
                (cosine, cosine_v),
                (sine, sine_v),
            ],
            load_sem,
        )
        load_pairs([(stage, tangent_all.at[me])], own_sem)

    gather = Gather(grid, tangent, tangent_all, send, recv, parts)
    soon = parts // 2

    def tangent_first():
        gather.send_own()
        for part in range(soon):
            gather.forward(1, part)

    gather_weights(
        grid, block, everything, weight_send, weight_recv, twin_send, twin_recv, meanwhile,
        tangent_first,
    )
    weights_copy = pltpu.make_async_copy(everything, weights_out, own_sem.at[1])
    weights_copy.start()
    units, run = everything.shape[0], everything.shape[1]
    for unit in range(units):
        for which in range(2):
            gain[which : which + 1, unit * run : (unit + 1) * run] = everything[
                unit, which : which + 1, extra:after
            ].astype(F32)

    def norm(source, target, which):
        def step(j, carry):
            here = pl.ds(pl.multiple_of(j * chunk, chunk), chunk)
            value = source[here, :].astype(F32)
            factor = lax.rsqrt(jnp.mean(value * value, axis=1, keepdims=True) + norm_eps)
            target[here, :] = (value * factor * gain[which : which + 1, :]).astype(BF)
            return carry

        lax.fori_loop(0, rows // chunk, step, 0)

    norm(token_v, first_normed, 0)

    def project(c):
        return dot(first_normed[...], everything[:, :, c].reshape(width, tile), NN)

    for first in range(0, narrow, tile):
        keyed[:, first : first + tile] = turn(project(slice(width + first, width + first + tile)), cosine_v, sine_v, 1.0)
        keyed[:, narrow + first : narrow + first + tile] = project(
            slice(width + narrow + first, width + narrow + first + tile)
        ).astype(BF)
    line_keys = Line(grid, keyed, keyed_all, key_send, key_recv)
    line_keys.send_own()
    for part in range(soon, parts):
        gather.forward(1, part, along=False)
    keyed_all[grid.z] = keyed[...]

    def query_step(j, carry):
        c = pl.ds(pl.multiple_of(j * tile, tile), tile)
        queries[:, c] = turn(project(c), cosine_v, sine_v, HEAD_SIZE ** (-0.5))
        return carry

    lax.fori_loop(0, width // tile, query_step, 0)
    for distance in range(1, line):
        line_keys.forward(distance)
    for part in range(soon, parts):
        gather.forward(1, part, wait=False, across=False)

    logs[...] = jnp.zeros_like(logs)
    pairs = width // (2 * HEAD_SIZE)
    group = pairs // (narrow // (2 * HEAD_SIZE))

    def advance(n):
        gather.forward(n // parts + 2, n % parts)

    def pair_step(i, carry):
        c = pl.ds(pl.multiple_of(i * 128, 128), 128)
        half = (i // (group // 2)) % 2
        first_key = pl.multiple_of((i // group) * 128, 128)
        keys = keyed_all[:, :, pl.ds(first_key, 128)].reshape(total, 128)
        values = keyed_all[:, :, pl.ds(first_key + narrow, 128)].reshape(total, 128)
        scores[...] = dot(halves(queries[:, c], half), keys, NT)

        def soft(j, inner):
            here = pl.ds(pl.multiple_of(j * rows, rows), rows)
            value = scores[here, :] + bias_v[...]
            top = jnp.max(value, axis=1, keepdims=True)
            power = jnp.exp(value - top)
            size = jnp.sum(power, axis=1, keepdims=True)
            probs[here, :] = power.astype(BF)
            sums[here, :] = jnp.broadcast_to(1.0 / size, (rows, 128))
            lane = lax.broadcasted_iota(jnp.int32, (rows, 128), 1)
            logs[here, :] = jnp.where(lane == i, top + jnp.log(size), logs[here, :])
            return inner

        lax.fori_loop(0, 2, soft, 0)
        out = dot(probs[...], values, NN) * sums[...]
        attended[:, c] = unhalves(out, half).astype(BF)

        pl.when(i % 2 == 1)(lambda: advance(i // 2))
        return carry

    lax.fori_loop(0, pairs, pair_step, 0)
    keyed_copy = pltpu.make_async_copy(keyed_all, keyed_out, load_sem.at[0])
    keyed_copy.start()

    def out_step(j, carry):
        c = pl.ds(pl.multiple_of(j * tile, tile), tile)
        w = pl.ds(pl.multiple_of(after + j * tile, 128), tile)
        out = dot(attended[...], everything[:, :, w].reshape(width, tile), NN)
        middle[:, c] = token_v[:, c].astype(F32) + out
        return carry

    lax.fori_loop(0, width // tile, out_step, 0)
    norm(middle, normed, 1)

    def rest(n, carry):
        advance(n)
        return carry

    lax.fori_loop(pairs // 2, (line - 2) * parts, rest, 0)
    for z in range(line):
        gather.wait_across(z)
    keyed_copy.wait()
    weights_copy.wait()
    line_keys.finish()
    gather.finish()


def front_call(pieces, tokens, tangent, bias, cosine, sine, line):
    rows, width = tokens.shape
    narrow = pieces[1].shape[1]
    unit = (pieces[0].shape[0], sum(p.shape[1] for p in pieces))
    total = bias.shape[1]
    blocks, parts = 2 * line, 4
    shapes = jax.ShapeDtypeStruct
    vmem = pl.BlockSpec(memory_space=pltpu.VMEM)
    like = lambda a: pltpu.VMEM(a.shape, a.dtype)
    return pl.pallas_call(
        functools.partial(front_kernel, line, parts),
        out_shape=(
            shapes((rows, width), BF), shapes((rows, width), F32), shapes((rows, width), BF),
            shapes((rows, width), BF), shapes((rows, width), BF),
            shapes((2 * rows, 128), F32), shapes((line, rows, 2 * narrow), BF),
            shapes((blocks, rows, width), BF), shapes((2 * blocks,) + unit, BF),
        ),
        in_specs=[ANY] * 10,
        out_specs=(vmem,) * 6 + (ANY,) * 3,
        scratch_shapes=[
            pltpu.VMEM((2 * blocks,) + unit, BF),
            pltpu.VMEM((rows, 2 * narrow), BF), pltpu.VMEM((line, rows, 2 * narrow), BF),
            like(bias), like(tokens), like(cosine), like(sine), pltpu.VMEM((2, width), F32),
            pltpu.VMEM((2 * rows, total), F32), pltpu.VMEM((2 * rows, total), BF),
            pltpu.VMEM((2 * rows, 128), F32), pltpu.VMEM((rows, width), BF), pltpu.SemaphoreType.DMA((6,)),
            pltpu.SemaphoreType.DMA((line, 2)), pltpu.SemaphoreType.DMA((line,)),
            pltpu.SemaphoreType.DMA((line, parts, 3)), pltpu.SemaphoreType.DMA((blocks, parts)),
            pltpu.SemaphoreType.DMA((2,)),
            pltpu.SemaphoreType.DMA((4, blocks, 4)), pltpu.SemaphoreType.DMA((4, blocks)),
            pltpu.SemaphoreType.DMA((4, blocks)), pltpu.SemaphoreType.DMA((4, blocks)),
        ],
        compiler_params=pltpu.CompilerParams(
            collective_id=5, has_side_effects=True, vmem_limit_bytes=62 * 2**20
        ),
        name="front",
    )(*pieces, tokens, tangent, bias, cosine, sine)


def back_kernel(
    line, parts,
    queries, keyed_all, grad_out, bias, logs, hidden_all, down_own, down_twin, weights, cosine, sine,
    gate_sum, up_sum, down_sum, _gate, _up, _down, normed, attended,
    branch, grad_qkv, gate_mirror, up_mirror, down_mirror, twin_normed, twin_attended, twin_out,
    out_across, both_attended, both_out, out_partial, out_send, out_recv,
    out_v, out_w, cosine_v, sine_v, grad_keyed, mirror_send, mirror_recv,
    query_v, keyed_v, grad_v, bias_v, log_v, scores, gradients, probs, slopes, key_sum, value_sum,
    down_w, hidden, load_sem,
    partial, from_across, from_line, total, across_send, across_recv, line_send, line_recv,
    key_partial, key_line, key_total, key_send, key_recv,
):
    grid = Grid(2, line)
    cols, width = down_own.shape
    rows = partial.shape[1]
    narrow = keyed_all.shape[2] // 2
    length = bias.shape[1]
    grid.greet(True, True)
    swapped = [
        remote(src, dst, mirror_send.at[3 + i], mirror_recv.at[3 + i], grid.twin)
        for i, (src, dst) in enumerate(
            ((normed, twin_normed), (attended, twin_attended), (grad_out, twin_out))
        )
    ]
    for copy in swapped:
        copy.start()
    left = pl.ds(EARLY * 256, width - EARLY * 256)
    mirrored = [
        remote(src, dst, mirror_send.at[i], mirror_recv.at[i], grid.mirror)
        for i, (src, dst) in enumerate(
            (
                (gate_sum.at[left, :], gate_mirror.at[left, :]),
                (up_sum.at[left, :], up_mirror.at[left, :]),
                (down_sum.at[:, left], down_mirror.at[:, left]),
            )
        )
    ]
    for copy in mirrored:
        copy.start()
    load_pairs(
        [
            (down_own, down_w.at[pl.ds(0, cols)]),
            (down_twin, down_w.at[pl.ds(cols, cols)]),
            (hidden_all, hidden),
            (queries, query_v),
            (keyed_all, keyed_v),
            (grad_out, out_v),
            (bias, bias_v),
            (logs, log_v),
            (cosine, cosine_v),
            (sine, sine_v),
        ],
        load_sem,
    )
    scatter = Scatter(
        grid, partial, from_across, from_line, total,
        (across_send, across_recv, line_send, line_recv), parts,
    )
    keyed_scatter = Scatter(
        grid, key_partial, None, key_line, key_total, (None, None, key_send, key_recv),
        key_partial.shape[1] // rows,
    )

    def work(i, carry):
        z = grid.order(line - 1 - i % line)
        slot = grid.slot(jnp.where(i < line, 1 - grid.x, grid.x), z)
        spot = pl.ds(pl.multiple_of(slot * rows, rows), rows)

        def tile(j, inner):
            c = pl.ds(pl.multiple_of(j * cols, cols), cols)
            partial[slot, :, c] = dot(hidden[spot, :], down_w[:, c], NN).astype(BF)
            return inner

        lax.fori_loop(0, width // cols, tile, 0)
        pl.when(i < line)(lambda: scatter.send_across(z))
        return carry

    lax.fori_loop(0, line, work, 0)
    tile = out_w.shape[0] * out_w.shape[1]
    after = weights.shape[2] - width

    def out_step(j, carry):
        units = pl.ds(j * out_w.shape[0], out_w.shape[0])
        load_pairs([(weights.at[units, :, pl.ds(after, width)], out_w)], load_sem)
        c = pl.ds(pl.multiple_of(j * tile, tile), tile)
        grad_v[:, c] = dot(out_v[...], out_w[...].reshape(tile, width), NT).astype(BF)
        return carry

    lax.fori_loop(0, width // tile, out_step, 0)
    work(line, 0)
    deep = 2 * rows
    chunk = rows // 2
    pairs = width // (2 * HEAD_SIZE)
    group = pairs // (narrow // (2 * HEAD_SIZE))

    def pair_step(i, carry):
        c = pl.ds(pl.multiple_of(i * 128, 128), 128)
        half = (i // (group // 2)) % 2
        key_cols = pl.ds(pl.multiple_of((i // group) * 128, 128), 128)
        value_cols = pl.ds(pl.multiple_of((i // group) * 128 + narrow, 128), 128)
        keys = keyed_v[:, :, key_cols].reshape(length, 128)
        values = keyed_v[:, :, value_cols].reshape(length, 128)
        query = halves(query_v[:, c], half)
        grad = halves(grad_v[:, c], half)
        scores[...] = dot(query, keys, NT)
        gradients[...] = dot(grad, values, NT)

        def soft(j, inner):
            here = pl.ds(pl.multiple_of(j * chunk, chunk), chunk)
            there = pl.ds(pl.multiple_of((j * chunk) % rows, chunk), chunk)
            lane = lax.broadcasted_iota(jnp.int32, (chunk, 128), 1)
            log = jnp.sum(jnp.where(lane == i, log_v[here, :], 0.0), axis=1, keepdims=True)
            prob = jnp.exp(scores[here, :] + bias_v[there, :] - log)
            slope = gradients[here, :]
            delta = jnp.sum(prob * slope, axis=1, keepdims=True)
            probs[here, :] = prob.astype(BF)
            slopes[here, :] = (prob * (slope - delta)).astype(BF)
            return inner

        lax.fori_loop(0, deep // chunk, soft, 0)
        back = dot(slopes[...], keys, NN) * HEAD_SIZE ** (-0.5)
        grad_qkv[:, c] = turn(unhalves(back, half), cosine_v, sine_v, 1.0)
        key_part = dot(slopes[...], query, TN)
        value_part = dot(probs[...], grad, TN)

        @pl.when(i % group == 0)
        def _():
            key_sum[...] = key_part
            value_sum[...] = value_part

        @pl.when(i % group != 0)
        def _():
            key_sum[...] += key_part
            value_sum[...] += value_part

        @pl.when(i % group == group - 1)
        def _():
            spot = pl.ds(pl.multiple_of((i // group) * rows, rows), rows)
            key_partial[:, spot, 0:128] = key_sum[...].astype(BF).reshape(line, rows, 128)
            key_partial[:, spot, 128:256] = value_sum[...].astype(BF).reshape(line, rows, 128)
            pl.when(i // group + early > 0)(lambda: keyed_steps(i // group + early - 1))

        @pl.when(i % 6 == 2)
        def _():
            work(line + 1 + i // 6, 0)

        pl.when(i == pairs // 2 - 2)(out_gradients)

        pl.when(i % pace == 0)(lambda: scatter.step(i // pace + early))
        return carry

    run = out_partial.shape[1]

    def outward(z):
        return remote(
            out_partial.at[z], out_across.at[z], out_send.at[z], out_recv.at[z], grid.across
        )

    def away(action):
        each(line, lambda z: pl.when(z != grid.z)(lambda: action(outward(z))))

    def out_gradients():
        for copy in swapped[1:]:
            copy.wait()
        own, twin = pl.ds(0, rows), pl.ds(rows, rows)
        load_pairs(
            [
                (attended, both_attended.at[own]),
                (twin_attended, both_attended.at[twin]),
                (grad_out, both_out.at[own]),
                (twin_out, both_out.at[twin]),
            ],
            load_sem,
        )
        tall = line * run
        first = pl.multiple_of(((1 - grid.x) * 2 + grid.core) * tall, tall)

        def tile_step(j):
            c = pl.ds(pl.multiple_of(j * 512, 512), 512)
            value = dot(both_attended[:, pl.ds(first, tall)], both_out[:, c], TN).astype(BF)
            out_partial[:, :, c] = value.reshape(line, run, 512)

        each(width // 512, tile_step)
        away(lambda c: c.start())

    def keyed_steps(g):
        each(line - 1, lambda j: keyed_scatter.pass_on(keyed_scatter.rank(j), g))

    pace = 4
    early = jnp.where(jnp.logical_and(grid.has_left, grid.has_right), 0, 1)
    pl.when(early == 1)(lambda: scatter.step(0))
    lax.fori_loop(0, pairs, pair_step, 0)

    def rest(n, carry):
        scatter.step(n)
        return carry

    lax.fori_loop(pairs // pace + early, scatter.steps(), rest, 0)

    pl.when(early == 0)(lambda: keyed_steps(pairs // group - 1))
    scatter.own(branch)
    keyed_scatter.own(grad_keyed)
    for g in range(pairs // group):
        both = grad_keyed[g * rows : (g + 1) * rows, :]
        first = width + g * 128
        grad_qkv[:, first : first + 128] = turn(both[:, :128], cosine_v, sine_v, 1.0)
        grad_qkv[:, first + narrow : first + narrow + 128] = both[:, 128:].astype(BF)
    for copy in mirrored + swapped[:1]:
        copy.wait()
    away(lambda c: c.wait())
    scatter.finish()
    keyed_scatter.finish()


def back_call(
    queries, keyed_all, grad_out, bias, logs, hidden_all, downs, weights, cosine, sine, sums,
    mirrors, normed, attended, line,
):
    rows, width = queries.shape
    both = keyed_all.shape[2]
    groups, run = both // 256, weights.shape[1]
    cols, length = downs[0].shape[0], bias.shape[1]
    parts = 2
    shapes = jax.ShapeDtypeStruct
    vmem = pl.BlockSpec(memory_space=pltpu.VMEM)
    return pl.pallas_call(
        functools.partial(back_kernel, line, parts),
        out_shape=(
            shapes((rows, width), F32), shapes((rows, width + both), BF),
            *(shapes(s.shape, BF) for s in sums), *(shapes((rows, width), BF),) * 3,
            shapes((line, run, width), BF),
        ),
        in_specs=[ANY] * 19,
        out_specs=(vmem,) * 2 + (ANY,) * 7,
        input_output_aliases={14: 2, 15: 3, 16: 4},
        scratch_shapes=[
            pltpu.VMEM((2 * rows, width), BF), pltpu.VMEM((2 * rows, width), BF),
            pltpu.VMEM((line, run, width), BF),
            pltpu.SemaphoreType.DMA((line,)), pltpu.SemaphoreType.DMA((line,)),
            pltpu.VMEM((rows, width), BF), pltpu.VMEM((4, run, width), BF),
            pltpu.VMEM(cosine.shape, F32), pltpu.VMEM(sine.shape, F32),
            pltpu.VMEM((groups * rows, 256), F32),
            pltpu.SemaphoreType.DMA((6,)), pltpu.SemaphoreType.DMA((6,)),
            pltpu.VMEM((rows, width), BF), pltpu.VMEM(keyed_all.shape, BF), pltpu.VMEM((rows, width), BF),
            pltpu.VMEM((rows, length), F32), pltpu.VMEM(logs.shape, F32),
            pltpu.VMEM((2 * rows, length), F32), pltpu.VMEM((2 * rows, length), F32),
            pltpu.VMEM((2 * rows, length), BF), pltpu.VMEM((2 * rows, length), BF),
            pltpu.VMEM((length, 128), F32), pltpu.VMEM((length, 128), F32),
            pltpu.VMEM((2 * cols, width), BF), pltpu.VMEM(hidden_all.shape, BF),
            pltpu.SemaphoreType.DMA((10,)),
            *scatter_scratch(line, rows, width, parts),
            pltpu.VMEM((line, groups * rows, 256), BF), pltpu.VMEM((2 * line - 2, groups * rows, 256), BF),
            pltpu.VMEM((rows, 256), F32),
            pltpu.SemaphoreType.DMA((line, groups)), pltpu.SemaphoreType.DMA((2 * line - 2, groups)),
        ],
        compiler_params=pltpu.CompilerParams(
            collective_id=6, has_side_effects=True, vmem_limit_bytes=62 * 2**20
        ),
        name="back",
    )(
        queries, keyed_all, grad_out, bias, logs, hidden_all, *downs, weights, cosine, sine, *sums,
        *mirrors, normed, attended,
    )


def body(
    tokens,
    places,
    cotangent,
    gain_attn,
    gain_mlp,
    w_query,
    key_projection,
    value_projection,
    w_out,
    w_gate,
    w_up,
    w_down,
):
    sequence_total, segment_length, width = tokens.shape
    total_length = places.shape[1]
    total_rows = sequence_total * segment_length
    position = lax.axis_index("context")
    local_positions = lax.dynamic_slice_in_dim(places, position * segment_length, segment_length, 1)
    rotary_angles = local_positions.reshape(total_rows).astype(jnp.float32)[:, None] * frequencies(
        HEAD_SIZE // 2
    )
    gain_one, gain_two, query_w, key_weight_local, value_w, out_w = (
        lax.all_gather(gain_attn, ("fsdp", "context"), axis=0, tiled=True),
        lax.all_gather(gain_mlp, ("fsdp", "context"), axis=0, tiled=True),
        lax.all_gather(w_query, ("fsdp", "context"), axis=0, tiled=True),
        lax.all_gather(key_projection, ("fsdp", "context"), axis=0, tiled=True),
        lax.all_gather(value_projection, ("fsdp", "context"), axis=0, tiled=True),
        lax.all_gather(w_out, ("fsdp", "context"), axis=0, tiled=True),
    )
    gain_first = gain_one.astype(jnp.float32)
    gain_second = gain_two.astype(jnp.float32)
    inputs_f = tokens.astype(jnp.float32).reshape(total_rows, width)
    factor_one = lax.rsqrt(jnp.mean(inputs_f * inputs_f, axis=-1, keepdims=True) + norm_eps)
    unit_one = inputs_f * factor_one
    normed_tokens = (unit_one * gain_first).astype(jnp.bfloat16)
    query_pre = jnp.dot(normed_tokens, query_w, preferred_element_type=jnp.float32).reshape(
        total_rows, QUERY_HEADS, HEAD_SIZE
    )
    key_unrotated = jnp.dot(
        normed_tokens, key_weight_local, preferred_element_type=jnp.float32
    ).reshape(total_rows, KEY_VALUE_HEADS, HEAD_SIZE)
    value_matrix_rows = jnp.dot(normed_tokens, value_w, preferred_element_type=jnp.float32).astype(
        jnp.bfloat16
    )
    query_rows = apply_rotary(query_pre, rotary_angles).astype(jnp.bfloat16)
    key_matrix_rows = (
        apply_rotary(key_unrotated, rotary_angles)
        .astype(jnp.bfloat16)
        .reshape(sequence_total, segment_length, KEY_VALUE_HEADS * HEAD_SIZE)
    )
    key_all, value_all = (
        lax.all_gather(key_matrix_rows, "context", axis=1, tiled=True),
        lax.all_gather(
            value_matrix_rows.reshape(sequence_total, segment_length, KEY_VALUE_HEADS * HEAD_SIZE),
            "context",
            axis=1,
            tiled=True,
        ),
    )
    head_query = query_head_rows(query_rows, sequence_total, segment_length)
    head_key = key_heads(key_all, sequence_total, total_length)
    head_value = key_heads(value_all, sequence_total, total_length)
    query_positions = jnp.repeat(local_positions, KEY_VALUE_HEADS, axis=0)
    key_positions = jnp.repeat(places, KEY_VALUE_HEADS, axis=0)
    attended = lax.map(
        forward_head, (head_query, head_key, head_value, query_positions, key_positions)
    )
    attended = merge_queries(attended, sequence_total, segment_length).astype(jnp.bfloat16)
    middle = inputs_f + jnp.dot(attended, out_w, preferred_element_type=jnp.float32)
    factor_two = lax.rsqrt(jnp.mean(middle * middle, axis=-1, keepdims=True) + norm_eps)
    unit_two = middle * factor_two
    normed_mlp = (unit_two * gain_second).astype(jnp.bfloat16)
    tangent = cotangent.reshape(total_rows, width)
    tangent_f = tangent.astype(jnp.float32)
    group = ("fsdp", "context")
    normed_all = lax.all_gather(normed_mlp, group, axis=0, tiled=True)
    tangent_all = lax.all_gather(tangent, group, axis=0, tiled=True)
    branch_part, kept_values = feed_forward(normed_all, w_gate, w_up, w_down)
    grad_part, grad_w_gate, grad_w_up, grad_w_down = feed_back(
        normed_all, tangent_all, w_gate, w_up, w_down, kept_values
    )
    grad_normed = lax.psum_scatter(
        grad_part.astype(jnp.bfloat16), group, scatter_dimension=0, tiled=True
    ).astype(jnp.float32)
    branch = lax.psum_scatter(
        branch_part.astype(jnp.bfloat16), group, scatter_dimension=0, tiled=True
    ).astype(jnp.float32)
    outcome = middle + branch
    scaled_two = grad_normed * gain_second
    term_gain_two = jnp.sum(grad_normed * unit_two, axis=0)
    grad_middle = tangent_f + factor_two * (
        scaled_two - unit_two * jnp.mean(scaled_two * unit_two, axis=-1, keepdims=True)
    )
    grad_branch = grad_middle.astype(jnp.bfloat16)
    term_out = times_t(attended, grad_branch)
    grad_attended = times_nt(grad_branch, out_w).astype(jnp.bfloat16)
    head_grad = query_head_rows(grad_attended, sequence_total, segment_length)
    grad_q, grad_k, grad_v = lax.map(
        backward_head, (head_query, head_key, head_value, head_grad, query_positions, key_positions)
    )
    local_key_gradient, local_value_gradient = (
        lax.psum_scatter(
            merge_keys(grad_k, sequence_total, total_length).astype(jnp.bfloat16),
            "context",
            scatter_dimension=1,
            tiled=True,
        ).astype(jnp.float32),
        lax.psum_scatter(
            merge_keys(grad_v, sequence_total, total_length).astype(jnp.bfloat16),
            "context",
            scatter_dimension=1,
            tiled=True,
        ).astype(jnp.float32),
    )
    grad_query = (
        inverse_rotary(
            merge_queries(grad_q, sequence_total, segment_length).reshape(
                total_rows, QUERY_HEADS, HEAD_SIZE
            ),
            rotary_angles,
        )
        .reshape(total_rows, QUERY_HEADS * HEAD_SIZE)
        .astype(jnp.bfloat16)
    )
    grad_key = (
        inverse_rotary(
            local_key_gradient.reshape(total_rows, KEY_VALUE_HEADS, HEAD_SIZE), rotary_angles
        )
        .reshape(total_rows, KEY_VALUE_HEADS * HEAD_SIZE)
        .astype(jnp.bfloat16)
    )
    value_gradient = local_value_gradient.reshape(total_rows, KEY_VALUE_HEADS * HEAD_SIZE).astype(
        jnp.bfloat16
    )
    grad_normed_one = (
        times_nt(grad_query, query_w)
        + times_nt(grad_key, key_weight_local)
        + times_nt(value_gradient, value_w)
    )
    term_query = times_t(normed_tokens, grad_query)
    term_key = times_t(normed_tokens, grad_key)
    term_value = times_t(normed_tokens, value_gradient)
    scaled_one = grad_normed_one * gain_first
    term_gain_one = jnp.sum(grad_normed_one * unit_one, axis=0)
    grad_inputs = grad_middle + factor_one * (
        scaled_one - unit_one * jnp.mean(scaled_one * unit_one, axis=-1, keepdims=True)
    )
    share_query, share_key, share_value, share_out, share_gain_one, share_gain_two = (
        lax.psum_scatter(term_query.astype(jnp.bfloat16), ("fsdp", "context"), scatter_dimension=0, tiled=True),
        lax.psum_scatter(term_key.astype(jnp.bfloat16), ("fsdp", "context"), scatter_dimension=0, tiled=True),
        lax.psum_scatter(term_value.astype(jnp.bfloat16), ("fsdp", "context"), scatter_dimension=0, tiled=True),
        lax.psum_scatter(term_out.astype(jnp.bfloat16), ("fsdp", "context"), scatter_dimension=0, tiled=True),
        lax.psum_scatter(term_gain_one, ("fsdp", "context"), scatter_dimension=0, tiled=True),
        lax.psum_scatter(term_gain_two, ("fsdp", "context"), scatter_dimension=0, tiled=True),
    )
    summed = (
        lax.psum(share_query.astype(jnp.bfloat16), "replica").astype(jnp.float32),
        lax.psum(share_key.astype(jnp.bfloat16), "replica").astype(jnp.float32),
        lax.psum(share_value.astype(jnp.bfloat16), "replica").astype(jnp.float32),
        lax.psum(share_out.astype(jnp.bfloat16), "replica").astype(jnp.float32),
        lax.psum(grad_w_gate.astype(jnp.bfloat16), "replica").astype(jnp.float32),
        lax.psum(grad_w_up.astype(jnp.bfloat16), "replica").astype(jnp.float32),
        lax.psum(grad_w_down.astype(jnp.bfloat16), "replica").astype(jnp.float32),
        lax.psum(share_gain_one.astype(jnp.bfloat16), "replica").astype(jnp.float32),
        lax.psum(share_gain_two.astype(jnp.bfloat16), "replica").astype(jnp.float32),
    )
    out = outcome.astype(jnp.bfloat16).reshape(sequence_total, segment_length, width)
    grad_tokens = grad_inputs.astype(jnp.bfloat16).reshape(sequence_total, segment_length, width)
    return (
        out,
        grad_tokens,
        summed[0],
        summed[1],
        summed[2],
        summed[3],
        summed[4],
        summed[5],
        summed[6],
        summed[7],
        summed[8],
    )


def kernel_body(
    tokens,
    places,
    cotangent,
    gain_attn,
    gain_mlp,
    w_query,
    key_projection,
    value_projection,
    w_out,
    w_gate,
    w_up,
    w_down,
):
    bf16, f32 = jnp.bfloat16, jnp.float32
    sequence_total, segment_length, width = tokens.shape
    total_length = places.shape[1]
    line = lax.axis_size("context")
    narrow = key_projection.shape[1]
    run = w_query.shape[0]
    swap = [(i, i ^ 1) for i in range(lax.axis_size("fsdp"))]
    gates, ups, downs = ((w, lax.ppermute(w, "fsdp", swap)) for w in (w_gate, w_up, w_down))
    position = lax.axis_index("context")
    local_positions = lax.dynamic_slice_in_dim(places, position * segment_length, segment_length, 1)
    rotary_angles = local_positions.reshape(segment_length).astype(f32)[:, None] * frequencies(
        HEAD_SIZE // 2
    )
    extra = jnp.pad(jnp.stack([gain_attn, gain_mlp]), ((0, run - 2), (0, 0)))
    pieces = (w_query, key_projection, value_projection, extra, w_out)
    cosine, sine = jnp.cos(rotary_angles), jnp.sin(rotary_angles)
    cosine = jnp.concatenate([cosine] * 4, axis=1)
    sine = jnp.concatenate([-sine, sine] * 2, axis=1)
    allowed = places.reshape(1, total_length) <= local_positions.reshape(segment_length, 1)
    bias = jnp.where(allowed, 0.0, -1e30).astype(f32)
    tangent = cotangent.reshape(segment_length, width)
    tangent_f = tangent.astype(f32)
    rows = tokens.reshape(segment_length, width)
    (
        attended, middle, normed_mlp, normed_tokens, scaled_query, logs, keyed_all, tangent_all, weights,
    ) = front_call(pieces, rows, tangent, bias, cosine, sine, line)
    mid = width + 2 * narrow
    gain_first = weights[:, 0, mid : mid + run].reshape(width).astype(f32)
    gain_second = weights[:, 1, mid : mid + run].reshape(width).astype(f32)
    grad_normed, _, hidden_all, *sums = feed_call(normed_mlp, tangent_all, gates, ups, downs, line)[:9]
    factor_two = lax.rsqrt(jnp.mean(middle * middle, axis=-1, keepdims=True) + norm_eps)
    unit_two = middle * factor_two
    scaled_two = grad_normed * gain_second
    term_gain_two = jnp.sum(grad_normed * unit_two, axis=0)
    grad_middle = tangent_f + factor_two * (
        scaled_two - unit_two * jnp.mean(scaled_two * unit_two, axis=-1, keepdims=True)
    )
    grad_branch = grad_middle.astype(bf16)
    branch, grad_qkv, *others = back_call(
        scaled_query, keyed_all, grad_branch, bias, logs, hidden_all, downs, weights, cosine, -sine,
        sums[:3], sums[3:], normed_tokens, attended, line,
    )
    outcome = middle + branch
    grad_w_gate, grad_w_up, grad_w_down = (
        a.astype(f32) + b.astype(f32) for a, b in zip(sums[:3], others[:3])
    )
    packed, grad_w_out, grad_tokens = sums_call(
        normed_tokens, attended, grad_qkv, grad_branch, others[3:], rows, grad_middle, weights,
        gain_first.reshape(1, width), term_gain_two.reshape(1, width), line,
    )
    gains = packed[run * 3 // 4 : run * 3 // 4 + 2, mid:]
    ends, start = [], 0
    for size in (width, narrow, narrow):
        ends.append(packed[:, start : start + size])
        start += size
    return (
        outcome.astype(bf16).reshape(tokens.shape),
        grad_tokens.reshape(tokens.shape),
        *ends,
        grad_w_out,
        grad_w_gate,
        grad_w_up,
        grad_w_down,
        gains[0],
        gains[1],
    )


def solution(mesh):
    placed = (
        P(("replica", "fsdp"), "context", None),
        P(("replica", "fsdp"), None),
        P(("replica", "fsdp"), "context", None),
        P(("fsdp", "context")),
        P(("fsdp", "context")),
        P(("fsdp", "context"), None),
        P(("fsdp", "context"), None),
        P(("fsdp", "context"), None),
        P(("fsdp", "context"), None),
        P(None, ("fsdp", "context")),
        P(None, ("fsdp", "context")),
        P(("fsdp", "context"), None),
    )
    kernels = (mesh.shape["replica"], mesh.shape["fsdp"], mesh.shape["context"]) == (2, 4, 4)
    return jax.shard_map(
        kernel_body if kernels else body,
        mesh=mesh,
        in_specs=placed,
        out_specs=(
            P(("replica", "fsdp"), "context", None),
            P(("replica", "fsdp"), "context", None),
            P(("fsdp", "context"), None),
            P(("fsdp", "context"), None),
            P(("fsdp", "context"), None),
            P(("fsdp", "context"), None),
            P(None, ("fsdp", "context")),
            P(None, ("fsdp", "context")),
            P(("fsdp", "context"), None),
            P(("fsdp", "context")),
            P(("fsdp", "context")),
        ),
        check_vma=False,
    )
```

```python
import functools

import jax
import jax.numpy as jnp
from jax import lax
from jax.experimental import pallas as pl
from jax.experimental.pallas import tpu as pltpu
from jax.sharding import PartitionSpec as P

QUERY_HEADS = 32
KEY_VALUE_HEADS = 8
HEAD_SIZE = 64


norm_eps = 1e-05
rope_base = 500000.0


def frequencies(half):
    return rope_base ** (-2.0 * jnp.arange(half, dtype=jnp.float32) / (2.0 * half))


def apply_rotary(angle_table, rotary_angles):
    half = angle_table.shape[-1] // 2
    first_half = angle_table[..., :half]
    second_half = angle_table[..., half:]
    cosine = jnp.cos(rotary_angles)[..., None, :]
    sine = jnp.sin(rotary_angles)[..., None, :]
    return jnp.concatenate(
        [first_half * cosine - second_half * sine, second_half * cosine + first_half * sine],
        axis=-1,
    )


def inverse_rotary(angle_table, rotary_angles):
    half = angle_table.shape[-1] // 2
    first_half = angle_table[..., :half]
    second_half = angle_table[..., half:]
    cosine = jnp.cos(rotary_angles)[..., None, :]
    sine = jnp.sin(rotary_angles)[..., None, :]
    return jnp.concatenate(
        [first_half * cosine + second_half * sine, second_half * cosine - first_half * sine],
        axis=-1,
    )


def times_t(left, right):
    return lax.dot_general(
        left, right, (((0,), (0,)), ((), ())), preferred_element_type=jnp.float32
    )


def times_nt(left, right):
    return lax.dot_general(
        left, right, (((1,), (1,)), ((), ())), preferred_element_type=jnp.float32
    )


def query_head_rows(angle_table, sequence_total, segment_length):
    reshaped_heads = angle_table.reshape(
        sequence_total, segment_length, KEY_VALUE_HEADS, QUERY_HEADS // KEY_VALUE_HEADS, HEAD_SIZE
    )
    return jnp.transpose(reshaped_heads, (0, 2, 1, 3, 4)).reshape(
        sequence_total * KEY_VALUE_HEADS, segment_length, QUERY_HEADS // KEY_VALUE_HEADS, HEAD_SIZE
    )


def key_heads(angle_table, sequence_total, total_length):
    reshaped_heads = angle_table.reshape(sequence_total, total_length, KEY_VALUE_HEADS, HEAD_SIZE)
    return jnp.transpose(reshaped_heads, (0, 2, 1, 3)).reshape(
        sequence_total * KEY_VALUE_HEADS, total_length, HEAD_SIZE
    )


def merge_queries(angle_table, sequence_total, segment_length):
    reshaped_heads = angle_table.reshape(
        sequence_total, KEY_VALUE_HEADS, segment_length, QUERY_HEADS // KEY_VALUE_HEADS, HEAD_SIZE
    )
    return jnp.transpose(reshaped_heads, (0, 2, 1, 3, 4)).reshape(
        sequence_total * segment_length, QUERY_HEADS * HEAD_SIZE
    )


def merge_keys(angle_table, sequence_total, total_length):
    reshaped_heads = angle_table.reshape(sequence_total, KEY_VALUE_HEADS, total_length, HEAD_SIZE)
    return jnp.transpose(reshaped_heads, (0, 2, 1, 3)).reshape(
        sequence_total, total_length, KEY_VALUE_HEADS * HEAD_SIZE
    )


def softmax_weights(part_query, part_key, place_query, place_key):
    allowed = place_key[None, :] <= place_query[:, None]
    scores = jnp.einsum(
        "qrd,kd->rqk", part_query, part_key, preferred_element_type=jnp.float32
    ) * HEAD_SIZE ** (-0.5)
    scores = jnp.where(allowed[None], scores, -1e30)
    return jax.nn.softmax(scores, axis=-1)


def forward_head(packed):
    part_query, part_key, part_value, place_query, place_key = packed
    probs = softmax_weights(part_query, part_key, place_query, place_key)
    return jnp.einsum(
        "rqk,kd->qrd", probs.astype(jnp.bfloat16), part_value, preferred_element_type=jnp.float32
    )


def backward_head(packed):
    part_query, part_key, part_value, part_grad, place_query, place_key = packed
    probs = softmax_weights(part_query, part_key, place_query, place_key)
    grad_probs = jnp.einsum(
        "qrd,kd->rqk", part_grad, part_value, preferred_element_type=jnp.float32
    )
    row_delta = jnp.sum(probs * grad_probs, axis=-1, keepdims=True)
    grad_scores = (probs * (grad_probs - row_delta)).astype(jnp.bfloat16)
    grad_query = jnp.einsum(
        "rqk,kd->qrd", grad_scores, part_key, preferred_element_type=jnp.float32
    ) * HEAD_SIZE ** (-0.5)
    grad_key = jnp.einsum(
        "rqk,qrd->kd", grad_scores, part_query, preferred_element_type=jnp.float32
    ) * HEAD_SIZE ** (-0.5)
    value_gradient = jnp.einsum(
        "rqk,qrd->kd", probs.astype(jnp.bfloat16), part_grad, preferred_element_type=jnp.float32
    )
    return (grad_query, grad_key, value_gradient)


def feed_forward(normed_rows, gate_w, up_w, down_w):
    gate_pre = jnp.dot(normed_rows, gate_w, preferred_element_type=jnp.float32)
    up_proj = jnp.dot(normed_rows, up_w, preferred_element_type=jnp.float32)
    sigmoid_gate = jax.nn.sigmoid(gate_pre)
    hidden = (gate_pre * sigmoid_gate * up_proj).astype(jnp.bfloat16)
    return (
        jnp.dot(hidden, down_w, preferred_element_type=jnp.float32),
        (gate_pre, up_proj, sigmoid_gate, hidden),
    )


def feed_back(normed_rows, grad_rows, gate_w, up_w, down_w, kept_values):
    gate_pre, up_proj, sigmoid_gate, hidden = kept_values
    grad_hidden = times_nt(grad_rows, down_w)
    term_down = times_t(hidden, grad_rows)
    grad_gate = (
        grad_hidden * up_proj * (sigmoid_gate * (1.0 + gate_pre * (1.0 - sigmoid_gate)))
    ).astype(jnp.bfloat16)
    grad_up = (grad_hidden * (gate_pre * sigmoid_gate)).astype(jnp.bfloat16)
    grad_normed = times_nt(grad_gate, gate_w) + times_nt(grad_up, up_w)
    return (grad_normed, times_t(normed_rows, grad_gate), times_t(normed_rows, grad_up), term_down)


MESH = pl.DeviceIdType.MESH
ANY = pl.BlockSpec(memory_space=pl.ANY)
BF = jnp.bfloat16
F32 = jnp.float32
NN = (((1,), (0,)), ((), ()))
NT = (((1,), (1,)), ((), ()))
TN = (((0,), (0,)), ((), ()))


EARLY = 3


def dot(left, right, dims):
    return lax.dot_general(left, right, dims, preferred_element_type=F32)


class Grid:
    def __init__(self, chips, line):
        self.chips, self.line = chips, line
        self.replica = lax.axis_index("replica")
        flat = lax.axis_index("fsdp")
        self.x, self.core = flat // 2, flat % 2
        self.z = lax.axis_index("context")
        self.has_left, self.has_right = self.z > 0, self.z + 1 < line
        self.left = (self.replica, flat, self.z - 1)
        self.right = (self.replica, flat, self.z + 1)
        self.across = (self.replica, (1 - self.x) * 2 + self.core, self.z)
        self.twin = (self.replica, self.x * 2 + 1 - self.core, self.z)
        self.mirror = (1 - self.replica, flat, self.z)

    def order(self, k):
        z, n = self.z, self.line
        low = 2 * z < n
        near = 2 * jnp.minimum(z, n - 1 - z)
        away = jnp.where(k % 2 == 1, -((k + 1) // 2), k // 2)
        return jnp.where(
            k <= near, z + jnp.where(low, away, -away), jnp.where(low, k, n - 1 - k)
        )

    def slot(self, x, z):
        return x * self.line + z

    def greet(self, twin, mirror=False):
        barrier = pltpu.get_barrier_semaphore()

        def tell(device):
            pl.semaphore_signal(barrier, inc=1, device_id=device, device_id_type=MESH)

        pl.when(self.has_left)(lambda: tell(self.left))
        pl.when(self.has_right)(lambda: tell(self.right))
        tell(self.across)
        if twin:
            tell(self.twin)
        if mirror:
            tell(self.mirror)
        count = 1 + int(twin) + int(mirror) + self.has_left.astype(jnp.int32) + self.has_right.astype(jnp.int32)
        pl.semaphore_wait(barrier, count)


def remote(src, dst, send, recv, device):
    return pltpu.make_async_remote_copy(
        src_ref=src, dst_ref=dst, send_sem=send, recv_sem=recv, device_id=device, device_id_type=MESH
    )


def each(count, action):
    def step(i, carry):
        action(i)
        return carry

    lax.fori_loop(0, count, step, 0)


class Gather:
    def __init__(self, grid, block, everything, send, recv, parts, cross=None):
        self.grid, self.everything, self.send, self.recv = grid, everything, send, recv
        self.block, self.cross = block, cross
        self.rows = everything.shape[1] // parts
        self.last = parts - 1
        self.early = parts if cross is None else parts - 1

    def piece(self, x, z, part):
        start = pl.multiple_of(part * self.rows, self.rows)
        return self.everything.at[self.grid.slot(x, z), pl.ds(start, self.rows)]

    def copy(self, z, part, link, first=False):
        grid = self.grid
        device = (grid.right, grid.left, grid.across)[link]
        there = self.piece(grid.x, z, part)
        start = pl.multiple_of(part * self.rows, self.rows)
        here = self.block.at[pl.ds(start, self.rows)] if first else there
        return remote(
            here, there, self.send.at[z, part, link], self.recv.at[grid.slot(grid.x, z), part], device
        )

    def other(self, z, link):
        grid = self.grid
        here = self.piece(1 - grid.x, z, self.last)
        sem = self.recv.at[grid.slot(1 - grid.x, z), self.last]
        return remote(here, here, self.cross.at[z, link], sem, (grid.right, grid.left)[link])

    def ways(self, z):
        grid = self.grid
        return (
            (0, jnp.logical_and(z <= grid.z, grid.has_right)),
            (1, jnp.logical_and(z >= grid.z, grid.has_left)),
        )

    def sides(self, distance):
        grid = self.grid
        return (
            (grid.z - distance, grid.z >= distance, 0, grid.has_right),
            (grid.z + distance, grid.z + distance < grid.line, 1, grid.has_left),
        )

    def links(self, z, part, action, first=False, across=True):
        for link, go in self.ways(z):
            pl.when(go)(lambda link=link: action(self.copy(z, part, link, first)))
        if across:
            action(self.copy(z, part, 2, first))

    def send_own(self):
        grid = self.grid
        start = lambda c: c.start()
        if self.cross is not None:
            self.copy(grid.z, self.last, 2, True).start()
        each(self.early, lambda part: self.links(grid.z, part, start, True))
        if self.cross is not None:
            self.links(grid.z, self.last, start, True, False)

    def turn_in(self):
        grid = self.grid
        self.other(grid.z, 0).wait_recv()
        for link, go in self.ways(grid.z):
            pl.when(go)(lambda link=link: self.other(grid.z, link).start())

    def forward(self, distance, part, wait=True, along=True, across=True):
        for z, there, link, go in self.sides(distance):

            @pl.when(there)
            def _(z=z, link=link, go=go):
                if wait:
                    self.copy(z, part, 2).wait_recv()
                if along:
                    pl.when(go)(lambda: self.copy(z, part, link).start())
                if across:
                    self.copy(z, part, 2).start()

    def forward_last(self, distance):
        for z, there, link, go in self.sides(distance):

            @pl.when(there)
            def _(z=z, link=link, go=go):
                self.copy(z, self.last, 2).wait_recv()
                pl.when(go)(lambda: self.copy(z, self.last, link).start())
                self.other(z, link).wait_recv()
                pl.when(go)(lambda: self.other(z, link).start())

    def wait_across(self, z):
        grid = self.grid

        def wait(part):
            here = self.piece(1 - grid.x, z, part)
            sem = self.recv.at[grid.slot(1 - grid.x, z), part]
            remote(here, here, self.send.at[z, part, 2], sem, grid.across).wait_recv()

        each(self.early, wait)

    def finish(self):
        done = lambda c: c.wait_send()

        def place(z):
            each(self.early, lambda part: self.links(z, part, done))
            if self.cross is not None:
                self.links(z, self.last, done, across=False)
                for link, go in self.ways(z):
                    pl.when(go)(lambda link=link: self.other(z, link).wait_send())

        each(self.grid.line, place)
        if self.cross is not None:
            self.copy(self.grid.z, self.last, 2).wait_send()


class Scatter:
    def __init__(self, grid, partial, from_across, from_line, total, sems, parts, cross=None):
        self.grid, self.partial, self.from_across = grid, partial, from_across
        self.from_line, self.total = from_line, total
        self.across_send, self.across_recv, self.line_send, self.line_recv = sems
        self.parts, self.cross = parts, cross
        self.rows = partial.shape[1] // parts
        self.early = parts if cross is None else parts - 1
        self.last = parts - 1

    def run(self, part):
        return pl.ds(pl.multiple_of(part * self.rows, self.rows), self.rows)

    def steps(self):
        return (self.grid.line - 1) * self.early

    def rank(self, j):
        return self.grid.order(self.grid.line - 1 - j)

    def step(self, n):
        self.pass_on(self.rank(n // self.early), n % self.early)

    def place(self, z):
        return z if self.from_across is None else self.grid.slot(self.grid.x, z)

    def across(self, z, part):
        grid = self.grid
        return remote(
            self.partial.at[grid.slot(1 - grid.x, z), self.run(part)],
            self.from_across.at[z, self.run(part)],
            self.across_send.at[z, part],
            self.across_recv.at[z, part],
            grid.across,
        )

    def arrival(self, z, leftward):
        return z if leftward else z - 1 + self.grid.line - 1

    def along(self, z, part, leftward):
        grid = self.grid
        arrival = self.arrival(z, leftward)
        return remote(
            self.partial.at[self.place(z), self.run(part)],
            self.from_line.at[arrival, self.run(part)],
            self.line_send.at[z, part],
            self.line_recv.at[arrival, part],
            grid.left if leftward else grid.right,
        )

    def other(self, z, leftward):
        grid = self.grid
        buffer, send, recv = self.cross
        arrival = self.arrival(z, leftward)
        return remote(
            self.partial.at[grid.slot(1 - grid.x, z), self.run(self.last)],
            buffer.at[arrival],
            send.at[z],
            recv.at[arrival],
            grid.left if leftward else grid.right,
        )

    def send_across(self, z):
        each(self.early, lambda part: self.across(z, part).start())

    def both_ways(self, z, action):
        grid = self.grid
        pl.when(jnp.logical_and(z <= grid.z, grid.has_right))(lambda: action(True))
        pl.when(jnp.logical_and(z >= grid.z, grid.has_left))(lambda: action(False))

    def add_line(self, z, part):
        def add(leftward):
            self.along(z, part, leftward).wait_recv()
            arrival = self.arrival(z, leftward)
            self.total[...] += self.from_line[arrival, self.run(part)].astype(F32)

        self.both_ways(z, add)

    def gather_sum(self, z, part):
        value = self.partial[self.place(z), self.run(part)].astype(F32)
        if self.from_across is not None:
            self.across(z, part).wait_recv()
            value = value + self.from_across[z, self.run(part)].astype(F32)
        self.total[...] = value
        self.add_line(z, part)

    def send_along(self, z, part):
        grid = self.grid
        self.partial[self.place(z), self.run(part)] = self.total[...].astype(BF)
        pl.when(z < grid.z)(lambda: self.along(z, part, True).start())
        pl.when(z > grid.z)(lambda: self.along(z, part, False).start())

    def pass_on(self, z, part):
        self.gather_sum(z, part)
        self.send_along(z, part)

    def add_other(self, z):
        grid, run = self.grid, self.run(self.last)
        slot = grid.slot(1 - grid.x, z)
        self.total[...] = self.partial[slot, run].astype(F32)

        def add(leftward):
            self.other(z, leftward).wait_recv()
            self.total[...] += self.cross[0][self.arrival(z, leftward)].astype(F32)

        self.both_ways(z, add)
        self.partial[slot, run] = self.total[...].astype(BF)

    def last_step(self, m):
        grid = self.grid
        z = grid.order(grid.line - 1 - m)
        self.add_other(z)

        @pl.when(z == grid.z)
        def _():
            self.across(z, self.last).start()

        @pl.when(z != grid.z)
        def _():
            pl.when(z < grid.z)(lambda: self.other(z, True).start())
            pl.when(z > grid.z)(lambda: self.other(z, False).start())
            self.total[...] = self.partial[self.place(z), self.run(self.last)].astype(F32)
            self.add_line(z, self.last)
            self.send_along(z, self.last)

    def own(self, result):
        def part_sum(part):
            self.gather_sum(self.grid.z, part)
            result[self.run(part)] = self.total[...]

        each(self.parts, part_sum)

    def finish(self):
        grid = self.grid

        def place(z):
            def part_done(part):
                pl.when(z < grid.z)(lambda: self.along(z, part, True).wait_send())
                pl.when(z > grid.z)(lambda: self.along(z, part, False).wait_send())

            each(self.parts, part_done)
            if self.from_across is not None:
                each(self.early, lambda part: self.across(z, part).wait_send())
            if self.cross is not None:
                pl.when(z < grid.z)(lambda: self.other(z, True).wait_send())
                pl.when(z > grid.z)(lambda: self.other(z, False).wait_send())

        each(grid.line, place)
        if self.cross is not None:
            self.across(grid.z, self.last).wait_send()


def scatter_scratch(line, rows, width, parts):
    return [
        pltpu.VMEM((2 * line, rows, width), BF),
        pltpu.VMEM((line, rows, width), BF),
        pltpu.VMEM((2 * line - 2, rows, width), BF),
        pltpu.VMEM((rows // parts, width), F32),
        pltpu.SemaphoreType.DMA((line, parts)),
        pltpu.SemaphoreType.DMA((line, parts)),
        pltpu.SemaphoreType.DMA((line, parts)),
        pltpu.SemaphoreType.DMA((2 * line - 2, parts)),
    ]


def load_pairs(pairs, sems):
    copies = [pltpu.make_async_copy(src, dst, sems.at[i]) for i, (src, dst) in enumerate(pairs)]
    for copy in copies:
        copy.start()
    for copy in copies:
        copy.wait()


def feed_kernel(
    line, parts, tile,
    normed, tangent_all, gate_own, gate_twin, up_own, up_twin, down_own, down_twin,
    grad_sum, normed_all, hidden_all, grad_gate, grad_up, grad_down,
    mirror_gate, mirror_up, mirror_down, part_gate, part_up, part_down,
    mirror_send, mirror_recv,
    gate_w, up_w, down_w, hidden, dgate, dup, rows_n, rows_t,
    partial, from_across, from_line, total, across_send, across_recv, line_send, line_recv,
    other_line, other_send, other_recv, gather_cross,
    gather_send, gather_recv, load_sem, wide, tile_sem, stage_a, stage_b, stage_sem, stage_recv, piece_a, piece_b, piece_sem, hidden_sem,
):
    grid = Grid(2, line)
    rows, width = normed.shape
    cols = gate_own.shape[1]
    blocks = 2 * line
    me = grid.slot(grid.x, grid.z)
    grid.greet(True, True)
    gather = Gather(grid, normed, normed_all, gather_send, gather_recv, parts, gather_cross)
    scatter = Scatter(
        grid, partial, from_across, from_line, total,
        (across_send, across_recv, line_send, line_recv), parts,
        (other_line, other_send, other_recv),
    )
    gather.send_own()
    load_pairs(
        [
            (gate_own, gate_w.at[:, pl.ds(0, cols)]),
            (gate_twin, gate_w.at[:, pl.ds(cols, cols)]),
            (up_own, up_w.at[:, pl.ds(0, cols)]),
            (up_twin, up_w.at[:, pl.ds(cols, cols)]),
            (down_own, down_w.at[pl.ds(0, cols)]),
            (down_twin, down_w.at[pl.ds(cols, cols)]),
            (normed, rows_n),
        ],
        load_sem,
    )
    load_pairs([(rows_n, normed_all.at[me])], load_sem)
    gather.turn_in()

    forwards = (line - 1) * parts

    def advance(n):
        distance, part = n // parts + 1, n % parts

        @pl.when(n < forwards)
        def _():
            pl.when(part < gather.early)(lambda: gather.forward(distance, part))
            pl.when(part == gather.last)(lambda: gather.forward_last(distance))

        return n + 1

    def work(slot, n):
        tangent_load = pltpu.make_async_copy(tangent_all.at[slot], rows_t, load_sem.at[1])
        tangent_load.start()
        load_pairs([(normed_all.at[slot], rows_n)], load_sem)
        spot = pl.ds(pl.multiple_of(slot * rows, rows), rows)

        def hidden_tile(j, n):
            c = pl.ds(pl.multiple_of(j * cols, cols), cols)
            gate = dot(rows_n[...], gate_w[:, c], NN)
            up = dot(rows_n[...], up_w[:, c], NN)
            pl.when(j == 0)(tangent_load.wait)
            grad = dot(rows_t[...], down_w[c, :], NT)
            sig = jax.nn.sigmoid(gate)
            silu = gate * sig
            hidden[spot, c] = (silu * up).astype(BF)
            dgate[spot, c] = (grad * up * (sig * (1.0 + gate * (1.0 - sig)))).astype(BF)
            dup[spot, c] = (grad * silu).astype(BF)
            return advance(n)

        n = lax.fori_loop(0, 2, hidden_tile, n)

        def back_tile(j, carry):
            c = pl.ds(pl.multiple_of(j * cols, cols), cols)
            sums = dot(dgate[spot, :], gate_w[c, :], NT) + dot(dup[spot, :], up_w[c, :], NT)
            partial[slot, :, c] = sums.astype(BF)
            return carry

        lax.fori_loop(0, width // cols, back_tile, 0)
        return advance(n)

    def stage(distance, n):
        def visit(i, n):
            z = grid.z + jnp.where(i % 2 == 0, -distance, distance)
            inside = jnp.logical_and(z >= 0, z < line)

            def block(n):
                n = lax.fori_loop(n, jnp.maximum(n, distance * parts), lambda m, c: advance(m), n)
                pl.when(i >= 2)(lambda: gather.wait_across(z))
                return work(grid.slot(jnp.where(i < 2, grid.x, 1 - grid.x), z), n)

            go = jnp.logical_and(inside, jnp.logical_or(distance > 0, i % 2 == 0))
            return lax.cond(go, block, lambda n: n, n)

        return lax.fori_loop(0, 4, visit, n)

    count = lax.fori_loop(0, line, stage, 0)
    lax.fori_loop(count, jnp.maximum(count, forwards), lambda m, c: advance(m), 0)
    hidden_copy = pltpu.make_async_copy(hidden, hidden_all, hidden_sem)
    hidden_copy.start()
    for j in range(line):
        scatter.send_across(scatter.rank(j))

    tiles = width // tile

    early_tiles = mirror_send.shape[0]

    def wide_loads(t, start):
        j, buf = t % tiles, t % 2
        c = pl.ds(pl.multiple_of(j * tile, tile), tile)
        for i, source in enumerate((normed_all, tangent_all)):
            copy = pltpu.make_async_copy(source.at[:, :, c], wide.at[buf, i], tile_sem.at[buf, i])
            copy.start() if start else copy.wait()

    def stages(t):
        j, buf = t % tiles, t % 2
        c = pl.ds(pl.multiple_of(j * tile, tile), tile)
        return [
            remote(src, dst, stage_sem.at[buf, i], stage_recv.at[j, i], grid.twin)
            for i, (src, dst) in enumerate(
                (
                    (stage_a.at[buf, 0], part_gate.at[c, :]),
                    (stage_a.at[buf, 1], part_up.at[c, :]),
                    (stage_b.at[buf], part_down.at[:, c]),
                )
            )
        ]

    def results(t):
        j, buf = t % tiles, t % 2
        c = pl.ds(pl.multiple_of(j * tile, tile), tile)
        return [
            pltpu.make_async_copy(src, dst, stage_sem.at[buf, i])
            for i, (src, dst) in enumerate(
                (
                    (stage_a.at[buf, 0], grad_gate.at[c, :]),
                    (stage_a.at[buf, 1], grad_up.at[c, :]),
                    (stage_b.at[buf], grad_down.at[:, c]),
                )
            )
        ]

    def mirrored(t):
        j = t % tiles
        c = pl.ds(pl.multiple_of(j * tile, tile), tile)
        return [
            remote(src, dst, mirror_send.at[j, i], mirror_recv.at[j, i], grid.mirror)
            for i, (src, dst) in enumerate(
                (
                    (grad_gate.at[c, :], mirror_gate.at[c, :]),
                    (grad_up.at[c, :], mirror_up.at[c, :]),
                    (grad_down.at[:, c], mirror_down.at[:, c]),
                )
            )
        ]

    def pieces(t):
        c = pl.ds(pl.multiple_of((t % tiles) * tile, tile), tile)
        return [
            (part_gate.at[c, :], piece_a.at[0]),
            (part_up.at[c, :], piece_a.at[1]),
            (part_down.at[:, c], piece_b),
        ]

    wide_loads(0, True)

    def weights(t, carry):
        buf = t % 2
        pl.when(t + 1 < 2 * tiles)(lambda: wide_loads(t + 1, True))
        wide_loads(t, False)
        tall = blocks * rows
        tokens = wide[buf, 0].reshape(tall, tile)
        tangents = wide[buf, 1].reshape(tall, tile)

        @pl.when(t < tiles)
        def _():
            theirs = slice(cols, 2 * cols)

            @pl.when(t >= 2)
            def _():
                for copy in stages(t - 2):
                    copy.wait_send()

            stage_a[buf, 0] = dot(tokens, dgate[:, theirs], TN).astype(BF)
            stage_a[buf, 1] = dot(tokens, dup[:, theirs], TN).astype(BF)
            stage_b[buf] = dot(hidden[:, theirs], tangents, TN).astype(BF)
            for copy in stages(t):
                copy.start()

        @pl.when(t >= tiles)
        def _():
            for copy in stages(t):
                copy.wait_recv()
            loads = [
                pltpu.make_async_copy(src, dst, piece_sem.at[i])
                for i, (src, dst) in enumerate(pieces(t))
            ]
            for copy in loads:
                copy.start()

            @pl.when(t < tiles + 2)
            def _():
                for copy in stages(t - 2):
                    copy.wait_send()

            @pl.when(t >= tiles + 2)
            def _():
                for copy in results(t - 2):
                    copy.wait()

                @pl.when(t < tiles + 2 + early_tiles)
                def _():
                    for copy in mirrored(t - 2):
                        copy.start()

            mine = slice(0, cols)
            own_gate = dot(tokens, dgate[:, mine], TN)
            own_up = dot(tokens, dup[:, mine], TN)
            own_down = dot(hidden[:, mine], tangents, TN)
            for copy in loads:
                copy.wait()
            stage_a[buf, 0] = (own_gate + piece_a[0].astype(F32)).astype(BF)
            stage_a[buf, 1] = (own_up + piece_a[1].astype(F32)).astype(BF)
            stage_b[buf] = (own_down + piece_b[...].astype(F32)).astype(BF)
            for copy in results(t):
                copy.start()

        n = t - 2 * lag
        pl.when(n >= 0)(lambda: scatter.step(n))
        m = t // 3 - lag
        ready = jnp.logical_and(t % 3 == 2, jnp.logical_and(m >= 0, m < line))
        pl.when(ready)(lambda: scatter.last_step(m))
        return carry

    lag = jnp.where(jnp.logical_and(grid.has_left, grid.has_right), 1, 0)
    lax.fori_loop(0, 2 * tiles, weights, 0)

    def rest(n, carry):
        scatter.step(n)
        return carry

    lax.fori_loop(2 * tiles - 2 * lag, scatter.steps(), rest, 0)
    scatter.own(grad_sum)
    for t in (2 * tiles - 2, 2 * tiles - 1):
        for copy in results(t):
            copy.wait()
    gather.finish()
    scatter.finish()
    hidden_copy.wait()
    for t in range(early_tiles):
        for copy in mirrored(t):
            copy.wait()


def feed_call(normed, tangent_all, gates, ups, downs, line):
    rows, width = normed.shape
    cols = gates[0].shape[1]
    blocks, parts, tile = 2 * line, 8, 256
    tiles = width // tile
    tall = blocks * rows
    shapes = jax.ShapeDtypeStruct
    hbm = lambda *s: shapes(s, BF)
    return pl.pallas_call(
        functools.partial(feed_kernel, line, parts, tile),
        out_shape=(
            shapes((rows, width), F32),
            hbm(blocks, rows, width), hbm(tall, 2 * cols),
            hbm(width, cols), hbm(width, cols), hbm(cols, width),
            hbm(width, cols), hbm(width, cols), hbm(cols, width),
            hbm(width, cols), hbm(width, cols), hbm(cols, width),
        ),
        in_specs=[ANY] * 8,
        out_specs=(pl.BlockSpec(memory_space=pltpu.VMEM),) + (ANY,) * 11,
        scratch_shapes=[
            pltpu.SemaphoreType.DMA((EARLY, 3)), pltpu.SemaphoreType.DMA((EARLY, 3)),
            pltpu.VMEM((width, 2 * cols), BF), pltpu.VMEM((width, 2 * cols), BF), pltpu.VMEM((2 * cols, width), BF),
            pltpu.VMEM((tall, 2 * cols), BF), pltpu.VMEM((tall, 2 * cols), BF), pltpu.VMEM((tall, 2 * cols), BF),
            pltpu.VMEM((rows, width), BF), pltpu.VMEM((rows, width), BF),
            *scatter_scratch(line, rows, width, parts),
            pltpu.VMEM((2 * line - 2, rows // parts, width), BF),
            pltpu.SemaphoreType.DMA((line,)), pltpu.SemaphoreType.DMA((2 * line - 2,)),
            pltpu.SemaphoreType.DMA((line, 2)),
            pltpu.SemaphoreType.DMA((line, parts, 3)), pltpu.SemaphoreType.DMA((blocks, parts)),
            pltpu.SemaphoreType.DMA((8,)),
            pltpu.VMEM((2, 2, blocks, rows, tile), BF), pltpu.SemaphoreType.DMA((2, 2)),
            pltpu.VMEM((2, 2, tile, cols), BF), pltpu.VMEM((2, cols, tile), BF),
            pltpu.SemaphoreType.DMA((2, 3)), pltpu.SemaphoreType.DMA((tiles, 3)),
            pltpu.VMEM((2, tile, cols), BF), pltpu.VMEM((cols, tile), BF), pltpu.SemaphoreType.DMA((3,)),
            pltpu.SemaphoreType.DMA,
        ],
        compiler_params=pltpu.CompilerParams(
            collective_id=1, has_side_effects=True, vmem_limit_bytes=63 * 2**20
        ),
        name="feed",
    )(normed, tangent_all, gates[0], gates[1], ups[0], ups[1], downs[0], downs[1])


class Thirds(Scatter):
    def run(self, part):
        quarter = self.rows
        start = jnp.where(part == 2, self.grid.replica, 2 + part) * quarter
        return pl.ds(pl.multiple_of(start, quarter), quarter)


def sums_kernel(
    line,
    normed, attended, grad_qkv, grad_out, twin_normed, twin_attended, twin_out, out_across,
    tokens, grad_middle, weights, gain, term_two,
    result, result_out, grad_tokens,
    across_v, out_partial, out_line, out_total, out_send, out_recv, out_mine, out_theirs, out_sem,
    near_send, near_recv, near_sem,
    both_normed, both_attended, both_qkv, both_out, load_sem, twin_send, twin_recv,
    partial, from_across, from_line, total, across_send, across_recv, line_send, line_recv,
    mine, theirs, mirror_send, mirror_recv, from_mirror, quarter_send, quarter_recv,
    in_weights, weight_sem, token_v, middle_v, grad_normed, terms, own_terms, twin_terms,
):
    grid = Grid(2, line)
    rows, width = normed.shape
    run = partial.shape[1]
    quarter = run // 4
    narrow = grad_qkv.shape[1]
    grid.greet(True, True)
    scatter = Thirds(
        grid, partial, from_across, from_line, total,
        (across_send, across_recv, line_send, line_recv), 3,
    )
    scatter.rows = quarter
    own, twin = pl.ds(0, rows), pl.ds(rows, rows)
    swap_qkv = remote(grad_qkv, both_qkv.at[twin], twin_send.at[0], twin_recv.at[0], grid.twin)
    swap_qkv.start()
    load_pairs(
        [
            (attended, both_attended.at[own]),
            (twin_attended, both_attended.at[twin]),
            (grad_out, both_out.at[own]),
            (twin_out, both_out.at[twin]),
            (out_across, across_v),
            (normed, both_normed.at[own]),
            (twin_normed, both_normed.at[twin]),
            (grad_qkv, both_qkv.at[own]),
        ],
        load_sem,
    )
    later = [
        pltpu.make_async_copy(src, dst, weight_sem.at[i])
        for i, (src, dst) in enumerate(
            (
                (weights.at[:, :, pl.ds(0, narrow)], in_weights),
                (tokens, token_v),
                (grad_middle, middle_v),
            )
        )
    ]
    for copy in later:
        copy.start()
    tall = line * run
    tile = 512
    away = pl.ds(pl.multiple_of((1 - grid.replica) * quarter, quarter), quarter)
    here = pl.ds(pl.multiple_of(grid.replica * quarter, quarter), quarter)

    outs = Scatter(
        grid, out_partial, None, out_line, out_total, (None, None, out_send, out_recv), 4
    )

    nears = [
        remote(near_send.at[j], near_recv.at[j], near_sem.at[0, j], near_sem.at[1, j], grid.across)
        for j in range(2)
    ]

    def near_step(i):
        c = pl.ds(pl.multiple_of(i * tile, tile), tile)
        for j in range(2):
            first = ((1 - grid.x) * 2 + grid.core) * tall + grid.order(j) * run
            theirs = pl.ds(pl.multiple_of(first, run), run)
            near_send[j, :, c] = dot(both_attended[:, theirs], both_out[:, c], TN).astype(BF)

    def sweep(part):
        each(line - 1, lambda i: scatter.pass_on(scatter.rank(i), part))

    def out_step(i):
        c = pl.ds(pl.multiple_of(i * tile, tile), tile)
        value = dot(both_attended[:, features(grid.x)], both_out[:, c], TN)
        value = value.reshape(line, run, tile) + across_v[:, :, c].astype(F32)
        out_partial[:, :, c] = value.astype(BF)

    def to_mirror(slot):
        return remote(
            partial.at[slot, away], from_mirror.at[slot],
            quarter_send.at[slot], quarter_recv.at[slot], grid.mirror,
        )

    def features(x):
        return pl.ds(pl.multiple_of((x * 2 + grid.core) * tall, tall), tall)

    def column(j, carry):
        x = jnp.where(j == 0, 1 - grid.x, grid.x)
        blocks = pl.ds(x * line, line)

        def wide(left, right, first):
            def step(i, inner):
                c = pl.ds(pl.multiple_of(i * tile, tile), tile)
                to = pl.ds(pl.multiple_of(first + i * tile, 128), tile)
                value = dot(left[:, features(x)], right[:, c], TN).astype(BF)
                partial[blocks, :, to] = value.reshape(line, run, tile)
                return inner

            lax.fori_loop(0, right.shape[1] // tile, step, 0)

        wide(both_normed, both_qkv, 0)
        partial[blocks, :, narrow:] = jnp.zeros((line, run, 128), BF)
        for k in range(line - 1, -1, -1):
            z = grid.order(k)
            to_mirror(grid.slot(x, z)).start()
            pl.when(j == 0)(lambda z=z: scatter.across(z, 0).start())
        return carry

    for j in range(2):
        across_v[grid.order(j)] = jnp.zeros((run, width), BF)
    each(width // tile, near_step)
    nears[1].start()
    each(width // tile, out_step)
    early_outs = (line - 2) * outs.early
    middling = jnp.logical_and(grid.has_left, grid.has_right)

    def when_end(action):
        pl.when(jnp.logical_not(middling))(action)

    when_end(lambda: each(early_outs, outs.step))
    swap_qkv.wait()
    lax.fori_loop(0, 2, column, 0)
    nears[0].start()
    when_end(lambda: sweep(0))
    for copy in later:
        copy.wait()

    def back_step(j, carry):
        units = pl.ds(j * (tile // run), tile // run)
        c = pl.ds(pl.multiple_of(j * tile, tile), tile)
        right = in_weights[units].reshape(tile, narrow)
        grad_normed[:, c] = dot(both_qkv[own, :], right, NT)
        return carry

    lax.fori_loop(0, width // tile, back_step, 0)
    terms[...] = jnp.zeros_like(terms)
    chunk = 64

    def norm_step(j, carry):
        r = pl.ds(pl.multiple_of(j * chunk, chunk), chunk)
        value = token_v[r, :].astype(F32)
        factor = lax.rsqrt(jnp.mean(value * value, axis=1, keepdims=True) + norm_eps)
        unit = value * factor
        grad = grad_normed[r, :]
        terms[0:1, :] += jnp.sum(grad * unit, axis=0, keepdims=True)
        scaled = grad * gain[0:1, :]
        mean = jnp.mean(scaled * unit, axis=1, keepdims=True)
        grad_tokens[r, :] = (middle_v[r, :] + factor * (scaled - unit * mean)).astype(BF)
        return carry

    lax.fori_loop(0, rows // chunk, norm_step, 0)
    terms[1:2, :] = term_two[...]
    own_terms[...] = terms[...].astype(BF)
    swap_terms = remote(own_terms, twin_terms, twin_send.at[1], twin_recv.at[1], grid.twin)
    swap_terms.start()
    swap_terms.wait()
    for x in range(2):
        for z in range(line):
            first = pl.multiple_of((x * 2 + grid.core) * tall + z * run, run)
            c = pl.ds(first, run)
            value = own_terms[:, c].astype(F32) + twin_terms[:, c].astype(F32)
            partial[x * line + z, 3 * quarter : 3 * quarter + 16, narrow:] = value.astype(BF)
    for k in range(line - 1, -1, -1):
        scatter.across(grid.order(k), 1).start()

    def add_mirror(x):
        def step(i, carry):
            slot = grid.slot(x, grid.order(line - 1 - i))
            to_mirror(slot).wait_recv()
            value = partial[slot, here].astype(F32) + from_mirror[slot].astype(F32)
            partial[slot, here] = value.astype(BF)
            return carry

        lax.fori_loop(0, line, step, 0)

    add_mirror(1 - grid.x)
    for k in range(line - 1, -1, -1):
        scatter.across(grid.order(k), 2).start()
    pl.when(middling)(lambda: each(early_outs, outs.step))
    nears[1].wait()
    next_place = grid.order(1)
    out_partial[next_place] = (
        out_partial[next_place].astype(F32) + near_recv[1].astype(F32)
    ).astype(BF)
    pl.when(middling)(lambda: sweep(0))

    def out_rest(n, carry):
        outs.step(n)
        return carry

    lax.fori_loop(early_outs, outs.steps(), out_rest, 0)
    sweep(1)

    def swap(part, whole=True):
        at = scatter.run(part)
        return remote(
            mine.at[at], theirs.at[at], mirror_send.at[part], mirror_recv.at[part], grid.mirror
        )

    def settle(part):
        scatter.gather_sum(grid.z, part)
        mine[scatter.run(part)] = total[...].astype(BF)
        swap(part).start()

    outs.own(result_out)
    nears[0].wait()
    result_out[...] += near_recv[0].astype(F32)
    out_mine[...] = result_out[...].astype(BF)
    out_swap = remote(out_mine, out_theirs, out_sem.at[0], out_sem.at[1], grid.mirror)
    out_swap.start()
    add_mirror(grid.x)
    settle(0)
    sweep(2)
    settle(1)
    settle(2)
    result[here] = mine[here].astype(F32)
    for part in range(2):
        swap(part).wait()
        at = scatter.run(part)
        result[at] = mine[at].astype(F32) + theirs[at].astype(F32)
    swap(2).wait_send()
    remote(mine.at[away], theirs.at[away], mirror_send.at[2], mirror_recv.at[2], grid.mirror).wait_recv()
    result[away] = theirs[away].astype(F32)
    out_swap.wait()
    result_out[...] = out_mine[...].astype(F32) + out_theirs[...].astype(F32)
    outs.finish()
    scatter.finish()

    def sent(slot, carry):
        to_mirror(slot).wait_send()
        return carry

    lax.fori_loop(0, 2 * line, sent, 0)


def sums_call(
    normed, attended, grad_qkv, grad_out, others, tokens, grad_middle, weights, gain, term_two, line
):
    rows, width = normed.shape
    narrow = grad_qkv.shape[1]
    run, whole = weights.shape[1], narrow + 128
    quarter = run // 4
    vmem = pl.BlockSpec(memory_space=pltpu.VMEM)
    dma = pltpu.SemaphoreType.DMA
    like = lambda a: pltpu.VMEM(a.shape, a.dtype)
    return pl.pallas_call(
        functools.partial(sums_kernel, line),
        out_shape=(
            jax.ShapeDtypeStruct((run, whole), F32), jax.ShapeDtypeStruct((run, width), F32),
            jax.ShapeDtypeStruct((rows, width), BF),
        ),
        in_specs=[ANY] * 11 + [vmem] * 2,
        out_specs=(vmem,) * 3,
        scratch_shapes=[
            pltpu.VMEM((line, run, width), BF), pltpu.VMEM((line, run, width), BF),
            pltpu.VMEM((2 * line - 2, run, width), BF), pltpu.VMEM((quarter, width), F32),
            dma((line, 4)), dma((2 * line - 2, 4)),
            pltpu.VMEM((run, width), BF), pltpu.VMEM((run, width), BF), dma((2,)),
            pltpu.VMEM((2, run, width), BF), pltpu.VMEM((2, run, width), BF), dma((2, 2)),
            pltpu.VMEM((2 * rows, width), BF), pltpu.VMEM((2 * rows, width), BF),
            pltpu.VMEM((2 * rows, narrow), BF), pltpu.VMEM((2 * rows, width), BF),
            dma((8,)), dma((2,)), dma((2,)),
            pltpu.VMEM((2 * line, run, whole), BF), pltpu.VMEM((line, run, whole), BF),
            pltpu.VMEM((2 * line - 2, run, whole), BF), pltpu.VMEM((quarter, whole), F32),
            dma((line, 3)), dma((line, 3)), dma((line, 3)), dma((2 * line - 2, 3)),
            pltpu.VMEM((run, whole), BF), pltpu.VMEM((run, whole), BF), dma((3,)), dma((3,)),
            pltpu.VMEM((2 * line, quarter, whole), BF), dma((2 * line,)), dma((2 * line,)),
            pltpu.VMEM((weights.shape[0], run, narrow), BF), dma((3,)),
            like(tokens), like(grad_middle), pltpu.VMEM((rows, width), F32),
            pltpu.VMEM((16, width), F32), pltpu.VMEM((16, width), BF), pltpu.VMEM((16, width), BF),
        ],
        compiler_params=pltpu.CompilerParams(
            collective_id=3, has_side_effects=True, vmem_limit_bytes=63 * 2**20
        ),
        name="sums",
    )(
        normed, attended, grad_qkv, grad_out, *others, tokens, grad_middle, weights, gain, term_two
    )


def gather_weights(
    grid, block, everything, send, recv, twin_send, twin_recv, meanwhile, afterwards
):
    line = grid.line
    rows = block.shape[0] // 4
    carry_a, carry_b = grid.replica * 2, grid.replica * 2 + 1
    other_a, other_b = (1 - grid.replica) * 2, (1 - grid.replica) * 2 + 1
    right, left, across, mirror = range(4)
    devices = (grid.right, grid.left, grid.across, grid.mirror)

    def run(quarter):
        return pl.ds(pl.multiple_of(quarter * rows, rows), rows)

    def place(x, core, z, quarter):
        return everything.at[(x * 2 + core) * line + z, run(quarter)]

    def copy(x, z, quarter, link, first=False):
        there = place(x, grid.core, z, quarter)
        here = block.at[run(quarter)] if first else there
        unit = x * line + z
        return remote(
            here, there, send.at[quarter, unit, link], recv.at[quarter, unit], devices[link]
        )

    def share(x, z, quarter, first=False):
        there = place(x, grid.core, z, quarter)
        here = block.at[run(quarter)] if first else there
        unit = x * line + z
        return remote(
            here, there, twin_send.at[quarter, unit], twin_recv.at[quarter, unit], grid.twin
        )

    def arrived(x, z, quarter):
        copy(x, z, quarter, across).wait_recv()
        share(x, z, quarter).start()

    copy(grid.x, grid.z, carry_b, across, True).start()
    copy(grid.x, grid.z, carry_a, across, True).start()
    copy(grid.x, grid.z, other_a, across, True).start()
    for link, go in ((right, grid.has_right), (left, grid.has_left)):

        @pl.when(go)
        def _(link=link):
            copy(grid.x, grid.z, carry_a, link, True).start()
            copy(grid.x, grid.z, carry_b, link, True).start()

    for quarter in range(4):
        share(grid.x, grid.z, quarter, True).start()
    meanwhile()

    arrived(1 - grid.x, grid.z, carry_b)
    copy(1 - grid.x, grid.z, carry_b, mirror).start()
    for link, go in ((right, grid.has_right), (left, grid.has_left)):
        pl.when(go)(lambda link=link: copy(1 - grid.x, grid.z, carry_b, link).start())

    def sides(distance):
        return (
            (grid.z - distance, grid.z >= distance, right, grid.has_right),
            (grid.z + distance, grid.z + distance < line, left, grid.has_left),
        )

    def step(distance, carry):
        for x, quarter in (
            (grid.x, carry_a),
            (grid.x, carry_b),
            (1 - grid.x, carry_b),
        ):
            for z, there, link, go in sides(distance):

                @pl.when(there)
                def _(x=x, quarter=quarter, z=z, link=link, go=go):
                    copy(x, z, quarter, across).wait_recv()
                    pl.when(go)(lambda: copy(x, z, quarter, link).start())
                    copy(x, z, quarter, mirror).start()
                    if quarter is carry_a:
                        copy(x, z, quarter, across).start()
                    share(x, z, quarter).start()

        for z, there, _, _ in sides(distance - 1):

            @pl.when(jnp.logical_and(there, distance > 1))
            def _(z=z):
                arrived(grid.x, z, other_a)
                copy(grid.x, z, other_a, across).start()

        return carry

    lax.fori_loop(1, line + 1, step, 0)
    afterwards()

    def last(z, carry):
        arrived(1 - grid.x, z, carry_a)
        arrived(1 - grid.x, z, other_a)
        arrived(1 - grid.x, z, other_b)
        pl.when(z != grid.z)(lambda: arrived(grid.x, z, other_b))
        return carry

    lax.fori_loop(0, line, last, 0)

    def finish(z, carry):
        away = z != grid.z
        for x in (grid.x, 1 - grid.x):
            for quarter in range(4):
                share(x, z, quarter).wait()
        for x, quarter in ((grid.x, carry_a), (grid.x, carry_b), (1 - grid.x, carry_b)):
            to_mirror = jnp.logical_or(away, jnp.bool_(x is not grid.x))
            pl.when(to_mirror)(
                lambda x=x, quarter=quarter: copy(x, z, quarter, mirror).wait_send()
            )
            for link, go in (
                (right, jnp.logical_and(z <= grid.z, grid.has_right)),
                (left, jnp.logical_and(z >= grid.z, grid.has_left)),
            ):
                pl.when(go)(
                    lambda x=x, quarter=quarter, link=link: copy(x, z, quarter, link).wait_send()
                )
        copy(grid.x, z, carry_a, across).wait_send()
        copy(grid.x, z, other_a, across).wait_send()
        return carry

    lax.fori_loop(0, line, finish, 0)
    copy(grid.x, grid.z, carry_b, across, True).wait_send()


def mask(places, own_places):
    return jnp.where(places[...] <= own_places[...], 0.0, -1e30).astype(F32)


class Line:
    def __init__(self, grid, block, everything, send, recv):
        self.grid, self.block, self.everything = grid, block, everything
        self.send, self.recv = send, recv

    def copy(self, z, link, first=False):
        grid = self.grid
        there = self.everything.at[z]
        here = self.block if first else there
        device = (grid.right, grid.left)[link]
        return remote(here, there, self.send.at[z, link], self.recv.at[z], device)

    def send_own(self):
        grid = self.grid
        for link, go in ((0, grid.has_right), (1, grid.has_left)):
            pl.when(go)(lambda link=link: self.copy(grid.z, link, True).start())

    def forward(self, distance):
        grid = self.grid
        for z, there, link, go in (
            (grid.z - distance, grid.z >= distance, 0, grid.has_right),
            (grid.z + distance, grid.z + distance < grid.line, 1, grid.has_left),
        ):

            @pl.when(there)
            def _(z=z, link=link, go=go):
                self.copy(z, link).wait_recv()
                pl.when(go)(lambda: self.copy(z, link).start())

    def finish(self):
        grid = self.grid

        def step(z, carry):
            for link, go in (
                (0, jnp.logical_and(z <= grid.z, grid.has_right)),
                (1, jnp.logical_and(z >= grid.z, grid.has_left)),
            ):
                pl.when(go)(lambda link=link: self.copy(z, link).wait_send())
            return carry

        lax.fori_loop(0, grid.line, step, 0)


def turn(value, cosine, sine, scale):
    parts = []
    lane = lax.broadcasted_iota(jnp.int32, (value.shape[0], 128), 1) % HEAD_SIZE
    for first in range(0, value.shape[1], 128):
        pair = value[:, first : first + 128]
        swapped = jnp.where(
            lane < HEAD_SIZE // 2,
            pltpu.roll(pair, 128 - HEAD_SIZE // 2, 1),
            pltpu.roll(pair, HEAD_SIZE // 2, 1),
        )
        parts.append(((pair * cosine[...] + swapped * sine[...]) * scale).astype(BF))
    return parts[0] if len(parts) == 1 else jnp.concatenate(parts, axis=1)


def halves(pair, half):
    pair = pair.astype(F32)
    turned = pltpu.roll(pair, HEAD_SIZE, 1)
    lane = lax.broadcasted_iota(jnp.int32, pair.shape, 1) // HEAD_SIZE
    first = jnp.where(half == 0, pair, turned)
    second = jnp.where(half == 0, turned, pair)
    both = jnp.concatenate([first, second], axis=0)
    return jnp.where(jnp.concatenate([lane, lane], axis=0) == half, both, 0.0).astype(BF)


def unhalves(both, half):
    rows = both.shape[0] // 2
    first, second = both[:rows], both[rows:]
    lane = lax.broadcasted_iota(jnp.int32, first.shape, 1) // HEAD_SIZE
    first = jnp.where(half == 0, first, pltpu.roll(first, HEAD_SIZE, 1))
    second = jnp.where(half == 0, pltpu.roll(second, HEAD_SIZE, 1), second)
    return jnp.where(lane == 0, first, second)


def front_kernel(
    line, parts,
    query_w, key_w, value_w, out_w, tokens, tangent, cosine, sine, gain_one, gain_two, places, own_places,
    attended, middle, normed, first_normed, queries, logs, gain, keyed_out, tangent_all, weights_out,
    everything, keyed, keyed_all, bias_v, token_v, cosine_v, sine_v, scores, probs, sums, stage, load_sem,
    key_send, key_recv, send, recv, own_sem, weight_send, weight_recv, twin_send, twin_recv,
):
    grid = Grid(2, line)
    rows, width = tokens.shape
    narrow = keyed.shape[1] // 2
    total = places.shape[1]
    extra = width + 2 * narrow
    after = extra + 128
    me = grid.slot(grid.x, grid.z)
    chunk = rows // 2
    tile = 512
    block = everything.at[(grid.x * 2 + grid.core) * line + grid.z]
    starts = (0, width, width + narrow, after)
    load_pairs(
        [
            (part, block.at[:, pl.ds(first, part.shape[1])])
            for first, part in zip(starts, (query_w, key_w, value_w, out_w))
        ],
        load_sem,
    )
    row = lax.broadcasted_iota(jnp.int32, (16, 128), 0)
    both_gains = jnp.where(row == 0, gain_one[...].astype(F32), gain_two[...].astype(F32))
    everything[(grid.x * 2 + grid.core) * line + grid.z, 0:16, extra:after] = both_gains.astype(BF)
    grid.greet(True, True)

    def meanwhile():
        load_pairs(
            [
                (tangent, stage),
                (tokens, token_v),
                (cosine, cosine_v),
                (sine, sine_v),
            ],
            load_sem,
        )
        load_pairs([(stage, tangent_all.at[me])], own_sem)
        bias_v[...] = mask(places, own_places)

    gather = Gather(grid, tangent, tangent_all, send, recv, parts)
    soon = 1

    def tangent_first():
        gather.send_own()
        for part in range(soon):
            gather.forward(1, part)

    gather_weights(
        grid, block, everything, weight_send, weight_recv, twin_send, twin_recv, meanwhile,
        tangent_first,
    )
    weights_copy = pltpu.make_async_copy(everything, weights_out, own_sem.at[1])
    weights_copy.start()
    units, run = everything.shape[0], everything.shape[1]
    for unit in range(units):
        for which in range(2):
            gain[which : which + 1, unit * run : (unit + 1) * run] = everything[
                unit, which : which + 1, extra:after
            ].astype(F32)

    def norm(source, target, which):
        def step(j, carry):
            here = pl.ds(pl.multiple_of(j * chunk, chunk), chunk)
            value = source[here, :].astype(F32)
            factor = lax.rsqrt(jnp.mean(value * value, axis=1, keepdims=True) + norm_eps)
            target[here, :] = (value * factor * gain[which : which + 1, :]).astype(BF)
            return carry

        lax.fori_loop(0, rows // chunk, step, 0)

    norm(token_v, first_normed, 0)

    def project(c):
        return dot(first_normed[...], everything[:, :, c].reshape(width, tile), NN)

    for first in range(0, narrow, tile):
        keyed[:, first : first + tile] = turn(project(slice(width + first, width + first + tile)), cosine_v, sine_v, 1.0)
        keyed[:, narrow + first : narrow + first + tile] = project(
            slice(width + narrow + first, width + narrow + first + tile)
        ).astype(BF)
    line_keys = Line(grid, keyed, keyed_all, key_send, key_recv)
    line_keys.send_own()
    for part in range(soon, parts):
        gather.forward(1, part, along=False)
    keyed_all[grid.z] = keyed[...]

    def query_step(j, carry):
        c = pl.ds(pl.multiple_of(j * tile, tile), tile)
        queries[:, c] = turn(project(c), cosine_v, sine_v, HEAD_SIZE ** (-0.5))
        return carry

    lax.fori_loop(0, width // tile, query_step, 0)
    def advance(n):
        gather.forward(n // parts + 2, n % parts)

    for distance in range(1, line - 1):
        line_keys.forward(distance)
    for part in range(soon, parts):
        gather.forward(1, part, wait=False, across=False)
    for n in range(soon):
        advance(n)
    line_keys.forward(line - 1)

    logs[...] = jnp.zeros_like(logs)
    pairs = width // (2 * HEAD_SIZE)
    group = pairs // (narrow // (2 * HEAD_SIZE))

    def pair_step(i, carry):
        c = pl.ds(pl.multiple_of(i * 128, 128), 128)
        half = (i // (group // 2)) % 2
        first_key = pl.multiple_of((i // group) * 128, 128)
        keys = keyed_all[:, :, pl.ds(first_key, 128)].reshape(total, 128)
        values = keyed_all[:, :, pl.ds(first_key + narrow, 128)].reshape(total, 128)
        scores[...] = dot(halves(queries[:, c], half), keys, NT)

        def soft(j, inner):
            here = pl.ds(pl.multiple_of(j * rows, rows), rows)
            value = scores[here, :] + bias_v[...]
            top = jnp.max(value, axis=1, keepdims=True)
            power = jnp.exp(value - top)
            size = jnp.sum(power, axis=1, keepdims=True)
            probs[here, :] = power.astype(BF)
            sums[here, :] = jnp.broadcast_to(1.0 / size, (rows, 128))
            lane = lax.broadcasted_iota(jnp.int32, (rows, 128), 1)
            logs[here, :] = jnp.where(lane == i, top + jnp.log(size), logs[here, :])
            return inner

        lax.fori_loop(0, 2, soft, 0)
        out = dot(probs[...], values, NN) * sums[...]
        attended[:, c] = unhalves(out, half).astype(BF)

        n = soon + i // 2
        pl.when(jnp.logical_and(i % 2 == 1, n < (line - 2) * parts))(lambda: advance(n))
        return carry

    lax.fori_loop(0, pairs, pair_step, 0)
    keyed_copy = pltpu.make_async_copy(keyed_all, keyed_out, load_sem.at[0])
    keyed_copy.start()

    def out_step(j, carry):
        c = pl.ds(pl.multiple_of(j * tile, tile), tile)
        w = pl.ds(pl.multiple_of(after + j * tile, 128), tile)
        out = dot(attended[...], everything[:, :, w].reshape(width, tile), NN)
        middle[:, c] = token_v[:, c].astype(F32) + out
        return carry

    lax.fori_loop(0, width // tile, out_step, 0)
    norm(middle, normed, 1)

    def rest(n, carry):
        advance(n)
        return carry

    lax.fori_loop(soon + pairs // 2, (line - 2) * parts, rest, 0)
    for z in range(line):
        gather.wait_across(z)
    keyed_copy.wait()
    weights_copy.wait()
    line_keys.finish()
    gather.finish()


def front_call(pieces, tokens, tangent, cosine, sine, gains, places, own_places, line):
    rows, width = tokens.shape
    narrow = pieces[1].shape[1]
    unit = (pieces[0].shape[0], sum(p.shape[1] for p in pieces) + 128)
    total = places.shape[1]
    blocks, parts = 2 * line, 4
    shapes = jax.ShapeDtypeStruct
    vmem = pl.BlockSpec(memory_space=pltpu.VMEM)
    like = lambda a: pltpu.VMEM(a.shape, a.dtype)
    return pl.pallas_call(
        functools.partial(front_kernel, line, parts),
        out_shape=(
            shapes((rows, width), BF), shapes((rows, width), F32), shapes((rows, width), BF),
            shapes((rows, width), BF), shapes((rows, width), BF),
            shapes((2 * rows, 128), F32), shapes((2, width), F32),
            shapes((line, rows, 2 * narrow), BF),
            shapes((blocks, rows, width), BF), shapes((2 * blocks,) + unit, BF),
        ),
        in_specs=[ANY] * 8 + [vmem] * 4,
        out_specs=(vmem,) * 7 + (ANY,) * 3,
        scratch_shapes=[
            pltpu.VMEM((2 * blocks,) + unit, BF),
            pltpu.VMEM((rows, 2 * narrow), BF), pltpu.VMEM((line, rows, 2 * narrow), BF),
            pltpu.VMEM((rows, total), F32), like(tokens), like(cosine), like(sine),
            pltpu.VMEM((2 * rows, total), F32), pltpu.VMEM((2 * rows, total), BF),
            pltpu.VMEM((2 * rows, 128), F32), pltpu.VMEM((rows, width), BF), pltpu.SemaphoreType.DMA((6,)),
            pltpu.SemaphoreType.DMA((line, 2)), pltpu.SemaphoreType.DMA((line,)),
            pltpu.SemaphoreType.DMA((line, parts, 3)), pltpu.SemaphoreType.DMA((blocks, parts)),
            pltpu.SemaphoreType.DMA((2,)),
            pltpu.SemaphoreType.DMA((4, blocks, 4)), pltpu.SemaphoreType.DMA((4, blocks)),
            pltpu.SemaphoreType.DMA((4, blocks)), pltpu.SemaphoreType.DMA((4, blocks)),
        ],
        compiler_params=pltpu.CompilerParams(
            collective_id=5, has_side_effects=True, vmem_limit_bytes=62 * 2**20
        ),
        name="front",
    )(*pieces, tokens, tangent, cosine, sine, *gains, places, own_places)


def back_kernel(
    line, parts,
    places, own_places, queries, keyed_all, middle, grad_normed, tangent, gain, logs, hidden_all,
    down_own, down_twin, weights, cosine, sine,
    gate_sum, up_sum, down_sum, _gate, _up, _down, normed, attended,
    branch, grad_qkv, term_two, gate_mirror, up_mirror, down_mirror,
    twin_normed, twin_attended, twin_out, grad_out, grad_middle,
    out_across, both_attended, both_out, out_partial, out_send, out_recv,
    norm_sem, gain_v, out_v, out_w, cosine_v, sine_v, grad_keyed, mirror_send, mirror_recv,
    query_v, keyed_v, grad_v, bias_v, log_v, scores, gradients, probs, slopes, key_sum, value_sum,
    down_w, hidden, load_sem,
    partial, from_across, from_line, total, across_send, across_recv, line_send, line_recv,
    key_partial, key_line, key_total, key_send, key_recv,
):
    grid = Grid(2, line)
    cols, width = down_own.shape
    rows = partial.shape[1]
    narrow = keyed_all.shape[2] // 2
    length = places.shape[1]
    grid.greet(True, True)
    swapped = [
        remote(src, dst, mirror_send.at[3 + i], mirror_recv.at[3 + i], grid.twin)
        for i, (src, dst) in enumerate(
            ((normed, twin_normed), (attended, twin_attended), (out_v, twin_out))
        )
    ]
    for copy in swapped[:2]:
        copy.start()
    left = pl.ds(EARLY * 256, width - EARLY * 256)
    mirrored = [
        remote(src, dst, mirror_send.at[i], mirror_recv.at[i], grid.mirror)
        for i, (src, dst) in enumerate(
            (
                (gate_sum.at[left, :], gate_mirror.at[left, :]),
                (up_sum.at[left, :], up_mirror.at[left, :]),
                (down_sum.at[:, left], down_mirror.at[:, left]),
            )
        )
    ]
    for copy in mirrored:
        copy.start()
    load_pairs(
        [
            (down_own, down_w.at[pl.ds(0, cols)]),
            (down_twin, down_w.at[pl.ds(cols, cols)]),
            (hidden_all, hidden),
            (queries, query_v),
            (keyed_all, keyed_v),
            (gain, gain_v),
            (logs, log_v),
            (cosine, cosine_v),
            (sine, sine_v),
        ],
        load_sem,
    )
    bias_v[...] = mask(places, own_places)
    scatter = Scatter(
        grid, partial, from_across, from_line, total,
        (across_send, across_recv, line_send, line_recv), parts,
    )
    keyed_scatter = Scatter(
        grid, key_partial, None, key_line, key_total, (None, None, key_send, key_recv),
        key_partial.shape[1] // rows,
    )

    def work(i, carry):
        z = grid.order(line - 1 - i % line)
        slot = grid.slot(jnp.where(i < line, 1 - grid.x, grid.x), z)
        spot = pl.ds(pl.multiple_of(slot * rows, rows), rows)

        def tile(j, inner):
            c = pl.ds(pl.multiple_of(j * cols, cols), cols)
            partial[slot, :, c] = dot(hidden[spot, :], down_w[:, c], NN).astype(BF)
            return inner

        lax.fori_loop(0, width // cols, tile, 0)
        pl.when(i < line)(lambda: scatter.send_across(z))
        return carry

    deep = 2 * rows
    middle_v, normed_v, tangent_v = scores, gradients, probs
    half_width = width // 2
    norm_loads = [
        pltpu.make_async_copy(
            src.at[:, pl.ds(h * half_width, half_width)], dst.at[pl.ds(h * rows, rows), :], norm_sem.at[i, h]
        )
        for i, (src, dst) in enumerate(
            ((middle, middle_v), (grad_normed, normed_v), (tangent, tangent_v))
        )
        for h in range(2)
    ]
    for copy in norm_loads:
        copy.start()
    lax.fori_loop(0, line, work, 0)
    for copy in norm_loads:
        copy.wait()
    term_two[...] = jnp.zeros_like(term_two)
    few = rows // 4

    def norm_step(j):
        spots = [pl.ds(pl.multiple_of(h * rows + j * few, few), few) for h in range(2)]
        here = pl.ds(pl.multiple_of(j * few, few), few)
        sides = [pl.ds(h * half_width, half_width) for h in range(2)]
        values = [middle_v[s, :] for s in spots]
        square = sum(jnp.sum(v * v, axis=1, keepdims=True) for v in values)
        factor = lax.rsqrt(square / width + norm_eps)
        units = [v * factor for v in values]
        grads = [normed_v[s, :] for s in spots]
        scaled = [g * gain_v[1:2, c] for g, c in zip(grads, sides)]
        dots = sum(jnp.sum(s * u, axis=1, keepdims=True) for s, u in zip(scaled, units))
        mean = dots / width
        for spot, c, grad, unit, scale in zip(spots, sides, grads, units, scaled):
            term_two[:, c] += jnp.sum(grad * unit, axis=0, keepdims=True)
            value = tangent_v[spot, :].astype(F32) + factor * (scale - unit * mean)
            branch[here, c] = value
            out_v[here, c] = value.astype(BF)

    each(rows // few, norm_step)
    norm_copies = [
        pltpu.make_async_copy(branch, grad_middle, norm_sem.at[0, 0]),
        pltpu.make_async_copy(out_v, grad_out, norm_sem.at[0, 1]),
    ]
    for copy in norm_copies + swapped[2:]:
        copy.start()
    work(line, 0)
    lag = jnp.where(jnp.logical_and(grid.has_left, grid.has_right), 2, 0)

    def paced(position):
        pl.when(position >= lag)(lambda: scatter.step(position - lag))

    paced(0)
    tile = out_w.shape[0] * out_w.shape[1]
    after = weights.shape[2] - width

    def out_step(j, carry):
        units = pl.ds(j * out_w.shape[0], out_w.shape[0])
        load_pairs([(weights.at[units, :, pl.ds(after, width)], out_w)], load_sem)
        c = pl.ds(pl.multiple_of(j * tile, tile), tile)
        grad_v[:, c] = dot(out_v[...], out_w[...].reshape(tile, width), NT).astype(BF)
        pl.when(j % 2 == 1)(lambda: paced(1 + j // 2))
        return carry

    lax.fori_loop(0, width // tile, out_step, 0)
    chunk = rows // 2
    pairs = width // (2 * HEAD_SIZE)
    group = pairs // (narrow // (2 * HEAD_SIZE))

    def pair_step(i, carry):
        c = pl.ds(pl.multiple_of(i * 128, 128), 128)
        half = (i // (group // 2)) % 2
        key_cols = pl.ds(pl.multiple_of((i // group) * 128, 128), 128)
        value_cols = pl.ds(pl.multiple_of((i // group) * 128 + narrow, 128), 128)
        keys = keyed_v[:, :, key_cols].reshape(length, 128)
        values = keyed_v[:, :, value_cols].reshape(length, 128)
        query = halves(query_v[:, c], half)
        grad = halves(grad_v[:, c], half)
        scores[...] = dot(query, keys, NT)
        gradients[...] = dot(grad, values, NT)

        def soft(j, inner):
            here = pl.ds(pl.multiple_of(j * chunk, chunk), chunk)
            there = pl.ds(pl.multiple_of((j * chunk) % rows, chunk), chunk)
            lane = lax.broadcasted_iota(jnp.int32, (chunk, 128), 1)
            log = jnp.sum(jnp.where(lane == i, log_v[here, :], 0.0), axis=1, keepdims=True)
            prob = jnp.exp(scores[here, :] + bias_v[there, :] - log)
            slope = gradients[here, :]
            delta = jnp.sum(prob * slope, axis=1, keepdims=True)
            probs[here, :] = prob.astype(BF)
            slopes[here, :] = (prob * (slope - delta)).astype(BF)
            return inner

        lax.fori_loop(0, deep // chunk, soft, 0)
        back = dot(slopes[...], keys, NN) * HEAD_SIZE ** (-0.5)
        grad_qkv[:, c] = turn(unhalves(back, half), cosine_v, sine_v, 1.0)
        key_part = dot(slopes[...], query, TN)
        value_part = dot(probs[...], grad, TN)

        @pl.when(i % group == 0)
        def _():
            key_sum[...] = key_part
            value_sum[...] = value_part

        @pl.when(i % group != 0)
        def _():
            key_sum[...] += key_part
            value_sum[...] += value_part

        @pl.when(i % group == group - 1)
        def _():
            spot = pl.ds(pl.multiple_of((i // group) * rows, rows), rows)
            key_partial[:, spot, 0:128] = key_sum[...].astype(BF).reshape(line, rows, 128)
            key_partial[:, spot, 128:256] = value_sum[...].astype(BF).reshape(line, rows, 128)
            pl.when(i // group + early > 0)(lambda: keyed_steps(i // group + early - 1))

        @pl.when(i % 6 == 2)
        def _():
            work(line + 1 + i // 6, 0)

        pl.when(i == pairs // 2 - 2)(out_gradients)

        done = (3 * i + 1) // 5
        pl.when((3 * i + 4) // 5 > done)(lambda: paced(3 + done))
        return carry

    run = out_partial.shape[1]

    def outward(z):
        return remote(
            out_partial.at[z], out_across.at[z], out_send.at[z], out_recv.at[z], grid.across
        )

    def away(action):
        for j in range(line - 2):
            action(outward(scatter.rank(j)))

    def out_gradients():
        for copy in swapped[1:]:
            copy.wait()
        own, twin = pl.ds(0, rows), pl.ds(rows, rows)
        load_pairs(
            [
                (attended, both_attended.at[own]),
                (twin_attended, both_attended.at[twin]),
                (out_v, both_out.at[own]),
                (twin_out, both_out.at[twin]),
            ],
            load_sem,
        )
        tall = line * run
        first = pl.multiple_of(((1 - grid.x) * 2 + grid.core) * tall, tall)

        def tile_step(j):
            c = pl.ds(pl.multiple_of(j * 512, 512), 512)
            value = dot(both_attended[:, pl.ds(first, tall)], both_out[:, c], TN).astype(BF)
            out_partial[:, :, c] = value.reshape(line, run, 512)

        each(width // 512, tile_step)
        away(lambda c: c.start())

    def keyed_steps(g):
        each(line - 1, lambda j: keyed_scatter.pass_on(keyed_scatter.rank(j), g))

    early = jnp.where(jnp.logical_and(grid.has_left, grid.has_right), 0, 1)
    lax.fori_loop(0, pairs, pair_step, 0)

    def rest(n, carry):
        scatter.step(n)
        return carry

    lax.fori_loop(3 + (3 * pairs + 1) // 5 - lag, scatter.steps(), rest, 0)

    pl.when(early == 0)(lambda: keyed_steps(pairs // group - 1))
    for copy in norm_copies:
        copy.wait()
    scatter.own(branch)
    keyed_scatter.own(grad_keyed)
    for g in range(pairs // group):
        both = grad_keyed[g * rows : (g + 1) * rows, :]
        first = width + g * 128
        grad_qkv[:, first : first + 128] = turn(both[:, :128], cosine_v, sine_v, 1.0)
        grad_qkv[:, first + narrow : first + narrow + 128] = both[:, 128:].astype(BF)
    for copy in mirrored + swapped[:1]:
        copy.wait()
    away(lambda c: c.wait())
    scatter.finish()
    keyed_scatter.finish()


def back_call(
    places, own_places, queries, keyed_all, middle, grad_normed, tangent, gain, logs, hidden_all, downs,
    weights, cosine, sine, sums,
    mirrors, normed, attended, line,
):
    rows, width = queries.shape
    both = keyed_all.shape[2]
    groups, run = both // 256, weights.shape[1]
    cols, length = downs[0].shape[0], places.shape[1]
    parts = 4
    shapes = jax.ShapeDtypeStruct
    vmem = pl.BlockSpec(memory_space=pltpu.VMEM)
    return pl.pallas_call(
        functools.partial(back_kernel, line, parts),
        out_shape=(
            shapes((rows, width), F32), shapes((rows, width + both), BF), shapes((1, width), F32),
            *(shapes(s.shape, BF) for s in sums), *(shapes((rows, width), BF),) * 4,
            shapes((rows, width), F32), shapes((line, run, width), BF),
        ),
        in_specs=[vmem] * 2 + [ANY] * 21,
        out_specs=(vmem,) * 3 + (ANY,) * 9,
        input_output_aliases={18: 3, 19: 4, 20: 5},
        scratch_shapes=[
            pltpu.VMEM((2 * rows, width), BF), pltpu.VMEM((2 * rows, width), BF),
            pltpu.VMEM((line, run, width), BF),
            pltpu.SemaphoreType.DMA((line,)), pltpu.SemaphoreType.DMA((line,)),
            pltpu.SemaphoreType.DMA((3, 2)), pltpu.VMEM(gain.shape, F32),
            pltpu.VMEM((rows, width), BF), pltpu.VMEM((4, run, width), BF),
            pltpu.VMEM(cosine.shape, F32), pltpu.VMEM(sine.shape, F32),
            pltpu.VMEM((groups * rows, 256), F32),
            pltpu.SemaphoreType.DMA((6,)), pltpu.SemaphoreType.DMA((6,)),
            pltpu.VMEM((rows, width), BF), pltpu.VMEM(keyed_all.shape, BF), pltpu.VMEM((rows, width), BF),
            pltpu.VMEM((rows, length), F32), pltpu.VMEM(logs.shape, F32),
            pltpu.VMEM((2 * rows, length), F32), pltpu.VMEM((2 * rows, length), F32),
            pltpu.VMEM((2 * rows, length), BF), pltpu.VMEM((2 * rows, length), BF),
            pltpu.VMEM((length, 128), F32), pltpu.VMEM((length, 128), F32),
            pltpu.VMEM((2 * cols, width), BF), pltpu.VMEM(hidden_all.shape, BF),
            pltpu.SemaphoreType.DMA((10,)),
            *scatter_scratch(line, rows, width, parts),
            pltpu.VMEM((line, groups * rows, 256), BF), pltpu.VMEM((2 * line - 2, groups * rows, 256), BF),
            pltpu.VMEM((rows, 256), F32),
            pltpu.SemaphoreType.DMA((line, groups)), pltpu.SemaphoreType.DMA((2 * line - 2, groups)),
        ],
        compiler_params=pltpu.CompilerParams(
            collective_id=6, has_side_effects=True, vmem_limit_bytes=62 * 2**20
        ),
        name="back",
    )(
        places, own_places, queries, keyed_all, middle, grad_normed, tangent, gain, logs, hidden_all,
        *downs, weights, cosine, sine, *sums,
        *mirrors, normed, attended,
    )


def body(
    tokens,
    places,
    cotangent,
    gain_attn,
    gain_mlp,
    w_query,
    key_projection,
    value_projection,
    w_out,
    w_gate,
    w_up,
    w_down,
):
    sequence_total, segment_length, width = tokens.shape
    total_length = places.shape[1]
    total_rows = sequence_total * segment_length
    position = lax.axis_index("context")
    local_positions = lax.dynamic_slice_in_dim(places, position * segment_length, segment_length, 1)
    rotary_angles = local_positions.reshape(total_rows).astype(jnp.float32)[:, None] * frequencies(
        HEAD_SIZE // 2
    )
    gain_one, gain_two, query_w, key_weight_local, value_w, out_w = (
        lax.all_gather(gain_attn, ("fsdp", "context"), axis=0, tiled=True),
        lax.all_gather(gain_mlp, ("fsdp", "context"), axis=0, tiled=True),
        lax.all_gather(w_query, ("fsdp", "context"), axis=0, tiled=True),
        lax.all_gather(key_projection, ("fsdp", "context"), axis=0, tiled=True),
        lax.all_gather(value_projection, ("fsdp", "context"), axis=0, tiled=True),
        lax.all_gather(w_out, ("fsdp", "context"), axis=0, tiled=True),
    )
    gain_first = gain_one.astype(jnp.float32)
    gain_second = gain_two.astype(jnp.float32)
    inputs_f = tokens.astype(jnp.float32).reshape(total_rows, width)
    factor_one = lax.rsqrt(jnp.mean(inputs_f * inputs_f, axis=-1, keepdims=True) + norm_eps)
    unit_one = inputs_f * factor_one
    normed_tokens = (unit_one * gain_first).astype(jnp.bfloat16)
    query_pre = jnp.dot(normed_tokens, query_w, preferred_element_type=jnp.float32).reshape(
        total_rows, QUERY_HEADS, HEAD_SIZE
    )
    key_unrotated = jnp.dot(
        normed_tokens, key_weight_local, preferred_element_type=jnp.float32
    ).reshape(total_rows, KEY_VALUE_HEADS, HEAD_SIZE)
    value_matrix_rows = jnp.dot(normed_tokens, value_w, preferred_element_type=jnp.float32).astype(
        jnp.bfloat16
    )
    query_rows = apply_rotary(query_pre, rotary_angles).astype(jnp.bfloat16)
    key_matrix_rows = (
        apply_rotary(key_unrotated, rotary_angles)
        .astype(jnp.bfloat16)
        .reshape(sequence_total, segment_length, KEY_VALUE_HEADS * HEAD_SIZE)
    )
    key_all, value_all = (
        lax.all_gather(key_matrix_rows, "context", axis=1, tiled=True),
        lax.all_gather(
            value_matrix_rows.reshape(sequence_total, segment_length, KEY_VALUE_HEADS * HEAD_SIZE),
            "context",
            axis=1,
            tiled=True,
        ),
    )
    head_query = query_head_rows(query_rows, sequence_total, segment_length)
    head_key = key_heads(key_all, sequence_total, total_length)
    head_value = key_heads(value_all, sequence_total, total_length)
    query_positions = jnp.repeat(local_positions, KEY_VALUE_HEADS, axis=0)
    key_positions = jnp.repeat(places, KEY_VALUE_HEADS, axis=0)
    attended = lax.map(
        forward_head, (head_query, head_key, head_value, query_positions, key_positions)
    )
    attended = merge_queries(attended, sequence_total, segment_length).astype(jnp.bfloat16)
    middle = inputs_f + jnp.dot(attended, out_w, preferred_element_type=jnp.float32)
    factor_two = lax.rsqrt(jnp.mean(middle * middle, axis=-1, keepdims=True) + norm_eps)
    unit_two = middle * factor_two
    normed_mlp = (unit_two * gain_second).astype(jnp.bfloat16)
    tangent = cotangent.reshape(total_rows, width)
    tangent_f = tangent.astype(jnp.float32)
    group = ("fsdp", "context")
    normed_all = lax.all_gather(normed_mlp, group, axis=0, tiled=True)
    tangent_all = lax.all_gather(tangent, group, axis=0, tiled=True)
    branch_part, kept_values = feed_forward(normed_all, w_gate, w_up, w_down)
    grad_part, grad_w_gate, grad_w_up, grad_w_down = feed_back(
        normed_all, tangent_all, w_gate, w_up, w_down, kept_values
    )
    grad_normed = lax.psum_scatter(
        grad_part.astype(jnp.bfloat16), group, scatter_dimension=0, tiled=True
    ).astype(jnp.float32)
    branch = lax.psum_scatter(
        branch_part.astype(jnp.bfloat16), group, scatter_dimension=0, tiled=True
    ).astype(jnp.float32)
    outcome = middle + branch
    scaled_two = grad_normed * gain_second
    term_gain_two = jnp.sum(grad_normed * unit_two, axis=0)
    grad_middle = tangent_f + factor_two * (
        scaled_two - unit_two * jnp.mean(scaled_two * unit_two, axis=-1, keepdims=True)
    )
    grad_branch = grad_middle.astype(jnp.bfloat16)
    term_out = times_t(attended, grad_branch)
    grad_attended = times_nt(grad_branch, out_w).astype(jnp.bfloat16)
    head_grad = query_head_rows(grad_attended, sequence_total, segment_length)
    grad_q, grad_k, grad_v = lax.map(
        backward_head, (head_query, head_key, head_value, head_grad, query_positions, key_positions)
    )
    local_key_gradient, local_value_gradient = (
        lax.psum_scatter(
            merge_keys(grad_k, sequence_total, total_length).astype(jnp.bfloat16),
            "context",
            scatter_dimension=1,
            tiled=True,
        ).astype(jnp.float32),
        lax.psum_scatter(
            merge_keys(grad_v, sequence_total, total_length).astype(jnp.bfloat16),
            "context",
            scatter_dimension=1,
            tiled=True,
        ).astype(jnp.float32),
    )
    grad_query = (
        inverse_rotary(
            merge_queries(grad_q, sequence_total, segment_length).reshape(
                total_rows, QUERY_HEADS, HEAD_SIZE
            ),
            rotary_angles,
        )
        .reshape(total_rows, QUERY_HEADS * HEAD_SIZE)
        .astype(jnp.bfloat16)
    )
    grad_key = (
        inverse_rotary(
            local_key_gradient.reshape(total_rows, KEY_VALUE_HEADS, HEAD_SIZE), rotary_angles
        )
        .reshape(total_rows, KEY_VALUE_HEADS * HEAD_SIZE)
        .astype(jnp.bfloat16)
    )
    value_gradient = local_value_gradient.reshape(total_rows, KEY_VALUE_HEADS * HEAD_SIZE).astype(
        jnp.bfloat16
    )
    grad_normed_one = (
        times_nt(grad_query, query_w)
        + times_nt(grad_key, key_weight_local)
        + times_nt(value_gradient, value_w)
    )
    term_query = times_t(normed_tokens, grad_query)
    term_key = times_t(normed_tokens, grad_key)
    term_value = times_t(normed_tokens, value_gradient)
    scaled_one = grad_normed_one * gain_first
    term_gain_one = jnp.sum(grad_normed_one * unit_one, axis=0)
    grad_inputs = grad_middle + factor_one * (
        scaled_one - unit_one * jnp.mean(scaled_one * unit_one, axis=-1, keepdims=True)
    )
    share_query, share_key, share_value, share_out, share_gain_one, share_gain_two = (
        lax.psum_scatter(term_query.astype(jnp.bfloat16), ("fsdp", "context"), scatter_dimension=0, tiled=True),
        lax.psum_scatter(term_key.astype(jnp.bfloat16), ("fsdp", "context"), scatter_dimension=0, tiled=True),
        lax.psum_scatter(term_value.astype(jnp.bfloat16), ("fsdp", "context"), scatter_dimension=0, tiled=True),
        lax.psum_scatter(term_out.astype(jnp.bfloat16), ("fsdp", "context"), scatter_dimension=0, tiled=True),
        lax.psum_scatter(term_gain_one, ("fsdp", "context"), scatter_dimension=0, tiled=True),
        lax.psum_scatter(term_gain_two, ("fsdp", "context"), scatter_dimension=0, tiled=True),
    )
    summed = (
        lax.psum(share_query.astype(jnp.bfloat16), "replica").astype(jnp.float32),
        lax.psum(share_key.astype(jnp.bfloat16), "replica").astype(jnp.float32),
        lax.psum(share_value.astype(jnp.bfloat16), "replica").astype(jnp.float32),
        lax.psum(share_out.astype(jnp.bfloat16), "replica").astype(jnp.float32),
        lax.psum(grad_w_gate.astype(jnp.bfloat16), "replica").astype(jnp.float32),
        lax.psum(grad_w_up.astype(jnp.bfloat16), "replica").astype(jnp.float32),
        lax.psum(grad_w_down.astype(jnp.bfloat16), "replica").astype(jnp.float32),
        lax.psum(share_gain_one.astype(jnp.bfloat16), "replica").astype(jnp.float32),
        lax.psum(share_gain_two.astype(jnp.bfloat16), "replica").astype(jnp.float32),
    )
    out = outcome.astype(jnp.bfloat16).reshape(sequence_total, segment_length, width)
    grad_tokens = grad_inputs.astype(jnp.bfloat16).reshape(sequence_total, segment_length, width)
    return (
        out,
        grad_tokens,
        summed[0],
        summed[1],
        summed[2],
        summed[3],
        summed[4],
        summed[5],
        summed[6],
        summed[7],
        summed[8],
    )


def kernel_body(
    tokens,
    places,
    cotangent,
    gain_attn,
    gain_mlp,
    w_query,
    key_projection,
    value_projection,
    w_out,
    w_gate,
    w_up,
    w_down,
):
    bf16, f32 = jnp.bfloat16, jnp.float32
    sequence_total, segment_length, width = tokens.shape
    total_length = places.shape[1]
    line = lax.axis_size("context")
    narrow = key_projection.shape[1]
    run = w_query.shape[0]
    swap = [(i, i ^ 1) for i in range(lax.axis_size("fsdp"))]
    gates, ups, downs = ((w, lax.ppermute(w, "fsdp", swap)) for w in (w_gate, w_up, w_down))
    position = lax.axis_index("context")
    local_positions = lax.dynamic_slice_in_dim(places, position * segment_length, segment_length, 1)
    rotary_angles = local_positions.reshape(segment_length).astype(f32)[:, None] * frequencies(
        HEAD_SIZE // 2
    )
    pieces = (w_query, key_projection, value_projection, w_out)
    cosine, sine = jnp.cos(rotary_angles), jnp.sin(rotary_angles)
    cosine = jnp.concatenate([cosine] * 4, axis=1)
    sine = jnp.concatenate([-sine, sine] * 2, axis=1)
    own_places = local_positions.reshape(segment_length, 1)
    places = places.reshape(1, total_length)
    gains = (gain_attn.reshape(1, run), gain_mlp.reshape(1, run))
    tangent = cotangent.reshape(segment_length, width)
    rows = tokens.reshape(segment_length, width)
    (
        attended, middle, normed_mlp, normed_tokens, scaled_query, logs, gain, keyed_all, tangent_all,
        weights,
    ) = front_call(pieces, rows, tangent, cosine, sine, gains, places, own_places, line)
    mid = width + 2 * narrow
    grad_normed, _, hidden_all, *sums = feed_call(normed_mlp, tangent_all, gates, ups, downs, line)[:9]
    branch, grad_qkv, term_two, *others = back_call(
        places, own_places, scaled_query, keyed_all, middle, grad_normed, tangent, gain, logs,
        hidden_all, downs, weights, cosine, -sine, sums[:3], sums[3:], normed_tokens, attended, line,
    )
    twins, (grad_branch, grad_middle, out_across) = others[3:6], others[6:]
    outcome = middle + branch
    grad_w_gate, grad_w_up, grad_w_down = (
        a.astype(f32) + b.astype(f32) for a, b in zip(sums[:3], others[:3])
    )
    packed, grad_w_out, grad_tokens = sums_call(
        normed_tokens, attended, grad_qkv, grad_branch, (*twins, out_across), rows, grad_middle,
        weights, gain, term_two, line,
    )
    gains = packed[run * 3 // 4 : run * 3 // 4 + 2, mid:]
    ends, start = [], 0
    for size in (width, narrow, narrow):
        ends.append(packed[:, start : start + size])
        start += size
    return (
        outcome.astype(bf16).reshape(tokens.shape),
        grad_tokens.reshape(tokens.shape),
        *ends,
        grad_w_out,
        grad_w_gate,
        grad_w_up,
        grad_w_down,
        gains[0],
        gains[1],
    )


def solution(mesh):
    placed = (
        P(("replica", "fsdp"), "context", None),
        P(("replica", "fsdp"), None),
        P(("replica", "fsdp"), "context", None),
        P(("fsdp", "context")),
        P(("fsdp", "context")),
        P(("fsdp", "context"), None),
        P(("fsdp", "context"), None),
        P(("fsdp", "context"), None),
        P(("fsdp", "context"), None),
        P(None, ("fsdp", "context")),
        P(None, ("fsdp", "context")),
        P(("fsdp", "context"), None),
    )
    kernels = (mesh.shape["replica"], mesh.shape["fsdp"], mesh.shape["context"]) == (2, 4, 4)
    return jax.shard_map(
        kernel_body if kernels else body,
        mesh=mesh,
        in_specs=placed,
        out_specs=(
            P(("replica", "fsdp"), "context", None),
            P(("replica", "fsdp"), "context", None),
            P(("fsdp", "context"), None),
            P(("fsdp", "context"), None),
            P(("fsdp", "context"), None),
            P(("fsdp", "context"), None),
            P(None, ("fsdp", "context")),
            P(None, ("fsdp", "context")),
            P(("fsdp", "context"), None),
            P(("fsdp", "context")),
            P(("fsdp", "context")),
        ),
        check_vma=False,
    )
```

```python
import functools

import jax
import jax.numpy as jnp
from jax import lax
from jax.experimental import pallas as pl
from jax.experimental.pallas import tpu as pltpu
from jax.sharding import PartitionSpec as P

QUERY_HEADS = 32
KEY_VALUE_HEADS = 8
HEAD_SIZE = 64


norm_eps = 1e-05
rope_base = 500000.0


def frequencies(half):
    return rope_base ** (-2.0 * jnp.arange(half, dtype=jnp.float32) / (2.0 * half))


def apply_rotary(angle_table, rotary_angles):
    half = angle_table.shape[-1] // 2
    first_half = angle_table[..., :half]
    second_half = angle_table[..., half:]
    cosine = jnp.cos(rotary_angles)[..., None, :]
    sine = jnp.sin(rotary_angles)[..., None, :]
    return jnp.concatenate(
        [first_half * cosine - second_half * sine, second_half * cosine + first_half * sine],
        axis=-1,
    )


def inverse_rotary(angle_table, rotary_angles):
    half = angle_table.shape[-1] // 2
    first_half = angle_table[..., :half]
    second_half = angle_table[..., half:]
    cosine = jnp.cos(rotary_angles)[..., None, :]
    sine = jnp.sin(rotary_angles)[..., None, :]
    return jnp.concatenate(
        [first_half * cosine + second_half * sine, second_half * cosine - first_half * sine],
        axis=-1,
    )


def times_t(left, right):
    return lax.dot_general(
        left, right, (((0,), (0,)), ((), ())), preferred_element_type=jnp.float32
    )


def times_nt(left, right):
    return lax.dot_general(
        left, right, (((1,), (1,)), ((), ())), preferred_element_type=jnp.float32
    )


def query_head_rows(angle_table, sequence_total, segment_length):
    reshaped_heads = angle_table.reshape(
        sequence_total, segment_length, KEY_VALUE_HEADS, QUERY_HEADS // KEY_VALUE_HEADS, HEAD_SIZE
    )
    return jnp.transpose(reshaped_heads, (0, 2, 1, 3, 4)).reshape(
        sequence_total * KEY_VALUE_HEADS, segment_length, QUERY_HEADS // KEY_VALUE_HEADS, HEAD_SIZE
    )


def key_heads(angle_table, sequence_total, total_length):
    reshaped_heads = angle_table.reshape(sequence_total, total_length, KEY_VALUE_HEADS, HEAD_SIZE)
    return jnp.transpose(reshaped_heads, (0, 2, 1, 3)).reshape(
        sequence_total * KEY_VALUE_HEADS, total_length, HEAD_SIZE
    )


def merge_queries(angle_table, sequence_total, segment_length):
    reshaped_heads = angle_table.reshape(
        sequence_total, KEY_VALUE_HEADS, segment_length, QUERY_HEADS // KEY_VALUE_HEADS, HEAD_SIZE
    )
    return jnp.transpose(reshaped_heads, (0, 2, 1, 3, 4)).reshape(
        sequence_total * segment_length, QUERY_HEADS * HEAD_SIZE
    )


def merge_keys(angle_table, sequence_total, total_length):
    reshaped_heads = angle_table.reshape(sequence_total, KEY_VALUE_HEADS, total_length, HEAD_SIZE)
    return jnp.transpose(reshaped_heads, (0, 2, 1, 3)).reshape(
        sequence_total, total_length, KEY_VALUE_HEADS * HEAD_SIZE
    )


def softmax_weights(part_query, part_key, place_query, place_key):
    allowed = place_key[None, :] <= place_query[:, None]
    scores = jnp.einsum(
        "qrd,kd->rqk", part_query, part_key, preferred_element_type=jnp.float32
    ) * HEAD_SIZE ** (-0.5)
    scores = jnp.where(allowed[None], scores, -1e30)
    return jax.nn.softmax(scores, axis=-1)


def forward_head(packed):
    part_query, part_key, part_value, place_query, place_key = packed
    probs = softmax_weights(part_query, part_key, place_query, place_key)
    return jnp.einsum(
        "rqk,kd->qrd", probs.astype(jnp.bfloat16), part_value, preferred_element_type=jnp.float32
    )


def backward_head(packed):
    part_query, part_key, part_value, part_grad, place_query, place_key = packed
    probs = softmax_weights(part_query, part_key, place_query, place_key)
    grad_probs = jnp.einsum(
        "qrd,kd->rqk", part_grad, part_value, preferred_element_type=jnp.float32
    )
    row_delta = jnp.sum(probs * grad_probs, axis=-1, keepdims=True)
    grad_scores = (probs * (grad_probs - row_delta)).astype(jnp.bfloat16)
    grad_query = jnp.einsum(
        "rqk,kd->qrd", grad_scores, part_key, preferred_element_type=jnp.float32
    ) * HEAD_SIZE ** (-0.5)
    grad_key = jnp.einsum(
        "rqk,qrd->kd", grad_scores, part_query, preferred_element_type=jnp.float32
    ) * HEAD_SIZE ** (-0.5)
    value_gradient = jnp.einsum(
        "rqk,qrd->kd", probs.astype(jnp.bfloat16), part_grad, preferred_element_type=jnp.float32
    )
    return (grad_query, grad_key, value_gradient)


def feed_forward(normed_rows, gate_w, up_w, down_w):
    gate_pre = jnp.dot(normed_rows, gate_w, preferred_element_type=jnp.float32)
    up_proj = jnp.dot(normed_rows, up_w, preferred_element_type=jnp.float32)
    sigmoid_gate = jax.nn.sigmoid(gate_pre)
    hidden = (gate_pre * sigmoid_gate * up_proj).astype(jnp.bfloat16)
    return (
        jnp.dot(hidden, down_w, preferred_element_type=jnp.float32),
        (gate_pre, up_proj, sigmoid_gate, hidden),
    )


def feed_back(normed_rows, grad_rows, gate_w, up_w, down_w, kept_values):
    gate_pre, up_proj, sigmoid_gate, hidden = kept_values
    grad_hidden = times_nt(grad_rows, down_w)
    term_down = times_t(hidden, grad_rows)
    grad_gate = (
        grad_hidden * up_proj * (sigmoid_gate * (1.0 + gate_pre * (1.0 - sigmoid_gate)))
    ).astype(jnp.bfloat16)
    grad_up = (grad_hidden * (gate_pre * sigmoid_gate)).astype(jnp.bfloat16)
    grad_normed = times_nt(grad_gate, gate_w) + times_nt(grad_up, up_w)
    return (grad_normed, times_t(normed_rows, grad_gate), times_t(normed_rows, grad_up), term_down)


MESH = pl.DeviceIdType.MESH
ANY = pl.BlockSpec(memory_space=pl.ANY)
BF = jnp.bfloat16
F32 = jnp.float32
NN = (((1,), (0,)), ((), ()))
NT = (((1,), (1,)), ((), ()))
TN = (((0,), (0,)), ((), ()))


EARLY = 2


def dot(left, right, dims):
    return lax.dot_general(left, right, dims, preferred_element_type=F32)


class Grid:
    def __init__(self, chips, line):
        self.chips, self.line = chips, line
        self.replica = lax.axis_index("replica")
        flat = lax.axis_index("fsdp")
        self.x, self.core = flat // 2, flat % 2
        self.z = lax.axis_index("context")
        self.has_left, self.has_right = self.z > 0, self.z + 1 < line
        self.left = (self.replica, flat, self.z - 1)
        self.right = (self.replica, flat, self.z + 1)
        self.across = (self.replica, (1 - self.x) * 2 + self.core, self.z)
        self.twin = (self.replica, self.x * 2 + 1 - self.core, self.z)
        self.mirror = (1 - self.replica, flat, self.z)

    def order(self, k):
        z, n = self.z, self.line
        low = 2 * z < n
        near = 2 * jnp.minimum(z, n - 1 - z)
        away = jnp.where(k % 2 == 1, -((k + 1) // 2), k // 2)
        return jnp.where(
            k <= near, z + jnp.where(low, away, -away), jnp.where(low, k, n - 1 - k)
        )

    def slot(self, x, z):
        return x * self.line + z

    def greet(self, twin, mirror=False):
        barrier = pltpu.get_barrier_semaphore()

        def tell(device):
            pl.semaphore_signal(barrier, inc=1, device_id=device, device_id_type=MESH)

        pl.when(self.has_left)(lambda: tell(self.left))
        pl.when(self.has_right)(lambda: tell(self.right))
        tell(self.across)
        if twin:
            tell(self.twin)
        if mirror:
            tell(self.mirror)
        count = 1 + int(twin) + int(mirror) + self.has_left.astype(jnp.int32) + self.has_right.astype(jnp.int32)
        pl.semaphore_wait(barrier, count)


def remote(src, dst, send, recv, device):
    return pltpu.make_async_remote_copy(
        src_ref=src, dst_ref=dst, send_sem=send, recv_sem=recv, device_id=device, device_id_type=MESH
    )


def each(count, action):
    def step(i, carry):
        action(i)
        return carry

    lax.fori_loop(0, count, step, 0)


class Gather:
    def __init__(self, grid, block, everything, send, recv, parts, cross=None):
        self.grid, self.everything, self.send, self.recv = grid, everything, send, recv
        self.block, self.cross = block, cross
        self.rows = everything.shape[1] // parts
        self.last = parts - 1
        self.early = parts if cross is None else parts - 1

    def piece(self, x, z, part):
        start = pl.multiple_of(part * self.rows, self.rows)
        return self.everything.at[self.grid.slot(x, z), pl.ds(start, self.rows)]

    def copy(self, z, part, link, first=False):
        grid = self.grid
        device = (grid.right, grid.left, grid.across)[link]
        there = self.piece(grid.x, z, part)
        start = pl.multiple_of(part * self.rows, self.rows)
        here = self.block.at[pl.ds(start, self.rows)] if first else there
        return remote(
            here, there, self.send.at[z, part, link], self.recv.at[grid.slot(grid.x, z), part], device
        )

    def other(self, z, link):
        grid = self.grid
        here = self.piece(1 - grid.x, z, self.last)
        sem = self.recv.at[grid.slot(1 - grid.x, z), self.last]
        return remote(here, here, self.cross.at[z, link], sem, (grid.right, grid.left)[link])

    def ways(self, z):
        grid = self.grid
        return (
            (0, jnp.logical_and(z <= grid.z, grid.has_right)),
            (1, jnp.logical_and(z >= grid.z, grid.has_left)),
        )

    def sides(self, distance):
        grid = self.grid
        return (
            (grid.z - distance, grid.z >= distance, 0, grid.has_right),
            (grid.z + distance, grid.z + distance < grid.line, 1, grid.has_left),
        )

    def links(self, z, part, action, first=False, across=True):
        for link, go in self.ways(z):
            pl.when(go)(lambda link=link: action(self.copy(z, part, link, first)))
        if across:
            action(self.copy(z, part, 2, first))

    def send_own(self):
        grid = self.grid
        start = lambda c: c.start()
        if self.cross is not None:
            self.copy(grid.z, self.last, 2, True).start()
        each(self.early, lambda part: self.links(grid.z, part, start, True))
        if self.cross is not None:
            self.links(grid.z, self.last, start, True, False)

    def turn_in(self):
        grid = self.grid
        self.other(grid.z, 0).wait_recv()
        for link, go in self.ways(grid.z):
            pl.when(go)(lambda link=link: self.other(grid.z, link).start())

    def forward(self, distance, part, wait=True, along=True, across=True):
        for z, there, link, go in self.sides(distance):

            @pl.when(there)
            def _(z=z, link=link, go=go):
                if wait:
                    self.copy(z, part, 2).wait_recv()
                if along:
                    pl.when(go)(lambda: self.copy(z, part, link).start())
                if across:
                    self.copy(z, part, 2).start()

    def forward_last(self, distance):
        for z, there, link, go in self.sides(distance):

            @pl.when(there)
            def _(z=z, link=link, go=go):
                self.copy(z, self.last, 2).wait_recv()
                pl.when(go)(lambda: self.copy(z, self.last, link).start())
                self.other(z, link).wait_recv()
                pl.when(go)(lambda: self.other(z, link).start())

    def wait_across(self, z):
        grid = self.grid

        def wait(part):
            here = self.piece(1 - grid.x, z, part)
            sem = self.recv.at[grid.slot(1 - grid.x, z), part]
            remote(here, here, self.send.at[z, part, 2], sem, grid.across).wait_recv()

        each(self.early, wait)

    def finish(self):
        done = lambda c: c.wait_send()

        def place(z):
            each(self.early, lambda part: self.links(z, part, done))
            if self.cross is not None:
                self.links(z, self.last, done, across=False)
                for link, go in self.ways(z):
                    pl.when(go)(lambda link=link: self.other(z, link).wait_send())

        each(self.grid.line, place)
        if self.cross is not None:
            self.copy(self.grid.z, self.last, 2).wait_send()


class Scatter:
    def __init__(self, grid, partial, from_across, from_line, total, sems, parts, cross=None):
        self.grid, self.partial, self.from_across = grid, partial, from_across
        self.from_line, self.total = from_line, total
        self.across_send, self.across_recv, self.line_send, self.line_recv = sems
        self.parts, self.cross = parts, cross
        self.rows = partial.shape[1] // parts
        self.early = parts if cross is None else parts - 1
        self.last = parts - 1

    def run(self, part):
        return pl.ds(pl.multiple_of(part * self.rows, self.rows), self.rows)

    def steps(self):
        return (self.grid.line - 1) * self.early

    def rank(self, j):
        return self.grid.order(self.grid.line - 1 - j)

    def step(self, n):
        self.pass_on(self.rank(n // self.early), n % self.early)

    def place(self, z):
        return z if self.from_across is None else self.grid.slot(self.grid.x, z)

    def across(self, z, part):
        grid = self.grid
        return remote(
            self.partial.at[grid.slot(1 - grid.x, z), self.run(part)],
            self.from_across.at[z, self.run(part)],
            self.across_send.at[z, part],
            self.across_recv.at[z, part],
            grid.across,
        )

    def arrival(self, z, leftward):
        return z if leftward else z - 1 + self.grid.line - 1

    def along(self, z, part, leftward):
        grid = self.grid
        arrival = self.arrival(z, leftward)
        return remote(
            self.partial.at[self.place(z), self.run(part)],
            self.from_line.at[arrival, self.run(part)],
            self.line_send.at[z, part],
            self.line_recv.at[arrival, part],
            grid.left if leftward else grid.right,
        )

    def other(self, z, leftward):
        grid = self.grid
        buffer, send, recv = self.cross
        arrival = self.arrival(z, leftward)
        return remote(
            self.partial.at[grid.slot(1 - grid.x, z), self.run(self.last)],
            buffer.at[arrival],
            send.at[z],
            recv.at[arrival],
            grid.left if leftward else grid.right,
        )

    def send_across(self, z):
        each(self.early, lambda part: self.across(z, part).start())

    def both_ways(self, z, action):
        grid = self.grid
        pl.when(jnp.logical_and(z <= grid.z, grid.has_right))(lambda: action(True))
        pl.when(jnp.logical_and(z >= grid.z, grid.has_left))(lambda: action(False))

    def add_line(self, z, part):
        def add(leftward):
            self.along(z, part, leftward).wait_recv()
            arrival = self.arrival(z, leftward)
            self.total[...] += self.from_line[arrival, self.run(part)].astype(F32)

        self.both_ways(z, add)

    def gather_sum(self, z, part):
        value = self.partial[self.place(z), self.run(part)].astype(F32)
        if self.from_across is not None:
            self.across(z, part).wait_recv()
            value = value + self.from_across[z, self.run(part)].astype(F32)
        self.total[...] = value
        self.add_line(z, part)

    def send_along(self, z, part):
        grid = self.grid
        self.partial[self.place(z), self.run(part)] = self.total[...].astype(BF)
        pl.when(z < grid.z)(lambda: self.along(z, part, True).start())
        pl.when(z > grid.z)(lambda: self.along(z, part, False).start())

    def pass_on(self, z, part):
        self.gather_sum(z, part)
        self.send_along(z, part)

    def add_other(self, z):
        grid, run = self.grid, self.run(self.last)
        slot = grid.slot(1 - grid.x, z)
        self.total[...] = self.partial[slot, run].astype(F32)

        def add(leftward):
            self.other(z, leftward).wait_recv()
            self.total[...] += self.cross[0][self.arrival(z, leftward)].astype(F32)

        self.both_ways(z, add)
        self.partial[slot, run] = self.total[...].astype(BF)

    def last_step(self, m):
        grid = self.grid
        z = grid.order(grid.line - 1 - m)
        self.add_other(z)

        @pl.when(z == grid.z)
        def _():
            self.across(z, self.last).start()

        @pl.when(z != grid.z)
        def _():
            pl.when(z < grid.z)(lambda: self.other(z, True).start())
            pl.when(z > grid.z)(lambda: self.other(z, False).start())
            self.total[...] = self.partial[self.place(z), self.run(self.last)].astype(F32)
            self.add_line(z, self.last)
            self.send_along(z, self.last)

    def own(self, result):
        def part_sum(part):
            self.gather_sum(self.grid.z, part)
            result[self.run(part)] = self.total[...]

        each(self.parts, part_sum)

    def finish(self):
        grid = self.grid

        def place(z):
            def part_done(part):
                pl.when(z < grid.z)(lambda: self.along(z, part, True).wait_send())
                pl.when(z > grid.z)(lambda: self.along(z, part, False).wait_send())

            each(self.parts, part_done)
            if self.from_across is not None:
                each(self.early, lambda part: self.across(z, part).wait_send())
            if self.cross is not None:
                pl.when(z < grid.z)(lambda: self.other(z, True).wait_send())
                pl.when(z > grid.z)(lambda: self.other(z, False).wait_send())

        each(grid.line, place)
        if self.cross is not None:
            self.across(grid.z, self.last).wait_send()


def scatter_scratch(line, rows, width, parts):
    return [
        pltpu.VMEM((2 * line, rows, width), BF),
        pltpu.VMEM((line, rows, width), BF),
        pltpu.VMEM((2 * line - 2, rows, width), BF),
        pltpu.VMEM((rows // parts, width), F32),
        pltpu.SemaphoreType.DMA((line, parts)),
        pltpu.SemaphoreType.DMA((line, parts)),
        pltpu.SemaphoreType.DMA((line, parts)),
        pltpu.SemaphoreType.DMA((2 * line - 2, parts)),
    ]


def load_pairs(pairs, sems):
    copies = [pltpu.make_async_copy(src, dst, sems.at[i]) for i, (src, dst) in enumerate(pairs)]
    for copy in copies:
        copy.start()
    for copy in copies:
        copy.wait()


def feed_kernel(
    line, parts, tile,
    normed, tangent_all, gate_own, gate_twin, up_own, up_twin, down_own, down_twin,
    grad_sum, normed_all, hidden_all, grad_gate, grad_up, grad_down,
    mirror_gate, mirror_up, mirror_down, part_gate, part_up, part_down,
    mirror_send, mirror_recv,
    gate_w, up_w, down_w, hidden, dgate, dup, rows_n, rows_t,
    partial, from_across, from_line, total, across_send, across_recv, line_send, line_recv,
    other_line, other_send, other_recv, gather_cross,
    gather_send, gather_recv, load_sem, wide, tile_sem, stage_a, stage_b, stage_sem, stage_recv, piece_a, piece_b, piece_sem, hidden_sem,
):
    grid = Grid(2, line)
    rows, width = normed.shape
    cols = gate_own.shape[1]
    blocks = 2 * line
    me = grid.slot(grid.x, grid.z)
    grid.greet(True, True)
    gather = Gather(grid, normed, normed_all, gather_send, gather_recv, parts, gather_cross)
    scatter = Scatter(
        grid, partial, from_across, from_line, total,
        (across_send, across_recv, line_send, line_recv), parts,
        (other_line, other_send, other_recv),
    )
    gather.send_own()
    load_pairs(
        [
            (gate_own, gate_w.at[:, pl.ds(0, cols)]),
            (gate_twin, gate_w.at[:, pl.ds(cols, cols)]),
            (up_own, up_w.at[:, pl.ds(0, cols)]),
            (up_twin, up_w.at[:, pl.ds(cols, cols)]),
            (down_own, down_w.at[pl.ds(0, cols)]),
            (down_twin, down_w.at[pl.ds(cols, cols)]),
            (normed, rows_n),
        ],
        load_sem,
    )
    load_pairs([(rows_n, normed_all.at[me])], load_sem)
    gather.turn_in()

    forwards = (line - 1) * parts

    def advance(n):
        distance, part = n // parts + 1, n % parts

        @pl.when(n < forwards)
        def _():
            pl.when(part < gather.early)(lambda: gather.forward(distance, part))
            pl.when(part == gather.last)(lambda: gather.forward_last(distance))

        return n + 1

    def work(slot, n):
        tangent_load = pltpu.make_async_copy(tangent_all.at[slot], rows_t, load_sem.at[1])
        tangent_load.start()
        load_pairs([(normed_all.at[slot], rows_n)], load_sem)
        spot = pl.ds(pl.multiple_of(slot * rows, rows), rows)

        def hidden_tile(j, n):
            c = pl.ds(pl.multiple_of(j * cols, cols), cols)
            gate = dot(rows_n[...], gate_w[:, c], NN)
            up = dot(rows_n[...], up_w[:, c], NN)
            pl.when(j == 0)(tangent_load.wait)
            grad = dot(rows_t[...], down_w[c, :], NT)
            sig = jax.nn.sigmoid(gate)
            silu = gate * sig
            hidden[spot, c] = (silu * up).astype(BF)
            dgate[spot, c] = (grad * up * (sig * (1.0 + gate * (1.0 - sig)))).astype(BF)
            dup[spot, c] = (grad * silu).astype(BF)
            return advance(n)

        n = lax.fori_loop(0, 2, hidden_tile, n)

        def back_tile(j, carry):
            c = pl.ds(pl.multiple_of(j * cols, cols), cols)
            sums = dot(dgate[spot, :], gate_w[c, :], NT) + dot(dup[spot, :], up_w[c, :], NT)
            partial[slot, :, c] = sums.astype(BF)
            return carry

        lax.fori_loop(0, width // cols, back_tile, 0)
        return advance(n)

    def stage(distance, n):
        def visit(i, n):
            z = grid.z + jnp.where(i % 2 == 0, -distance, distance)
            inside = jnp.logical_and(z >= 0, z < line)

            def block(n):
                n = lax.fori_loop(n, jnp.maximum(n, distance * parts), lambda m, c: advance(m), n)
                pl.when(i >= 2)(lambda: gather.wait_across(z))
                return work(grid.slot(jnp.where(i < 2, grid.x, 1 - grid.x), z), n)

            go = jnp.logical_and(inside, jnp.logical_or(distance > 0, i % 2 == 0))
            return lax.cond(go, block, lambda n: n, n)

        return lax.fori_loop(0, 4, visit, n)

    count = lax.fori_loop(0, line, stage, 0)
    lax.fori_loop(count, jnp.maximum(count, forwards), lambda m, c: advance(m), 0)
    hidden_copy = pltpu.make_async_copy(hidden, hidden_all, hidden_sem)
    hidden_copy.start()
    for j in range(line):
        scatter.send_across(scatter.rank(j))

    tiles = width // tile

    early_tiles = mirror_send.shape[0]

    def wide_loads(t, start):
        j, buf = t % tiles, t % 2
        c = pl.ds(pl.multiple_of(j * tile, tile), tile)
        for i, source in enumerate((normed_all, tangent_all)):
            copy = pltpu.make_async_copy(source.at[:, :, c], wide.at[buf, i], tile_sem.at[buf, i])
            copy.start() if start else copy.wait()

    def stages(t):
        j, buf = t % tiles, t % 2
        c = pl.ds(pl.multiple_of(j * tile, tile), tile)
        return [
            remote(src, dst, stage_sem.at[buf, i], stage_recv.at[j, i], grid.twin)
            for i, (src, dst) in enumerate(
                (
                    (stage_a.at[buf, 0], part_gate.at[c, :]),
                    (stage_a.at[buf, 1], part_up.at[c, :]),
                    (stage_b.at[buf], part_down.at[:, c]),
                )
            )
        ]

    def results(t):
        j, buf = t % tiles, t % 2
        c = pl.ds(pl.multiple_of(j * tile, tile), tile)
        return [
            pltpu.make_async_copy(src, dst, stage_sem.at[buf, i])
            for i, (src, dst) in enumerate(
                (
                    (stage_a.at[buf, 0], grad_gate.at[c, :]),
                    (stage_a.at[buf, 1], grad_up.at[c, :]),
                    (stage_b.at[buf], grad_down.at[:, c]),
                )
            )
        ]

    def mirrored(t):
        j = t % tiles
        c = pl.ds(pl.multiple_of(j * tile, tile), tile)
        return [
            remote(src, dst, mirror_send.at[j, i], mirror_recv.at[j, i], grid.mirror)
            for i, (src, dst) in enumerate(
                (
                    (grad_gate.at[c, :], mirror_gate.at[c, :]),
                    (grad_up.at[c, :], mirror_up.at[c, :]),
                    (grad_down.at[:, c], mirror_down.at[:, c]),
                )
            )
        ]

    def pieces(t):
        c = pl.ds(pl.multiple_of((t % tiles) * tile, tile), tile)
        return [
            (part_gate.at[c, :], piece_a.at[0]),
            (part_up.at[c, :], piece_a.at[1]),
            (part_down.at[:, c], piece_b),
        ]

    wide_loads(0, True)

    def weights(t, carry):
        buf = t % 2
        pl.when(t + 1 < 2 * tiles)(lambda: wide_loads(t + 1, True))
        wide_loads(t, False)
        tall = blocks * rows
        tokens = wide[buf, 0].reshape(tall, tile)
        tangents = wide[buf, 1].reshape(tall, tile)

        @pl.when(t < tiles)
        def _():
            theirs = slice(cols, 2 * cols)

            @pl.when(t >= 2)
            def _():
                for copy in stages(t - 2):
                    copy.wait_send()

            stage_a[buf, 0] = dot(tokens, dgate[:, theirs], TN).astype(BF)
            stage_a[buf, 1] = dot(tokens, dup[:, theirs], TN).astype(BF)
            stage_b[buf] = dot(hidden[:, theirs], tangents, TN).astype(BF)
            for copy in stages(t):
                copy.start()

        @pl.when(t >= tiles)
        def _():
            for copy in stages(t):
                copy.wait_recv()
            loads = [
                pltpu.make_async_copy(src, dst, piece_sem.at[i])
                for i, (src, dst) in enumerate(pieces(t))
            ]
            for copy in loads:
                copy.start()

            @pl.when(t < tiles + 2)
            def _():
                for copy in stages(t - 2):
                    copy.wait_send()

            @pl.when(t >= tiles + 2)
            def _():
                for copy in results(t - 2):
                    copy.wait()

                @pl.when(t < tiles + 2 + early_tiles)
                def _():
                    for copy in mirrored(t - 2):
                        copy.start()

            mine = slice(0, cols)
            own_gate = dot(tokens, dgate[:, mine], TN)
            own_up = dot(tokens, dup[:, mine], TN)
            own_down = dot(hidden[:, mine], tangents, TN)
            for copy in loads:
                copy.wait()
            stage_a[buf, 0] = (own_gate + piece_a[0].astype(F32)).astype(BF)
            stage_a[buf, 1] = (own_up + piece_a[1].astype(F32)).astype(BF)
            stage_b[buf] = (own_down + piece_b[...].astype(F32)).astype(BF)
            for copy in results(t):
                copy.start()

        n = t - 3 * lag
        pl.when(n >= 0)(lambda: scatter.step(n))
        m = t // 3 - lag
        ready = jnp.logical_and(t % 3 == 2, jnp.logical_and(m >= 0, m < line))
        pl.when(ready)(lambda: scatter.last_step(m))
        return carry

    lag = jnp.where(jnp.logical_and(grid.has_left, grid.has_right), 1, 0)
    lax.fori_loop(0, 2 * tiles, weights, 0)

    def rest(n, carry):
        scatter.step(n)
        return carry

    lax.fori_loop(2 * tiles - 3 * lag, scatter.steps(), rest, 0)
    scatter.own(grad_sum)
    for t in (2 * tiles - 2, 2 * tiles - 1):
        for copy in results(t):
            copy.wait()
    gather.finish()
    scatter.finish()
    hidden_copy.wait()
    for t in range(early_tiles):
        for copy in mirrored(t):
            copy.wait()


def feed_call(normed, tangent_all, gates, ups, downs, line):
    rows, width = normed.shape
    cols = gates[0].shape[1]
    blocks, parts, tile = 2 * line, 8, 256
    tiles = width // tile
    tall = blocks * rows
    shapes = jax.ShapeDtypeStruct
    hbm = lambda *s: shapes(s, BF)
    return pl.pallas_call(
        functools.partial(feed_kernel, line, parts, tile),
        out_shape=(
            shapes((rows, width), F32),
            hbm(blocks, rows, width), hbm(tall, 2 * cols),
            hbm(width, cols), hbm(width, cols), hbm(cols, width),
            hbm(width, cols), hbm(width, cols), hbm(cols, width),
            hbm(width, cols), hbm(width, cols), hbm(cols, width),
        ),
        in_specs=[ANY] * 8,
        out_specs=(pl.BlockSpec(memory_space=pltpu.VMEM),) + (ANY,) * 11,
        scratch_shapes=[
            pltpu.SemaphoreType.DMA((EARLY, 3)), pltpu.SemaphoreType.DMA((EARLY, 3)),
            pltpu.VMEM((width, 2 * cols), BF), pltpu.VMEM((width, 2 * cols), BF), pltpu.VMEM((2 * cols, width), BF),
            pltpu.VMEM((tall, 2 * cols), BF), pltpu.VMEM((tall, 2 * cols), BF), pltpu.VMEM((tall, 2 * cols), BF),
            pltpu.VMEM((rows, width), BF), pltpu.VMEM((rows, width), BF),
            *scatter_scratch(line, rows, width, parts),
            pltpu.VMEM((2 * line - 2, rows // parts, width), BF),
            pltpu.SemaphoreType.DMA((line,)), pltpu.SemaphoreType.DMA((2 * line - 2,)),
            pltpu.SemaphoreType.DMA((line, 2)),
            pltpu.SemaphoreType.DMA((line, parts, 3)), pltpu.SemaphoreType.DMA((blocks, parts)),
            pltpu.SemaphoreType.DMA((8,)),
            pltpu.VMEM((2, 2, blocks, rows, tile), BF), pltpu.SemaphoreType.DMA((2, 2)),
            pltpu.VMEM((2, 2, tile, cols), BF), pltpu.VMEM((2, cols, tile), BF),
            pltpu.SemaphoreType.DMA((2, 3)), pltpu.SemaphoreType.DMA((tiles, 3)),
            pltpu.VMEM((2, tile, cols), BF), pltpu.VMEM((cols, tile), BF), pltpu.SemaphoreType.DMA((3,)),
            pltpu.SemaphoreType.DMA,
        ],
        compiler_params=pltpu.CompilerParams(
            collective_id=1, has_side_effects=True, vmem_limit_bytes=63 * 2**20
        ),
        name="feed",
    )(normed, tangent_all, gates[0], gates[1], ups[0], ups[1], downs[0], downs[1])


class Thirds(Scatter):
    def run(self, part):
        quarter = self.rows
        start = jnp.where(part == 2, self.grid.replica, 2 + part) * quarter
        return pl.ds(pl.multiple_of(start, quarter), quarter)


def sums_kernel(
    line,
    normed, attended, grad_qkv, grad_out, twin_normed, twin_attended, twin_out, out_across,
    tokens, grad_middle, weights, gain, term_two,
    result, result_out, grad_tokens,
    across_v, out_partial, out_line, out_total, out_send, out_recv, out_mine, out_theirs, out_sem,
    near_send, near_recv, near_sem,
    both_normed, both_attended, both_qkv, both_out, load_sem, twin_send, twin_recv,
    partial, from_across, from_line, total, across_send, across_recv, line_send, line_recv,
    mine, theirs, mirror_send, mirror_recv, from_mirror, quarter_send, quarter_recv,
    in_weights, weight_sem, token_v, middle_v, grad_normed, terms, own_terms, twin_terms,
):
    grid = Grid(2, line)
    rows, width = normed.shape
    run = partial.shape[1]
    quarter = run // 4
    narrow = grad_qkv.shape[1]
    grid.greet(True, True)
    scatter = Thirds(
        grid, partial, from_across, from_line, total,
        (across_send, across_recv, line_send, line_recv), 3,
    )
    scatter.rows = quarter
    own, twin = pl.ds(0, rows), pl.ds(rows, rows)
    swap_qkv = remote(grad_qkv, both_qkv.at[twin], twin_send.at[0], twin_recv.at[0], grid.twin)
    swap_qkv.start()
    load_pairs(
        [
            (attended, both_attended.at[own]),
            (twin_attended, both_attended.at[twin]),
            (grad_out, both_out.at[own]),
            (twin_out, both_out.at[twin]),
            (out_across, across_v),
            (normed, both_normed.at[own]),
            (twin_normed, both_normed.at[twin]),
            (grad_qkv, both_qkv.at[own]),
        ],
        load_sem,
    )
    later = [
        pltpu.make_async_copy(src, dst, weight_sem.at[i])
        for i, (src, dst) in enumerate(
            (
                (weights.at[:, :, pl.ds(0, narrow)], in_weights),
                (tokens, token_v),
                (grad_middle, middle_v),
            )
        )
    ]
    for copy in later:
        copy.start()
    tall = line * run
    tile = 512
    away = pl.ds(pl.multiple_of((1 - grid.replica) * quarter, quarter), quarter)
    here = pl.ds(pl.multiple_of(grid.replica * quarter, quarter), quarter)

    outs = Scatter(
        grid, out_partial, None, out_line, out_total, (None, None, out_send, out_recv), 4
    )

    nears = [
        remote(near_send.at[j], near_recv.at[j], near_sem.at[0, j], near_sem.at[1, j], grid.across)
        for j in range(2)
    ]

    def near_step(i):
        c = pl.ds(pl.multiple_of(i * tile, tile), tile)
        for j in range(2):
            first = ((1 - grid.x) * 2 + grid.core) * tall + grid.order(j) * run
            theirs = pl.ds(pl.multiple_of(first, run), run)
            near_send[j, :, c] = dot(both_attended[:, theirs], both_out[:, c], TN).astype(BF)

    def sweep(part):
        each(line - 1, lambda i: scatter.pass_on(scatter.rank(i), part))

    def out_step(i):
        c = pl.ds(pl.multiple_of(i * tile, tile), tile)
        value = dot(both_attended[:, features(grid.x)], both_out[:, c], TN)
        value = value.reshape(line, run, tile) + across_v[:, :, c].astype(F32)
        out_partial[:, :, c] = value.astype(BF)

    def to_mirror(slot):
        return remote(
            partial.at[slot, away], from_mirror.at[slot],
            quarter_send.at[slot], quarter_recv.at[slot], grid.mirror,
        )

    def features(x):
        return pl.ds(pl.multiple_of((x * 2 + grid.core) * tall, tall), tall)

    def column(j, carry):
        x = jnp.where(j == 0, 1 - grid.x, grid.x)
        blocks = pl.ds(x * line, line)

        def wide(left, right, first):
            def step(i, inner):
                c = pl.ds(pl.multiple_of(i * tile, tile), tile)
                to = pl.ds(pl.multiple_of(first + i * tile, 128), tile)
                value = dot(left[:, features(x)], right[:, c], TN).astype(BF)
                partial[blocks, :, to] = value.reshape(line, run, tile)
                return inner

            lax.fori_loop(0, right.shape[1] // tile, step, 0)

        wide(both_normed, both_qkv, 0)
        partial[blocks, :, narrow:] = jnp.zeros((line, run, 128), BF)
        for k in range(line - 1, -1, -1):
            z = grid.order(k)
            to_mirror(grid.slot(x, z)).start()
            pl.when(j == 0)(lambda z=z: scatter.across(z, 0).start())
        return carry

    for j in range(2):
        across_v[grid.order(j)] = jnp.zeros((run, width), BF)
    each(width // tile, near_step)
    nears[1].start()
    each(width // tile, out_step)
    early_outs = (line - 2) * outs.early
    middling = jnp.logical_and(grid.has_left, grid.has_right)

    def when_end(action):
        pl.when(jnp.logical_not(middling))(action)

    when_end(lambda: each(early_outs, outs.step))
    swap_qkv.wait()
    lax.fori_loop(0, 2, column, 0)
    nears[0].start()
    when_end(lambda: sweep(0))
    for copy in later:
        copy.wait()

    def back_step(j, carry):
        units = pl.ds(j * (tile // run), tile // run)
        c = pl.ds(pl.multiple_of(j * tile, tile), tile)
        right = in_weights[units].reshape(tile, narrow)
        grad_normed[:, c] = dot(both_qkv[own, :], right, NT)
        return carry

    lax.fori_loop(0, width // tile, back_step, 0)
    terms[...] = jnp.zeros_like(terms)
    chunk = 64

    def norm_step(j, carry):
        r = pl.ds(pl.multiple_of(j * chunk, chunk), chunk)
        value = token_v[r, :].astype(F32)
        factor = lax.rsqrt(jnp.mean(value * value, axis=1, keepdims=True) + norm_eps)
        unit = value * factor
        grad = grad_normed[r, :]
        terms[0:1, :] += jnp.sum(grad * unit, axis=0, keepdims=True)
        scaled = grad * gain[0:1, :]
        mean = jnp.mean(scaled * unit, axis=1, keepdims=True)
        grad_tokens[r, :] = (middle_v[r, :] + factor * (scaled - unit * mean)).astype(BF)
        return carry

    lax.fori_loop(0, rows // chunk, norm_step, 0)
    terms[1:2, :] = term_two[...]
    own_terms[...] = terms[...].astype(BF)
    swap_terms = remote(own_terms, twin_terms, twin_send.at[1], twin_recv.at[1], grid.twin)
    swap_terms.start()
    swap_terms.wait()
    for x in range(2):
        for z in range(line):
            first = pl.multiple_of((x * 2 + grid.core) * tall + z * run, run)
            c = pl.ds(first, run)
            value = own_terms[:, c].astype(F32) + twin_terms[:, c].astype(F32)
            partial[x * line + z, 3 * quarter : 3 * quarter + 16, narrow:] = value.astype(BF)
    for k in range(line - 1, -1, -1):
        scatter.across(grid.order(k), 1).start()

    def add_mirror(x):
        def step(i, carry):
            slot = grid.slot(x, grid.order(line - 1 - i))
            to_mirror(slot).wait_recv()
            value = partial[slot, here].astype(F32) + from_mirror[slot].astype(F32)
            partial[slot, here] = value.astype(BF)
            return carry

        lax.fori_loop(0, line, step, 0)

    add_mirror(1 - grid.x)
    for k in range(line - 1, -1, -1):
        scatter.across(grid.order(k), 2).start()
    pl.when(middling)(lambda: each(early_outs, outs.step))
    nears[1].wait()
    next_place = grid.order(1)
    out_partial[next_place] = (
        out_partial[next_place].astype(F32) + near_recv[1].astype(F32)
    ).astype(BF)
    pl.when(middling)(lambda: sweep(0))

    def out_rest(n, carry):
        outs.step(n)
        return carry

    lax.fori_loop(early_outs, outs.steps(), out_rest, 0)
    sweep(1)

    def swap(part, whole=True):
        at = scatter.run(part)
        return remote(
            mine.at[at], theirs.at[at], mirror_send.at[part], mirror_recv.at[part], grid.mirror
        )

    def settle(part):
        scatter.gather_sum(grid.z, part)
        mine[scatter.run(part)] = total[...].astype(BF)
        swap(part).start()

    outs.own(result_out)
    nears[0].wait()
    result_out[...] += near_recv[0].astype(F32)
    out_mine[...] = result_out[...].astype(BF)
    out_swap = remote(out_mine, out_theirs, out_sem.at[0], out_sem.at[1], grid.mirror)
    out_swap.start()
    add_mirror(grid.x)
    settle(0)
    sweep(2)
    settle(1)
    settle(2)
    result[here] = mine[here].astype(F32)
    for part in range(2):
        swap(part).wait()
        at = scatter.run(part)
        result[at] = mine[at].astype(F32) + theirs[at].astype(F32)
    swap(2).wait_send()
    remote(mine.at[away], theirs.at[away], mirror_send.at[2], mirror_recv.at[2], grid.mirror).wait_recv()
    result[away] = theirs[away].astype(F32)
    out_swap.wait()
    result_out[...] = out_mine[...].astype(F32) + out_theirs[...].astype(F32)
    outs.finish()
    scatter.finish()

    def sent(slot, carry):
        to_mirror(slot).wait_send()
        return carry

    lax.fori_loop(0, 2 * line, sent, 0)


def sums_call(
    normed, attended, grad_qkv, grad_out, others, tokens, grad_middle, weights, gain, term_two, line
):
    rows, width = normed.shape
    narrow = grad_qkv.shape[1]
    run, whole = weights.shape[1], narrow + 128
    quarter = run // 4
    vmem = pl.BlockSpec(memory_space=pltpu.VMEM)
    dma = pltpu.SemaphoreType.DMA
    like = lambda a: pltpu.VMEM(a.shape, a.dtype)
    return pl.pallas_call(
        functools.partial(sums_kernel, line),
        out_shape=(
            jax.ShapeDtypeStruct((run, whole), F32), jax.ShapeDtypeStruct((run, width), F32),
            jax.ShapeDtypeStruct((rows, width), BF),
        ),
        in_specs=[ANY] * 11 + [vmem] * 2,
        out_specs=(vmem,) * 3,
        scratch_shapes=[
            pltpu.VMEM((line, run, width), BF), pltpu.VMEM((line, run, width), BF),
            pltpu.VMEM((2 * line - 2, run, width), BF), pltpu.VMEM((quarter, width), F32),
            dma((line, 4)), dma((2 * line - 2, 4)),
            pltpu.VMEM((run, width), BF), pltpu.VMEM((run, width), BF), dma((2,)),
            pltpu.VMEM((2, run, width), BF), pltpu.VMEM((2, run, width), BF), dma((2, 2)),
            pltpu.VMEM((2 * rows, width), BF), pltpu.VMEM((2 * rows, width), BF),
            pltpu.VMEM((2 * rows, narrow), BF), pltpu.VMEM((2 * rows, width), BF),
            dma((8,)), dma((2,)), dma((2,)),
            pltpu.VMEM((2 * line, run, whole), BF), pltpu.VMEM((line, run, whole), BF),
            pltpu.VMEM((2 * line - 2, run, whole), BF), pltpu.VMEM((quarter, whole), F32),
            dma((line, 3)), dma((line, 3)), dma((line, 3)), dma((2 * line - 2, 3)),
            pltpu.VMEM((run, whole), BF), pltpu.VMEM((run, whole), BF), dma((3,)), dma((3,)),
            pltpu.VMEM((2 * line, quarter, whole), BF), dma((2 * line,)), dma((2 * line,)),
            pltpu.VMEM((weights.shape[0], run, narrow), BF), dma((3,)),
            like(tokens), like(grad_middle), pltpu.VMEM((rows, width), F32),
            pltpu.VMEM((16, width), F32), pltpu.VMEM((16, width), BF), pltpu.VMEM((16, width), BF),
        ],
        compiler_params=pltpu.CompilerParams(
            collective_id=3, has_side_effects=True, vmem_limit_bytes=63 * 2**20
        ),
        name="sums",
    )(
        normed, attended, grad_qkv, grad_out, *others, tokens, grad_middle, weights, gain, term_two
    )


def gather_weights(
    grid, block, everything, send, recv, twin_send, twin_recv, meanwhile, afterwards
):
    line = grid.line
    rows = block.shape[0] // 4
    carry_a, carry_b = grid.replica * 2, grid.replica * 2 + 1
    other_a, other_b = (1 - grid.replica) * 2, (1 - grid.replica) * 2 + 1
    right, left, across, mirror = range(4)
    devices = (grid.right, grid.left, grid.across, grid.mirror)

    def run(quarter):
        return pl.ds(pl.multiple_of(quarter * rows, rows), rows)

    def place(x, core, z, quarter):
        return everything.at[(x * 2 + core) * line + z, run(quarter)]

    def copy(x, z, quarter, link, first=False):
        there = place(x, grid.core, z, quarter)
        here = block.at[run(quarter)] if first else there
        unit = x * line + z
        return remote(
            here, there, send.at[quarter, unit, link], recv.at[quarter, unit], devices[link]
        )

    def share(x, z, quarter, first=False):
        there = place(x, grid.core, z, quarter)
        here = block.at[run(quarter)] if first else there
        unit = x * line + z
        return remote(
            here, there, twin_send.at[quarter, unit], twin_recv.at[quarter, unit], grid.twin
        )

    def arrived(x, z, quarter):
        copy(x, z, quarter, across).wait_recv()
        share(x, z, quarter).start()

    copy(grid.x, grid.z, carry_b, across, True).start()
    copy(grid.x, grid.z, carry_a, across, True).start()
    copy(grid.x, grid.z, other_a, across, True).start()
    for link, go in ((right, grid.has_right), (left, grid.has_left)):

        @pl.when(go)
        def _(link=link):
            copy(grid.x, grid.z, carry_a, link, True).start()
            copy(grid.x, grid.z, carry_b, link, True).start()

    for quarter in range(4):
        share(grid.x, grid.z, quarter, True).start()
    meanwhile()

    arrived(1 - grid.x, grid.z, carry_b)
    copy(1 - grid.x, grid.z, carry_b, mirror).start()
    for link, go in ((right, grid.has_right), (left, grid.has_left)):
        pl.when(go)(lambda link=link: copy(1 - grid.x, grid.z, carry_b, link).start())

    def sides(distance):
        return (
            (grid.z - distance, grid.z >= distance, right, grid.has_right),
            (grid.z + distance, grid.z + distance < line, left, grid.has_left),
        )

    def step(distance, carry):
        for x, quarter in (
            (grid.x, carry_a),
            (grid.x, carry_b),
            (1 - grid.x, carry_b),
        ):
            for z, there, link, go in sides(distance):

                @pl.when(there)
                def _(x=x, quarter=quarter, z=z, link=link, go=go):
                    copy(x, z, quarter, across).wait_recv()
                    pl.when(go)(lambda: copy(x, z, quarter, link).start())
                    copy(x, z, quarter, mirror).start()
                    if quarter is carry_a:
                        copy(x, z, quarter, across).start()
                    share(x, z, quarter).start()

        for z, there, _, _ in sides(distance - 1):

            @pl.when(jnp.logical_and(there, distance > 1))
            def _(z=z):
                arrived(grid.x, z, other_a)
                copy(grid.x, z, other_a, across).start()

        return carry

    lax.fori_loop(1, line + 1, step, 0)
    afterwards()

    def last(z, carry):
        arrived(1 - grid.x, z, carry_a)
        arrived(1 - grid.x, z, other_a)
        arrived(1 - grid.x, z, other_b)
        pl.when(z != grid.z)(lambda: arrived(grid.x, z, other_b))
        return carry

    lax.fori_loop(0, line, last, 0)

    def finish(z, carry):
        away = z != grid.z
        for x in (grid.x, 1 - grid.x):
            for quarter in range(4):
                share(x, z, quarter).wait()
        for x, quarter in ((grid.x, carry_a), (grid.x, carry_b), (1 - grid.x, carry_b)):
            to_mirror = jnp.logical_or(away, jnp.bool_(x is not grid.x))
            pl.when(to_mirror)(
                lambda x=x, quarter=quarter: copy(x, z, quarter, mirror).wait_send()
            )
            for link, go in (
                (right, jnp.logical_and(z <= grid.z, grid.has_right)),
                (left, jnp.logical_and(z >= grid.z, grid.has_left)),
            ):
                pl.when(go)(
                    lambda x=x, quarter=quarter, link=link: copy(x, z, quarter, link).wait_send()
                )
        copy(grid.x, z, carry_a, across).wait_send()
        copy(grid.x, z, other_a, across).wait_send()
        return carry

    lax.fori_loop(0, line, finish, 0)
    copy(grid.x, grid.z, carry_b, across, True).wait_send()


def mask(places, own_places):
    return jnp.where(places[...] <= own_places[...], 0.0, -1e30).astype(F32)


class Line:
    def __init__(self, grid, block, everything, send, recv):
        self.grid, self.block, self.everything = grid, block, everything
        self.send, self.recv = send, recv

    def copy(self, z, link, first=False):
        grid = self.grid
        there = self.everything.at[z]
        here = self.block if first else there
        device = (grid.right, grid.left)[link]
        return remote(here, there, self.send.at[z, link], self.recv.at[z], device)

    def send_own(self):
        grid = self.grid
        for link, go in ((0, grid.has_right), (1, grid.has_left)):
            pl.when(go)(lambda link=link: self.copy(grid.z, link, True).start())

    def forward(self, distance):
        grid = self.grid
        for z, there, link, go in (
            (grid.z - distance, grid.z >= distance, 0, grid.has_right),
            (grid.z + distance, grid.z + distance < grid.line, 1, grid.has_left),
        ):

            @pl.when(there)
            def _(z=z, link=link, go=go):
                self.copy(z, link).wait_recv()
                pl.when(go)(lambda: self.copy(z, link).start())

    def finish(self):
        grid = self.grid

        def step(z, carry):
            for link, go in (
                (0, jnp.logical_and(z <= grid.z, grid.has_right)),
                (1, jnp.logical_and(z >= grid.z, grid.has_left)),
            ):
                pl.when(go)(lambda link=link: self.copy(z, link).wait_send())
            return carry

        lax.fori_loop(0, grid.line, step, 0)


def turn(value, cosine, sine, scale):
    parts = []
    lane = lax.broadcasted_iota(jnp.int32, (value.shape[0], 128), 1) % HEAD_SIZE
    for first in range(0, value.shape[1], 128):
        pair = value[:, first : first + 128]
        swapped = jnp.where(
            lane < HEAD_SIZE // 2,
            pltpu.roll(pair, 128 - HEAD_SIZE // 2, 1),
            pltpu.roll(pair, HEAD_SIZE // 2, 1),
        )
        parts.append(((pair * cosine[...] + swapped * sine[...]) * scale).astype(BF))
    return parts[0] if len(parts) == 1 else jnp.concatenate(parts, axis=1)


def halves(pair, half):
    pair = pair.astype(F32)
    turned = pltpu.roll(pair, HEAD_SIZE, 1)
    lane = lax.broadcasted_iota(jnp.int32, pair.shape, 1) // HEAD_SIZE
    first = jnp.where(half == 0, pair, turned)
    second = jnp.where(half == 0, turned, pair)
    both = jnp.concatenate([first, second], axis=0)
    return jnp.where(jnp.concatenate([lane, lane], axis=0) == half, both, 0.0).astype(BF)


def unhalves(both, half):
    rows = both.shape[0] // 2
    first, second = both[:rows], both[rows:]
    lane = lax.broadcasted_iota(jnp.int32, first.shape, 1) // HEAD_SIZE
    first = jnp.where(half == 0, first, pltpu.roll(first, HEAD_SIZE, 1))
    second = jnp.where(half == 0, pltpu.roll(second, HEAD_SIZE, 1), second)
    return jnp.where(lane == 0, first, second)


def front_kernel(
    line, parts,
    query_w, key_w, value_w, out_w, tokens, tangent, cosine, sine, gain_one, gain_two, places, own_places,
    attended, middle, normed, first_normed, queries, logs, gain, keyed_out, tangent_all, weights_out,
    everything, keyed, keyed_all, bias_v, token_v, cosine_v, sine_v, scores, probs, sums, stage, load_sem,
    key_send, key_recv, send, recv, own_sem, weight_send, weight_recv, twin_send, twin_recv,
):
    grid = Grid(2, line)
    rows, width = tokens.shape
    narrow = keyed.shape[1] // 2
    total = places.shape[1]
    extra = width + 2 * narrow
    after = extra + 128
    me = grid.slot(grid.x, grid.z)
    chunk = rows // 2
    tile = 512
    block = everything.at[(grid.x * 2 + grid.core) * line + grid.z]
    starts = (0, width, width + narrow, after)
    load_pairs(
        [
            (part, block.at[:, pl.ds(first, part.shape[1])])
            for first, part in zip(starts, (query_w, key_w, value_w, out_w))
        ],
        load_sem,
    )
    row = lax.broadcasted_iota(jnp.int32, (16, 128), 0)
    both_gains = jnp.where(row == 0, gain_one[...].astype(F32), gain_two[...].astype(F32))
    everything[(grid.x * 2 + grid.core) * line + grid.z, 0:16, extra:after] = both_gains.astype(BF)
    grid.greet(True, True)

    def meanwhile():
        load_pairs(
            [
                (tangent, stage),
                (tokens, token_v),
                (cosine, cosine_v),
                (sine, sine_v),
            ],
            load_sem,
        )
        load_pairs([(stage, tangent_all.at[me])], own_sem)
        bias_v[...] = mask(places, own_places)

    gather = Gather(grid, tangent, tangent_all, send, recv, parts)
    soon = 1

    def tangent_first():
        gather.send_own()
        for part in range(soon):
            gather.forward(1, part)

    gather_weights(
        grid, block, everything, weight_send, weight_recv, twin_send, twin_recv, meanwhile,
        tangent_first,
    )
    weights_copy = pltpu.make_async_copy(everything, weights_out, own_sem.at[1])
    weights_copy.start()
    units, run = everything.shape[0], everything.shape[1]
    for unit in range(units):
        for which in range(2):
            gain[which : which + 1, unit * run : (unit + 1) * run] = everything[
                unit, which : which + 1, extra:after
            ].astype(F32)

    def norm(source, target, which):
        def step(j, carry):
            here = pl.ds(pl.multiple_of(j * chunk, chunk), chunk)
            value = source[here, :].astype(F32)
            factor = lax.rsqrt(jnp.mean(value * value, axis=1, keepdims=True) + norm_eps)
            target[here, :] = (value * factor * gain[which : which + 1, :]).astype(BF)
            return carry

        lax.fori_loop(0, rows // chunk, step, 0)

    norm(token_v, first_normed, 0)

    def project(c):
        return dot(first_normed[...], everything[:, :, c].reshape(width, tile), NN)

    for first in range(0, narrow, tile):
        keyed[:, first : first + tile] = turn(project(slice(width + first, width + first + tile)), cosine_v, sine_v, 1.0)
        keyed[:, narrow + first : narrow + first + tile] = project(
            slice(width + narrow + first, width + narrow + first + tile)
        ).astype(BF)
    line_keys = Line(grid, keyed, keyed_all, key_send, key_recv)
    line_keys.send_own()
    for part in range(soon, parts):
        gather.forward(1, part, along=False)
    keyed_all[grid.z] = keyed[...]

    def query_step(j, carry):
        c = pl.ds(pl.multiple_of(j * tile, tile), tile)
        queries[:, c] = turn(project(c), cosine_v, sine_v, HEAD_SIZE ** (-0.5))
        return carry

    lax.fori_loop(0, width // tile, query_step, 0)
    def advance(n):
        gather.forward(n // parts + 2, n % parts)

    for distance in range(1, line - 1):
        line_keys.forward(distance)
    for part in range(soon, parts):
        gather.forward(1, part, wait=False, across=False)
    for n in range(soon):
        advance(n)
    line_keys.forward(line - 1)

    logs[...] = jnp.zeros_like(logs)
    pairs = width // (2 * HEAD_SIZE)
    group = pairs // (narrow // (2 * HEAD_SIZE))

    def pair_step(i, carry):
        c = pl.ds(pl.multiple_of(i * 128, 128), 128)
        half = (i // (group // 2)) % 2
        first_key = pl.multiple_of((i // group) * 128, 128)
        keys = keyed_all[:, :, pl.ds(first_key, 128)].reshape(total, 128)
        values = keyed_all[:, :, pl.ds(first_key + narrow, 128)].reshape(total, 128)
        scores[...] = dot(halves(queries[:, c], half), keys, NT)

        def soft(j, inner):
            here = pl.ds(pl.multiple_of(j * rows, rows), rows)
            value = scores[here, :] + bias_v[...]
            top = jnp.max(value, axis=1, keepdims=True)
            power = jnp.exp(value - top)
            size = jnp.sum(power, axis=1, keepdims=True)
            probs[here, :] = power.astype(BF)
            sums[here, :] = jnp.broadcast_to(1.0 / size, (rows, 128))
            lane = lax.broadcasted_iota(jnp.int32, (rows, 128), 1)
            logs[here, :] = jnp.where(lane == i, top + jnp.log(size), logs[here, :])
            return inner

        lax.fori_loop(0, 2, soft, 0)
        out = dot(probs[...], values, NN) * sums[...]
        attended[:, c] = unhalves(out, half).astype(BF)

        n = soon + i // 2
        pl.when(jnp.logical_and(i % 2 == 1, n < (line - 2) * parts))(lambda: advance(n))
        return carry

    lax.fori_loop(0, pairs, pair_step, 0)
    keyed_copy = pltpu.make_async_copy(keyed_all, keyed_out, load_sem.at[0])
    keyed_copy.start()

    def out_step(j, carry):
        c = pl.ds(pl.multiple_of(j * tile, tile), tile)
        w = pl.ds(pl.multiple_of(after + j * tile, 128), tile)
        out = dot(attended[...], everything[:, :, w].reshape(width, tile), NN)
        middle[:, c] = token_v[:, c].astype(F32) + out
        return carry

    lax.fori_loop(0, width // tile, out_step, 0)
    norm(middle, normed, 1)

    def rest(n, carry):
        advance(n)
        return carry

    lax.fori_loop(soon + pairs // 2, (line - 2) * parts, rest, 0)
    for z in range(line):
        gather.wait_across(z)
    keyed_copy.wait()
    weights_copy.wait()
    line_keys.finish()
    gather.finish()


def front_call(pieces, tokens, tangent, cosine, sine, gains, places, own_places, line):
    rows, width = tokens.shape
    narrow = pieces[1].shape[1]
    unit = (pieces[0].shape[0], sum(p.shape[1] for p in pieces) + 128)
    total = places.shape[1]
    blocks, parts = 2 * line, 4
    shapes = jax.ShapeDtypeStruct
    vmem = pl.BlockSpec(memory_space=pltpu.VMEM)
    like = lambda a: pltpu.VMEM(a.shape, a.dtype)
    return pl.pallas_call(
        functools.partial(front_kernel, line, parts),
        out_shape=(
            shapes((rows, width), BF), shapes((rows, width), F32), shapes((rows, width), BF),
            shapes((rows, width), BF), shapes((rows, width), BF),
            shapes((2 * rows, 128), F32), shapes((2, width), F32),
            shapes((line, rows, 2 * narrow), BF),
            shapes((blocks, rows, width), BF), shapes((2 * blocks,) + unit, BF),
        ),
        in_specs=[ANY] * 8 + [vmem] * 4,
        out_specs=(vmem,) * 7 + (ANY,) * 3,
        scratch_shapes=[
            pltpu.VMEM((2 * blocks,) + unit, BF),
            pltpu.VMEM((rows, 2 * narrow), BF), pltpu.VMEM((line, rows, 2 * narrow), BF),
            pltpu.VMEM((rows, total), F32), like(tokens), like(cosine), like(sine),
            pltpu.VMEM((2 * rows, total), F32), pltpu.VMEM((2 * rows, total), BF),
            pltpu.VMEM((2 * rows, 128), F32), pltpu.VMEM((rows, width), BF), pltpu.SemaphoreType.DMA((6,)),
            pltpu.SemaphoreType.DMA((line, 2)), pltpu.SemaphoreType.DMA((line,)),
            pltpu.SemaphoreType.DMA((line, parts, 3)), pltpu.SemaphoreType.DMA((blocks, parts)),
            pltpu.SemaphoreType.DMA((2,)),
            pltpu.SemaphoreType.DMA((4, blocks, 4)), pltpu.SemaphoreType.DMA((4, blocks)),
            pltpu.SemaphoreType.DMA((4, blocks)), pltpu.SemaphoreType.DMA((4, blocks)),
        ],
        compiler_params=pltpu.CompilerParams(
            collective_id=5, has_side_effects=True, vmem_limit_bytes=62 * 2**20
        ),
        name="front",
    )(*pieces, tokens, tangent, cosine, sine, *gains, places, own_places)


def back_kernel(
    line, parts,
    places, own_places, queries, keyed_all, middle, grad_normed, tangent, gain, logs, hidden_all,
    down_own, down_twin, weights, cosine, sine,
    gate_sum, up_sum, down_sum, _gate, _up, _down, normed, attended,
    branch, grad_qkv, term_two, gate_mirror, up_mirror, down_mirror,
    twin_normed, twin_attended, twin_out, grad_out, grad_middle,
    out_across, both_attended, both_out, out_partial, out_send, out_recv,
    norm_sem, gain_v, out_v, out_w, cosine_v, sine_v, grad_keyed, mirror_send, mirror_recv,
    query_v, keyed_v, grad_v, bias_v, log_v, scores, gradients, probs, slopes, key_sum, value_sum,
    down_w, hidden, load_sem,
    partial, from_across, from_line, total, across_send, across_recv, line_send, line_recv,
    key_partial, key_line, key_total, key_send, key_recv,
):
    grid = Grid(2, line)
    cols, width = down_own.shape
    rows = partial.shape[1]
    narrow = keyed_all.shape[2] // 2
    length = places.shape[1]
    grid.greet(True, True)
    swapped = [
        remote(src, dst, mirror_send.at[3 + i], mirror_recv.at[3 + i], grid.twin)
        for i, (src, dst) in enumerate(
            ((normed, twin_normed), (attended, twin_attended), (out_v, twin_out))
        )
    ]
    for copy in swapped[:2]:
        copy.start()
    left = pl.ds(EARLY * 256, width - EARLY * 256)
    mirrored = [
        remote(src, dst, mirror_send.at[i], mirror_recv.at[i], grid.mirror)
        for i, (src, dst) in enumerate(
            (
                (gate_sum.at[left, :], gate_mirror.at[left, :]),
                (up_sum.at[left, :], up_mirror.at[left, :]),
                (down_sum.at[:, left], down_mirror.at[:, left]),
            )
        )
    ]
    for copy in mirrored:
        copy.start()
    load_pairs(
        [
            (down_own, down_w.at[pl.ds(0, cols)]),
            (down_twin, down_w.at[pl.ds(cols, cols)]),
            (hidden_all, hidden),
            (queries, query_v),
            (keyed_all, keyed_v),
            (gain, gain_v),
            (logs, log_v),
            (cosine, cosine_v),
            (sine, sine_v),
        ],
        load_sem,
    )
    bias_v[...] = mask(places, own_places)
    scatter = Scatter(
        grid, partial, from_across, from_line, total,
        (across_send, across_recv, line_send, line_recv), parts,
    )
    keyed_scatter = Scatter(
        grid, key_partial, None, key_line, key_total, (None, None, key_send, key_recv),
        key_partial.shape[1] // rows,
    )

    def work(i, carry):
        z = grid.order(line - 1 - i % line)
        slot = grid.slot(jnp.where(i < line, 1 - grid.x, grid.x), z)
        spot = pl.ds(pl.multiple_of(slot * rows, rows), rows)

        def tile(j, inner):
            c = pl.ds(pl.multiple_of(j * cols, cols), cols)
            partial[slot, :, c] = dot(hidden[spot, :], down_w[:, c], NN).astype(BF)
            return inner

        lax.fori_loop(0, width // cols, tile, 0)
        pl.when(i < line)(lambda: scatter.send_across(z))
        return carry

    deep = 2 * rows
    middle_v, normed_v, tangent_v = scores, gradients, probs
    half_width = width // 2
    norm_loads = [
        pltpu.make_async_copy(
            src.at[:, pl.ds(h * half_width, half_width)], dst.at[pl.ds(h * rows, rows), :], norm_sem.at[i, h]
        )
        for i, (src, dst) in enumerate(
            ((middle, middle_v), (grad_normed, normed_v), (tangent, tangent_v))
        )
        for h in range(2)
    ]
    for copy in norm_loads:
        copy.start()
    lax.fori_loop(0, line, work, 0)
    for copy in norm_loads:
        copy.wait()
    term_two[...] = jnp.zeros_like(term_two)
    few = rows // 4

    def norm_step(j):
        spots = [pl.ds(pl.multiple_of(h * rows + j * few, few), few) for h in range(2)]
        here = pl.ds(pl.multiple_of(j * few, few), few)
        sides = [pl.ds(h * half_width, half_width) for h in range(2)]
        values = [middle_v[s, :] for s in spots]
        square = sum(jnp.sum(v * v, axis=1, keepdims=True) for v in values)
        factor = lax.rsqrt(square / width + norm_eps)
        units = [v * factor for v in values]
        grads = [normed_v[s, :] for s in spots]
        scaled = [g * gain_v[1:2, c] for g, c in zip(grads, sides)]
        dots = sum(jnp.sum(s * u, axis=1, keepdims=True) for s, u in zip(scaled, units))
        mean = dots / width
        for spot, c, grad, unit, scale in zip(spots, sides, grads, units, scaled):
            term_two[:, c] += jnp.sum(grad * unit, axis=0, keepdims=True)
            value = tangent_v[spot, :].astype(F32) + factor * (scale - unit * mean)
            branch[here, c] = value
            out_v[here, c] = value.astype(BF)

    each(rows // few, norm_step)
    norm_copies = [
        pltpu.make_async_copy(branch, grad_middle, norm_sem.at[0, 0]),
        pltpu.make_async_copy(out_v, grad_out, norm_sem.at[0, 1]),
    ]
    for copy in norm_copies + swapped[2:]:
        copy.start()
    work(line, 0)
    lag = jnp.where(jnp.logical_and(grid.has_left, grid.has_right), 2, 0)

    def paced(position):
        pl.when(position >= lag)(lambda: scatter.step(position - lag))

    paced(0)
    tile = out_w.shape[0] * out_w.shape[1]
    after = weights.shape[2] - width

    def out_step(j, carry):
        units = pl.ds(j * out_w.shape[0], out_w.shape[0])
        load_pairs([(weights.at[units, :, pl.ds(after, width)], out_w)], load_sem)
        c = pl.ds(pl.multiple_of(j * tile, tile), tile)
        grad_v[:, c] = dot(out_v[...], out_w[...].reshape(tile, width), NT).astype(BF)
        pl.when(j % 2 == 1)(lambda: paced(1 + j // 2))
        return carry

    lax.fori_loop(0, width // tile, out_step, 0)
    chunk = rows // 2
    pairs = width // (2 * HEAD_SIZE)
    group = pairs // (narrow // (2 * HEAD_SIZE))

    def pair_step(i, carry):
        c = pl.ds(pl.multiple_of(i * 128, 128), 128)
        half = (i // (group // 2)) % 2
        key_cols = pl.ds(pl.multiple_of((i // group) * 128, 128), 128)
        value_cols = pl.ds(pl.multiple_of((i // group) * 128 + narrow, 128), 128)
        keys = keyed_v[:, :, key_cols].reshape(length, 128)
        values = keyed_v[:, :, value_cols].reshape(length, 128)
        query = halves(query_v[:, c], half)
        grad = halves(grad_v[:, c], half)
        scores[...] = dot(query, keys, NT)
        gradients[...] = dot(grad, values, NT)

        def soft(j, inner):
            here = pl.ds(pl.multiple_of(j * chunk, chunk), chunk)
            there = pl.ds(pl.multiple_of((j * chunk) % rows, chunk), chunk)
            lane = lax.broadcasted_iota(jnp.int32, (chunk, 128), 1)
            log = jnp.sum(jnp.where(lane == i, log_v[here, :], 0.0), axis=1, keepdims=True)
            prob = jnp.exp(scores[here, :] + bias_v[there, :] - log)
            slope = gradients[here, :]
            delta = jnp.sum(prob * slope, axis=1, keepdims=True)
            probs[here, :] = prob.astype(BF)
            slopes[here, :] = (prob * (slope - delta)).astype(BF)
            return inner

        lax.fori_loop(0, deep // chunk, soft, 0)
        back = dot(slopes[...], keys, NN) * HEAD_SIZE ** (-0.5)
        grad_qkv[:, c] = turn(unhalves(back, half), cosine_v, sine_v, 1.0)
        key_part = dot(slopes[...], query, TN)
        value_part = dot(probs[...], grad, TN)

        @pl.when(i % group == 0)
        def _():
            key_sum[...] = key_part
            value_sum[...] = value_part

        @pl.when(i % group != 0)
        def _():
            key_sum[...] += key_part
            value_sum[...] += value_part

        @pl.when(i % group == group - 1)
        def _():
            spot = pl.ds(pl.multiple_of((i // group) * rows, rows), rows)
            key_partial[:, spot, 0:128] = key_sum[...].astype(BF).reshape(line, rows, 128)
            key_partial[:, spot, 128:256] = value_sum[...].astype(BF).reshape(line, rows, 128)
            pl.when(i // group + early > 0)(lambda: keyed_steps(i // group + early - 1))

        @pl.when(i % 6 == 2)
        def _():
            work(line + 1 + i // 6, 0)

        pl.when(i == pairs // 2 - 2)(out_gradients)

        done = (3 * i + 1) // 5
        pl.when((3 * i + 4) // 5 > done)(lambda: paced(3 + done))
        return carry

    run = out_partial.shape[1]

    def outward(z):
        return remote(
            out_partial.at[z], out_across.at[z], out_send.at[z], out_recv.at[z], grid.across
        )

    def away(action):
        for j in range(line - 2):
            action(outward(scatter.rank(j)))

    def out_gradients():
        for copy in swapped[1:]:
            copy.wait()
        own, twin = pl.ds(0, rows), pl.ds(rows, rows)
        load_pairs(
            [
                (attended, both_attended.at[own]),
                (twin_attended, both_attended.at[twin]),
                (out_v, both_out.at[own]),
                (twin_out, both_out.at[twin]),
            ],
            load_sem,
        )
        tall = line * run
        first = pl.multiple_of(((1 - grid.x) * 2 + grid.core) * tall, tall)

        def tile_step(j):
            c = pl.ds(pl.multiple_of(j * 512, 512), 512)
            value = dot(both_attended[:, pl.ds(first, tall)], both_out[:, c], TN).astype(BF)
            out_partial[:, :, c] = value.reshape(line, run, 512)

        each(width // 512, tile_step)
        away(lambda c: c.start())

    def keyed_steps(g):
        each(line - 1, lambda j: keyed_scatter.pass_on(keyed_scatter.rank(j), g))

    early = jnp.where(jnp.logical_and(grid.has_left, grid.has_right), 0, 1)
    lax.fori_loop(0, pairs, pair_step, 0)

    def rest(n, carry):
        scatter.step(n)
        return carry

    lax.fori_loop(3 + (3 * pairs + 1) // 5 - lag, scatter.steps(), rest, 0)

    pl.when(early == 0)(lambda: keyed_steps(pairs // group - 1))
    for copy in norm_copies:
        copy.wait()
    scatter.own(branch)
    keyed_scatter.own(grad_keyed)
    for g in range(pairs // group):
        both = grad_keyed[g * rows : (g + 1) * rows, :]
        first = width + g * 128
        grad_qkv[:, first : first + 128] = turn(both[:, :128], cosine_v, sine_v, 1.0)
        grad_qkv[:, first + narrow : first + narrow + 128] = both[:, 128:].astype(BF)
    for copy in mirrored + swapped[:1]:
        copy.wait()
    away(lambda c: c.wait())
    scatter.finish()
    keyed_scatter.finish()


def back_call(
    places, own_places, queries, keyed_all, middle, grad_normed, tangent, gain, logs, hidden_all, downs,
    weights, cosine, sine, sums,
    mirrors, normed, attended, line,
):
    rows, width = queries.shape
    both = keyed_all.shape[2]
    groups, run = both // 256, weights.shape[1]
    cols, length = downs[0].shape[0], places.shape[1]
    parts = 4
    shapes = jax.ShapeDtypeStruct
    vmem = pl.BlockSpec(memory_space=pltpu.VMEM)
    return pl.pallas_call(
        functools.partial(back_kernel, line, parts),
        out_shape=(
            shapes((rows, width), F32), shapes((rows, width + both), BF), shapes((1, width), F32),
            *(shapes(s.shape, BF) for s in sums), *(shapes((rows, width), BF),) * 4,
            shapes((rows, width), F32), shapes((line, run, width), BF),
        ),
        in_specs=[vmem] * 2 + [ANY] * 21,
        out_specs=(vmem,) * 3 + (ANY,) * 9,
        input_output_aliases={18: 3, 19: 4, 20: 5},
        scratch_shapes=[
            pltpu.VMEM((2 * rows, width), BF), pltpu.VMEM((2 * rows, width), BF),
            pltpu.VMEM((line, run, width), BF),
            pltpu.SemaphoreType.DMA((line,)), pltpu.SemaphoreType.DMA((line,)),
            pltpu.SemaphoreType.DMA((3, 2)), pltpu.VMEM(gain.shape, F32),
            pltpu.VMEM((rows, width), BF), pltpu.VMEM((4, run, width), BF),
            pltpu.VMEM(cosine.shape, F32), pltpu.VMEM(sine.shape, F32),
            pltpu.VMEM((groups * rows, 256), F32),
            pltpu.SemaphoreType.DMA((6,)), pltpu.SemaphoreType.DMA((6,)),
            pltpu.VMEM((rows, width), BF), pltpu.VMEM(keyed_all.shape, BF), pltpu.VMEM((rows, width), BF),
            pltpu.VMEM((rows, length), F32), pltpu.VMEM(logs.shape, F32),
            pltpu.VMEM((2 * rows, length), F32), pltpu.VMEM((2 * rows, length), F32),
            pltpu.VMEM((2 * rows, length), BF), pltpu.VMEM((2 * rows, length), BF),
            pltpu.VMEM((length, 128), F32), pltpu.VMEM((length, 128), F32),
            pltpu.VMEM((2 * cols, width), BF), pltpu.VMEM(hidden_all.shape, BF),
            pltpu.SemaphoreType.DMA((10,)),
            *scatter_scratch(line, rows, width, parts),
            pltpu.VMEM((line, groups * rows, 256), BF), pltpu.VMEM((2 * line - 2, groups * rows, 256), BF),
            pltpu.VMEM((rows, 256), F32),
            pltpu.SemaphoreType.DMA((line, groups)), pltpu.SemaphoreType.DMA((2 * line - 2, groups)),
        ],
        compiler_params=pltpu.CompilerParams(
            collective_id=6, has_side_effects=True, vmem_limit_bytes=62 * 2**20
        ),
        name="back",
    )(
        places, own_places, queries, keyed_all, middle, grad_normed, tangent, gain, logs, hidden_all,
        *downs, weights, cosine, sine, *sums,
        *mirrors, normed, attended,
    )


def body(
    tokens,
    places,
    cotangent,
    gain_attn,
    gain_mlp,
    w_query,
    key_projection,
    value_projection,
    w_out,
    w_gate,
    w_up,
    w_down,
):
    sequence_total, segment_length, width = tokens.shape
    total_length = places.shape[1]
    total_rows = sequence_total * segment_length
    position = lax.axis_index("context")
    local_positions = lax.dynamic_slice_in_dim(places, position * segment_length, segment_length, 1)
    rotary_angles = local_positions.reshape(total_rows).astype(jnp.float32)[:, None] * frequencies(
        HEAD_SIZE // 2
    )
    gain_one, gain_two, query_w, key_weight_local, value_w, out_w = (
        lax.all_gather(gain_attn, ("fsdp", "context"), axis=0, tiled=True),
        lax.all_gather(gain_mlp, ("fsdp", "context"), axis=0, tiled=True),
        lax.all_gather(w_query, ("fsdp", "context"), axis=0, tiled=True),
        lax.all_gather(key_projection, ("fsdp", "context"), axis=0, tiled=True),
        lax.all_gather(value_projection, ("fsdp", "context"), axis=0, tiled=True),
        lax.all_gather(w_out, ("fsdp", "context"), axis=0, tiled=True),
    )
    gain_first = gain_one.astype(jnp.float32)
    gain_second = gain_two.astype(jnp.float32)
    inputs_f = tokens.astype(jnp.float32).reshape(total_rows, width)
    factor_one = lax.rsqrt(jnp.mean(inputs_f * inputs_f, axis=-1, keepdims=True) + norm_eps)
    unit_one = inputs_f * factor_one
    normed_tokens = (unit_one * gain_first).astype(jnp.bfloat16)
    query_pre = jnp.dot(normed_tokens, query_w, preferred_element_type=jnp.float32).reshape(
        total_rows, QUERY_HEADS, HEAD_SIZE
    )
    key_unrotated = jnp.dot(
        normed_tokens, key_weight_local, preferred_element_type=jnp.float32
    ).reshape(total_rows, KEY_VALUE_HEADS, HEAD_SIZE)
    value_matrix_rows = jnp.dot(normed_tokens, value_w, preferred_element_type=jnp.float32).astype(
        jnp.bfloat16
    )
    query_rows = apply_rotary(query_pre, rotary_angles).astype(jnp.bfloat16)
    key_matrix_rows = (
        apply_rotary(key_unrotated, rotary_angles)
        .astype(jnp.bfloat16)
        .reshape(sequence_total, segment_length, KEY_VALUE_HEADS * HEAD_SIZE)
    )
    key_all, value_all = (
        lax.all_gather(key_matrix_rows, "context", axis=1, tiled=True),
        lax.all_gather(
            value_matrix_rows.reshape(sequence_total, segment_length, KEY_VALUE_HEADS * HEAD_SIZE),
            "context",
            axis=1,
            tiled=True,
        ),
    )
    head_query = query_head_rows(query_rows, sequence_total, segment_length)
    head_key = key_heads(key_all, sequence_total, total_length)
    head_value = key_heads(value_all, sequence_total, total_length)
    query_positions = jnp.repeat(local_positions, KEY_VALUE_HEADS, axis=0)
    key_positions = jnp.repeat(places, KEY_VALUE_HEADS, axis=0)
    attended = lax.map(
        forward_head, (head_query, head_key, head_value, query_positions, key_positions)
    )
    attended = merge_queries(attended, sequence_total, segment_length).astype(jnp.bfloat16)
    middle = inputs_f + jnp.dot(attended, out_w, preferred_element_type=jnp.float32)
    factor_two = lax.rsqrt(jnp.mean(middle * middle, axis=-1, keepdims=True) + norm_eps)
    unit_two = middle * factor_two
    normed_mlp = (unit_two * gain_second).astype(jnp.bfloat16)
    tangent = cotangent.reshape(total_rows, width)
    tangent_f = tangent.astype(jnp.float32)
    group = ("fsdp", "context")
    normed_all = lax.all_gather(normed_mlp, group, axis=0, tiled=True)
    tangent_all = lax.all_gather(tangent, group, axis=0, tiled=True)
    branch_part, kept_values = feed_forward(normed_all, w_gate, w_up, w_down)
    grad_part, grad_w_gate, grad_w_up, grad_w_down = feed_back(
        normed_all, tangent_all, w_gate, w_up, w_down, kept_values
    )
    grad_normed = lax.psum_scatter(
        grad_part.astype(jnp.bfloat16), group, scatter_dimension=0, tiled=True
    ).astype(jnp.float32)
    branch = lax.psum_scatter(
        branch_part.astype(jnp.bfloat16), group, scatter_dimension=0, tiled=True
    ).astype(jnp.float32)
    outcome = middle + branch
    scaled_two = grad_normed * gain_second
    term_gain_two = jnp.sum(grad_normed * unit_two, axis=0)
    grad_middle = tangent_f + factor_two * (
        scaled_two - unit_two * jnp.mean(scaled_two * unit_two, axis=-1, keepdims=True)
    )
    grad_branch = grad_middle.astype(jnp.bfloat16)
    term_out = times_t(attended, grad_branch)
    grad_attended = times_nt(grad_branch, out_w).astype(jnp.bfloat16)
    head_grad = query_head_rows(grad_attended, sequence_total, segment_length)
    grad_q, grad_k, grad_v = lax.map(
        backward_head, (head_query, head_key, head_value, head_grad, query_positions, key_positions)
    )
    local_key_gradient, local_value_gradient = (
        lax.psum_scatter(
            merge_keys(grad_k, sequence_total, total_length).astype(jnp.bfloat16),
            "context",
            scatter_dimension=1,
            tiled=True,
        ).astype(jnp.float32),
        lax.psum_scatter(
            merge_keys(grad_v, sequence_total, total_length).astype(jnp.bfloat16),
            "context",
            scatter_dimension=1,
            tiled=True,
        ).astype(jnp.float32),
    )
    grad_query = (
        inverse_rotary(
            merge_queries(grad_q, sequence_total, segment_length).reshape(
                total_rows, QUERY_HEADS, HEAD_SIZE
            ),
            rotary_angles,
        )
        .reshape(total_rows, QUERY_HEADS * HEAD_SIZE)
        .astype(jnp.bfloat16)
    )
    grad_key = (
        inverse_rotary(
            local_key_gradient.reshape(total_rows, KEY_VALUE_HEADS, HEAD_SIZE), rotary_angles
        )
        .reshape(total_rows, KEY_VALUE_HEADS * HEAD_SIZE)
        .astype(jnp.bfloat16)
    )
    value_gradient = local_value_gradient.reshape(total_rows, KEY_VALUE_HEADS * HEAD_SIZE).astype(
        jnp.bfloat16
    )
    grad_normed_one = (
        times_nt(grad_query, query_w)
        + times_nt(grad_key, key_weight_local)
        + times_nt(value_gradient, value_w)
    )
    term_query = times_t(normed_tokens, grad_query)
    term_key = times_t(normed_tokens, grad_key)
    term_value = times_t(normed_tokens, value_gradient)
    scaled_one = grad_normed_one * gain_first
    term_gain_one = jnp.sum(grad_normed_one * unit_one, axis=0)
    grad_inputs = grad_middle + factor_one * (
        scaled_one - unit_one * jnp.mean(scaled_one * unit_one, axis=-1, keepdims=True)
    )
    share_query, share_key, share_value, share_out, share_gain_one, share_gain_two = (
        lax.psum_scatter(term_query.astype(jnp.bfloat16), ("fsdp", "context"), scatter_dimension=0, tiled=True),
        lax.psum_scatter(term_key.astype(jnp.bfloat16), ("fsdp", "context"), scatter_dimension=0, tiled=True),
        lax.psum_scatter(term_value.astype(jnp.bfloat16), ("fsdp", "context"), scatter_dimension=0, tiled=True),
        lax.psum_scatter(term_out.astype(jnp.bfloat16), ("fsdp", "context"), scatter_dimension=0, tiled=True),
        lax.psum_scatter(term_gain_one, ("fsdp", "context"), scatter_dimension=0, tiled=True),
        lax.psum_scatter(term_gain_two, ("fsdp", "context"), scatter_dimension=0, tiled=True),
    )
    summed = (
        lax.psum(share_query.astype(jnp.bfloat16), "replica").astype(jnp.float32),
        lax.psum(share_key.astype(jnp.bfloat16), "replica").astype(jnp.float32),
        lax.psum(share_value.astype(jnp.bfloat16), "replica").astype(jnp.float32),
        lax.psum(share_out.astype(jnp.bfloat16), "replica").astype(jnp.float32),
        lax.psum(grad_w_gate.astype(jnp.bfloat16), "replica").astype(jnp.float32),
        lax.psum(grad_w_up.astype(jnp.bfloat16), "replica").astype(jnp.float32),
        lax.psum(grad_w_down.astype(jnp.bfloat16), "replica").astype(jnp.float32),
        lax.psum(share_gain_one.astype(jnp.bfloat16), "replica").astype(jnp.float32),
        lax.psum(share_gain_two.astype(jnp.bfloat16), "replica").astype(jnp.float32),
    )
    out = outcome.astype(jnp.bfloat16).reshape(sequence_total, segment_length, width)
    grad_tokens = grad_inputs.astype(jnp.bfloat16).reshape(sequence_total, segment_length, width)
    return (
        out,
        grad_tokens,
        summed[0],
        summed[1],
        summed[2],
        summed[3],
        summed[4],
        summed[5],
        summed[6],
        summed[7],
        summed[8],
    )


def kernel_body(
    tokens,
    places,
    cotangent,
    gain_attn,
    gain_mlp,
    w_query,
    key_projection,
    value_projection,
    w_out,
    w_gate,
    w_up,
    w_down,
):
    bf16, f32 = jnp.bfloat16, jnp.float32
    sequence_total, segment_length, width = tokens.shape
    total_length = places.shape[1]
    line = lax.axis_size("context")
    narrow = key_projection.shape[1]
    run = w_query.shape[0]
    swap = [(i, i ^ 1) for i in range(lax.axis_size("fsdp"))]
    gates, ups, downs = ((w, lax.ppermute(w, "fsdp", swap)) for w in (w_gate, w_up, w_down))
    position = lax.axis_index("context")
    local_positions = lax.dynamic_slice_in_dim(places, position * segment_length, segment_length, 1)
    rotary_angles = local_positions.reshape(segment_length).astype(f32)[:, None] * frequencies(
        HEAD_SIZE // 2
    )
    pieces = (w_query, key_projection, value_projection, w_out)
    cosine, sine = jnp.cos(rotary_angles), jnp.sin(rotary_angles)
    cosine = jnp.concatenate([cosine] * 4, axis=1)
    sine = jnp.concatenate([-sine, sine] * 2, axis=1)
    own_places = local_positions.reshape(segment_length, 1)
    places = places.reshape(1, total_length)
    gains = (gain_attn.reshape(1, run), gain_mlp.reshape(1, run))
    tangent = cotangent.reshape(segment_length, width)
    rows = tokens.reshape(segment_length, width)
    (
        attended, middle, normed_mlp, normed_tokens, scaled_query, logs, gain, keyed_all, tangent_all,
        weights,
    ) = front_call(pieces, rows, tangent, cosine, sine, gains, places, own_places, line)
    mid = width + 2 * narrow
    grad_normed, _, hidden_all, *sums = feed_call(normed_mlp, tangent_all, gates, ups, downs, line)[:9]
    branch, grad_qkv, term_two, *others = back_call(
        places, own_places, scaled_query, keyed_all, middle, grad_normed, tangent, gain, logs,
        hidden_all, downs, weights, cosine, -sine, sums[:3], sums[3:], normed_tokens, attended, line,
    )
    twins, (grad_branch, grad_middle, out_across) = others[3:6], others[6:]
    outcome = middle + branch
    grad_w_gate, grad_w_up, grad_w_down = (
        a.astype(f32) + b.astype(f32) for a, b in zip(sums[:3], others[:3])
    )
    packed, grad_w_out, grad_tokens = sums_call(
        normed_tokens, attended, grad_qkv, grad_branch, (*twins, out_across), rows, grad_middle,
        weights, gain, term_two, line,
    )
    gains = packed[run * 3 // 4 : run * 3 // 4 + 2, mid:]
    ends, start = [], 0
    for size in (width, narrow, narrow):
        ends.append(packed[:, start : start + size])
        start += size
    return (
        outcome.astype(bf16).reshape(tokens.shape),
        grad_tokens.reshape(tokens.shape),
        *ends,
        grad_w_out,
        grad_w_gate,
        grad_w_up,
        grad_w_down,
        gains[0],
        gains[1],
    )


def solution(mesh):
    placed = (
        P(("replica", "fsdp"), "context", None),
        P(("replica", "fsdp"), None),
        P(("replica", "fsdp"), "context", None),
        P(("fsdp", "context")),
        P(("fsdp", "context")),
        P(("fsdp", "context"), None),
        P(("fsdp", "context"), None),
        P(("fsdp", "context"), None),
        P(("fsdp", "context"), None),
        P(None, ("fsdp", "context")),
        P(None, ("fsdp", "context")),
        P(("fsdp", "context"), None),
    )
    kernels = (mesh.shape["replica"], mesh.shape["fsdp"], mesh.shape["context"]) == (2, 4, 4)
    return jax.shard_map(
        kernel_body if kernels else body,
        mesh=mesh,
        in_specs=placed,
        out_specs=(
            P(("replica", "fsdp"), "context", None),
            P(("replica", "fsdp"), "context", None),
            P(("fsdp", "context"), None),
            P(("fsdp", "context"), None),
            P(("fsdp", "context"), None),
            P(("fsdp", "context"), None),
            P(None, ("fsdp", "context")),
            P(None, ("fsdp", "context")),
            P(("fsdp", "context"), None),
            P(("fsdp", "context")),
            P(("fsdp", "context")),
        ),
        check_vma=False,
    )
```

```python
import functools

import jax
import jax.numpy as jnp
from jax import lax
from jax.experimental import pallas as pl
from jax.experimental.pallas import tpu as pltpu
from jax.sharding import PartitionSpec as P

QUERY_HEADS = 32
KEY_VALUE_HEADS = 8
HEAD_SIZE = 64


norm_eps = 1e-05
rope_base = 500000.0


def frequencies(half):
    return rope_base ** (-2.0 * jnp.arange(half, dtype=jnp.float32) / (2.0 * half))


def apply_rotary(angle_table, rotary_angles):
    half = angle_table.shape[-1] // 2
    first_half = angle_table[..., :half]
    second_half = angle_table[..., half:]
    cosine = jnp.cos(rotary_angles)[..., None, :]
    sine = jnp.sin(rotary_angles)[..., None, :]
    return jnp.concatenate(
        [first_half * cosine - second_half * sine, second_half * cosine + first_half * sine],
        axis=-1,
    )


def inverse_rotary(angle_table, rotary_angles):
    half = angle_table.shape[-1] // 2
    first_half = angle_table[..., :half]
    second_half = angle_table[..., half:]
    cosine = jnp.cos(rotary_angles)[..., None, :]
    sine = jnp.sin(rotary_angles)[..., None, :]
    return jnp.concatenate(
        [first_half * cosine + second_half * sine, second_half * cosine - first_half * sine],
        axis=-1,
    )


def times_t(left, right):
    return lax.dot_general(
        left, right, (((0,), (0,)), ((), ())), preferred_element_type=jnp.float32
    )


def times_nt(left, right):
    return lax.dot_general(
        left, right, (((1,), (1,)), ((), ())), preferred_element_type=jnp.float32
    )


def query_head_rows(angle_table, sequence_total, segment_length):
    reshaped_heads = angle_table.reshape(
        sequence_total, segment_length, KEY_VALUE_HEADS, QUERY_HEADS // KEY_VALUE_HEADS, HEAD_SIZE
    )
    return jnp.transpose(reshaped_heads, (0, 2, 1, 3, 4)).reshape(
        sequence_total * KEY_VALUE_HEADS, segment_length, QUERY_HEADS // KEY_VALUE_HEADS, HEAD_SIZE
    )


def key_heads(angle_table, sequence_total, total_length):
    reshaped_heads = angle_table.reshape(sequence_total, total_length, KEY_VALUE_HEADS, HEAD_SIZE)
    return jnp.transpose(reshaped_heads, (0, 2, 1, 3)).reshape(
        sequence_total * KEY_VALUE_HEADS, total_length, HEAD_SIZE
    )


def merge_queries(angle_table, sequence_total, segment_length):
    reshaped_heads = angle_table.reshape(
        sequence_total, KEY_VALUE_HEADS, segment_length, QUERY_HEADS // KEY_VALUE_HEADS, HEAD_SIZE
    )
    return jnp.transpose(reshaped_heads, (0, 2, 1, 3, 4)).reshape(
        sequence_total * segment_length, QUERY_HEADS * HEAD_SIZE
    )


def merge_keys(angle_table, sequence_total, total_length):
    reshaped_heads = angle_table.reshape(sequence_total, KEY_VALUE_HEADS, total_length, HEAD_SIZE)
    return jnp.transpose(reshaped_heads, (0, 2, 1, 3)).reshape(
        sequence_total, total_length, KEY_VALUE_HEADS * HEAD_SIZE
    )


def softmax_weights(part_query, part_key, place_query, place_key):
    allowed = place_key[None, :] <= place_query[:, None]
    scores = jnp.einsum(
        "qrd,kd->rqk", part_query, part_key, preferred_element_type=jnp.float32
    ) * HEAD_SIZE ** (-0.5)
    scores = jnp.where(allowed[None], scores, -1e30)
    return jax.nn.softmax(scores, axis=-1)


def forward_head(packed):
    part_query, part_key, part_value, place_query, place_key = packed
    probs = softmax_weights(part_query, part_key, place_query, place_key)
    return jnp.einsum(
        "rqk,kd->qrd", probs.astype(jnp.bfloat16), part_value, preferred_element_type=jnp.float32
    )


def backward_head(packed):
    part_query, part_key, part_value, part_grad, place_query, place_key = packed
    probs = softmax_weights(part_query, part_key, place_query, place_key)
    grad_probs = jnp.einsum(
        "qrd,kd->rqk", part_grad, part_value, preferred_element_type=jnp.float32
    )
    row_delta = jnp.sum(probs * grad_probs, axis=-1, keepdims=True)
    grad_scores = (probs * (grad_probs - row_delta)).astype(jnp.bfloat16)
    grad_query = jnp.einsum(
        "rqk,kd->qrd", grad_scores, part_key, preferred_element_type=jnp.float32
    ) * HEAD_SIZE ** (-0.5)
    grad_key = jnp.einsum(
        "rqk,qrd->kd", grad_scores, part_query, preferred_element_type=jnp.float32
    ) * HEAD_SIZE ** (-0.5)
    value_gradient = jnp.einsum(
        "rqk,qrd->kd", probs.astype(jnp.bfloat16), part_grad, preferred_element_type=jnp.float32
    )
    return (grad_query, grad_key, value_gradient)


def feed_forward(normed_rows, gate_w, up_w, down_w):
    gate_pre = jnp.dot(normed_rows, gate_w, preferred_element_type=jnp.float32)
    up_proj = jnp.dot(normed_rows, up_w, preferred_element_type=jnp.float32)
    sigmoid_gate = jax.nn.sigmoid(gate_pre)
    hidden = (gate_pre * sigmoid_gate * up_proj).astype(jnp.bfloat16)
    return (
        jnp.dot(hidden, down_w, preferred_element_type=jnp.float32),
        (gate_pre, up_proj, sigmoid_gate, hidden),
    )


def feed_back(normed_rows, grad_rows, gate_w, up_w, down_w, kept_values):
    gate_pre, up_proj, sigmoid_gate, hidden = kept_values
    grad_hidden = times_nt(grad_rows, down_w)
    term_down = times_t(hidden, grad_rows)
    grad_gate = (
        grad_hidden * up_proj * (sigmoid_gate * (1.0 + gate_pre * (1.0 - sigmoid_gate)))
    ).astype(jnp.bfloat16)
    grad_up = (grad_hidden * (gate_pre * sigmoid_gate)).astype(jnp.bfloat16)
    grad_normed = times_nt(grad_gate, gate_w) + times_nt(grad_up, up_w)
    return (grad_normed, times_t(normed_rows, grad_gate), times_t(normed_rows, grad_up), term_down)


MESH = pl.DeviceIdType.MESH
ANY = pl.BlockSpec(memory_space=pl.ANY)
BF = jnp.bfloat16
F32 = jnp.float32
NN = (((1,), (0,)), ((), ()))
NT = (((1,), (1,)), ((), ()))
TN = (((0,), (0,)), ((), ()))


EARLY = 2


def dot(left, right, dims):
    return lax.dot_general(left, right, dims, preferred_element_type=F32)


class Grid:
    def __init__(self, chips, line):
        self.chips, self.line = chips, line
        self.replica = lax.axis_index("replica")
        flat = lax.axis_index("fsdp")
        self.x, self.core = flat // 2, flat % 2
        self.z = lax.axis_index("context")
        self.has_left, self.has_right = self.z > 0, self.z + 1 < line
        self.left = (self.replica, flat, self.z - 1)
        self.right = (self.replica, flat, self.z + 1)
        self.across = (self.replica, (1 - self.x) * 2 + self.core, self.z)
        self.twin = (self.replica, self.x * 2 + 1 - self.core, self.z)
        self.mirror = (1 - self.replica, flat, self.z)

    def order(self, k):
        z, n = self.z, self.line
        low = 2 * z < n
        near = 2 * jnp.minimum(z, n - 1 - z)
        away = jnp.where(k % 2 == 1, -((k + 1) // 2), k // 2)
        return jnp.where(
            k <= near, z + jnp.where(low, away, -away), jnp.where(low, k, n - 1 - k)
        )

    def slot(self, x, z):
        return x * self.line + z

    def greet(self, twin, mirror=False):
        barrier = pltpu.get_barrier_semaphore()

        def tell(device):
            pl.semaphore_signal(barrier, inc=1, device_id=device, device_id_type=MESH)

        pl.when(self.has_left)(lambda: tell(self.left))
        pl.when(self.has_right)(lambda: tell(self.right))
        tell(self.across)
        if twin:
            tell(self.twin)
        if mirror:
            tell(self.mirror)
        count = 1 + int(twin) + int(mirror) + self.has_left.astype(jnp.int32) + self.has_right.astype(jnp.int32)
        pl.semaphore_wait(barrier, count)


def remote(src, dst, send, recv, device):
    return pltpu.make_async_remote_copy(
        src_ref=src, dst_ref=dst, send_sem=send, recv_sem=recv, device_id=device, device_id_type=MESH
    )


def each(count, action):
    def step(i, carry):
        action(i)
        return carry

    lax.fori_loop(0, count, step, 0)


class Gather:
    def __init__(self, grid, block, everything, send, recv, parts, cross=None):
        self.grid, self.everything, self.send, self.recv = grid, everything, send, recv
        self.block, self.cross = block, cross
        self.rows = everything.shape[1] // parts
        self.last = parts - 1
        self.early = parts if cross is None else parts - 1

    def piece(self, x, z, part):
        start = pl.multiple_of(part * self.rows, self.rows)
        return self.everything.at[self.grid.slot(x, z), pl.ds(start, self.rows)]

    def copy(self, z, part, link, first=False):
        grid = self.grid
        device = (grid.right, grid.left, grid.across)[link]
        there = self.piece(grid.x, z, part)
        start = pl.multiple_of(part * self.rows, self.rows)
        here = self.block.at[pl.ds(start, self.rows)] if first else there
        return remote(
            here, there, self.send.at[z, part, link], self.recv.at[grid.slot(grid.x, z), part], device
        )

    def other(self, z, link):
        grid = self.grid
        here = self.piece(1 - grid.x, z, self.last)
        sem = self.recv.at[grid.slot(1 - grid.x, z), self.last]
        return remote(here, here, self.cross.at[z, link], sem, (grid.right, grid.left)[link])

    def ways(self, z):
        grid = self.grid
        return (
            (0, jnp.logical_and(z <= grid.z, grid.has_right)),
            (1, jnp.logical_and(z >= grid.z, grid.has_left)),
        )

    def sides(self, distance):
        grid = self.grid
        return (
            (grid.z - distance, grid.z >= distance, 0, grid.has_right),
            (grid.z + distance, grid.z + distance < grid.line, 1, grid.has_left),
        )

    def links(self, z, part, action, first=False, across=True):
        for link, go in self.ways(z):
            pl.when(go)(lambda link=link: action(self.copy(z, part, link, first)))
        if across:
            action(self.copy(z, part, 2, first))

    def send_own(self):
        grid = self.grid
        start = lambda c: c.start()
        if self.cross is not None:
            self.copy(grid.z, self.last, 2, True).start()
        each(self.early, lambda part: self.links(grid.z, part, start, True))
        if self.cross is not None:
            self.links(grid.z, self.last, start, True, False)

    def turn_in(self):
        grid = self.grid
        self.other(grid.z, 0).wait_recv()
        for link, go in self.ways(grid.z):
            pl.when(go)(lambda link=link: self.other(grid.z, link).start())

    def forward(self, distance, part, wait=True, along=True, across=True):
        for z, there, link, go in self.sides(distance):

            @pl.when(there)
            def _(z=z, link=link, go=go):
                if wait:
                    self.copy(z, part, 2).wait_recv()
                if along:
                    pl.when(go)(lambda: self.copy(z, part, link).start())
                if across:
                    self.copy(z, part, 2).start()

    def forward_last(self, distance):
        for z, there, link, go in self.sides(distance):

            @pl.when(there)
            def _(z=z, link=link, go=go):
                self.copy(z, self.last, 2).wait_recv()
                pl.when(go)(lambda: self.copy(z, self.last, link).start())
                self.other(z, link).wait_recv()
                pl.when(go)(lambda: self.other(z, link).start())

    def wait_across(self, z):
        grid = self.grid

        def wait(part):
            here = self.piece(1 - grid.x, z, part)
            sem = self.recv.at[grid.slot(1 - grid.x, z), part]
            remote(here, here, self.send.at[z, part, 2], sem, grid.across).wait_recv()

        each(self.early, wait)

    def finish(self):
        done = lambda c: c.wait_send()

        def place(z):
            each(self.early, lambda part: self.links(z, part, done))
            if self.cross is not None:
                self.links(z, self.last, done, across=False)
                for link, go in self.ways(z):
                    pl.when(go)(lambda link=link: self.other(z, link).wait_send())

        each(self.grid.line, place)
        if self.cross is not None:
            self.copy(self.grid.z, self.last, 2).wait_send()


class Scatter:
    def __init__(self, grid, partial, from_across, from_line, total, sems, parts, cross=None):
        self.grid, self.partial, self.from_across = grid, partial, from_across
        self.from_line, self.total = from_line, total
        self.across_send, self.across_recv, self.line_send, self.line_recv = sems
        self.parts, self.cross = parts, cross
        self.rows = partial.shape[1] // parts
        self.early = parts if cross is None else parts - 1
        self.last = parts - 1

    def run(self, part):
        return pl.ds(pl.multiple_of(part * self.rows, self.rows), self.rows)

    def steps(self):
        return (self.grid.line - 1) * self.early

    def rank(self, j):
        return self.grid.order(self.grid.line - 1 - j)

    def step(self, n):
        self.pass_on(self.rank(n // self.early), n % self.early)

    def place(self, z):
        return z if self.from_across is None else self.grid.slot(self.grid.x, z)

    def across(self, z, part):
        grid = self.grid
        return remote(
            self.partial.at[grid.slot(1 - grid.x, z), self.run(part)],
            self.from_across.at[z, self.run(part)],
            self.across_send.at[z, part],
            self.across_recv.at[z, part],
            grid.across,
        )

    def arrival(self, z, leftward):
        return z if leftward else z - 1 + self.grid.line - 1

    def along(self, z, part, leftward):
        grid = self.grid
        arrival = self.arrival(z, leftward)
        return remote(
            self.partial.at[self.place(z), self.run(part)],
            self.from_line.at[arrival, self.run(part)],
            self.line_send.at[z, part],
            self.line_recv.at[arrival, part],
            grid.left if leftward else grid.right,
        )

    def other(self, z, leftward):
        grid = self.grid
        buffer, send, recv = self.cross
        arrival = self.arrival(z, leftward)
        return remote(
            self.partial.at[grid.slot(1 - grid.x, z), self.run(self.last)],
            buffer.at[arrival],
            send.at[z],
            recv.at[arrival],
            grid.left if leftward else grid.right,
        )

    def send_across(self, z):
        each(self.early, lambda part: self.across(z, part).start())

    def both_ways(self, z, action):
        grid = self.grid
        pl.when(jnp.logical_and(z <= grid.z, grid.has_right))(lambda: action(True))
        pl.when(jnp.logical_and(z >= grid.z, grid.has_left))(lambda: action(False))

    def add_line(self, z, part):
        def add(leftward):
            self.along(z, part, leftward).wait_recv()
            arrival = self.arrival(z, leftward)
            self.total[...] += self.from_line[arrival, self.run(part)].astype(F32)

        self.both_ways(z, add)

    def gather_sum(self, z, part):
        value = self.partial[self.place(z), self.run(part)].astype(F32)
        if self.from_across is not None:
            self.across(z, part).wait_recv()
            value = value + self.from_across[z, self.run(part)].astype(F32)
        self.total[...] = value
        self.add_line(z, part)

    def send_along(self, z, part):
        grid = self.grid
        self.partial[self.place(z), self.run(part)] = self.total[...].astype(BF)
        pl.when(z < grid.z)(lambda: self.along(z, part, True).start())
        pl.when(z > grid.z)(lambda: self.along(z, part, False).start())

    def pass_on(self, z, part):
        self.gather_sum(z, part)
        self.send_along(z, part)

    def add_other(self, z):
        grid, run = self.grid, self.run(self.last)
        slot = grid.slot(1 - grid.x, z)
        self.total[...] = self.partial[slot, run].astype(F32)

        def add(leftward):
            self.other(z, leftward).wait_recv()
            self.total[...] += self.cross[0][self.arrival(z, leftward)].astype(F32)

        self.both_ways(z, add)
        self.partial[slot, run] = self.total[...].astype(BF)

    def last_step(self, m):
        grid = self.grid
        z = grid.order(grid.line - 1 - m)
        self.add_other(z)

        @pl.when(z == grid.z)
        def _():
            self.across(z, self.last).start()

        @pl.when(z != grid.z)
        def _():
            pl.when(z < grid.z)(lambda: self.other(z, True).start())
            pl.when(z > grid.z)(lambda: self.other(z, False).start())
            self.total[...] = self.partial[self.place(z), self.run(self.last)].astype(F32)
            self.add_line(z, self.last)
            self.send_along(z, self.last)

    def own(self, result):
        def part_sum(part):
            self.gather_sum(self.grid.z, part)
            result[self.run(part)] = self.total[...]

        each(self.parts, part_sum)

    def finish(self):
        grid = self.grid

        def place(z):
            def part_done(part):
                pl.when(z < grid.z)(lambda: self.along(z, part, True).wait_send())
                pl.when(z > grid.z)(lambda: self.along(z, part, False).wait_send())

            each(self.parts, part_done)
            if self.from_across is not None:
                each(self.early, lambda part: self.across(z, part).wait_send())
            if self.cross is not None:
                pl.when(z < grid.z)(lambda: self.other(z, True).wait_send())
                pl.when(z > grid.z)(lambda: self.other(z, False).wait_send())

        each(grid.line, place)
        if self.cross is not None:
            self.across(grid.z, self.last).wait_send()


def scatter_scratch(line, rows, width, parts):
    return [
        pltpu.VMEM((2 * line, rows, width), BF),
        pltpu.VMEM((line, rows, width), BF),
        pltpu.VMEM((2 * line - 2, rows, width), BF),
        pltpu.VMEM((rows // parts, width), F32),
        pltpu.SemaphoreType.DMA((line, parts)),
        pltpu.SemaphoreType.DMA((line, parts)),
        pltpu.SemaphoreType.DMA((line, parts)),
        pltpu.SemaphoreType.DMA((2 * line - 2, parts)),
    ]


def load_pairs(pairs, sems):
    copies = [pltpu.make_async_copy(src, dst, sems.at[i]) for i, (src, dst) in enumerate(pairs)]
    for copy in copies:
        copy.start()
    for copy in copies:
        copy.wait()


def feed_kernel(
    line, parts, tile,
    normed, tangent_all, gate_own, gate_twin, up_own, up_twin, down_own, down_twin,
    grad_sum, normed_all, hidden_all, grad_gate, grad_up, grad_down,
    mirror_gate, mirror_up, mirror_down, part_gate, part_up, part_down,
    mirror_send, mirror_recv,
    gate_w, up_w, down_w, hidden, dgate, dup, rows_n, rows_t,
    partial, from_across, from_line, total, across_send, across_recv, line_send, line_recv,
    other_line, other_send, other_recv, gather_cross,
    gather_send, gather_recv, load_sem, wide, tile_sem, stage_a, stage_b, stage_sem, stage_recv, piece_a, piece_b, piece_sem, hidden_sem,
):
    grid = Grid(2, line)
    rows, width = normed.shape
    cols = gate_own.shape[1]
    blocks = 2 * line
    me = grid.slot(grid.x, grid.z)
    grid.greet(True, True)
    gather = Gather(grid, normed, normed_all, gather_send, gather_recv, parts, gather_cross)
    scatter = Scatter(
        grid, partial, from_across, from_line, total,
        (across_send, across_recv, line_send, line_recv), parts,
        (other_line, other_send, other_recv),
    )
    gather.send_own()
    load_pairs(
        [
            (gate_own, gate_w.at[:, pl.ds(0, cols)]),
            (gate_twin, gate_w.at[:, pl.ds(cols, cols)]),
            (up_own, up_w.at[:, pl.ds(0, cols)]),
            (up_twin, up_w.at[:, pl.ds(cols, cols)]),
            (down_own, down_w.at[pl.ds(0, cols)]),
            (down_twin, down_w.at[pl.ds(cols, cols)]),
            (normed, rows_n),
        ],
        load_sem,
    )
    load_pairs([(rows_n, normed_all.at[me])], load_sem)
    gather.turn_in()

    forwards = (line - 1) * parts

    def advance(n):
        distance, part = n // parts + 1, n % parts

        @pl.when(n < forwards)
        def _():
            pl.when(part < gather.early)(lambda: gather.forward(distance, part))
            pl.when(part == gather.last)(lambda: gather.forward_last(distance))

        return n + 1

    def work(slot, n):
        tangent_load = pltpu.make_async_copy(tangent_all.at[slot], rows_t, load_sem.at[1])
        tangent_load.start()
        load_pairs([(normed_all.at[slot], rows_n)], load_sem)
        spot = pl.ds(pl.multiple_of(slot * rows, rows), rows)

        def hidden_tile(j, n):
            c = pl.ds(pl.multiple_of(j * cols, cols), cols)
            gate = dot(rows_n[...], gate_w[:, c], NN)
            up = dot(rows_n[...], up_w[:, c], NN)
            pl.when(j == 0)(tangent_load.wait)
            grad = dot(rows_t[...], down_w[c, :], NT)
            sig = jax.nn.sigmoid(gate)
            silu = gate * sig
            hidden[spot, c] = (silu * up).astype(BF)
            dgate[spot, c] = (grad * up * (sig * (1.0 + gate * (1.0 - sig)))).astype(BF)
            dup[spot, c] = (grad * silu).astype(BF)
            return advance(n)

        n = lax.fori_loop(0, 2, hidden_tile, n)

        def back_tile(j, carry):
            c = pl.ds(pl.multiple_of(j * cols, cols), cols)
            sums = dot(dgate[spot, :], gate_w[c, :], NT) + dot(dup[spot, :], up_w[c, :], NT)
            partial[slot, :, c] = sums.astype(BF)
            return carry

        lax.fori_loop(0, width // cols, back_tile, 0)
        return advance(n)

    def stage(distance, n):
        def visit(i, n):
            z = grid.z + jnp.where(i % 2 == 0, -distance, distance)
            inside = jnp.logical_and(z >= 0, z < line)

            def block(n):
                n = lax.fori_loop(n, jnp.maximum(n, distance * parts), lambda m, c: advance(m), n)
                pl.when(i >= 2)(lambda: gather.wait_across(z))
                return work(grid.slot(jnp.where(i < 2, grid.x, 1 - grid.x), z), n)

            go = jnp.logical_and(inside, jnp.logical_or(distance > 0, i % 2 == 0))
            return lax.cond(go, block, lambda n: n, n)

        return lax.fori_loop(0, 4, visit, n)

    count = lax.fori_loop(0, line, stage, 0)
    lax.fori_loop(count, jnp.maximum(count, forwards), lambda m, c: advance(m), 0)
    hidden_copy = pltpu.make_async_copy(hidden, hidden_all, hidden_sem)
    hidden_copy.start()
    for j in range(line):
        scatter.send_across(scatter.rank(j))

    tiles = width // tile

    early_tiles = mirror_send.shape[0]

    def wide_loads(t, start):
        j, buf = t % tiles, t % 2
        c = pl.ds(pl.multiple_of(j * tile, tile), tile)
        for i, source in enumerate((normed_all, tangent_all)):
            copy = pltpu.make_async_copy(source.at[:, :, c], wide.at[buf, i], tile_sem.at[buf, i])
            copy.start() if start else copy.wait()

    def stages(t):
        j, buf = t % tiles, t % 2
        c = pl.ds(pl.multiple_of(j * tile, tile), tile)
        return [
            remote(src, dst, stage_sem.at[buf, i], stage_recv.at[j, i], grid.twin)
            for i, (src, dst) in enumerate(
                (
                    (stage_a.at[buf, 0], part_gate.at[c, :]),
                    (stage_a.at[buf, 1], part_up.at[c, :]),
                    (stage_b.at[buf], part_down.at[:, c]),
                )
            )
        ]

    def results(t):
        j, buf = t % tiles, t % 2
        c = pl.ds(pl.multiple_of(j * tile, tile), tile)
        return [
            pltpu.make_async_copy(src, dst, stage_sem.at[buf, i])
            for i, (src, dst) in enumerate(
                (
                    (stage_a.at[buf, 0], grad_gate.at[c, :]),
                    (stage_a.at[buf, 1], grad_up.at[c, :]),
                    (stage_b.at[buf], grad_down.at[:, c]),
                )
            )
        ]

    def mirrored(t):
        j = t % tiles
        c = pl.ds(pl.multiple_of(j * tile, tile), tile)
        return [
            remote(src, dst, mirror_send.at[j, i], mirror_recv.at[j, i], grid.mirror)
            for i, (src, dst) in enumerate(
                (
                    (grad_gate.at[c, :], mirror_gate.at[c, :]),
                    (grad_up.at[c, :], mirror_up.at[c, :]),
                    (grad_down.at[:, c], mirror_down.at[:, c]),
                )
            )
        ]

    def pieces(t):
        c = pl.ds(pl.multiple_of((t % tiles) * tile, tile), tile)
        return [
            (part_gate.at[c, :], piece_a.at[0]),
            (part_up.at[c, :], piece_a.at[1]),
            (part_down.at[:, c], piece_b),
        ]

    wide_loads(0, True)

    def weights(t, carry):
        buf = t % 2
        pl.when(t + 1 < 2 * tiles)(lambda: wide_loads(t + 1, True))
        wide_loads(t, False)
        tall = blocks * rows
        tokens = wide[buf, 0].reshape(tall, tile)
        tangents = wide[buf, 1].reshape(tall, tile)

        @pl.when(t < tiles)
        def _():
            theirs = slice(cols, 2 * cols)

            @pl.when(t >= 2)
            def _():
                for copy in stages(t - 2):
                    copy.wait_send()

            stage_a[buf, 0] = dot(tokens, dgate[:, theirs], TN).astype(BF)
            stage_a[buf, 1] = dot(tokens, dup[:, theirs], TN).astype(BF)
            stage_b[buf] = dot(hidden[:, theirs], tangents, TN).astype(BF)
            for copy in stages(t):
                copy.start()

        @pl.when(t >= tiles)
        def _():
            for copy in stages(t):
                copy.wait_recv()
            loads = [
                pltpu.make_async_copy(src, dst, piece_sem.at[i])
                for i, (src, dst) in enumerate(pieces(t))
            ]
            for copy in loads:
                copy.start()

            @pl.when(t < tiles + 2)
            def _():
                for copy in stages(t - 2):
                    copy.wait_send()

            @pl.when(t >= tiles + 2)
            def _():
                for copy in results(t - 2):
                    copy.wait()

                @pl.when(t < tiles + 2 + early_tiles)
                def _():
                    for copy in mirrored(t - 2):
                        copy.start()

            mine = slice(0, cols)
            own_gate = dot(tokens, dgate[:, mine], TN)
            own_up = dot(tokens, dup[:, mine], TN)
            own_down = dot(hidden[:, mine], tangents, TN)
            for copy in loads:
                copy.wait()
            stage_a[buf, 0] = (own_gate + piece_a[0].astype(F32)).astype(BF)
            stage_a[buf, 1] = (own_up + piece_a[1].astype(F32)).astype(BF)
            stage_b[buf] = (own_down + piece_b[...].astype(F32)).astype(BF)
            for copy in results(t):
                copy.start()

        n = t - 3 * lag
        pl.when(n >= 0)(lambda: scatter.step(n))
        m = t // 3 - lag
        ready = jnp.logical_and(t % 3 == 2, jnp.logical_and(m >= 0, m < line))
        pl.when(ready)(lambda: scatter.last_step(m))
        return carry

    lag = jnp.where(jnp.logical_and(grid.has_left, grid.has_right), 1, 0)
    lax.fori_loop(0, 2 * tiles, weights, 0)

    def rest(n, carry):
        scatter.step(n)
        return carry

    lax.fori_loop(2 * tiles - 3 * lag, scatter.steps(), rest, 0)
    scatter.own(grad_sum)
    for t in (2 * tiles - 2, 2 * tiles - 1):
        for copy in results(t):
            copy.wait()
    gather.finish()
    scatter.finish()
    hidden_copy.wait()
    for t in range(early_tiles):
        for copy in mirrored(t):
            copy.wait()


def feed_call(normed, tangent_all, gates, ups, downs, line):
    rows, width = normed.shape
    cols = gates[0].shape[1]
    blocks, parts, tile = 2 * line, 8, 256
    tiles = width // tile
    tall = blocks * rows
    shapes = jax.ShapeDtypeStruct
    hbm = lambda *s: shapes(s, BF)
    return pl.pallas_call(
        functools.partial(feed_kernel, line, parts, tile),
        out_shape=(
            shapes((rows, width), F32),
            hbm(blocks, rows, width), hbm(tall, 2 * cols),
            hbm(width, cols), hbm(width, cols), hbm(cols, width),
            hbm(width, cols), hbm(width, cols), hbm(cols, width),
            hbm(width, cols), hbm(width, cols), hbm(cols, width),
        ),
        in_specs=[ANY] * 8,
        out_specs=(pl.BlockSpec(memory_space=pltpu.VMEM),) + (ANY,) * 11,
        scratch_shapes=[
            pltpu.SemaphoreType.DMA((EARLY, 3)), pltpu.SemaphoreType.DMA((EARLY, 3)),
            pltpu.VMEM((width, 2 * cols), BF), pltpu.VMEM((width, 2 * cols), BF), pltpu.VMEM((2 * cols, width), BF),
            pltpu.VMEM((tall, 2 * cols), BF), pltpu.VMEM((tall, 2 * cols), BF), pltpu.VMEM((tall, 2 * cols), BF),
            pltpu.VMEM((rows, width), BF), pltpu.VMEM((rows, width), BF),
            *scatter_scratch(line, rows, width, parts),
            pltpu.VMEM((2 * line - 2, rows // parts, width), BF),
            pltpu.SemaphoreType.DMA((line,)), pltpu.SemaphoreType.DMA((2 * line - 2,)),
            pltpu.SemaphoreType.DMA((line, 2)),
            pltpu.SemaphoreType.DMA((line, parts, 3)), pltpu.SemaphoreType.DMA((blocks, parts)),
            pltpu.SemaphoreType.DMA((8,)),
            pltpu.VMEM((2, 2, blocks, rows, tile), BF), pltpu.SemaphoreType.DMA((2, 2)),
            pltpu.VMEM((2, 2, tile, cols), BF), pltpu.VMEM((2, cols, tile), BF),
            pltpu.SemaphoreType.DMA((2, 3)), pltpu.SemaphoreType.DMA((tiles, 3)),
            pltpu.VMEM((2, tile, cols), BF), pltpu.VMEM((cols, tile), BF), pltpu.SemaphoreType.DMA((3,)),
            pltpu.SemaphoreType.DMA,
        ],
        compiler_params=pltpu.CompilerParams(
            collective_id=1, has_side_effects=True, vmem_limit_bytes=63 * 2**20
        ),
        name="feed",
    )(normed, tangent_all, gates[0], gates[1], ups[0], ups[1], downs[0], downs[1])


class Thirds(Scatter):
    def run(self, part):
        quarter = self.rows
        start = jnp.where(part == 2, self.grid.replica, 2 + part) * quarter
        return pl.ds(pl.multiple_of(start, quarter), quarter)


def sums_kernel(
    line,
    normed, attended, grad_qkv, grad_out, twin_normed, twin_attended, twin_out, out_across,
    tokens, grad_middle, weights, gain, term_two,
    result, result_out, grad_tokens,
    across_v, out_partial, out_line, out_total, out_send, out_recv, out_mine, out_theirs, out_sem,
    near_send, near_recv, near_sem,
    both_normed, both_attended, both_qkv, both_out, load_sem, twin_send, twin_recv,
    partial, from_across, from_line, total, across_send, across_recv, line_send, line_recv,
    mine, theirs, mirror_send, mirror_recv, from_mirror, quarter_send, quarter_recv,
    in_weights, weight_sem, token_v, middle_v, grad_normed, terms, own_terms, twin_terms,
):
    grid = Grid(2, line)
    rows, width = normed.shape
    run = partial.shape[1]
    quarter = run // 4
    narrow = grad_qkv.shape[1]
    grid.greet(True, True)
    scatter = Thirds(
        grid, partial, from_across, from_line, total,
        (across_send, across_recv, line_send, line_recv), 3,
    )
    scatter.rows = quarter
    own, twin = pl.ds(0, rows), pl.ds(rows, rows)
    swap_qkv = remote(grad_qkv, both_qkv.at[twin], twin_send.at[0], twin_recv.at[0], grid.twin)
    swap_qkv.start()
    load_pairs(
        [
            (attended, both_attended.at[own]),
            (twin_attended, both_attended.at[twin]),
            (grad_out, both_out.at[own]),
            (twin_out, both_out.at[twin]),
            (out_across, across_v),
            (normed, both_normed.at[own]),
            (twin_normed, both_normed.at[twin]),
            (grad_qkv, both_qkv.at[own]),
        ],
        load_sem,
    )
    later = [
        pltpu.make_async_copy(src, dst, weight_sem.at[i])
        for i, (src, dst) in enumerate(
            (
                (weights.at[:, :, pl.ds(0, narrow)], in_weights),
                (tokens, token_v),
                (grad_middle, middle_v),
            )
        )
    ]
    for copy in later:
        copy.start()
    tall = line * run
    tile = 512
    away = pl.ds(pl.multiple_of((1 - grid.replica) * quarter, quarter), quarter)
    here = pl.ds(pl.multiple_of(grid.replica * quarter, quarter), quarter)

    outs = Scatter(
        grid, out_partial, None, out_line, out_total, (None, None, out_send, out_recv), 4
    )

    nears = [
        remote(near_send.at[j], near_recv.at[j], near_sem.at[0, j], near_sem.at[1, j], grid.across)
        for j in range(2)
    ]

    def near_step(i):
        c = pl.ds(pl.multiple_of(i * tile, tile), tile)
        for j in range(2):
            first = ((1 - grid.x) * 2 + grid.core) * tall + grid.order(j) * run
            theirs = pl.ds(pl.multiple_of(first, run), run)
            near_send[j, :, c] = dot(both_attended[:, theirs], both_out[:, c], TN).astype(BF)

    def sweep(part):
        each(line - 1, lambda i: scatter.pass_on(scatter.rank(i), part))

    def out_step(i):
        c = pl.ds(pl.multiple_of(i * tile, tile), tile)
        value = dot(both_attended[:, features(grid.x)], both_out[:, c], TN)
        value = value.reshape(line, run, tile) + across_v[:, :, c].astype(F32)
        out_partial[:, :, c] = value.astype(BF)

    def to_mirror(slot):
        return remote(
            partial.at[slot, away], from_mirror.at[slot],
            quarter_send.at[slot], quarter_recv.at[slot], grid.mirror,
        )

    def features(x):
        return pl.ds(pl.multiple_of((x * 2 + grid.core) * tall, tall), tall)

    def column(j, carry):
        x = jnp.where(j == 0, 1 - grid.x, grid.x)
        blocks = pl.ds(x * line, line)

        def wide(left, right, first):
            def step(i, inner):
                c = pl.ds(pl.multiple_of(i * tile, tile), tile)
                to = pl.ds(pl.multiple_of(first + i * tile, 128), tile)
                value = dot(left[:, features(x)], right[:, c], TN).astype(BF)
                partial[blocks, :, to] = value.reshape(line, run, tile)
                return inner

            lax.fori_loop(0, right.shape[1] // tile, step, 0)

        wide(both_normed, both_qkv, 0)
        partial[blocks, :, narrow:] = jnp.zeros((line, run, 128), BF)
        for k in range(line - 1, -1, -1):
            z = grid.order(k)
            to_mirror(grid.slot(x, z)).start()
            pl.when(j == 0)(lambda z=z: scatter.across(z, 0).start())
        return carry

    for j in range(2):
        across_v[grid.order(j)] = jnp.zeros((run, width), BF)
    each(width // tile, near_step)
    nears[1].start()
    each(width // tile, out_step)
    early_outs = (line - 2) * outs.early
    middling = jnp.logical_and(grid.has_left, grid.has_right)

    def when_end(action):
        pl.when(jnp.logical_not(middling))(action)

    when_end(lambda: each(early_outs, outs.step))
    swap_qkv.wait()
    lax.fori_loop(0, 2, column, 0)
    nears[0].start()
    when_end(lambda: sweep(0))
    for copy in later:
        copy.wait()

    def back_step(j, carry):
        units = pl.ds(j * (tile // run), tile // run)
        c = pl.ds(pl.multiple_of(j * tile, tile), tile)
        right = in_weights[units].reshape(tile, narrow)
        grad_normed[:, c] = dot(both_qkv[own, :], right, NT)
        return carry

    lax.fori_loop(0, width // tile, back_step, 0)
    terms[...] = jnp.zeros_like(terms)
    chunk = 64

    def norm_step(j, carry):
        r = pl.ds(pl.multiple_of(j * chunk, chunk), chunk)
        value = token_v[r, :].astype(F32)
        factor = lax.rsqrt(jnp.mean(value * value, axis=1, keepdims=True) + norm_eps)
        unit = value * factor
        grad = grad_normed[r, :]
        terms[0:1, :] += jnp.sum(grad * unit, axis=0, keepdims=True)
        scaled = grad * gain[0:1, :]
        mean = jnp.mean(scaled * unit, axis=1, keepdims=True)
        grad_tokens[r, :] = (middle_v[r, :] + factor * (scaled - unit * mean)).astype(BF)
        return carry

    lax.fori_loop(0, rows // chunk, norm_step, 0)
    terms[1:2, :] = term_two[...]
    own_terms[...] = terms[...].astype(BF)
    swap_terms = remote(own_terms, twin_terms, twin_send.at[1], twin_recv.at[1], grid.twin)
    swap_terms.start()
    swap_terms.wait()
    for x in range(2):
        for z in range(line):
            first = pl.multiple_of((x * 2 + grid.core) * tall + z * run, run)
            c = pl.ds(first, run)
            value = own_terms[:, c].astype(F32) + twin_terms[:, c].astype(F32)
            partial[x * line + z, 3 * quarter : 3 * quarter + 16, narrow:] = value.astype(BF)
    for k in range(line - 1, -1, -1):
        scatter.across(grid.order(k), 1).start()

    def add_mirror(x):
        def step(i, carry):
            slot = grid.slot(x, grid.order(line - 1 - i))
            to_mirror(slot).wait_recv()
            value = partial[slot, here].astype(F32) + from_mirror[slot].astype(F32)
            partial[slot, here] = value.astype(BF)
            return carry

        lax.fori_loop(0, line, step, 0)

    add_mirror(1 - grid.x)
    for k in range(line - 1, -1, -1):
        scatter.across(grid.order(k), 2).start()
    pl.when(middling)(lambda: each(early_outs, outs.step))
    nears[1].wait()
    next_place = grid.order(1)
    out_partial[next_place] = (
        out_partial[next_place].astype(F32) + near_recv[1].astype(F32)
    ).astype(BF)
    pl.when(middling)(lambda: sweep(0))

    def out_rest(n, carry):
        outs.step(n)
        return carry

    lax.fori_loop(early_outs, outs.steps(), out_rest, 0)
    sweep(1)

    def swap(part, whole=True):
        at = scatter.run(part)
        return remote(
            mine.at[at], theirs.at[at], mirror_send.at[part], mirror_recv.at[part], grid.mirror
        )

    def settle(part):
        scatter.gather_sum(grid.z, part)
        mine[scatter.run(part)] = total[...].astype(BF)
        swap(part).start()

    outs.own(result_out)
    nears[0].wait()
    result_out[...] += near_recv[0].astype(F32)
    out_mine[...] = result_out[...].astype(BF)
    out_swap = remote(out_mine, out_theirs, out_sem.at[0], out_sem.at[1], grid.mirror)
    out_swap.start()
    add_mirror(grid.x)
    settle(0)
    sweep(2)
    settle(1)
    settle(2)
    result[here] = mine[here].astype(F32)
    for part in range(2):
        swap(part).wait()
        at = scatter.run(part)
        result[at] = mine[at].astype(F32) + theirs[at].astype(F32)
    swap(2).wait_send()
    remote(mine.at[away], theirs.at[away], mirror_send.at[2], mirror_recv.at[2], grid.mirror).wait_recv()
    result[away] = theirs[away].astype(F32)
    out_swap.wait()
    result_out[...] = out_mine[...].astype(F32) + out_theirs[...].astype(F32)
    outs.finish()
    scatter.finish()

    def sent(slot, carry):
        to_mirror(slot).wait_send()
        return carry

    lax.fori_loop(0, 2 * line, sent, 0)


def sums_call(
    normed, attended, grad_qkv, grad_out, others, tokens, grad_middle, weights, gain, term_two, line
):
    rows, width = normed.shape
    narrow = grad_qkv.shape[1]
    run, whole = weights.shape[1], narrow + 128
    quarter = run // 4
    vmem = pl.BlockSpec(memory_space=pltpu.VMEM)
    dma = pltpu.SemaphoreType.DMA
    like = lambda a: pltpu.VMEM(a.shape, a.dtype)
    return pl.pallas_call(
        functools.partial(sums_kernel, line),
        out_shape=(
            jax.ShapeDtypeStruct((run, whole), F32), jax.ShapeDtypeStruct((run, width), F32),
            jax.ShapeDtypeStruct((rows, width), BF),
        ),
        in_specs=[ANY] * 11 + [vmem] * 2,
        out_specs=(vmem,) * 3,
        scratch_shapes=[
            pltpu.VMEM((line, run, width), BF), pltpu.VMEM((line, run, width), BF),
            pltpu.VMEM((2 * line - 2, run, width), BF), pltpu.VMEM((quarter, width), F32),
            dma((line, 4)), dma((2 * line - 2, 4)),
            pltpu.VMEM((run, width), BF), pltpu.VMEM((run, width), BF), dma((2,)),
            pltpu.VMEM((2, run, width), BF), pltpu.VMEM((2, run, width), BF), dma((2, 2)),
            pltpu.VMEM((2 * rows, width), BF), pltpu.VMEM((2 * rows, width), BF),
            pltpu.VMEM((2 * rows, narrow), BF), pltpu.VMEM((2 * rows, width), BF),
            dma((8,)), dma((2,)), dma((2,)),
            pltpu.VMEM((2 * line, run, whole), BF), pltpu.VMEM((line, run, whole), BF),
            pltpu.VMEM((2 * line - 2, run, whole), BF), pltpu.VMEM((quarter, whole), F32),
            dma((line, 3)), dma((line, 3)), dma((line, 3)), dma((2 * line - 2, 3)),
            pltpu.VMEM((run, whole), BF), pltpu.VMEM((run, whole), BF), dma((3,)), dma((3,)),
            pltpu.VMEM((2 * line, quarter, whole), BF), dma((2 * line,)), dma((2 * line,)),
            pltpu.VMEM((weights.shape[0], run, narrow), BF), dma((3,)),
            like(tokens), like(grad_middle), pltpu.VMEM((rows, width), F32),
            pltpu.VMEM((16, width), F32), pltpu.VMEM((16, width), BF), pltpu.VMEM((16, width), BF),
        ],
        compiler_params=pltpu.CompilerParams(
            collective_id=3, has_side_effects=True, vmem_limit_bytes=63 * 2**20
        ),
        name="sums",
    )(
        normed, attended, grad_qkv, grad_out, *others, tokens, grad_middle, weights, gain, term_two
    )


def gather_weights(
    grid, block, everything, send, recv, twin_send, twin_recv, meanwhile, afterwards
):
    line = grid.line
    rows = block.shape[0] // 4
    carry_a, carry_b = grid.replica * 2, grid.replica * 2 + 1
    other_a, other_b = (1 - grid.replica) * 2, (1 - grid.replica) * 2 + 1
    right, left, across, mirror = range(4)
    devices = (grid.right, grid.left, grid.across, grid.mirror)

    def run(quarter):
        return pl.ds(pl.multiple_of(quarter * rows, rows), rows)

    def place(x, core, z, quarter):
        return everything.at[(x * 2 + core) * line + z, run(quarter)]

    def copy(x, z, quarter, link, first=False):
        there = place(x, grid.core, z, quarter)
        here = block.at[run(quarter)] if first else there
        unit = x * line + z
        return remote(
            here, there, send.at[quarter, unit, link], recv.at[quarter, unit], devices[link]
        )

    def share(x, z, quarter, first=False):
        there = place(x, grid.core, z, quarter)
        here = block.at[run(quarter)] if first else there
        unit = x * line + z
        return remote(
            here, there, twin_send.at[quarter, unit], twin_recv.at[quarter, unit], grid.twin
        )

    def arrived(x, z, quarter):
        copy(x, z, quarter, across).wait_recv()
        share(x, z, quarter).start()

    copy(grid.x, grid.z, carry_b, across, True).start()
    copy(grid.x, grid.z, carry_a, across, True).start()
    copy(grid.x, grid.z, other_a, across, True).start()
    for link, go in ((right, grid.has_right), (left, grid.has_left)):

        @pl.when(go)
        def _(link=link):
            copy(grid.x, grid.z, carry_a, link, True).start()
            copy(grid.x, grid.z, carry_b, link, True).start()

    for quarter in range(4):
        share(grid.x, grid.z, quarter, True).start()
    meanwhile()

    arrived(1 - grid.x, grid.z, carry_b)
    copy(1 - grid.x, grid.z, carry_b, mirror).start()
    for link, go in ((right, grid.has_right), (left, grid.has_left)):
        pl.when(go)(lambda link=link: copy(1 - grid.x, grid.z, carry_b, link).start())

    def sides(distance):
        return (
            (grid.z - distance, grid.z >= distance, right, grid.has_right),
            (grid.z + distance, grid.z + distance < line, left, grid.has_left),
        )

    def step(distance, carry):
        for x, quarter in (
            (grid.x, carry_a),
            (grid.x, carry_b),
            (1 - grid.x, carry_b),
        ):
            for z, there, link, go in sides(distance):

                @pl.when(there)
                def _(x=x, quarter=quarter, z=z, link=link, go=go):
                    copy(x, z, quarter, across).wait_recv()
                    pl.when(go)(lambda: copy(x, z, quarter, link).start())
                    copy(x, z, quarter, mirror).start()
                    if quarter is carry_a:
                        copy(x, z, quarter, across).start()
                    share(x, z, quarter).start()

        for z, there, _, _ in sides(distance - 1):

            @pl.when(jnp.logical_and(there, distance > 1))
            def _(z=z):
                arrived(grid.x, z, other_a)
                copy(grid.x, z, other_a, across).start()

        return carry

    lax.fori_loop(1, line + 1, step, 0)
    afterwards()

    def last(z, carry):
        arrived(1 - grid.x, z, carry_a)
        arrived(1 - grid.x, z, other_a)
        arrived(1 - grid.x, z, other_b)
        pl.when(z != grid.z)(lambda: arrived(grid.x, z, other_b))
        return carry

    lax.fori_loop(0, line, last, 0)

    def finish(z, carry):
        away = z != grid.z
        for x in (grid.x, 1 - grid.x):
            for quarter in range(4):
                share(x, z, quarter).wait()
        for x, quarter in ((grid.x, carry_a), (grid.x, carry_b), (1 - grid.x, carry_b)):
            to_mirror = jnp.logical_or(away, jnp.bool_(x is not grid.x))
            pl.when(to_mirror)(
                lambda x=x, quarter=quarter: copy(x, z, quarter, mirror).wait_send()
            )
            for link, go in (
                (right, jnp.logical_and(z <= grid.z, grid.has_right)),
                (left, jnp.logical_and(z >= grid.z, grid.has_left)),
            ):
                pl.when(go)(
                    lambda x=x, quarter=quarter, link=link: copy(x, z, quarter, link).wait_send()
                )
        copy(grid.x, z, carry_a, across).wait_send()
        copy(grid.x, z, other_a, across).wait_send()
        return carry

    lax.fori_loop(0, line, finish, 0)
    copy(grid.x, grid.z, carry_b, across, True).wait_send()


def mask(places, own_places):
    return jnp.where(places[...] <= own_places[...], 0.0, -1e30).astype(F32)


class Line:
    def __init__(self, grid, block, everything, send, recv):
        self.grid, self.block, self.everything = grid, block, everything
        self.send, self.recv = send, recv

    def copy(self, z, link, first=False):
        grid = self.grid
        there = self.everything.at[z]
        here = self.block if first else there
        device = (grid.right, grid.left)[link]
        return remote(here, there, self.send.at[z, link], self.recv.at[z], device)

    def send_own(self):
        grid = self.grid
        for link, go in ((0, grid.has_right), (1, grid.has_left)):
            pl.when(go)(lambda link=link: self.copy(grid.z, link, True).start())

    def forward(self, distance):
        grid = self.grid
        for z, there, link, go in (
            (grid.z - distance, grid.z >= distance, 0, grid.has_right),
            (grid.z + distance, grid.z + distance < grid.line, 1, grid.has_left),
        ):

            @pl.when(there)
            def _(z=z, link=link, go=go):
                self.copy(z, link).wait_recv()
                pl.when(go)(lambda: self.copy(z, link).start())

    def finish(self):
        grid = self.grid

        def step(z, carry):
            for link, go in (
                (0, jnp.logical_and(z <= grid.z, grid.has_right)),
                (1, jnp.logical_and(z >= grid.z, grid.has_left)),
            ):
                pl.when(go)(lambda link=link: self.copy(z, link).wait_send())
            return carry

        lax.fori_loop(0, grid.line, step, 0)


def turn(value, cosine, sine, scale):
    parts = []
    lane = lax.broadcasted_iota(jnp.int32, (value.shape[0], 128), 1) % HEAD_SIZE
    for first in range(0, value.shape[1], 128):
        pair = value[:, first : first + 128]
        swapped = jnp.where(
            lane < HEAD_SIZE // 2,
            pltpu.roll(pair, 128 - HEAD_SIZE // 2, 1),
            pltpu.roll(pair, HEAD_SIZE // 2, 1),
        )
        parts.append(((pair * cosine[...] + swapped * sine[...]) * scale).astype(BF))
    return parts[0] if len(parts) == 1 else jnp.concatenate(parts, axis=1)


def halves(pair, half):
    pair = pair.astype(F32)
    turned = pltpu.roll(pair, HEAD_SIZE, 1)
    lane = lax.broadcasted_iota(jnp.int32, pair.shape, 1) // HEAD_SIZE
    first = jnp.where(half == 0, pair, turned)
    second = jnp.where(half == 0, turned, pair)
    both = jnp.concatenate([first, second], axis=0)
    return jnp.where(jnp.concatenate([lane, lane], axis=0) == half, both, 0.0).astype(BF)


def unhalves(both, half):
    rows = both.shape[0] // 2
    first, second = both[:rows], both[rows:]
    lane = lax.broadcasted_iota(jnp.int32, first.shape, 1) // HEAD_SIZE
    first = jnp.where(half == 0, first, pltpu.roll(first, HEAD_SIZE, 1))
    second = jnp.where(half == 0, pltpu.roll(second, HEAD_SIZE, 1), second)
    return jnp.where(lane == 0, first, second)


def front_kernel(
    line, parts,
    query_w, key_w, value_w, out_w, tokens, tangent, cosine, sine, gain_one, gain_two, places, own_places,
    attended, middle, normed, first_normed, queries, logs, gain, keyed_out, tangent_all, weights_out,
    everything, keyed, keyed_all, bias_v, token_v, cosine_v, sine_v, scores, probs, sums, stage, load_sem,
    key_send, key_recv, send, recv, own_sem, weight_send, weight_recv, twin_send, twin_recv,
):
    grid = Grid(2, line)
    rows, width = tokens.shape
    narrow = keyed.shape[1] // 2
    total = places.shape[1]
    extra = width + 2 * narrow
    after = extra + 128
    me = grid.slot(grid.x, grid.z)
    chunk = rows // 2
    tile = 512
    block = everything.at[(grid.x * 2 + grid.core) * line + grid.z]
    starts = (0, width, width + narrow, after)
    load_pairs(
        [
            (part, block.at[:, pl.ds(first, part.shape[1])])
            for first, part in zip(starts, (query_w, key_w, value_w, out_w))
        ],
        load_sem,
    )
    row = lax.broadcasted_iota(jnp.int32, (16, 128), 0)
    both_gains = jnp.where(row == 0, gain_one[...].astype(F32), gain_two[...].astype(F32))
    everything[(grid.x * 2 + grid.core) * line + grid.z, 0:16, extra:after] = both_gains.astype(BF)
    grid.greet(True, True)

    def meanwhile():
        load_pairs(
            [
                (tangent, stage),
                (tokens, token_v),
                (cosine, cosine_v),
                (sine, sine_v),
            ],
            load_sem,
        )
        load_pairs([(stage, tangent_all.at[me])], own_sem)
        bias_v[...] = mask(places, own_places)

    gather = Gather(grid, tangent, tangent_all, send, recv, parts)
    soon = 1

    def tangent_first():
        gather.send_own()
        for part in range(soon):
            gather.forward(1, part)

    gather_weights(
        grid, block, everything, weight_send, weight_recv, twin_send, twin_recv, meanwhile,
        tangent_first,
    )
    weights_copy = pltpu.make_async_copy(everything, weights_out, own_sem.at[1])
    weights_copy.start()
    units, run = everything.shape[0], everything.shape[1]
    for unit in range(units):
        for which in range(2):
            gain[which : which + 1, unit * run : (unit + 1) * run] = everything[
                unit, which : which + 1, extra:after
            ].astype(F32)

    def norm(source, target, which):
        def step(j, carry):
            here = pl.ds(pl.multiple_of(j * chunk, chunk), chunk)
            value = source[here, :].astype(F32)
            factor = lax.rsqrt(jnp.mean(value * value, axis=1, keepdims=True) + norm_eps)
            target[here, :] = (value * factor * gain[which : which + 1, :]).astype(BF)
            return carry

        lax.fori_loop(0, rows // chunk, step, 0)

    norm(token_v, first_normed, 0)

    def project(c):
        return dot(first_normed[...], everything[:, :, c].reshape(width, tile), NN)

    for first in range(0, narrow, tile):
        keyed[:, first : first + tile] = turn(project(slice(width + first, width + first + tile)), cosine_v, sine_v, 1.0)
        keyed[:, narrow + first : narrow + first + tile] = project(
            slice(width + narrow + first, width + narrow + first + tile)
        ).astype(BF)
    line_keys = Line(grid, keyed, keyed_all, key_send, key_recv)
    line_keys.send_own()
    for part in range(soon, parts):
        gather.forward(1, part, along=False)
    keyed_all[grid.z] = keyed[...]

    def query_step(j, carry):
        c = pl.ds(pl.multiple_of(j * tile, tile), tile)
        queries[:, c] = turn(project(c), cosine_v, sine_v, HEAD_SIZE ** (-0.5))
        return carry

    lax.fori_loop(0, width // tile, query_step, 0)
    def advance(n):
        gather.forward(n // parts + 2, n % parts)

    for distance in range(1, line - 1):
        line_keys.forward(distance)
    for part in range(soon, parts):
        gather.forward(1, part, wait=False, across=False)
    for n in range(soon):
        advance(n)
    line_keys.forward(line - 1)

    logs[...] = jnp.zeros_like(logs)
    pairs = width // (2 * HEAD_SIZE)
    group = pairs // (narrow // (2 * HEAD_SIZE))

    def pair_step(i, carry):
        c = pl.ds(pl.multiple_of(i * 128, 128), 128)
        half = (i // (group // 2)) % 2
        first_key = pl.multiple_of((i // group) * 128, 128)
        keys = keyed_all[:, :, pl.ds(first_key, 128)].reshape(total, 128)
        values = keyed_all[:, :, pl.ds(first_key + narrow, 128)].reshape(total, 128)
        scores[...] = dot(halves(queries[:, c], half), keys, NT)

        def soft(j, inner):
            here = pl.ds(pl.multiple_of(j * rows, rows), rows)
            value = scores[here, :] + bias_v[...]
            top = jnp.max(value, axis=1, keepdims=True)
            power = jnp.exp(value - top)
            size = jnp.sum(power, axis=1, keepdims=True)
            probs[here, :] = power.astype(BF)
            sums[here, :] = jnp.broadcast_to(1.0 / size, (rows, 128))
            lane = lax.broadcasted_iota(jnp.int32, (rows, 128), 1)
            logs[here, :] = jnp.where(lane == i, top + jnp.log(size), logs[here, :])
            return inner

        lax.fori_loop(0, 2, soft, 0)
        out = dot(probs[...], values, NN) * sums[...]
        attended[:, c] = unhalves(out, half).astype(BF)

        n = soon + i // 2
        pl.when(jnp.logical_and(i % 2 == 1, n < (line - 2) * parts))(lambda: advance(n))
        return carry

    lax.fori_loop(0, pairs, pair_step, 0)
    keyed_copy = pltpu.make_async_copy(keyed_all, keyed_out, load_sem.at[0])
    keyed_copy.start()

    def out_step(j, carry):
        c = pl.ds(pl.multiple_of(j * tile, tile), tile)
        w = pl.ds(pl.multiple_of(after + j * tile, 128), tile)
        out = dot(attended[...], everything[:, :, w].reshape(width, tile), NN)
        middle[:, c] = token_v[:, c].astype(F32) + out
        return carry

    lax.fori_loop(0, width // tile, out_step, 0)
    norm(middle, normed, 1)

    def rest(n, carry):
        advance(n)
        return carry

    lax.fori_loop(soon + pairs // 2, (line - 2) * parts, rest, 0)
    for z in range(line):
        gather.wait_across(z)
    keyed_copy.wait()
    weights_copy.wait()
    line_keys.finish()
    gather.finish()


def front_call(pieces, tokens, tangent, cosine, sine, gains, places, own_places, line):
    rows, width = tokens.shape
    narrow = pieces[1].shape[1]
    unit = (pieces[0].shape[0], sum(p.shape[1] for p in pieces) + 128)
    total = places.shape[1]
    blocks, parts = 2 * line, 4
    shapes = jax.ShapeDtypeStruct
    vmem = pl.BlockSpec(memory_space=pltpu.VMEM)
    like = lambda a: pltpu.VMEM(a.shape, a.dtype)
    return pl.pallas_call(
        functools.partial(front_kernel, line, parts),
        out_shape=(
            shapes((rows, width), BF), shapes((rows, width), F32), shapes((rows, width), BF),
            shapes((rows, width), BF), shapes((rows, width), BF),
            shapes((2 * rows, 128), F32), shapes((2, width), F32),
            shapes((line, rows, 2 * narrow), BF),
            shapes((blocks, rows, width), BF), shapes((2 * blocks,) + unit, BF),
        ),
        in_specs=[ANY] * 8 + [vmem] * 4,
        out_specs=(vmem,) * 7 + (ANY,) * 3,
        scratch_shapes=[
            pltpu.VMEM((2 * blocks,) + unit, BF),
            pltpu.VMEM((rows, 2 * narrow), BF), pltpu.VMEM((line, rows, 2 * narrow), BF),
            pltpu.VMEM((rows, total), F32), like(tokens), like(cosine), like(sine),
            pltpu.VMEM((2 * rows, total), F32), pltpu.VMEM((2 * rows, total), BF),
            pltpu.VMEM((2 * rows, 128), F32), pltpu.VMEM((rows, width), BF), pltpu.SemaphoreType.DMA((6,)),
            pltpu.SemaphoreType.DMA((line, 2)), pltpu.SemaphoreType.DMA((line,)),
            pltpu.SemaphoreType.DMA((line, parts, 3)), pltpu.SemaphoreType.DMA((blocks, parts)),
            pltpu.SemaphoreType.DMA((2,)),
            pltpu.SemaphoreType.DMA((4, blocks, 4)), pltpu.SemaphoreType.DMA((4, blocks)),
            pltpu.SemaphoreType.DMA((4, blocks)), pltpu.SemaphoreType.DMA((4, blocks)),
        ],
        compiler_params=pltpu.CompilerParams(
            collective_id=5, has_side_effects=True, vmem_limit_bytes=62 * 2**20
        ),
        name="front",
    )(*pieces, tokens, tangent, cosine, sine, *gains, places, own_places)


def back_kernel(
    line, parts,
    places, own_places, queries, keyed_all, middle, grad_normed, tangent, gain, logs, hidden_all,
    down_own, down_twin, weights, cosine, sine,
    gate_sum, up_sum, down_sum, _gate, _up, _down, normed, attended,
    out_v, grad_qkv, term_two, gate_mirror, up_mirror, down_mirror,
    twin_normed, twin_attended, twin_out, grad_out, grad_middle,
    out_across, both_attended, both_out, out_partial, out_send, out_recv,
    norm_sem, gain_v, branch, out_w, cosine_v, sine_v, grad_keyed, mirror_send, mirror_recv,
    query_v, keyed_v, grad_v, bias_v, log_v, scores, gradients, probs, slopes, key_sum, value_sum,
    down_w, hidden, load_sem,
    partial, from_across, from_line, total, across_send, across_recv, line_send, line_recv,
    key_partial, key_line, key_total, key_send, key_recv,
):
    grid = Grid(2, line)
    cols, width = down_own.shape
    rows = partial.shape[1]
    narrow = keyed_all.shape[2] // 2
    length = places.shape[1]
    grid.greet(True, True)
    swapped = [
        remote(src, dst, mirror_send.at[3 + i], mirror_recv.at[3 + i], grid.twin)
        for i, (src, dst) in enumerate(
            ((normed, twin_normed), (attended, twin_attended), (out_v, twin_out))
        )
    ]
    for copy in swapped[:2]:
        copy.start()
    left = pl.ds(EARLY * 256, width - EARLY * 256)
    mirrored = [
        remote(src, dst, mirror_send.at[i], mirror_recv.at[i], grid.mirror)
        for i, (src, dst) in enumerate(
            (
                (gate_sum.at[left, :], gate_mirror.at[left, :]),
                (up_sum.at[left, :], up_mirror.at[left, :]),
                (down_sum.at[:, left], down_mirror.at[:, left]),
            )
        )
    ]
    for copy in mirrored:
        copy.start()
    load_pairs(
        [
            (down_own, down_w.at[pl.ds(0, cols)]),
            (down_twin, down_w.at[pl.ds(cols, cols)]),
            (hidden_all, hidden),
            (queries, query_v),
            (keyed_all, keyed_v),
            (gain, gain_v),
            (logs, log_v),
            (cosine, cosine_v),
            (sine, sine_v),
        ],
        load_sem,
    )
    bias_v[...] = mask(places, own_places)
    scatter = Scatter(
        grid, partial, from_across, from_line, total,
        (across_send, across_recv, line_send, line_recv), parts,
    )
    keyed_scatter = Scatter(
        grid, key_partial, None, key_line, key_total, (None, None, key_send, key_recv),
        key_partial.shape[1] // rows,
    )

    def work(i, carry):
        z = grid.order(line - 1 - i % line)
        slot = grid.slot(jnp.where(i < line, 1 - grid.x, grid.x), z)
        spot = pl.ds(pl.multiple_of(slot * rows, rows), rows)

        def tile(j, inner):
            c = pl.ds(pl.multiple_of(j * cols, cols), cols)
            partial[slot, :, c] = dot(hidden[spot, :], down_w[:, c], NN).astype(BF)
            return inner

        lax.fori_loop(0, width // cols, tile, 0)
        pl.when(i < line)(lambda: scatter.send_across(z))
        return carry

    deep = 2 * rows
    middle_v, normed_v, tangent_v = scores, gradients, probs
    half_width = width // 2
    norm_loads = [
        pltpu.make_async_copy(
            src.at[:, pl.ds(h * half_width, half_width)], dst.at[pl.ds(h * rows, rows), :], norm_sem.at[i, h]
        )
        for i, (src, dst) in enumerate(
            ((middle, middle_v), (grad_normed, normed_v), (tangent, tangent_v))
        )
        for h in range(2)
    ]
    for copy in norm_loads:
        copy.start()
    lax.fori_loop(0, line, work, 0)
    for copy in norm_loads:
        copy.wait()
    term_two[...] = jnp.zeros_like(term_two)
    few = rows // 4

    def norm_step(j):
        spots = [pl.ds(pl.multiple_of(h * rows + j * few, few), few) for h in range(2)]
        here = pl.ds(pl.multiple_of(j * few, few), few)
        sides = [pl.ds(h * half_width, half_width) for h in range(2)]
        values = [middle_v[s, :] for s in spots]
        square = sum(jnp.sum(v * v, axis=1, keepdims=True) for v in values)
        factor = lax.rsqrt(square / width + norm_eps)
        units = [v * factor for v in values]
        grads = [normed_v[s, :] for s in spots]
        scaled = [g * gain_v[1:2, c] for g, c in zip(grads, sides)]
        dots = sum(jnp.sum(s * u, axis=1, keepdims=True) for s, u in zip(scaled, units))
        mean = dots / width
        for spot, c, grad, unit, scale in zip(spots, sides, grads, units, scaled):
            term_two[:, c] += jnp.sum(grad * unit, axis=0, keepdims=True)
            value = tangent_v[spot, :].astype(F32) + factor * (scale - unit * mean)
            branch[here, c] = value
            out_v[here, c] = value.astype(BF)

    each(rows // few, norm_step)
    norm_copies = [
        pltpu.make_async_copy(branch, grad_middle, norm_sem.at[0, 0]),
        pltpu.make_async_copy(out_v, grad_out, norm_sem.at[0, 1]),
    ]
    for copy in norm_copies + swapped[2:]:
        copy.start()
    work(line, 0)
    lag = jnp.where(jnp.logical_and(grid.has_left, grid.has_right), 2, 0)

    def paced(position):
        pl.when(position >= lag)(lambda: scatter.step(position - lag))

    paced(0)
    tile = out_w.shape[0] * out_w.shape[1]
    after = weights.shape[2] - width

    def out_step(j, carry):
        units = pl.ds(j * out_w.shape[0], out_w.shape[0])
        load_pairs([(weights.at[units, :, pl.ds(after, width)], out_w)], load_sem)
        c = pl.ds(pl.multiple_of(j * tile, tile), tile)
        grad_v[:, c] = dot(out_v[...], out_w[...].reshape(tile, width), NT).astype(BF)
        pl.when(j % 2 == 1)(lambda: paced(1 + j // 2))
        return carry

    lax.fori_loop(0, width // tile, out_step, 0)
    chunk = rows // 2
    pairs = width // (2 * HEAD_SIZE)
    group = pairs // (narrow // (2 * HEAD_SIZE))

    def pair_step(i, carry):
        c = pl.ds(pl.multiple_of(i * 128, 128), 128)
        half = (i // (group // 2)) % 2
        key_cols = pl.ds(pl.multiple_of((i // group) * 128, 128), 128)
        value_cols = pl.ds(pl.multiple_of((i // group) * 128 + narrow, 128), 128)
        keys = keyed_v[:, :, key_cols].reshape(length, 128)
        values = keyed_v[:, :, value_cols].reshape(length, 128)
        query = halves(query_v[:, c], half)
        grad = halves(grad_v[:, c], half)
        scores[...] = dot(query, keys, NT)
        gradients[...] = dot(grad, values, NT)

        def soft(j, inner):
            here = pl.ds(pl.multiple_of(j * chunk, chunk), chunk)
            there = pl.ds(pl.multiple_of((j * chunk) % rows, chunk), chunk)
            lane = lax.broadcasted_iota(jnp.int32, (chunk, 128), 1)
            log = jnp.sum(jnp.where(lane == i, log_v[here, :], 0.0), axis=1, keepdims=True)
            prob = jnp.exp(scores[here, :] + bias_v[there, :] - log)
            slope = gradients[here, :]
            delta = jnp.sum(prob * slope, axis=1, keepdims=True)
            probs[here, :] = prob.astype(BF)
            slopes[here, :] = (prob * (slope - delta)).astype(BF)
            return inner

        lax.fori_loop(0, deep // chunk, soft, 0)
        back = dot(slopes[...], keys, NN) * HEAD_SIZE ** (-0.5)
        grad_qkv[:, c] = turn(unhalves(back, half), cosine_v, sine_v, 1.0)
        key_part = dot(slopes[...], query, TN)
        value_part = dot(probs[...], grad, TN)

        @pl.when(i % group == 0)
        def _():
            key_sum[...] = key_part
            value_sum[...] = value_part

        @pl.when(i % group != 0)
        def _():
            key_sum[...] += key_part
            value_sum[...] += value_part

        @pl.when(i % group == group - 1)
        def _():
            spot = pl.ds(pl.multiple_of((i // group) * rows, rows), rows)
            key_partial[:, spot, 0:128] = key_sum[...].astype(BF).reshape(line, rows, 128)
            key_partial[:, spot, 128:256] = value_sum[...].astype(BF).reshape(line, rows, 128)
            pl.when(i // group + early > 0)(lambda: keyed_steps(i // group + early - 1))

        @pl.when(i % 6 == 2)
        def _():
            work(line + 1 + i // 6, 0)

        pl.when(i == pairs // 2 - 2)(out_gradients)

        done = (3 * i + 1) // 5
        pl.when((3 * i + 4) // 5 > done)(lambda: paced(3 + done))
        return carry

    run = out_partial.shape[1]

    def outward(z):
        return remote(
            out_partial.at[z], out_across.at[z], out_send.at[z], out_recv.at[z], grid.across
        )

    def away(action):
        for j in range(line - 2):
            action(outward(scatter.rank(j)))

    def out_gradients():
        for copy in swapped[1:]:
            copy.wait()
        own, twin = pl.ds(0, rows), pl.ds(rows, rows)
        load_pairs(
            [
                (attended, both_attended.at[own]),
                (twin_attended, both_attended.at[twin]),
                (out_v, both_out.at[own]),
                (twin_out, both_out.at[twin]),
            ],
            load_sem,
        )
        tall = line * run
        first = pl.multiple_of(((1 - grid.x) * 2 + grid.core) * tall, tall)

        def tile_step(j):
            c = pl.ds(pl.multiple_of(j * 512, 512), 512)
            value = dot(both_attended[:, pl.ds(first, tall)], both_out[:, c], TN).astype(BF)
            out_partial[:, :, c] = value.reshape(line, run, 512)

        each(width // 512, tile_step)
        away(lambda c: c.start())

    def keyed_steps(g):
        each(line - 1, lambda j: keyed_scatter.pass_on(keyed_scatter.rank(j), g))

    early = jnp.where(jnp.logical_and(grid.has_left, grid.has_right), 0, 1)
    lax.fori_loop(0, pairs, pair_step, 0)

    def rest(n, carry):
        scatter.step(n)
        return carry

    lax.fori_loop(3 + (3 * pairs + 1) // 5 - lag, scatter.steps(), rest, 0)

    pl.when(early == 0)(lambda: keyed_steps(pairs // group - 1))
    for copy in norm_copies:
        copy.wait()
    for copy in norm_loads[:2]:
        copy.start()
    scatter.own(branch)
    for copy in norm_loads[:2]:
        copy.wait()
    for h in range(2):
        c = slice(h * half_width, (h + 1) * half_width)
        out_v[:, c] = (middle_v[h * rows : (h + 1) * rows, :] + branch[:, c]).astype(BF)
    keyed_scatter.own(grad_keyed)
    for g in range(pairs // group):
        both = grad_keyed[g * rows : (g + 1) * rows, :]
        first = width + g * 128
        grad_qkv[:, first : first + 128] = turn(both[:, :128], cosine_v, sine_v, 1.0)
        grad_qkv[:, first + narrow : first + narrow + 128] = both[:, 128:].astype(BF)
    for copy in mirrored + swapped[:1]:
        copy.wait()
    away(lambda c: c.wait())
    scatter.finish()
    keyed_scatter.finish()


def back_call(
    places, own_places, queries, keyed_all, middle, grad_normed, tangent, gain, logs, hidden_all, downs,
    weights, cosine, sine, sums,
    mirrors, normed, attended, line,
):
    rows, width = queries.shape
    both = keyed_all.shape[2]
    groups, run = both // 256, weights.shape[1]
    cols, length = downs[0].shape[0], places.shape[1]
    parts = 4
    shapes = jax.ShapeDtypeStruct
    vmem = pl.BlockSpec(memory_space=pltpu.VMEM)
    return pl.pallas_call(
        functools.partial(back_kernel, line, parts),
        out_shape=(
            shapes((rows, width), BF), shapes((rows, width + both), BF), shapes((1, width), F32),
            *(shapes(s.shape, BF) for s in sums), *(shapes((rows, width), BF),) * 4,
            shapes((rows, width), F32), shapes((line, run, width), BF),
        ),
        in_specs=[vmem] * 2 + [ANY] * 21,
        out_specs=(vmem,) * 3 + (ANY,) * 9,
        input_output_aliases={18: 3, 19: 4, 20: 5},
        scratch_shapes=[
            pltpu.VMEM((2 * rows, width), BF), pltpu.VMEM((2 * rows, width), BF),
            pltpu.VMEM((line, run, width), BF),
            pltpu.SemaphoreType.DMA((line,)), pltpu.SemaphoreType.DMA((line,)),
            pltpu.SemaphoreType.DMA((3, 2)), pltpu.VMEM(gain.shape, F32),
            pltpu.VMEM((rows, width), F32), pltpu.VMEM((4, run, width), BF),
            pltpu.VMEM(cosine.shape, F32), pltpu.VMEM(sine.shape, F32),
            pltpu.VMEM((groups * rows, 256), F32),
            pltpu.SemaphoreType.DMA((6,)), pltpu.SemaphoreType.DMA((6,)),
            pltpu.VMEM((rows, width), BF), pltpu.VMEM(keyed_all.shape, BF), pltpu.VMEM((rows, width), BF),
            pltpu.VMEM((rows, length), F32), pltpu.VMEM(logs.shape, F32),
            pltpu.VMEM((2 * rows, length), F32), pltpu.VMEM((2 * rows, length), F32),
            pltpu.VMEM((2 * rows, length), BF), pltpu.VMEM((2 * rows, length), BF),
            pltpu.VMEM((length, 128), F32), pltpu.VMEM((length, 128), F32),
            pltpu.VMEM((2 * cols, width), BF), pltpu.VMEM(hidden_all.shape, BF),
            pltpu.SemaphoreType.DMA((10,)),
            *scatter_scratch(line, rows, width, parts),
            pltpu.VMEM((line, groups * rows, 256), BF), pltpu.VMEM((2 * line - 2, groups * rows, 256), BF),
            pltpu.VMEM((rows, 256), F32),
            pltpu.SemaphoreType.DMA((line, groups)), pltpu.SemaphoreType.DMA((2 * line - 2, groups)),
        ],
        compiler_params=pltpu.CompilerParams(
            collective_id=6, has_side_effects=True, vmem_limit_bytes=62 * 2**20
        ),
        name="back",
    )(
        places, own_places, queries, keyed_all, middle, grad_normed, tangent, gain, logs, hidden_all,
        *downs, weights, cosine, sine, *sums,
        *mirrors, normed, attended,
    )


def body(
    tokens,
    places,
    cotangent,
    gain_attn,
    gain_mlp,
    w_query,
    key_projection,
    value_projection,
    w_out,
    w_gate,
    w_up,
    w_down,
):
    sequence_total, segment_length, width = tokens.shape
    total_length = places.shape[1]
    total_rows = sequence_total * segment_length
    position = lax.axis_index("context")
    local_positions = lax.dynamic_slice_in_dim(places, position * segment_length, segment_length, 1)
    rotary_angles = local_positions.reshape(total_rows).astype(jnp.float32)[:, None] * frequencies(
        HEAD_SIZE // 2
    )
    gain_one, gain_two, query_w, key_weight_local, value_w, out_w = (
        lax.all_gather(gain_attn, ("fsdp", "context"), axis=0, tiled=True),
        lax.all_gather(gain_mlp, ("fsdp", "context"), axis=0, tiled=True),
        lax.all_gather(w_query, ("fsdp", "context"), axis=0, tiled=True),
        lax.all_gather(key_projection, ("fsdp", "context"), axis=0, tiled=True),
        lax.all_gather(value_projection, ("fsdp", "context"), axis=0, tiled=True),
        lax.all_gather(w_out, ("fsdp", "context"), axis=0, tiled=True),
    )
    gain_first = gain_one.astype(jnp.float32)
    gain_second = gain_two.astype(jnp.float32)
    inputs_f = tokens.astype(jnp.float32).reshape(total_rows, width)
    factor_one = lax.rsqrt(jnp.mean(inputs_f * inputs_f, axis=-1, keepdims=True) + norm_eps)
    unit_one = inputs_f * factor_one
    normed_tokens = (unit_one * gain_first).astype(jnp.bfloat16)
    query_pre = jnp.dot(normed_tokens, query_w, preferred_element_type=jnp.float32).reshape(
        total_rows, QUERY_HEADS, HEAD_SIZE
    )
    key_unrotated = jnp.dot(
        normed_tokens, key_weight_local, preferred_element_type=jnp.float32
    ).reshape(total_rows, KEY_VALUE_HEADS, HEAD_SIZE)
    value_matrix_rows = jnp.dot(normed_tokens, value_w, preferred_element_type=jnp.float32).astype(
        jnp.bfloat16
    )
    query_rows = apply_rotary(query_pre, rotary_angles).astype(jnp.bfloat16)
    key_matrix_rows = (
        apply_rotary(key_unrotated, rotary_angles)
        .astype(jnp.bfloat16)
        .reshape(sequence_total, segment_length, KEY_VALUE_HEADS * HEAD_SIZE)
    )
    key_all, value_all = (
        lax.all_gather(key_matrix_rows, "context", axis=1, tiled=True),
        lax.all_gather(
            value_matrix_rows.reshape(sequence_total, segment_length, KEY_VALUE_HEADS * HEAD_SIZE),
            "context",
            axis=1,
            tiled=True,
        ),
    )
    head_query = query_head_rows(query_rows, sequence_total, segment_length)
    head_key = key_heads(key_all, sequence_total, total_length)
    head_value = key_heads(value_all, sequence_total, total_length)
    query_positions = jnp.repeat(local_positions, KEY_VALUE_HEADS, axis=0)
    key_positions = jnp.repeat(places, KEY_VALUE_HEADS, axis=0)
    attended = lax.map(
        forward_head, (head_query, head_key, head_value, query_positions, key_positions)
    )
    attended = merge_queries(attended, sequence_total, segment_length).astype(jnp.bfloat16)
    middle = inputs_f + jnp.dot(attended, out_w, preferred_element_type=jnp.float32)
    factor_two = lax.rsqrt(jnp.mean(middle * middle, axis=-1, keepdims=True) + norm_eps)
    unit_two = middle * factor_two
    normed_mlp = (unit_two * gain_second).astype(jnp.bfloat16)
    tangent = cotangent.reshape(total_rows, width)
    tangent_f = tangent.astype(jnp.float32)
    group = ("fsdp", "context")
    normed_all = lax.all_gather(normed_mlp, group, axis=0, tiled=True)
    tangent_all = lax.all_gather(tangent, group, axis=0, tiled=True)
    branch_part, kept_values = feed_forward(normed_all, w_gate, w_up, w_down)
    grad_part, grad_w_gate, grad_w_up, grad_w_down = feed_back(
        normed_all, tangent_all, w_gate, w_up, w_down, kept_values
    )
    grad_normed = lax.psum_scatter(
        grad_part.astype(jnp.bfloat16), group, scatter_dimension=0, tiled=True
    ).astype(jnp.float32)
    branch = lax.psum_scatter(
        branch_part.astype(jnp.bfloat16), group, scatter_dimension=0, tiled=True
    ).astype(jnp.float32)
    outcome = middle + branch
    scaled_two = grad_normed * gain_second
    term_gain_two = jnp.sum(grad_normed * unit_two, axis=0)
    grad_middle = tangent_f + factor_two * (
        scaled_two - unit_two * jnp.mean(scaled_two * unit_two, axis=-1, keepdims=True)
    )
    grad_branch = grad_middle.astype(jnp.bfloat16)
    term_out = times_t(attended, grad_branch)
    grad_attended = times_nt(grad_branch, out_w).astype(jnp.bfloat16)
    head_grad = query_head_rows(grad_attended, sequence_total, segment_length)
    grad_q, grad_k, grad_v = lax.map(
        backward_head, (head_query, head_key, head_value, head_grad, query_positions, key_positions)
    )
    local_key_gradient, local_value_gradient = (
        lax.psum_scatter(
            merge_keys(grad_k, sequence_total, total_length).astype(jnp.bfloat16),
            "context",
            scatter_dimension=1,
            tiled=True,
        ).astype(jnp.float32),
        lax.psum_scatter(
            merge_keys(grad_v, sequence_total, total_length).astype(jnp.bfloat16),
            "context",
            scatter_dimension=1,
            tiled=True,
        ).astype(jnp.float32),
    )
    grad_query = (
        inverse_rotary(
            merge_queries(grad_q, sequence_total, segment_length).reshape(
                total_rows, QUERY_HEADS, HEAD_SIZE
            ),
            rotary_angles,
        )
        .reshape(total_rows, QUERY_HEADS * HEAD_SIZE)
        .astype(jnp.bfloat16)
    )
    grad_key = (
        inverse_rotary(
            local_key_gradient.reshape(total_rows, KEY_VALUE_HEADS, HEAD_SIZE), rotary_angles
        )
        .reshape(total_rows, KEY_VALUE_HEADS * HEAD_SIZE)
        .astype(jnp.bfloat16)
    )
    value_gradient = local_value_gradient.reshape(total_rows, KEY_VALUE_HEADS * HEAD_SIZE).astype(
        jnp.bfloat16
    )
    grad_normed_one = (
        times_nt(grad_query, query_w)
        + times_nt(grad_key, key_weight_local)
        + times_nt(value_gradient, value_w)
    )
    term_query = times_t(normed_tokens, grad_query)
    term_key = times_t(normed_tokens, grad_key)
    term_value = times_t(normed_tokens, value_gradient)
    scaled_one = grad_normed_one * gain_first
    term_gain_one = jnp.sum(grad_normed_one * unit_one, axis=0)
    grad_inputs = grad_middle + factor_one * (
        scaled_one - unit_one * jnp.mean(scaled_one * unit_one, axis=-1, keepdims=True)
    )
    share_query, share_key, share_value, share_out, share_gain_one, share_gain_two = (
        lax.psum_scatter(term_query.astype(jnp.bfloat16), ("fsdp", "context"), scatter_dimension=0, tiled=True),
        lax.psum_scatter(term_key.astype(jnp.bfloat16), ("fsdp", "context"), scatter_dimension=0, tiled=True),
        lax.psum_scatter(term_value.astype(jnp.bfloat16), ("fsdp", "context"), scatter_dimension=0, tiled=True),
        lax.psum_scatter(term_out.astype(jnp.bfloat16), ("fsdp", "context"), scatter_dimension=0, tiled=True),
        lax.psum_scatter(term_gain_one, ("fsdp", "context"), scatter_dimension=0, tiled=True),
        lax.psum_scatter(term_gain_two, ("fsdp", "context"), scatter_dimension=0, tiled=True),
    )
    summed = (
        lax.psum(share_query.astype(jnp.bfloat16), "replica").astype(jnp.float32),
        lax.psum(share_key.astype(jnp.bfloat16), "replica").astype(jnp.float32),
        lax.psum(share_value.astype(jnp.bfloat16), "replica").astype(jnp.float32),
        lax.psum(share_out.astype(jnp.bfloat16), "replica").astype(jnp.float32),
        lax.psum(grad_w_gate.astype(jnp.bfloat16), "replica").astype(jnp.float32),
        lax.psum(grad_w_up.astype(jnp.bfloat16), "replica").astype(jnp.float32),
        lax.psum(grad_w_down.astype(jnp.bfloat16), "replica").astype(jnp.float32),
        lax.psum(share_gain_one.astype(jnp.bfloat16), "replica").astype(jnp.float32),
        lax.psum(share_gain_two.astype(jnp.bfloat16), "replica").astype(jnp.float32),
    )
    out = outcome.astype(jnp.bfloat16).reshape(sequence_total, segment_length, width)
    grad_tokens = grad_inputs.astype(jnp.bfloat16).reshape(sequence_total, segment_length, width)
    return (
        out,
        grad_tokens,
        summed[0],
        summed[1],
        summed[2],
        summed[3],
        summed[4],
        summed[5],
        summed[6],
        summed[7],
        summed[8],
    )


def kernel_body(
    tokens,
    places,
    cotangent,
    gain_attn,
    gain_mlp,
    w_query,
    key_projection,
    value_projection,
    w_out,
    w_gate,
    w_up,
    w_down,
):
    bf16, f32 = jnp.bfloat16, jnp.float32
    sequence_total, segment_length, width = tokens.shape
    total_length = places.shape[1]
    line = lax.axis_size("context")
    narrow = key_projection.shape[1]
    run = w_query.shape[0]
    swap = [(i, i ^ 1) for i in range(lax.axis_size("fsdp"))]
    gates, ups, downs = ((w, lax.ppermute(w, "fsdp", swap)) for w in (w_gate, w_up, w_down))
    position = lax.axis_index("context")
    local_positions = lax.dynamic_slice_in_dim(places, position * segment_length, segment_length, 1)
    rotary_angles = local_positions.reshape(segment_length).astype(f32)[:, None] * frequencies(
        HEAD_SIZE // 2
    )
    pieces = (w_query, key_projection, value_projection, w_out)
    cosine, sine = jnp.cos(rotary_angles), jnp.sin(rotary_angles)
    cosine = jnp.concatenate([cosine] * 4, axis=1)
    sine = jnp.concatenate([-sine, sine] * 2, axis=1)
    own_places = local_positions.reshape(segment_length, 1)
    places = places.reshape(1, total_length)
    gains = (gain_attn.reshape(1, run), gain_mlp.reshape(1, run))
    tangent = cotangent.reshape(segment_length, width)
    rows = tokens.reshape(segment_length, width)
    (
        attended, middle, normed_mlp, normed_tokens, scaled_query, logs, gain, keyed_all, tangent_all,
        weights,
    ) = front_call(pieces, rows, tangent, cosine, sine, gains, places, own_places, line)
    mid = width + 2 * narrow
    grad_normed, _, hidden_all, *sums = feed_call(normed_mlp, tangent_all, gates, ups, downs, line)[:9]
    out, grad_qkv, term_two, *others = back_call(
        places, own_places, scaled_query, keyed_all, middle, grad_normed, tangent, gain, logs,
        hidden_all, downs, weights, cosine, -sine, sums[:3], sums[3:], normed_tokens, attended, line,
    )
    twins, (grad_branch, grad_middle, out_across) = others[3:6], others[6:]
    grad_w_gate, grad_w_up, grad_w_down = (
        a.astype(f32) + b.astype(f32) for a, b in zip(sums[:3], others[:3])
    )
    packed, grad_w_out, grad_tokens = sums_call(
        normed_tokens, attended, grad_qkv, grad_branch, (*twins, out_across), rows, grad_middle,
        weights, gain, term_two, line,
    )
    gains = packed[run * 3 // 4 : run * 3 // 4 + 2, mid:]
    ends, start = [], 0
    for size in (width, narrow, narrow):
        ends.append(packed[:, start : start + size])
        start += size
    return (
        out.reshape(tokens.shape),
        grad_tokens.reshape(tokens.shape),
        *ends,
        grad_w_out,
        grad_w_gate,
        grad_w_up,
        grad_w_down,
        gains[0],
        gains[1],
    )


def solution(mesh):
    placed = (
        P(("replica", "fsdp"), "context", None),
        P(("replica", "fsdp"), None),
        P(("replica", "fsdp"), "context", None),
        P(("fsdp", "context")),
        P(("fsdp", "context")),
        P(("fsdp", "context"), None),
        P(("fsdp", "context"), None),
        P(("fsdp", "context"), None),
        P(("fsdp", "context"), None),
        P(None, ("fsdp", "context")),
        P(None, ("fsdp", "context")),
        P(("fsdp", "context"), None),
    )
    kernels = (mesh.shape["replica"], mesh.shape["fsdp"], mesh.shape["context"]) == (2, 4, 4)
    return jax.shard_map(
        kernel_body if kernels else body,
        mesh=mesh,
        in_specs=placed,
        out_specs=(
            P(("replica", "fsdp"), "context", None),
            P(("replica", "fsdp"), "context", None),
            P(("fsdp", "context"), None),
            P(("fsdp", "context"), None),
            P(("fsdp", "context"), None),
            P(("fsdp", "context"), None),
            P(None, ("fsdp", "context")),
            P(None, ("fsdp", "context")),
            P(("fsdp", "context"), None),
            P(("fsdp", "context")),
            P(("fsdp", "context")),
        ),
        check_vma=False,
    )
```
